32 devices in a mesh: ctx: 8 (over y, x, core), fsdp: 4 (over z).
Axes of the slice: x: 2, y: 2, z: 4, core: 2. Of those that a mesh axis runs over, the one named last changes fastest.
Arguments:
- layer_input: bfloat16 [4, 1024, 2880], P('fsdp', 'ctx'), may hold values from -6 to 6
- cotangent: bfloat16 [4, 1024, 2880], P('fsdp', 'ctx'), may hold values from -6 to 6
- gate_weights: bfloat16 [4, 1024, 4], P('fsdp', 'ctx'), may hold values from 0.14941406 to 0.34960938
- routes: int32 [4, 1024, 4], P('fsdp', 'ctx'), may hold values from 0 to 7, all different within a row; in each aligned block of 128 rows (0 to 127, 128 to 255, ..., all dimensions but the last counted through in order) at most 68 rows name the same one
- w_query: bfloat16 [2880, 4096], P(None, ('ctx', 'fsdp')), may hold values from -0.109375 to 0.109375
- key_projection: bfloat16 [2880, 512], P(None, ('ctx', 'fsdp')), may hold values from -0.109375 to 0.109375
- value_projection: bfloat16 [2880, 512], P(None, ('ctx', 'fsdp')), may hold values from -0.109375 to 0.109375
- w_out: bfloat16 [4096, 2880], P(('ctx', 'fsdp')), may hold values from -0.5 to 0.5
- b_query: bfloat16 [4096], P(('ctx', 'fsdp')), may hold values from -1.1953125 to 1.1953125
- key_bias_vector: bfloat16 [512], P(('ctx', 'fsdp')), may hold values from -1.1953125 to 1.1953125
- value_bias_vector: bfloat16 [512], P(('ctx', 'fsdp')), may hold values from -1.1953125 to 1.1953125
- b_out: bfloat16 [2880], replicated, may hold values from -0.59765625 to 0.59765625
- learned_sink_logits: bfloat16 [64], replicated, may hold values from 1 to 5
- gain_attn: bfloat16 [2880], replicated, may hold values from 0.5 to 1.5
- gain_ffn: bfloat16 [2880], replicated, may hold values from 0.5 to 1.5
- w_gate: bfloat16 [8, 2880, 2880], P('ctx', None, 'fsdp'), may hold values from -0.109375 to 0.109375
- w_up: bfloat16 [8, 2880, 2880], P('ctx', None, 'fsdp'), may hold values from -0.109375 to 0.109375
- w_down: bfloat16 [8, 2880, 2880], P('ctx', 'fsdp'), may hold values from -0.109375 to 0.109375
- b_gate: bfloat16 [8, 2880], P('ctx', 'fsdp'), may hold values from -0.59765625 to 0.59765625
- b_up: bfloat16 [8, 2880], P('ctx', 'fsdp'), may hold values from -0.59765625 to 0.59765625
- b_down: bfloat16 [8, 2880], P('ctx', 'fsdp'), may hold values from -0.59765625 to 0.59765625
Outputs:
- final_out: bfloat16 [4, 1024, 2880], P('fsdp', 'ctx')
- input_grad: float32 [4, 1024, 2880], P('fsdp', 'ctx')
- grad_w_query: float32 [2880, 4096], P(None, ('ctx', 'fsdp'))
- grad_w_key: float32 [2880, 512], P(None, ('ctx', 'fsdp'))
- grad_w_value: float32 [2880, 512], P(None, ('ctx', 'fsdp'))
- grad_w_out: float32 [4096, 2880], P(('ctx', 'fsdp'))
- grad_b_query: float32 [4096], P(('ctx', 'fsdp'))
- grad_b_key: float32 [512], P(('ctx', 'fsdp'))
- grad_b_value: float32 [512], P(('ctx', 'fsdp'))
- grad_b_out: float32 [2880], replicated
- grad_sink_logits: float32 [64], replicated
- grad_gain_attn: float32 [2880], replicated
- grad_gain_ffn: float32 [2880], replicated
- grad_w_gate: float32 [8, 2880, 2880], P('ctx', None, 'fsdp')
- grad_w_up: float32 [8, 2880, 2880], P('ctx', None, 'fsdp')
- grad_w_down: float32 [8, 2880, 2880], P('ctx', 'fsdp')
- grad_b_gate: float32 [8, 2880], P('ctx', 'fsdp')
- grad_b_up: float32 [8, 2880], P('ctx', 'fsdp')
- grad_b_down: float32 [8, 2880], P('ctx', 'fsdp')
The draws below stay inside these ranges and needn't reach their ends.
Inputs may be any that keep to these rules, and one draw needn't show every extreme that they name: `routes`: each row names 4 different experts. Among the rows of one device no expert is named by more than 68 rows, a bound that some block reaches.
All inputs are finite; a program needn't handle non-finite values.
Results may differ from the reference program's by a relative error of at most 0.019.
Values may be sent and summed in bfloat16 or wider, within the bound.
A program may use at most 512 MiB of HBM per device.

```python
import math
import jax
import jax.numpy as jnp
import numpy as np
from jax import lax

MODEL_DIM = 2880
F = 2880
QUERY_HEADS = 64
KEY_VALUE_HEADS = 8
HEAD_SIZE = 64
TOP = 4
TOK_DEV = 128
SEQUENCE_LENGTH = 1024
SEQUENCE_COUNT = 4
EXPERTS = 8
CAP = 68


def steps_of(key, extent, cuts, least, high):
    def one(axis_at, shards_of):
        heights = jax.random.uniform(jax.random.fold_in(jax.random.fold_in(key, 6), axis_at), (shards_of,), jnp.float32, least / len(cuts), high / len(cuts))
        return jnp.repeat(jnp.exp(heights), extent[axis_at] // shards_of).reshape((-1,) + (1,) * (len(extent) - axis_at - 1))

    level = one(*cuts[0])
    for cut in cuts[1:]:
        level = level * one(*cut)
    return level


def shared_out(stream_key, own, number, rows, count, top, reach, skew):
    sequence = jax.random.permutation(stream_key, count)
    heavy_load, ordinary = portions_of(count, rows * top, reach, skew, True), portions_of(count, rows * top, reach, skew, False)
    places = jnp.arange(count)

    def named(tallies, turn):
        used = int((tallies > 0).sum())
        fixed = max(1, used // 4)
        shifted = fixed + (places - fixed + turn * (used - fixed)) % max(1, count - fixed)
        return jnp.zeros((count,), jnp.int32).at[sequence[jnp.where(places < fixed, places, shifted)]].set(jnp.asarray(tallies, jnp.int32))

    tallies = jnp.where(number % 4 == 0, named(heavy_load, number // 4), named(ordinary, number - number // 4 - 1))
    mixed = jax.random.permutation(jax.random.fold_in(own, 3), count)
    donor, taker = mixed[0:count // 2 * 2:2], mixed[1:count // 2 * 2:2]
    margin = jnp.minimum(tallies[donor] - 1, reach - tallies[taker]) // 2
    margin = jnp.where((donor == sequence[0]) | (taker == sequence[0]) | (tallies[taker] == 0), 0, jnp.maximum(margin, 0))
    shifted = jax.random.randint(jax.random.fold_in(own, 4), (count // 2,), 0, 1 << 20) % (margin + 1)
    tallies = tallies.at[donor].add(-shifted).at[taker].add(shifted)
    items = jnp.searchsorted(jnp.cumsum(tallies), jnp.arange(rows * top), side="right").astype(jnp.int32)
    grid = items.reshape(top, rows).T
    grid = grid[jax.random.permutation(jax.random.fold_in(own, 1), rows)]
    turn = jax.random.randint(jax.random.fold_in(own, 2), (rows, 1), 0, top)
    return jnp.take_along_axis(grid, (jnp.arange(top)[None, :] + turn) % top, axis=1)


def portions_of(number_of, total, most, slope, full):
    loads = [(1 << 20) // math.isqrt(rank ** slope) + 1 for rank in range(1, number_of + 1)]
    largest = most if full else min(most, max(-(-total // number_of), total * loads[0] // sum(loads)))
    least = 1 if total - largest >= number_of - 1 else 0
    given, surplus = [largest] + [least] * (number_of - 1), total - largest - least * (number_of - 1)
    while surplus > 0:
        free = [i for i in range(1, number_of) if given[i] < largest] or [i for i in range(1, number_of) if given[i] < most]
        pool, budget = sum([loads[i] for i in free]), surplus
        for i in free:
            addition = min(most - given[i], max(1, budget * loads[i] // pool), surplus)
            given[i] = given[i] + addition
            surplus = surplus - addition
    return np.array(given)


def bell_draw(own_key, extent, deviation, reach, cuts=(), kind=jnp.bfloat16):
    drawn = deviation * jax.random.normal(own_key, extent, jnp.float32)
    if cuts:
        drawn = drawn * steps_of(own_key, extent, cuts, -0.22, 0.18)
    return jnp.clip(drawn, -reach, reach).astype(kind)


def setup_inputs(seed: int = 0) -> dict:
    keys = jax.random.split(jax.random.key(seed), 22)
    layer_input = bell_draw(keys[0], (SEQUENCE_COUNT, SEQUENCE_LENGTH, MODEL_DIM), 1.0, 6.0, ((0, 4), (1, 8)))
    cotangent = bell_draw(keys[1], (SEQUENCE_COUNT, SEQUENCE_LENGTH, MODEL_DIM), 1.0, 6.0, ((0, 4), (1, 8)))
    gate_weights = jnp.clip(0.14941406 + 0.20019531 * jax.random.uniform(keys[2], (SEQUENCE_COUNT, SEQUENCE_LENGTH, TOP), jnp.float32) ** steps_of(keys[2], (SEQUENCE_COUNT, SEQUENCE_LENGTH, TOP), ((0, 4), (1, 8)), -0.2, 0.2), 0.14941406, 0.34960938).astype(jnp.bfloat16)
    routes_keys = jax.random.split(jax.random.fold_in(keys[3], 1), SEQUENCE_COUNT * SEQUENCE_LENGTH // TOK_DEV)
    routes_turns = jax.random.permutation(jax.random.fold_in(keys[3], 3), SEQUENCE_COUNT * SEQUENCE_LENGTH // TOK_DEV)
    routes = jax.vmap(lambda own, number: shared_out(jax.random.fold_in(keys[3], 2), own, number, TOK_DEV, EXPERTS, TOP, CAP, 1))(routes_keys, routes_turns).reshape((SEQUENCE_COUNT, SEQUENCE_LENGTH, TOP))
    w_query = bell_draw(keys[4], (MODEL_DIM, QUERY_HEADS * HEAD_SIZE), MODEL_DIM ** -0.5, 0.109375, ((1, 32),))
    key_projection = bell_draw(keys[5], (MODEL_DIM, KEY_VALUE_HEADS * HEAD_SIZE), MODEL_DIM ** -0.5, 0.109375, ((1, 32),))
    value_projection = bell_draw(keys[6], (MODEL_DIM, KEY_VALUE_HEADS * HEAD_SIZE), MODEL_DIM ** -0.5, 0.109375, ((1, 32),))
    w_out = bell_draw(keys[7], (QUERY_HEADS * HEAD_SIZE, MODEL_DIM), (2 * HEAD_SIZE) ** -0.5, 0.5, ((0, 32),))
    b_query = bell_draw(keys[8], (QUERY_HEADS * HEAD_SIZE,), 0.2, 1.1953125, ((0, 32),))
    key_bias_vector = bell_draw(keys[9], (KEY_VALUE_HEADS * HEAD_SIZE,), 0.2, 1.1953125, ((0, 32),))
    value_bias_vector = bell_draw(keys[10], (KEY_VALUE_HEADS * HEAD_SIZE,), 0.2, 1.1953125, ((0, 32),))
    b_out = bell_draw(keys[11], (MODEL_DIM,), 0.1, 0.59765625)
    learned_sink_logits = jnp.clip(jax.random.uniform(keys[12], (QUERY_HEADS,), jnp.float32, 1.0, 5.0), 1.0, 5.0).astype(jnp.bfloat16)
    gain_attn = jnp.clip(1.0 + 0.1 * jax.random.normal(keys[13], (MODEL_DIM,), jnp.float32), 0.5, 1.5).astype(jnp.bfloat16)
    gain_ffn = jnp.clip(1.0 + 0.1 * jax.random.normal(keys[14], (MODEL_DIM,), jnp.float32), 0.5, 1.5).astype(jnp.bfloat16)
    w_gate = bell_draw(keys[15], (EXPERTS, MODEL_DIM, F), MODEL_DIM ** -0.5, 0.109375, ((0, 8), (2, 4)))
    w_up = bell_draw(keys[16], (EXPERTS, MODEL_DIM, F), MODEL_DIM ** -0.5, 0.109375, ((0, 8), (2, 4)))
    w_down = bell_draw(keys[17], (EXPERTS, F, MODEL_DIM), F ** -0.5, 0.109375, ((0, 8), (1, 4)))
    b_gate = bell_draw(keys[18], (EXPERTS, F), 0.1, 0.59765625, ((0, 8), (1, 4)))
    b_up = bell_draw(keys[19], (EXPERTS, F), 0.1, 0.59765625, ((0, 8), (1, 4)))
    b_down = bell_draw(keys[20], (EXPERTS, MODEL_DIM), 0.1, 0.59765625, ((0, 8), (1, 4)))
    return dict(layer_input=layer_input, cotangent=cotangent, gate_weights=gate_weights, routes=routes, w_query=w_query, key_projection=key_projection, value_projection=value_projection, w_out=w_out, b_query=b_query, key_bias_vector=key_bias_vector, value_bias_vector=value_bias_vector, b_out=b_out, learned_sink_logits=learned_sink_logits, gain_attn=gain_attn, gain_ffn=gain_ffn, w_gate=w_gate, w_up=w_up, w_down=w_down, b_gate=b_gate, b_up=b_up, b_down=b_down)


EPSILON = 1e-05
THETA_BASE = 150000.0
CLAMP_LIMIT = 7.0
GLU_ALPHA = 1.702
MASK_FILL = -1e+30

@jax.custom_vjp
def reduced_precision(v):
    return lax.optimization_barrier(v.astype(jnp.bfloat16)).astype(jnp.float32)

@jax.custom_vjp
def low_back(v):
    return v

def low_keep(v):
    return (reduced_precision(v), None)

def low_pass(kept, grad):
    return (grad,)

def back_keep(v):
    return (v, None)

def back_low(kept, grad):
    return (reduced_precision(grad),)
reduced_precision.defvjp(low_keep, low_pass)
low_back.defvjp(back_keep, back_low)

def matmul_high(left_mat, right_mat):
    return jnp.dot(left_mat, right_mat, precision=lax.Precision.HIGHEST)

def norm_scale(value_rows, gain_vec):
    return value_rows * lax.rsqrt(lax.optimization_barrier(jnp.mean(value_rows * value_rows, axis=-1, keepdims=True)) + EPSILON) * gain_vec

def rotary_tables(positions, half_dim):
    inverse = THETA_BASE ** (-jnp.arange(half_dim, dtype=jnp.float32) / half_dim)
    angles = positions.astype(jnp.float32)[:, None] * inverse[None, :]
    return (jnp.cos(angles)[:, None, :], jnp.sin(angles)[:, None, :])

def apply_rotary(value_rows, cosine_lookup, sine_lookup):
    half_dim = value_rows.shape[-1] // 2
    first_half = value_rows[..., :half_dim]
    second_half = value_rows[..., half_dim:]
    return jnp.concatenate([first_half * cosine_lookup - second_half * sine_lookup, second_half * cosine_lookup + first_half * sine_lookup], axis=-1)

def soft_clamp(value_rows):
    return CLAMP_LIMIT * jnp.tanh(value_rows / CLAMP_LIMIT)

def glu_units(gate_lin, up_lin):
    gated = soft_clamp(gate_lin)
    return (soft_clamp(up_lin) + 1.0) * gated * jax.nn.sigmoid(GLU_ALPHA * gated)

def slot_places(route_rows, experts, capacity):
    expert_hits = (route_rows[:, None] == jnp.arange(experts, dtype=jnp.int32)[None, :]).astype(jnp.int32)
    before = jnp.cumsum(expert_hits, axis=0) - expert_hits
    return (route_rows * capacity + lax.optimization_barrier(jnp.sum(before * expert_hits, axis=1))).astype(jnp.int32)

def sequence_attention(query_sequence, k_seq, v_seq, heads_sink_logit):
    sequence_length = query_sequence.shape[0]
    heads_of_queries = query_sequence.reshape(sequence_length, KEY_VALUE_HEADS, QUERY_HEADS // KEY_VALUE_HEADS, HEAD_SIZE).transpose(1, 2, 0, 3)
    heads_of_keys = k_seq.transpose(1, 0, 2)
    heads_of_values = v_seq.transpose(1, 0, 2)
    visible = jnp.arange(sequence_length)[None, :] <= jnp.arange(sequence_length)[:, None]

    def one_head(pieces):
        query_head, key_head, value_head, sink_logit = pieces
        scores = low_back(jnp.einsum('gtd,ld->gtl', query_head, key_head, precision=lax.Precision.HIGHEST) * HEAD_SIZE ** (-0.5))
        scores = jnp.where(visible[None], scores, MASK_FILL)
        row_top = jnp.maximum(lax.optimization_barrier(jnp.max(scores, axis=-1)), sink_logit[:, None])
        weights = jnp.where(visible[None], jnp.exp(scores - row_top[..., None]), 0.0)
        denominator = lax.optimization_barrier(jnp.sum(weights, axis=-1)) + jnp.exp(sink_logit[:, None] - row_top)
        probabilities = reduced_precision(weights / denominator[..., None])
        return jnp.einsum('gtl,ld->gtd', probabilities, value_head, precision=lax.Precision.HIGHEST)
    head_out = lax.map(jax.checkpoint(one_head), (heads_of_queries, heads_of_keys, heads_of_values, heads_sink_logit))
    return head_out.transpose(2, 0, 1, 3).reshape(sequence_length, QUERY_HEADS * HEAD_SIZE)

def expert_rows(pieces):
    row_block, gate_weight, up_weight, down_weight, gate_bias, up_bias, down_bias = pieces
    gate_lin = low_back(matmul_high(row_block, gate_weight) + gate_bias)
    up_lin = low_back(matmul_high(row_block, up_weight) + up_bias)
    hidden_units = reduced_precision(glu_units(gate_lin, up_lin))
    return reduced_precision(low_back(matmul_high(hidden_units, down_weight) + down_bias))

def expert_layer(normed_ffn, w_gate, w_up, w_down, b_gate, b_up, b_down, gate_vals, routes):
    groups = SEQUENCE_COUNT * SEQUENCE_LENGTH // TOK_DEV
    normed_groups = normed_ffn.reshape(groups, TOK_DEV, MODEL_DIM)
    route_groups = routes.reshape(groups, TOK_DEV * TOP)
    gate_groups = gate_vals.reshape(groups, TOK_DEV * TOP)
    places = jax.vmap(lambda route_rows: slot_places(route_rows, EXPERTS, CAP))(route_groups)
    copies = low_back(jnp.repeat(normed_groups, TOP, axis=1))
    buffer = jax.vmap(lambda copy_rows, place_rows: jnp.zeros((EXPERTS * CAP, MODEL_DIM), jnp.float32).at[place_rows].set(copy_rows))(copies, places)
    slot_rows = buffer.reshape(groups, EXPERTS, CAP, MODEL_DIM).transpose(1, 0, 2, 3).reshape(EXPERTS, groups * CAP, MODEL_DIM)
    outputs = lax.map(jax.checkpoint(expert_rows), (slot_rows, w_gate, w_up, w_down, b_gate, b_up, b_down))
    returned = outputs.reshape(EXPERTS, groups, CAP, MODEL_DIM).transpose(1, 0, 2, 3).reshape(groups, EXPERTS * CAP, MODEL_DIM)
    picked = jnp.take_along_axis(returned, places[..., None], axis=1)
    mixed_rows = lax.optimization_barrier(jnp.sum((picked * gate_groups[..., None]).reshape(groups, TOK_DEV, TOP, MODEL_DIM), axis=2))
    return mixed_rows.reshape(SEQUENCE_COUNT, SEQUENCE_LENGTH, MODEL_DIM)

def block_forward(layer_input, w_query, key_projection, value_projection, w_out, b_query, key_bias_vector, value_bias_vector, b_out, learned_sink_logits, gain_attn, gain_ffn, w_gate, w_up, w_down, b_gate, b_up, b_down, gate_vals, routes):
    normed_attn = reduced_precision(norm_scale(layer_input, gain_attn))
    query_lin = low_back(matmul_high(normed_attn, w_query) + b_query)
    key_linear = low_back(matmul_high(normed_attn, key_projection) + key_bias_vector)
    value_linear = low_back(matmul_high(normed_attn, value_projection) + value_bias_vector)
    cosine_lookup, sine_lookup = rotary_tables(jnp.arange(SEQUENCE_LENGTH, dtype=jnp.int32), HEAD_SIZE // 2)
    query_rows = reduced_precision(apply_rotary(query_lin.reshape(SEQUENCE_COUNT, SEQUENCE_LENGTH, QUERY_HEADS, HEAD_SIZE), cosine_lookup, sine_lookup))
    key_rows = reduced_precision(apply_rotary(key_linear.reshape(SEQUENCE_COUNT, SEQUENCE_LENGTH, KEY_VALUE_HEADS, HEAD_SIZE), cosine_lookup, sine_lookup))
    value_rows = reduced_precision(value_linear.reshape(SEQUENCE_COUNT, SEQUENCE_LENGTH, KEY_VALUE_HEADS, HEAD_SIZE))
    heads_sink_logit = learned_sink_logits.reshape(KEY_VALUE_HEADS, QUERY_HEADS // KEY_VALUE_HEADS)
    attended = lax.map(lambda pieces: sequence_attention(pieces[0], pieces[1], pieces[2], heads_sink_logit), (query_rows, key_rows, value_rows))
    attended = reduced_precision(low_back(attended))
    branch = low_back(matmul_high(attended, w_out) + b_out)
    middle = layer_input + branch
    normed_ffn = reduced_precision(norm_scale(middle, gain_ffn))
    expert_mix = expert_layer(normed_ffn, w_gate, w_up, w_down, b_gate, b_up, b_down, gate_vals, routes)
    return middle + expert_mix

def reference(layer_input, cotangent, gate_weights, routes, w_query, key_projection, value_projection, w_out, b_query, key_bias_vector, value_bias_vector, b_out, learned_sink_logits, gain_attn, gain_ffn, w_gate, w_up, w_down, b_gate, b_up, b_down):
    gate_vals = gate_weights.astype(jnp.float32)

    def forward(input_float, *weights_float):
        return block_forward(input_float, *weights_float, gate_vals, routes)
    weight_list = (w_query, key_projection, value_projection, w_out, b_query, key_bias_vector, value_bias_vector, b_out, learned_sink_logits, gain_attn, gain_ffn, w_gate, w_up, w_down, b_gate, b_up, b_down)
    final_f32, pullback = jax.vjp(forward, layer_input.astype(jnp.float32), *[weight.astype(jnp.float32) for weight in weight_list])
    gradients = pullback(cotangent.astype(jnp.float32))
    return (final_f32.astype(jnp.bfloat16), gradients[0], gradients[1], gradients[2], gradients[3], gradients[4], gradients[5], gradients[6], gradients[7], gradients[8], gradients[9], gradients[10], gradients[11], gradients[12], gradients[13], gradients[14], gradients[15], gradients[16], gradients[17])
```

```python
import jax
import jax.numpy as jnp
from jax import lax
from jax.experimental import pallas as pl
from jax.experimental.pallas import tpu as pltpu
from jax.sharding import PartitionSpec as P

MESH = pl.DeviceIdType.MESH
MIB = 1 << 20


def remote(src, dst, send_sem, recv_sem, device):
    return pltpu.make_async_remote_copy(
        src_ref=src,
        dst_ref=dst,
        send_sem=send_sem,
        recv_sem=recv_sem,
        device_id=device,
        device_id_type=MESH,
    )


def neighbours():
    me = lax.axis_index("ctx")
    core = lax.rem(me, 2)
    x_at = lax.rem(me // 2, 2)
    y_at = me // 4
    return me, me + 1 - 2 * core, me + 2 - 4 * x_at, me + 4 - 8 * y_at, 2 - 4 * x_at


def greet(others, line, z_at):
    barrier = pltpu.get_barrier_semaphore()
    for other in others:
        pl.semaphore_signal(barrier, 1, device_id=(other, z_at), device_id_type=MESH)
    if line == 1:
        pl.semaphore_wait(barrier, len(others))
        return
    me = lax.axis_index("ctx")

    @pl.when(z_at > 0)
    def _():
        pl.semaphore_signal(barrier, 1, device_id=(me, z_at - 1), device_id_type=MESH)

    @pl.when(z_at < line - 1)
    def _():
        pl.semaphore_signal(barrier, 1, device_id=(me, z_at + 1), device_id_type=MESH)

    inner = (lax.rem(z_at, 3) + 1) // 2
    pl.semaphore_wait(barrier, len(others) + 1 + inner)


def gather_kernel(line, x_ref, o_ref, own_sem, z_send, z_recv, p_send, p_recv):
    z_at = lax.axis_index("fsdp") if line > 1 else lax.axis_index("fsdp")
    me, mate, near_x, near_y, step_x = neighbours()
    across = near_y + step_x
    rows = x_ref.shape[0]
    half = rows // 2
    top, low = pl.ds(0, half), pl.ds(half, half)
    greet((mate, near_x, near_y), line, z_at)
    if line == 1:
        slots = [0]
        keep = 0
    else:
        slots = [z_at, z_at + 1 - 2 * lax.rem(z_at, 2), 2 - z_at // 2, 3 - 3 * (z_at // 2)]
        keep = z_at
    own = pltpu.make_async_copy(x_ref, o_ref.at[keep, me], own_sem)
    own.start()
    middle = (z_at == 1) | (z_at == 2) if line > 1 else None

    def z_copy(src_ref, slot, way, target):
        return remote(
            src_ref, o_ref.at[slot, me], z_send.at[slot, way], z_recv.at[slot], (me, target)
        )

    def up():
        return z_copy(x_ref, z_at, 0, z_at + 1)

    def down():
        return z_copy(x_ref, z_at, 1, z_at - 1)

    def onward(order):
        slot = slots[order]
        target = 3 - z_at if order == 1 else 3 * z_at - 3
        return z_copy(o_ref.at[slot, me], slot, 0, target)

    def from_line(order):
        slot = slots[order]
        return z_copy(o_ref.at[slot, me], slot, 0, 0)

    def pieces(order):
        slot = slots[order]
        source = x_ref if order == 0 else o_ref.at[slot, me]

        def copy(src_ref, place, kind, device, part=None):
            dst_ref = o_ref.at[slot, place]
            if part is not None:
                src_ref, dst_ref = src_ref.at[part], dst_ref.at[part]
            return remote(
                src_ref, dst_ref, p_send.at[order, kind], p_recv.at[order, kind], (device, z_at)
            )

        def there(place):
            return o_ref.at[slot, place]

        return dict(
            out_x=copy(source, me, 0, near_x),
            out_y=copy(source, me, 1, near_y),
            out_m=copy(source, me, 2, mate),
            fwd_y=copy(there(near_x), near_x, 3, near_y, top),
            fwd_x=copy(there(near_y), near_y, 4, near_x, low),
            m_x=copy(there(near_x), near_x, 5, mate),
            m_y=copy(there(near_y), near_y, 6, mate),
            m_top=copy(there(across), across, 7, mate, top),
            m_low=copy(there(across), across, 8, mate, low),
            in_x=copy(there(near_x), near_x, 0, near_x),
            in_y=copy(there(near_y), near_y, 1, near_y),
            in_m=copy(there(mate), mate, 2, mate),
            in_top=copy(there(across), across, 3, near_y, top),
            in_low=copy(there(across), across, 4, near_x, low),
            in_mx=copy(there(near_x), near_x, 5, mate),
            in_my=copy(there(near_y), near_y, 6, mate),
            in_mt=copy(there(across), across, 7, mate, top),
            in_ml=copy(there(across), across, 8, mate, low),
        )

    parts = [pieces(order) for order in range(line)]

    def first(order):
        if order > 0:
            from_line(order).wait_recv()

            @pl.when(middle)
            def _():
                onward(order).start()
        else:
            if line > 1:

                @pl.when(z_at < line - 1)
                def _():
                    up().start()

                @pl.when(z_at > 0)
                def _():
                    down().start()

        for name in ("out_x", "out_y", "out_m"):
            parts[order][name].start()

    def second(order):
        piece = parts[order]
        piece["in_x"].wait_recv()
        piece["fwd_y"].start()
        piece["m_x"].start()
        piece["in_y"].wait_recv()
        piece["fwd_x"].start()
        piece["m_y"].start()

    def third(order):
        piece = parts[order]
        piece["in_top"].wait_recv()
        piece["m_top"].start()
        piece["in_low"].wait_recv()
        piece["m_low"].start()

    for order in range(line + 2):
        if order < line:
            first(order)
        if 0 <= order - 1 < line:
            second(order - 1)
        if 0 <= order - 2 < line:
            third(order - 2)
    for order in range(line):
        piece = parts[order]
        for name in ("in_m", "in_mx", "in_my", "in_mt", "in_ml"):
            piece[name].wait_recv()
        for name in ("out_x", "out_y", "out_m", "fwd_y", "fwd_x", "m_x", "m_y", "m_top", "m_low"):
            piece[name].wait_send()
    if line > 1:

        @pl.when(z_at < line - 1)
        def _():
            up().wait_send()

        @pl.when(z_at > 0)
        def _():
            down().wait_send()

        @pl.when(middle)
        def _():
            for order in range(1, line):
                onward(order).wait_send()

    own.wait()


def gather_blocks(x, line, collective, name):
    rows, width = x.shape

    def kernel(*refs):
        gather_kernel(line, *refs)

    return pl.pallas_call(
        kernel,
        out_shape=jax.ShapeDtypeStruct((line, 8, rows, width), x.dtype),
        in_specs=[pl.BlockSpec(memory_space=pl.ANY)],
        out_specs=pl.BlockSpec(memory_space=pl.ANY),
        scratch_shapes=[
            pltpu.SemaphoreType.DMA,
            pltpu.SemaphoreType.DMA((line, 2)),
            pltpu.SemaphoreType.DMA((line,)),
            pltpu.SemaphoreType.DMA((line, 9)),
            pltpu.SemaphoreType.DMA((line, 9)),
        ],
        compiler_params=pltpu.CompilerParams(collective_id=collective, has_side_effects=True),
        name=name,
    )(x)


def scatter_kernel(
    line, x_ref, o_ref, mine, theirs, halves, from_x, from_y, from_z, total,
    load_sem, m_send, m_recv, p_send, p_recv, z_send, z_recv, out_sem,
):
    z_at = lax.axis_index("fsdp")
    me, mate, near_x, near_y, step_x = neighbours()
    across = near_y + step_x
    rows = x_ref.shape[2]
    half = rows // 2
    top, low = pl.ds(0, half), pl.ds(half, half)
    greet((mate, near_x, near_y), line, z_at)
    if line == 1:
        slots = [0]
    else:
        slots = [3 - 3 * (z_at // 2), 2 - z_at // 2, z_at + 1 - 2 * lax.rem(z_at, 2), z_at]
    middle = (z_at == 1) | (z_at == 2)
    mine_at = (across, near_x, near_y, me)
    mate_step = mate - me
    loads, gives = [], []
    for order in range(line):
        for k in range(4):
            give = remote(
                x_ref.at[slots[order], mine_at[k] + mate_step],
                theirs.at[order, k],
                m_send.at[order, k],
                m_recv.at[order, k],
                (mate, z_at),
            )
            load = pltpu.make_async_copy(
                x_ref.at[slots[order], mine_at[k]], mine.at[order, k], load_sem.at[order, k]
            )
            give.start()
            load.start()
            gives.append(give)
            loads.append(load)
    chunk = 16

    def add(dst_ref, src_refs, start, count):
        def body(i, carry):
            at = pl.ds(pl.multiple_of(start + i * chunk, chunk), chunk)
            value = dst_ref[at, :].astype(jnp.float32)
            for src_ref in src_refs:
                value = value + src_ref[at, :].astype(jnp.float32)
            dst_ref[at, :] = value.astype(dst_ref.dtype)
            return carry

        lax.fori_loop(0, count // chunk, body, 0)

    def copies(order):
        def send(kind, src_ref, dst_ref, device):
            return remote(
                src_ref, dst_ref, p_send.at[order, kind], p_recv.at[order, kind], (device, z_at)
            )

        return dict(
            a_top=send(0, mine.at[order, 0, top], halves.at[order, top], near_x),
            a_low=send(1, mine.at[order, 0, low], halves.at[order, low], near_y),
            x_top=send(2, mine.at[order, 1, top], from_x.at[order, top], near_x),
            x_low=send(3, mine.at[order, 1, low], from_x.at[order, low], near_x),
            y_low=send(4, mine.at[order, 2, low], from_y.at[order, low], near_y),
            y_top=send(5, mine.at[order, 2, top], from_y.at[order, top], near_y),
        )

    parts = [copies(order) for order in range(line)]

    def first(order):
        piece = parts[order]
        for k in range(4):
            gives[order * 4 + k].wait_recv()
            loads[order * 4 + k].wait()
            add(mine.at[order, k], [theirs.at[order, k]], 0, rows)
            if k == 0:
                piece["a_top"].start()
                piece["a_low"].start()
            if k == 1:
                piece["x_top"].start()
            if k == 2:
                piece["y_low"].start()

    def second(order):
        piece = parts[order]
        piece["a_low"].wait_recv()
        add(mine.at[order, 1], [halves.at[order]], half, half)
        piece["x_low"].start()
        piece["a_top"].wait_recv()
        add(mine.at[order, 2], [halves.at[order]], 0, half)
        piece["y_top"].start()

    def z_copy(order, slot_at, target):
        return remote(
            mine.at[order, 3], from_z.at[slot_at], z_send.at[order], z_recv.at[slot_at], (me, target)
        )

    def z_out(order):
        if order == 2:
            target = slots[2]
        else:
            target = z_at + 1 - 2 * (z_at // 2)
        slot_at = slots[order]
        ends = jnp.where(target == slot_at, 1, 0)
        slot_at = ends * (4 + (z_at - target + 1) // 2) + (1 - ends) * slot_at
        return z_copy(order, slot_at, target)

    def third(order):
        piece = parts[order]
        for name in ("x_top", "x_low", "y_top", "y_low"):
            piece[name].wait_recv()
        add(mine.at[order, 3], [from_x.at[order], from_y.at[order]], 0, rows)

    def pass_on(order):
        z_copy(order, slots[order], z_at).wait_recv()
        add(mine.at[order, 3], [from_z.at[slots[order]]], 0, rows)
        z_out(order).start()

    def last(order):
        @pl.when(z_at > 0)
        def _():
            z_copy(order, 4, z_at).wait_recv()

        @pl.when(z_at < line - 1)
        def _():
            z_copy(order, 5, z_at).wait_recv()

        def finish(slots_in):
            def body(i, carry):
                at = pl.ds(pl.multiple_of(i * chunk, chunk), chunk)
                value = mine[order, 3, at, :].astype(jnp.float32)
                for slot_in in slots_in:
                    value = value + from_z[slot_in, at, :].astype(jnp.float32)
                total[at, :] = value
                return carry

            lax.fori_loop(0, rows // chunk, body, 0)

        pl.when(z_at == 0)(lambda: finish([5]))
        pl.when(z_at == line - 1)(lambda: finish([4]))
        pl.when(middle)(lambda: finish([4, 5]))

    def plane_finish():
        def body(i, carry):
            at = pl.ds(pl.multiple_of(i * chunk, chunk), chunk)
            value = mine[0, 3, at, :].astype(jnp.float32)
            value = value + from_x[0, at, :].astype(jnp.float32)
            total[at, :] = value + from_y[0, at, :].astype(jnp.float32)
            return carry

        for name in ("x_top", "x_low", "y_top", "y_low"):
            parts[0][name].wait_recv()
        lax.fori_loop(0, rows // chunk, body, 0)

    if line == 1:
        first(0)
        second(0)
        plane_finish()
    else:
        first(0)
        for order in range(line):
            second(order)
            if order + 1 < line:
                first(order + 1)
            third(order)
            if order + 1 < line:

                @pl.when(jnp.logical_not(middle))
                def _():
                    z_out(order).start()

                if order > 0:

                    @pl.when(middle)
                    def _():
                        for late in (0,) if order == 1 else (1, 2):
                            pass_on(late)

        last(line - 1)
    out = pltpu.make_async_copy(total, o_ref, out_sem)
    out.start()
    for give in gives:
        give.wait_send()
    for piece in parts:
        for copy in piece.values():
            copy.wait_send()
    for order in range(line - 1):
        z_out(order).wait_send()
    out.wait()


def scatter_blocks(x, collective, name):
    line, eight, rows, width = x.shape

    def kernel(*refs):
        scatter_kernel(line, *refs)

    shard = (rows, width)
    return pl.pallas_call(
        kernel,
        out_shape=jax.ShapeDtypeStruct(shard, jnp.float32),
        in_specs=[pl.BlockSpec(memory_space=pl.ANY)],
        out_specs=pl.BlockSpec(memory_space=pl.ANY),
        scratch_shapes=[
            pltpu.VMEM((line, 4) + shard, x.dtype),
            pltpu.VMEM((line, 4) + shard, x.dtype),
            pltpu.VMEM((line,) + shard, x.dtype),
            pltpu.VMEM((line,) + shard, x.dtype),
            pltpu.VMEM((line,) + shard, x.dtype),
            pltpu.VMEM((6 if line > 1 else 1,) + shard, x.dtype),
            pltpu.VMEM(shard, jnp.float32),
            pltpu.SemaphoreType.DMA((line, 4)),
            pltpu.SemaphoreType.DMA((line, 4)),
            pltpu.SemaphoreType.DMA((line, 4)),
            pltpu.SemaphoreType.DMA((line, 6)),
            pltpu.SemaphoreType.DMA((line, 6)),
            pltpu.SemaphoreType.DMA((line,)),
            pltpu.SemaphoreType.DMA((6,)),
            pltpu.SemaphoreType.DMA,
        ],
        compiler_params=pltpu.CompilerParams(
            collective_id=collective, has_side_effects=True, vmem_limit_bytes=52 * MIB
        ),
        name=name,
    )(x)


QUERY_HEADS = 64
KEY_VALUE_HEADS = 8
HEAD_SIZE = 64
TOP = 4
EPSILON = 1e-05
THETA_BASE = 150000.0
CLAMP_LIMIT = 7.0
GLU_ALPHA = 1.702
MASK_FILL = -1e30
SPAN = 256
SCALE = HEAD_SIZE**-0.5


def contract(left, right, left_axis, right_axis):
    return lax.dot_general(
        left, right, (((left_axis,), (right_axis,)), ((), ())), preferred_element_type=jnp.float32
    )


def norm_scale(value_rows, gain_vec):
    return (
        value_rows
        * lax.rsqrt(jnp.mean(value_rows * value_rows, axis=-1, keepdims=True) + EPSILON)
        * gain_vec
    )


def soft_clamp(value_rows):
    return CLAMP_LIMIT * jnp.tanh(value_rows / CLAMP_LIMIT)


def glu_units(gate_lin, up_lin):
    gated = soft_clamp(gate_lin)
    return (soft_clamp(up_lin) + 1.0) * gated * jax.nn.sigmoid(GLU_ALPHA * gated)


def rotary_tables(length):
    half = HEAD_SIZE // 2
    inverse = THETA_BASE ** (-jnp.arange(half, dtype=jnp.float32) / half)
    angles = inverse[:, None] * jnp.arange(length, dtype=jnp.int32).astype(jnp.float32)[None, :]
    return jnp.cos(angles), jnp.sin(angles)


def turned(value, cosine, sine):
    half = HEAD_SIZE // 2
    first, second = value[:, :half], value[:, half:]
    return jnp.concatenate(
        [first * cosine - second * sine, second * cosine + first * sine], axis=1
    )


def diagonal(length):
    return lax.broadcasted_iota(jnp.int32, (length, length), 0) <= lax.broadcasted_iota(
        jnp.int32, (length, length), 1
    )


def masked_scores(key_rows, query_cols, count):
    scores = contract(key_rows, query_cols, 1, 0)
    edge = jnp.where(diagonal(SPAN), scores[count - SPAN :], MASK_FILL)
    if count == SPAN:
        return edge
    return jnp.concatenate([scores[: count - SPAN], edge], axis=0)


def attend_kernel(sink_ref, q_ref, k_ref, v_ref, out_ref, log_ref):
    sink = sink_ref[pl.program_id(0)]
    length = q_ref.shape[1]
    for start in range(0, length, SPAN):
        count = start + SPAN
        at = pl.ds(start, SPAN)
        query = q_ref[:, at] * jnp.bfloat16(SCALE)
        scores = masked_scores(k_ref[:count, :], query, count)
        row_top = jnp.maximum(jnp.max(scores, axis=0, keepdims=True), sink)
        weights = jnp.exp(scores - row_top)
        denominator = jnp.sum(weights, axis=0, keepdims=True) + jnp.exp(sink - row_top)
        probabilities = (weights / denominator).astype(jnp.bfloat16)
        out_ref[:, at] = contract(v_ref[:, :count], probabilities, 1, 0).astype(jnp.bfloat16)
        log_ref[0, :, at] = row_top + jnp.log(denominator)


def attend(sinks, queries, keys, values):
    heads, length = queries.shape[0] // HEAD_SIZE, queries.shape[1]
    per_head = pl.BlockSpec((HEAD_SIZE, length), lambda h: (h, 0))
    return pl.pallas_call(
        attend_kernel,
        grid=(heads,),
        out_shape=(
            jax.ShapeDtypeStruct(queries.shape, jnp.bfloat16),
            jax.ShapeDtypeStruct((heads, 1, length), jnp.float32),
        ),
        in_specs=[
            pl.BlockSpec(memory_space=pltpu.SMEM),
            per_head,
            pl.BlockSpec((length, HEAD_SIZE), lambda h: (0, 0)),
            pl.BlockSpec((HEAD_SIZE, length), lambda h: (0, 0)),
        ],
        out_specs=(per_head, pl.BlockSpec((1, 1, length), lambda h: (h, 0, 0))),
        compiler_params=pltpu.CompilerParams(vmem_limit_bytes=40 * MIB),
        cost_estimate=pl.CostEstimate(
            flops=heads * length * length * HEAD_SIZE * 4,
            bytes_accessed=heads * length * HEAD_SIZE * 4,
            transcendentals=heads * length * length,
        ),
        name="attend",
    )(sinks, queries, keys, values)


def attend_back_kernel(
    sink_ref, q_ref, k_ref, kt_ref, v_ref, grad_ref, log_ref, cos_ref, sin_ref,
    dq_ref, dk_ref, dv_ref, dsink_ref,
):
    head = pl.program_id(0)
    sink = sink_ref[head]
    length = q_ref.shape[1]
    half = HEAD_SIZE // 2

    @pl.when(head == 0)
    def _():
        dk_ref[...] = jnp.zeros_like(dk_ref)
        dv_ref[...] = jnp.zeros_like(dv_ref)

    grad_sink = jnp.zeros((1, SPAN), jnp.float32)
    for start in range(0, length, SPAN):
        count = start + SPAN
        at = pl.ds(start, SPAN)
        query = q_ref[:, at] * jnp.bfloat16(SCALE)
        grad = grad_ref[:, at]
        log_sum = log_ref[0, :, at]
        probabilities = jnp.exp(masked_scores(k_ref[:count, :], query, count) - log_sum)
        grad_probs = contract(v_ref[:count, :], grad, 1, 0)
        inner_sum = jnp.sum(probabilities * grad_probs, axis=0, keepdims=True)
        grad_scores = (probabilities * (grad_probs - inner_sum)).astype(jnp.bfloat16)
        grad_query = contract(kt_ref[:, :count], grad_scores, 1, 0) * SCALE
        first, second = grad_query[:half], grad_query[half:]
        cosine, sine = cos_ref[:, at], sin_ref[:, at]
        dq_ref[:half, at] = (first * cosine + second * sine).astype(jnp.bfloat16)
        dq_ref[half:, at] = (second * cosine - first * sine).astype(jnp.bfloat16)
        dk_ref[:count, :] += contract(grad_scores, query, 1, 1)
        dv_ref[:count, :] += contract(probabilities.astype(jnp.bfloat16), grad, 1, 1)
        grad_sink = grad_sink - jnp.exp(sink - log_sum) * inner_sum
    dsink_ref[0] = grad_sink


def attend_back(sinks, queries, keys, keys_t, values, grads, log_sums, cosine, sine):
    heads, length = queries.shape[0] // HEAD_SIZE, queries.shape[1]
    per_head = pl.BlockSpec((HEAD_SIZE, length), lambda h: (h, 0))

    def whole(*shape):
        return pl.BlockSpec(shape, lambda h: (0,) * len(shape))

    return pl.pallas_call(
        attend_back_kernel,
        grid=(heads,),
        out_shape=(
            jax.ShapeDtypeStruct(queries.shape, jnp.bfloat16),
            jax.ShapeDtypeStruct((length, HEAD_SIZE), jnp.float32),
            jax.ShapeDtypeStruct((length, HEAD_SIZE), jnp.float32),
            jax.ShapeDtypeStruct((heads, 1, SPAN), jnp.float32),
        ),
        in_specs=[
            pl.BlockSpec(memory_space=pltpu.SMEM),
            per_head,
            whole(length, HEAD_SIZE),
            whole(HEAD_SIZE, length),
            whole(length, HEAD_SIZE),
            per_head,
            pl.BlockSpec((1, 1, length), lambda h: (h, 0, 0)),
            whole(HEAD_SIZE // 2, length),
            whole(HEAD_SIZE // 2, length),
        ],
        out_specs=(
            per_head,
            whole(length, HEAD_SIZE),
            whole(length, HEAD_SIZE),
            pl.BlockSpec((1, 1, SPAN), lambda h: (h, 0, 0)),
        ),
        compiler_params=pltpu.CompilerParams(vmem_limit_bytes=48 * MIB),
        cost_estimate=pl.CostEstimate(
            flops=heads * length * length * HEAD_SIZE * 10,
            bytes_accessed=heads * length * HEAD_SIZE * 8,
            transcendentals=heads * length * length,
        ),
        name="attend_back",
    )(sinks, queries, keys, keys_t, values, grads, log_sums, cosine, sine)


def shards(
    layer_input, cotangent, gate_weights, routes, w_query, key_projection, value_projection, w_out,
    b_query, key_bias_vector, value_bias_vector, b_out, learned_sink_logits, gain_attn, gain_ffn,
    w_gate, w_up, w_down, b_gate, b_up, b_down,
):
    low = jnp.bfloat16
    ctx_n, z_n = lax.axis_size("ctx"), lax.axis_size("fsdp")
    ctx_at, z_at = lax.axis_index("ctx"), lax.axis_index("fsdp")
    tuned = ctx_n == 8 and z_n == 4
    width = layer_input.shape[-1]
    rows = layer_input.shape[0] * layer_input.shape[1]
    length = rows * ctx_n
    blocks = ctx_n * z_n
    capacity = max(2, rows * TOP * 17 // (16 * ctx_n))
    heads = QUERY_HEADS // ctx_n
    spread = ctx_n // KEY_VALUE_HEADS
    f32 = jnp.float32

    def gather_plane(value, call):
        if tuned:
            return gather_blocks(value, 1, call, f"gather_plane_{call}").reshape(length, width)
        return lax.all_gather(value, "ctx", axis=0, tiled=True)

    def scatter_plane(value, call):
        if tuned:
            return scatter_blocks(value.reshape(1, 8, rows, width), call, f"scatter_plane_{call}")
        return lax.psum_scatter(value, "ctx", scatter_dimension=0, tiled=True).astype(f32)

    def gather_all(value, call):
        if tuned:
            return gather_blocks(value, 4, call, f"gather_all_{call}").reshape(blocks * rows, width)
        return value

    residual = layer_input.reshape(rows, width).astype(f32)
    grad_final = cotangent.reshape(rows, width)
    gain_attn_f, gain_ffn_f = gain_attn.astype(f32), gain_ffn.astype(f32)
    cosine, sine = rotary_tables(length)

    q_cols, k_cols = w_query.shape[1], key_projection.shape[1]
    own_rows = q_cols + 2 * k_cols
    padded = own_rows + 8
    biases = jnp.concatenate([b_query, key_bias_vector, value_bias_vector])
    own_weights = jnp.concatenate(
        [
            w_query.T,
            key_projection.T,
            value_projection.T,
            jnp.pad(biases[None, :], ((0, 7), (0, width - own_rows))),
        ],
        axis=0,
    )
    head_weights = lax.all_gather(own_weights, "fsdp", axis=0, tiled=True)
    out_weights = lax.all_gather(w_out, "fsdp", axis=0, tiled=True)

    own_routes = jnp.concatenate(
        [routes.reshape(rows, TOP).astype(low).T, gate_weights.reshape(rows, TOP).T], axis=0
    )
    if tuned:
        pack = 2
        all_routes = lax.all_gather(own_routes, ("fsdp", "ctx"), axis=0, tiled=True)
        all_routes = all_routes.reshape(blocks, 2, TOP, rows).astype(f32)
        named = all_routes[:, 0] == ctx_at.astype(f32)
    else:
        pack = 1
        all_routes = own_routes.reshape(1, 2, TOP, rows).astype(f32)
        named = all_routes[:, 0] == jnp.arange(ctx_n, dtype=f32)[:, None, None]
    count = named.shape[0]
    hits = jnp.sum(named.astype(f32), axis=1)
    gates = jnp.sum(jnp.where(named, all_routes[:, 1], 0.0), axis=1)
    earlier = (
        lax.broadcasted_iota(jnp.int32, (rows, rows), 0)
        < lax.broadcasted_iota(jnp.int32, (rows, rows), 1)
    ).astype(low)
    places = jnp.dot(hits.astype(low), earlier, preferred_element_type=f32).astype(jnp.int32)
    groups = count // pack
    starts = (jnp.arange(count, dtype=jnp.int32) % pack) * capacity
    places = jnp.where(hits > 0, places + starts[:, None], -1).reshape(groups, 1, pack * rows)
    slots = jnp.arange(pack * capacity, dtype=jnp.int32)[None, :, None]
    picked = places == slots
    select = picked.astype(low)
    mixing = jnp.where(picked, gates.reshape(groups, 1, pack * rows), 0.0).astype(low)
    slot_rows = blocks * capacity

    def exchanged(slot_values):
        moved = slot_values.reshape(ctx_n, capacity, width)
        return lax.all_to_all(moved, "ctx", split_axis=0, concat_axis=0, tiled=True)

    def to_slots(picks, token_rows):
        if tuned:
            token_rows = token_rows.reshape(groups, pack * rows, width)
            dims = (((2,), (1,)), ((0,), (0,)))
        else:
            dims = (((2,), (0,)), ((), ()))
        moved = lax.dot_general(picks, token_rows, dims, preferred_element_type=f32).astype(low)
        if not tuned:
            moved = lax.all_gather(exchanged(moved), "fsdp", axis=0, tiled=True)
        return moved.reshape(slot_rows, width)

    def to_tokens(picks, slot_values, call):
        if not tuned:
            slot_values = exchanged(
                lax.psum_scatter(slot_values, "fsdp", scatter_dimension=0, tiled=True)
            )
        moved = lax.dot_general(
            picks,
            slot_values.reshape(groups, pack * capacity, width),
            (((1,), (1,)), ((0,), (0,))),
            preferred_element_type=f32,
        )
        if not tuned:
            return jnp.sum(moved, axis=0)
        return scatter_blocks(moved.astype(low).reshape(4, 8, rows, width), call, f"scatter_all_{call}")

    normed_own = norm_scale(residual, gain_attn_f).astype(low)
    normed_attn = gather_plane(normed_own, 1)
    lin = contract(head_weights, normed_attn, 1, 1).reshape(z_n, padded, length)
    head_bias = head_weights.reshape(z_n, padded, width)[:, own_rows, :own_rows].astype(f32)
    lin = lin[:, :own_rows] + head_bias[:, :, None]
    query_lin = lin[:, :q_cols].reshape(heads, HEAD_SIZE, length)
    kv_lin = jnp.stack([lin[:, q_cols : q_cols + k_cols], lin[:, q_cols + k_cols :]])
    kv_lin = kv_lin.reshape(2, z_n * k_cols, length)
    swap = [(i, i ^ 1) for i in range(ctx_n)]
    odd = lax.rem(ctx_at, 2) == 1
    if spread == 2:
        other = lax.ppermute(kv_lin, "ctx", swap)
        kv_lin = jnp.where(
            odd,
            jnp.concatenate([other, kv_lin], axis=1),
            jnp.concatenate([kv_lin, other], axis=1),
        )
    queries = turned(query_lin, cosine, sine).astype(low).reshape(heads * HEAD_SIZE, length)
    keys_t = turned(kv_lin[:1], cosine, sine)[0].astype(low)
    values_t = kv_lin[1].astype(low)
    keys, values = keys_t.T, values_t.T
    sinks = lax.dynamic_slice(learned_sink_logits.astype(f32), (ctx_at * heads,), (heads,))
    attended, log_sums = attend(sinks, queries, keys, values_t)
    branch_part = contract(attended, out_weights, 0, 0).astype(low)
    branch = scatter_plane(branch_part, 2) + b_out.astype(f32)
    middle = residual + branch
    normed_ffn = norm_scale(middle, gain_ffn_f).astype(low)

    all_normed = gather_all(normed_ffn, 3)
    expert_in = to_slots(select, all_normed)
    all_grads = gather_all(grad_final, 4)
    gate_w, up_w, down_w = w_gate[0], w_up[0], w_down[0]
    gate_lin = contract(expert_in, gate_w, 1, 0) + b_gate[0].astype(f32)
    up_lin = contract(expert_in, up_w, 1, 0) + b_up[0].astype(f32)
    hidden_f, unit_back = jax.vjp(glu_units, gate_lin, up_lin)
    hidden_units = hidden_f.astype(low)
    share = b_down.shape[1]
    down_bias = lax.dynamic_update_slice(
        jnp.zeros((width,), f32), b_down[0].astype(f32), (z_at * share,)
    )
    expert_out = (contract(hidden_units, down_w, 1, 0) + down_bias).astype(low)
    expert_mix = to_tokens(mixing, expert_out, 5)
    final_out = (middle + expert_mix).astype(low).reshape(layer_input.shape)

    grad_expert_out = to_slots(mixing, all_grads)
    grad_w_down = contract(hidden_units, grad_expert_out, 0, 0)
    grad_b_down = lax.dynamic_slice(
        jnp.sum(grad_expert_out.astype(f32), axis=0), (z_at * share,), (share,)
    )
    grad_units = contract(grad_expert_out, down_w, 1, 1)
    grad_gate_f, grad_up_f = unit_back(grad_units)
    grad_gate_lin, grad_up_lin = grad_gate_f.astype(low), grad_up_f.astype(low)
    grad_copy = (
        contract(grad_gate_lin, gate_w, 1, 1) + contract(grad_up_lin, up_w, 1, 1)
    ).astype(low)
    grad_normed_ffn = to_tokens(select, grad_copy, 6)
    grad_w_gate = contract(expert_in, grad_gate_lin, 0, 0)
    grad_w_up = contract(expert_in, grad_up_lin, 0, 0)
    grad_b_gate = jnp.sum(grad_gate_lin.astype(f32), axis=0)
    grad_b_up = jnp.sum(grad_up_lin.astype(f32), axis=0)

    unused, norm_back = jax.vjp(norm_scale, middle, gain_ffn_f)
    grad_middle_part, grad_gain_ffn = norm_back(grad_normed_ffn)
    grad_middle = grad_final.astype(f32) + grad_middle_part
    grad_branch_own = grad_middle.astype(low)
    grad_branch = gather_plane(grad_branch_own, 7)
    grad_b_out = jnp.sum(grad_branch_own.astype(f32), axis=0)
    grad_attended = contract(out_weights, grad_branch, 1, 1).astype(low)
    grad_out_part = contract(attended, grad_branch, 1, 0).astype(low)
    grad_query, grad_keys, grad_values, grad_sink_parts = attend_back(
        sinks, queries, keys, keys_t, values, grad_attended, log_sums, cosine, sine
    )
    grad_kv = jnp.stack([turned(grad_keys.T[None], cosine, -sine)[0], grad_values.T])
    if spread == 2:
        grad_kv = grad_kv + lax.ppermute(grad_kv, "ctx", swap)
        halves = grad_kv.reshape(2, 2, HEAD_SIZE // 2, length)
        grad_kv = jnp.where(odd, halves[:, 1], halves[:, 0])
    grad_kv = grad_kv.astype(low).reshape(2, z_n, k_cols, length)
    grad_lin = jnp.concatenate(
        [
            grad_query.reshape(z_n, q_cols, length),
            grad_kv[0],
            grad_kv[1],
            jnp.zeros((z_n, padded - own_rows, length), low),
        ],
        axis=1,
    )
    grad_normed_part = contract(grad_lin.reshape(z_n * padded, length), head_weights, 0, 0)
    grad_normed_attn = scatter_plane(grad_normed_part.astype(low), 8)
    grad_weights = contract(grad_lin.reshape(z_n * padded, length), normed_attn, 1, 0)
    grad_weights = grad_weights.reshape(z_n, padded, width)[:, :own_rows]
    grad_biases = jnp.sum(grad_lin[:, :own_rows].astype(f32), axis=2)
    grad_weights = jnp.concatenate(
        [
            grad_weights.astype(low),
            jnp.pad(grad_biases[:, None, :], ((0, 0), (0, 7), (0, width - own_rows))).astype(low),
        ],
        axis=1,
    ).reshape(z_n * padded, width)
    grad_w_out = lax.psum_scatter(grad_out_part, "fsdp", scatter_dimension=0, tiled=True).astype(f32)
    own_grads = lax.psum_scatter(grad_weights, "fsdp", scatter_dimension=0, tiled=True).astype(f32)
    grad_w_query = own_grads[:q_cols].T
    grad_w_key = own_grads[q_cols : q_cols + k_cols].T
    grad_w_value = own_grads[q_cols + k_cols : own_rows].T
    own_bias_grads = own_grads[own_rows, :own_rows]
    unused, norm_back = jax.vjp(norm_scale, residual, gain_attn_f)
    grad_residual_part, grad_gain_attn = norm_back(grad_normed_attn)
    input_grad = (grad_middle + grad_residual_part).reshape(layer_input.shape)
    grad_sinks = lax.dynamic_update_slice(
        jnp.zeros((QUERY_HEADS,), f32), jnp.sum(grad_sink_parts, axis=(1, 2)), (ctx_at * heads,)
    )
    grad_b_out, grad_sink_logits, grad_gain_attn, grad_gain_ffn = lax.psum(
        (grad_b_out, grad_sinks, grad_gain_attn, grad_gain_ffn), ("ctx", "fsdp")
    )
    return (
        final_out,
        input_grad,
        grad_w_query,
        grad_w_key,
        grad_w_value,
        grad_w_out,
        own_bias_grads[:q_cols],
        own_bias_grads[q_cols : q_cols + k_cols],
        own_bias_grads[q_cols + k_cols :],
        grad_b_out,
        grad_sink_logits,
        grad_gain_attn,
        grad_gain_ffn,
        grad_w_gate[None],
        grad_w_up[None],
        grad_w_down[None],
        grad_b_gate[None],
        grad_b_up[None],
        grad_b_down[None],
    )


def solution(mesh):
    return jax.shard_map(
        shards,
        mesh=mesh,
        in_specs=(
            P("fsdp", "ctx", None),
            P("fsdp", "ctx", None),
            P("fsdp", "ctx", None),
            P("fsdp", "ctx", None),
            P(None, ("ctx", "fsdp")),
            P(None, ("ctx", "fsdp")),
            P(None, ("ctx", "fsdp")),
            P(("ctx", "fsdp"), None),
            P(("ctx", "fsdp")),
            P(("ctx", "fsdp")),
            P(("ctx", "fsdp")),
            P(),
            P(),
            P(),
            P(),
            P("ctx", None, "fsdp"),
            P("ctx", None, "fsdp"),
            P("ctx", "fsdp", None),
            P("ctx", "fsdp"),
            P("ctx", "fsdp"),
            P("ctx", "fsdp"),
        ),
        out_specs=(
            P("fsdp", "ctx", None),
            P("fsdp", "ctx", None),
            P(None, ("ctx", "fsdp")),
            P(None, ("ctx", "fsdp")),
            P(None, ("ctx", "fsdp")),
            P(("ctx", "fsdp"), None),
            P(("ctx", "fsdp")),
            P(("ctx", "fsdp")),
            P(("ctx", "fsdp")),
            P(),
            P(),
            P(),
            P(),
            P("ctx", None, "fsdp"),
            P("ctx", None, "fsdp"),
            P("ctx", "fsdp", None),
            P("ctx", "fsdp"),
            P("ctx", "fsdp"),
            P("ctx", "fsdp"),
        ),
        check_vma=False,
    )
```

```python
import jax
import jax.numpy as jnp
from jax import lax
from jax.experimental import pallas as pl
from jax.experimental.pallas import tpu as pltpu
from jax.sharding import PartitionSpec as P

MESH = pl.DeviceIdType.MESH
MIB = 1 << 20


def remote(src, dst, send_sem, recv_sem, device):
    return pltpu.make_async_remote_copy(
        src_ref=src,
        dst_ref=dst,
        send_sem=send_sem,
        recv_sem=recv_sem,
        device_id=device,
        device_id_type=MESH,
    )


def neighbours():
    me = lax.axis_index("ctx")
    core = lax.rem(me, 2)
    x_at = lax.rem(me // 2, 2)
    y_at = me // 4
    return me, me + 1 - 2 * core, me + 2 - 4 * x_at, me + 4 - 8 * y_at, 2 - 4 * x_at


def greet(others, line, z_at):
    barrier = pltpu.get_barrier_semaphore()
    for other in others:
        pl.semaphore_signal(barrier, 1, device_id=(other, z_at), device_id_type=MESH)
    if line == 1:
        pl.semaphore_wait(barrier, len(others))
        return
    me = lax.axis_index("ctx")

    @pl.when(z_at > 0)
    def _():
        pl.semaphore_signal(barrier, 1, device_id=(me, z_at - 1), device_id_type=MESH)

    @pl.when(z_at < line - 1)
    def _():
        pl.semaphore_signal(barrier, 1, device_id=(me, z_at + 1), device_id_type=MESH)

    inner = (lax.rem(z_at, 3) + 1) // 2
    pl.semaphore_wait(barrier, len(others) + 1 + inner)


def gather_sems(line):
    return [
        pltpu.SemaphoreType.DMA,
        pltpu.SemaphoreType.DMA((line, 2)),
        pltpu.SemaphoreType.DMA((line,)),
        pltpu.SemaphoreType.DMA((line, 9)),
        pltpu.SemaphoreType.DMA((line, 9)),
    ]


class Gather:
    def __init__(self, line, x_ref, o_ref, sems):
        self.line, self.x_ref, self.o_ref = line, x_ref, o_ref
        self.own_sem, self.z_send, self.z_recv, self.p_send, self.p_recv = sems
        self.z_at = lax.axis_index("fsdp")
        self.me, self.mate, self.near_x, self.near_y, step_x = neighbours()
        self.across = self.near_y + step_x
        self.rows = x_ref.shape[0]
        self.half = self.rows // 2
        self.middle = (self.z_at == 1) | (self.z_at == 2)
        self.first_slot = self.z_at if line > 1 else 0

    def slot(self, order):
        z_at = self.z_at
        if self.line == 1:
            return 0
        second = z_at + 1 - 2 * lax.rem(z_at, 2)
        third = 2 - z_at // 2
        fourth = 3 - 3 * (z_at // 2)
        return jnp.where(
            order == 0, z_at, jnp.where(order == 1, second, jnp.where(order == 2, third, fourth))
        )

    def there(self, slot, place, part=None):
        start, count = (slot * 8 + place) * self.rows, self.rows
        if part is not None:
            start, count = start + part * self.half, self.half
        return self.o_ref.at[pl.ds(pl.multiple_of(start, self.half), count)]

    def z_copy(self, src_ref, slot, way, target):
        return remote(
            src_ref,
            self.there(slot, self.me),
            self.z_send.at[slot, way],
            self.z_recv.at[slot],
            (self.me, target),
        )

    def up(self):
        return self.z_copy(self.x_ref, self.z_at, 0, self.z_at + 1)

    def down(self):
        return self.z_copy(self.x_ref, self.z_at, 1, self.z_at - 1)

    def onward(self, order):
        slot = self.slot(order)
        target = jnp.where(order == 1, 3 - self.z_at, 3 * self.z_at - 3)
        return self.z_copy(self.there(slot, self.me), slot, 0, target)

    def copy(self, order, place, kind, device, part=None, src_ref=None):
        dst_ref = self.there(self.slot(order), place, part)
        return remote(
            dst_ref if src_ref is None else src_ref,
            dst_ref,
            self.p_send.at[order, kind],
            self.p_recv.at[order, kind],
            (device, self.z_at),
        )

    def out(self, order, src_ref=None):
        return [
            self.copy(order, self.me, 0, self.near_x, None, src_ref),
            self.copy(order, self.me, 1, self.near_y, None, src_ref),
            self.copy(order, self.me, 2, self.mate, None, src_ref),
        ]

    def passed(self, order, *which):
        places = (
            (self.near_x, 3, self.near_y, 0),
            (self.near_x, 5, self.mate, None),
            (self.near_y, 4, self.near_x, 1),
            (self.near_y, 6, self.mate, None),
            (self.across, 7, self.mate, 0),
            (self.across, 8, self.mate, 1),
        )
        return [self.copy(order, *places[k]) for k in which]

    def begin(self):
        line, z_at = self.line, self.z_at
        greet((self.mate, self.near_x, self.near_y), line, z_at)
        own = pltpu.make_async_copy(
            self.x_ref, self.there(self.first_slot, self.me), self.own_sem
        )
        own.start()
        if line > 1:
            pl.when(z_at < line - 1)(lambda: self.up().start())
            pl.when(z_at > 0)(lambda: self.down().start())
        for copy in self.out(0, self.x_ref):
            copy.start()

    def own_block(self):
        pltpu.make_async_copy(
            self.x_ref, self.there(self.first_slot, self.me), self.own_sem
        ).wait()

    def first(self, order):
        slot = self.slot(order)
        self.z_copy(self.there(slot, self.me), slot, 0, self.z_at).wait_recv()
        pl.when(self.middle)(lambda: self.onward(order).start())
        for copy in self.out(order):
            copy.start()

    def second(self, order):
        to_y, mate_x, to_x, mate_y = self.passed(order, 0, 1, 2, 3)
        self.copy(order, self.near_x, 0, self.near_x).wait_recv()
        to_y.start()
        mate_x.start()
        self.copy(order, self.near_y, 1, self.near_y).wait_recv()
        to_x.start()
        mate_y.start()

    def near(self, order):
        step = self.mate - self.me
        self.copy(order, self.mate, 2, self.mate).wait_recv()
        self.copy(order, self.near_x + step, 5, self.mate).wait_recv()

    def third(self, order):
        step = self.mate - self.me
        top, low = self.passed(order, 4, 5)
        self.copy(order, self.across, 3, self.near_y, 0).wait_recv()
        top.start()
        self.copy(order, self.across, 4, self.near_x, 1).wait_recv()
        low.start()
        self.copy(order, self.near_y + step, 6, self.mate).wait_recv()
        self.copy(order, self.across + step, 7, self.mate, 0).wait_recv()
        self.copy(order, self.across + step, 8, self.mate, 1).wait_recv()

    def end(self):
        line, z_at = self.line, self.z_at

        def sent(order, carry):
            for copy in self.out(order) + self.passed(order, 0, 1, 2, 3, 4, 5):
                copy.wait_send()
            return carry

        lax.fori_loop(0, line, sent, 0)
        if line > 1:
            pl.when(z_at < line - 1)(lambda: self.up().wait_send())
            pl.when(z_at > 0)(lambda: self.down().wait_send())

            @pl.when(self.middle)
            def _():
                for order in range(1, line):
                    self.onward(order).wait_send()


def gather_blocks(x, line, collective, name):
    rows, width = x.shape

    def kernel(x_ref, o_ref, *sems):
        gather = Gather(line, x_ref, o_ref, sems)
        gather.begin()

        def body(order, carry):
            gather.second(order)
            if line > 1:
                pl.when(order + 1 < line)(lambda: gather.first(order + 1))
            gather.near(order)
            gather.third(order)
            return carry

        lax.fori_loop(0, line, body, 0)
        gather.own_block()
        gather.end()

    return pl.pallas_call(
        kernel,
        out_shape=jax.ShapeDtypeStruct((line * 8 * rows, width), x.dtype),
        in_specs=[pl.BlockSpec(memory_space=pl.ANY)],
        out_specs=pl.BlockSpec(memory_space=pl.ANY),
        scratch_shapes=gather_sems(line),
        compiler_params=pltpu.CompilerParams(collective_id=collective, has_side_effects=True),
        name=name,
    )(x)


CHUNK = 16


def add_rows(dst_ref, src_refs, start, count, out_ref=None):
    def body(i, carry):
        at = pl.ds(pl.multiple_of(start + i * CHUNK, CHUNK), CHUNK)
        value = dst_ref[at, :].astype(jnp.float32)
        for src_ref in src_refs:
            value = value + src_ref[at, :].astype(jnp.float32)
        to_ref = dst_ref if out_ref is None else out_ref
        to_ref[at, :] = value.astype(to_ref.dtype)
        return carry

    lax.fori_loop(0, count // CHUNK, body, 0)


class Scatter:
    def __init__(self, line, x_ref, o_ref, scratch):
        (
            self.mine, self.theirs, self.halves, self.from_x, self.from_y, self.from_z, self.total,
            self.load_sem, self.m_send, self.m_recv, self.p_send, self.p_recv, self.z_send,
            self.z_recv, self.out_sem,
        ) = scratch
        self.line, self.x_ref, self.o_ref = line, x_ref, o_ref
        self.z_at = lax.axis_index("fsdp")
        self.me, self.mate, self.near_x, self.near_y, step_x = neighbours()
        self.places = (self.near_y + step_x, self.near_x, self.near_y, self.me)
        self.rows = self.total.shape[0]
        self.half = self.rows // 2
        self.middle = (self.z_at == 1) | (self.z_at == 2)

    def slot(self, order):
        z_at = self.z_at
        if self.line == 1:
            return 0
        far, next_far, near = 3 - 3 * (z_at // 2), 2 - z_at // 2, z_at + 1 - 2 * lax.rem(z_at, 2)
        return jnp.where(
            order == 0, far, jnp.where(order == 1, next_far, jnp.where(order == 2, near, z_at))
        )

    def there(self, slot, place):
        return self.x_ref.at[pl.ds(pl.multiple_of((slot * 8 + place) * self.rows, 16), self.rows)]

    def give(self, order, k):
        return remote(
            self.there(self.slot(order), self.places[k] + self.mate - self.me),
            self.theirs.at[order, k],
            self.m_send.at[order, k],
            self.m_recv.at[order, k],
            (self.mate, self.z_at),
        )

    def load(self, order, k):
        return pltpu.make_async_copy(
            self.there(self.slot(order), self.places[k]),
            self.mine.at[order, k],
            self.load_sem.at[order, k],
        )

    def send(self, order, kind):
        top, low = pl.ds(0, self.half), pl.ds(self.half, self.half)
        k, part, to, device = (
            (0, top, self.halves, self.near_x),
            (0, low, self.halves, self.near_y),
            (1, top, self.from_x, self.near_x),
            (1, low, self.from_x, self.near_x),
            (2, low, self.from_y, self.near_y),
            (2, top, self.from_y, self.near_y),
        )[kind]
        return remote(
            self.mine.at[order, k, part],
            to.at[order, part],
            self.p_send.at[order, kind],
            self.p_recv.at[order, kind],
            (device, self.z_at),
        )

    def begin(self):
        greet((self.mate, self.near_x, self.near_y), self.line, self.z_at)

        def body(order, carry):
            for k in range(4):
                self.give(order, k).start()
                self.load(order, k).start()
            return carry

        lax.fori_loop(0, self.line, body, 0)

    def first(self, order):
        for k in range(4):
            self.give(order, k).wait_recv()
            self.load(order, k).wait()
            add_rows(self.mine.at[order, k], [self.theirs.at[order, k]], 0, self.rows)
            for kind in ((0, 1), (2,), (4,), ())[k]:
                self.send(order, kind).start()

    def second(self, order):
        self.send(order, 1).wait_recv()
        add_rows(self.mine.at[order, 1], [self.halves.at[order]], self.half, self.half)
        self.send(order, 3).start()
        self.send(order, 0).wait_recv()
        add_rows(self.mine.at[order, 2], [self.halves.at[order]], 0, self.half)
        self.send(order, 5).start()

    def third(self, order, out_ref=None):
        for kind in (2, 3, 4, 5):
            self.send(order, kind).wait_recv()
        sources = [self.from_x.at[order], self.from_y.at[order]]
        add_rows(self.mine.at[order, 3], sources, 0, self.rows, out_ref)

    def z_copy(self, order, slot_at, target):
        return remote(
            self.mine.at[order, 3],
            self.from_z.at[slot_at],
            self.z_send.at[order],
            self.z_recv.at[slot_at],
            (self.me, target),
        )

    def z_out(self, order):
        z_at, slot = self.z_at, self.slot(order)
        target = jnp.where(order == 2, slot, z_at + 1 - 2 * (z_at // 2))
        ends = jnp.where(target == slot, 1, 0)
        return self.z_copy(order, ends * (4 + (z_at - target + 1) // 2) + (1 - ends) * slot, target)

    def pass_on(self, order):
        slot = self.slot(order)
        self.z_copy(order, slot, self.z_at).wait_recv()
        add_rows(self.mine.at[order, 3], [self.from_z.at[slot]], 0, self.rows)
        self.z_out(order).start()

    def along(self, order):
        @pl.when((order < self.line - 1) & jnp.logical_not(self.middle))
        def _():
            self.z_out(order).start()

        pl.when((order == 1) & self.middle)(lambda: self.pass_on(0))

        @pl.when((order == 2) & self.middle)
        def _():
            self.pass_on(1)
            self.pass_on(2)

    def last(self):
        z_at, line = self.z_at, self.line
        pl.when(z_at > 0)(lambda: self.z_copy(line - 1, 4, z_at).wait_recv())
        pl.when(z_at < line - 1)(lambda: self.z_copy(line - 1, 5, z_at).wait_recv())
        mine = self.mine.at[line - 1, 3]
        below, above = self.from_z.at[4], self.from_z.at[5]
        pl.when(z_at == 0)(lambda: add_rows(mine, [above], 0, self.rows, self.total))
        pl.when(z_at == line - 1)(lambda: add_rows(mine, [below], 0, self.rows, self.total))
        pl.when(self.middle)(lambda: add_rows(mine, [below, above], 0, self.rows, self.total))

    def end(self):
        out = pltpu.make_async_copy(self.total, self.o_ref, self.out_sem)
        out.start()

        def sent(order, carry):
            for k in range(4):
                self.give(order, k).wait_send()
            for kind in range(6):
                self.send(order, kind).wait_send()
            if self.line > 1:
                pl.when(order < self.line - 1)(lambda: self.z_out(order).wait_send())
            return carry

        lax.fori_loop(0, self.line, sent, 0)
        out.wait()

    def run(self, work=None, extra=0):
        self.begin()
        self.first(0)
        if self.line == 1:
            self.second(0)
            self.third(0, self.total)
            self.end()
            return

        def body(step, carry):
            order, phase = step // 3, lax.rem(step, 3)

            @pl.when((phase == 0) & (order < self.line))
            def _():
                self.second(order)
                pl.when(order + 1 < self.line)(lambda: self.first(order + 1))

            pl.when((phase == 1) & (order < self.line))(lambda: self.third(order))
            pl.when((phase == 2) & (order < self.line))(lambda: self.along(order))
            if work is not None:
                work(step)
            return carry

        lax.fori_loop(0, 3 * self.line + extra, body, 0)
        self.last()
        self.end()


def scatter_scratch(line, rows, width, dtype):
    shard = (rows, width)
    return [
        pltpu.VMEM((line, 4) + shard, dtype),
        pltpu.VMEM((line, 4) + shard, dtype),
        pltpu.VMEM((line,) + shard, dtype),
        pltpu.VMEM((line,) + shard, dtype),
        pltpu.VMEM((line,) + shard, dtype),
        pltpu.VMEM((6 if line > 1 else 1,) + shard, dtype),
        pltpu.VMEM(shard, jnp.float32),
        pltpu.SemaphoreType.DMA((line, 4)),
        pltpu.SemaphoreType.DMA((line, 4)),
        pltpu.SemaphoreType.DMA((line, 4)),
        pltpu.SemaphoreType.DMA((line, 6)),
        pltpu.SemaphoreType.DMA((line, 6)),
        pltpu.SemaphoreType.DMA((line,)),
        pltpu.SemaphoreType.DMA((6,)),
        pltpu.SemaphoreType.DMA,
    ]


def scatter_blocks(x, line, collective, name):
    rows, width = x.shape[0] // (line * 8), x.shape[1]

    def kernel(x_ref, o_ref, *scratch):
        Scatter(line, x_ref, o_ref, scratch).run()

    return pl.pallas_call(
        kernel,
        out_shape=jax.ShapeDtypeStruct((rows, width), jnp.float32),
        in_specs=[pl.BlockSpec(memory_space=pl.ANY)],
        out_specs=pl.BlockSpec(memory_space=pl.ANY),
        scratch_shapes=scatter_scratch(line, rows, width, x.dtype),
        compiler_params=pltpu.CompilerParams(
            collective_id=collective, has_side_effects=True, vmem_limit_bytes=52 * MIB
        ),
        name=name,
    )(x)


QUERY_HEADS = 64
KEY_VALUE_HEADS = 8
HEAD_SIZE = 64
TOP = 4
EPSILON = 1e-05
THETA_BASE = 150000.0
CLAMP_LIMIT = 7.0
GLU_ALPHA = 1.702
MASK_FILL = -1e30
SPAN = 256
SCALE = HEAD_SIZE**-0.5


def contract(left, right, left_axis, right_axis):
    return lax.dot_general(
        left, right, (((left_axis,), (right_axis,)), ((), ())), preferred_element_type=jnp.float32
    )


def norm_scale(value_rows, gain_vec):
    return (
        value_rows
        * lax.rsqrt(jnp.mean(value_rows * value_rows, axis=-1, keepdims=True) + EPSILON)
        * gain_vec
    )


def soft_clamp(value_rows):
    return CLAMP_LIMIT * jnp.tanh(value_rows / CLAMP_LIMIT)


def glu_units(gate_lin, up_lin):
    gated = soft_clamp(gate_lin)
    return (soft_clamp(up_lin) + 1.0) * gated * jax.nn.sigmoid(GLU_ALPHA * gated)


def rotary_tables(length):
    half = HEAD_SIZE // 2
    inverse = THETA_BASE ** (-jnp.arange(half, dtype=jnp.float32) / half)
    angles = inverse[:, None] * jnp.arange(length, dtype=jnp.int32).astype(jnp.float32)[None, :]
    return jnp.cos(angles), jnp.sin(angles)


def turned(value, cosine, sine):
    half = HEAD_SIZE // 2
    first, second = value[:, :half], value[:, half:]
    return jnp.concatenate(
        [first * cosine - second * sine, second * cosine + first * sine], axis=1
    )


def diagonal(length):
    return lax.broadcasted_iota(jnp.int32, (length, length), 0) <= lax.broadcasted_iota(
        jnp.int32, (length, length), 1
    )


def masked_scores(key_rows, query_cols, count):
    scores = contract(key_rows, query_cols, 1, 0)
    edge = jnp.where(diagonal(SPAN), scores[count - SPAN :], MASK_FILL)
    if count == SPAN:
        return edge
    return jnp.concatenate([scores[: count - SPAN], edge], axis=0)


def attend_kernel(sink_ref, q_ref, k_ref, v_ref, out_ref, log_ref):
    sink = sink_ref[pl.program_id(0)]
    length = q_ref.shape[1]
    for start in range(0, length, SPAN):
        count = start + SPAN
        at = pl.ds(start, SPAN)
        query = q_ref[:, at] * jnp.bfloat16(SCALE)
        scores = masked_scores(k_ref[:count, :], query, count)
        row_top = jnp.maximum(jnp.max(scores, axis=0, keepdims=True), sink)
        weights = jnp.exp(scores - row_top)
        denominator = jnp.sum(weights, axis=0, keepdims=True) + jnp.exp(sink - row_top)
        probabilities = (weights / denominator).astype(jnp.bfloat16)
        out_ref[:, at] = contract(v_ref[:, :count], probabilities, 1, 0).astype(jnp.bfloat16)
        log_ref[0, :, at] = row_top + jnp.log(denominator)


def attend(sinks, queries, keys, values):
    heads, length = queries.shape[0] // HEAD_SIZE, queries.shape[1]
    per_head = pl.BlockSpec((HEAD_SIZE, length), lambda h: (h, 0))
    return pl.pallas_call(
        attend_kernel,
        grid=(heads,),
        out_shape=(
            jax.ShapeDtypeStruct(queries.shape, jnp.bfloat16),
            jax.ShapeDtypeStruct((heads, 1, length), jnp.float32),
        ),
        in_specs=[
            pl.BlockSpec(memory_space=pltpu.SMEM),
            per_head,
            pl.BlockSpec((length, HEAD_SIZE), lambda h: (0, 0)),
            pl.BlockSpec((HEAD_SIZE, length), lambda h: (0, 0)),
        ],
        out_specs=(per_head, pl.BlockSpec((1, 1, length), lambda h: (h, 0, 0))),
        compiler_params=pltpu.CompilerParams(vmem_limit_bytes=40 * MIB),
        cost_estimate=pl.CostEstimate(
            flops=heads * length * length * HEAD_SIZE * 4,
            bytes_accessed=heads * length * HEAD_SIZE * 4,
            transcendentals=heads * length * length,
        ),
        name="attend",
    )(sinks, queries, keys, values)


def attend_back_kernel(
    sink_ref, q_ref, k_ref, kt_ref, v_ref, grad_ref, log_ref, cos_ref, sin_ref,
    dq_ref, dk_ref, dv_ref, dsink_ref,
):
    head = pl.program_id(0)
    sink = sink_ref[head]
    length = q_ref.shape[1]
    half = HEAD_SIZE // 2

    @pl.when(head == 0)
    def _():
        dk_ref[...] = jnp.zeros_like(dk_ref)
        dv_ref[...] = jnp.zeros_like(dv_ref)

    grad_sink = jnp.zeros((1, SPAN), jnp.float32)
    for start in range(0, length, SPAN):
        count = start + SPAN
        at = pl.ds(start, SPAN)
        query = q_ref[:, at] * jnp.bfloat16(SCALE)
        grad = grad_ref[:, at]
        log_sum = log_ref[0, :, at]
        probabilities = jnp.exp(masked_scores(k_ref[:count, :], query, count) - log_sum)
        grad_probs = contract(v_ref[:count, :], grad, 1, 0)
        inner_sum = jnp.sum(probabilities * grad_probs, axis=0, keepdims=True)
        grad_scores = (probabilities * (grad_probs - inner_sum)).astype(jnp.bfloat16)
        grad_query = contract(kt_ref[:, :count], grad_scores, 1, 0) * SCALE
        first, second = grad_query[:half], grad_query[half:]
        cosine, sine = cos_ref[:, at], sin_ref[:, at]
        dq_ref[:half, at] = (first * cosine + second * sine).astype(jnp.bfloat16)
        dq_ref[half:, at] = (second * cosine - first * sine).astype(jnp.bfloat16)
        dk_ref[:count, :] += contract(grad_scores, query, 1, 1)
        dv_ref[:count, :] += contract(probabilities.astype(jnp.bfloat16), grad, 1, 1)
        grad_sink = grad_sink - jnp.exp(sink - log_sum) * inner_sum
    dsink_ref[0] = grad_sink


def attend_back(sinks, queries, keys, keys_t, values, grads, log_sums, cosine, sine):
    heads, length = queries.shape[0] // HEAD_SIZE, queries.shape[1]
    per_head = pl.BlockSpec((HEAD_SIZE, length), lambda h: (h, 0))

    def whole(*shape):
        return pl.BlockSpec(shape, lambda h: (0,) * len(shape))

    return pl.pallas_call(
        attend_back_kernel,
        grid=(heads,),
        out_shape=(
            jax.ShapeDtypeStruct(queries.shape, jnp.bfloat16),
            jax.ShapeDtypeStruct((length, HEAD_SIZE), jnp.float32),
            jax.ShapeDtypeStruct((length, HEAD_SIZE), jnp.float32),
            jax.ShapeDtypeStruct((heads, 1, SPAN), jnp.float32),
        ),
        in_specs=[
            pl.BlockSpec(memory_space=pltpu.SMEM),
            per_head,
            whole(length, HEAD_SIZE),
            whole(HEAD_SIZE, length),
            whole(length, HEAD_SIZE),
            per_head,
            pl.BlockSpec((1, 1, length), lambda h: (h, 0, 0)),
            whole(HEAD_SIZE // 2, length),
            whole(HEAD_SIZE // 2, length),
        ],
        out_specs=(
            per_head,
            whole(length, HEAD_SIZE),
            whole(length, HEAD_SIZE),
            pl.BlockSpec((1, 1, SPAN), lambda h: (h, 0, 0)),
        ),
        compiler_params=pltpu.CompilerParams(vmem_limit_bytes=48 * MIB),
        cost_estimate=pl.CostEstimate(
            flops=heads * length * length * HEAD_SIZE * 10,
            bytes_accessed=heads * length * HEAD_SIZE * 8,
            transcendentals=heads * length * length,
        ),
        name="attend_back",
    )(sinks, queries, keys, keys_t, values, grads, log_sums, cosine, sine)


PAIR = 2
STEP = 4


def routed(cols, capacity):
    expert = lax.axis_index("ctx")
    cols = cols.astype(jnp.float32)
    lane = lax.broadcasted_iota(jnp.int32, cols.shape, 1)
    place = jnp.sum(jnp.where(lane == 64 + expert, cols, 0.0), axis=1, keepdims=True)
    gate = jnp.sum(jnp.where(lane == 72 + expert, cols, 0.0), axis=1, keepdims=True)
    slot = lax.broadcasted_iota(jnp.int32, (cols.shape[0], PAIR * capacity), 1)
    picked = place.astype(jnp.int32) == slot
    return (
        jnp.where(picked, 1.0, 0.0).astype(jnp.bfloat16),
        jnp.where(picked, gate, 0.0).astype(jnp.bfloat16),
    )


class Stream:
    def __init__(self, arrays, sems, inward):
        self.arrays, self.sems, self.inward = arrays, sems, inward

    def copies(self, slot, block):
        made = []
        for k, (array, slots, count, column) in enumerate(self.arrays):
            at = pl.ds(pl.multiple_of(block * count, 16), count)
            far = array.at[at] if column is None else array.at[at, column]
            pair = (far, slots.at[slot]) if self.inward else (slots.at[slot], far)
            made.append(pltpu.make_async_copy(*pair, self.sems.at[slot, k]))
        return made

    def start(self, slot, block):
        for copy in self.copies(slot, block):
            copy.start()

    def wait(self, slot, block):
        for copy in self.copies(slot, block):
            copy.wait()


def two_of(shape, dtype):
    return pltpu.VMEM((2,) + shape, dtype)


def gather_and_compute(gather, held, loads, stores, compute):
    y_at = gather.me // 4
    for copy in held:
        copy.start()
    gather.begin()

    def block(step):
        half = lax.rem(step, 2)
        return gather.slot(step // 2) * 2 + (1 - half) * y_at + half * (1 - y_at)

    def body(step, carry):
        order, half = step // 2, lax.rem(step, 2)

        @pl.when(half == 0)
        def _():
            gather.second(order)
            pl.when(order + 1 < gather.line)(lambda: gather.first(order + 1))
            gather.near(order)

        pl.when(half == 1)(lambda: gather.third(order))

        @pl.when(step == 0)
        def _():
            gather.own_block()
            for copy in held:
                copy.wait()

        loads.start(half, block(step))

        pl.when(step >= 2)(lambda: stores.wait(half, block(step - 2)))
        loads.wait(half, block(step))
        compute(half)
        stores.start(half, block(step))
        return carry

    steps = 2 * gather.line
    lax.fori_loop(0, steps, body, 0)
    stores.wait(0, block(steps - 2))
    stores.wait(1, block(steps - 1))
    gather.end()


def expert_forward(sent, gate_w, up_w, down_w, gate_b, up_b, down_b, capacity, collective):
    low, f32 = jnp.bfloat16, jnp.float32
    block_rows, wide = sent.shape
    width, share = gate_w.shape
    span = PAIR * block_rows
    pairs = STEP // PAIR
    count = PAIR * capacity
    tokens = 32 * block_rows
    slot_rows = 32 * capacity

    def kernel(
        sent_ref, gate_hbm, up_hbm, down_hbm, gate_b_ref, up_b_ref, down_b_ref,
        all_ref, rows_out, gate_out, up_out, hidden_out, mix_out,
        gate_v, up_v, down_v, x_s, rows_s, gate_s, up_s, hidden_s, mix_s,
        held_sems, in_sems, out_sems, *sems,
    ):
        held = [
            pltpu.make_async_copy(source, target, held_sems.at[k])
            for k, (source, target) in enumerate(
                ((gate_hbm, gate_v), (up_hbm, up_v), (down_hbm, down_v))
            )
        ]
        loads = Stream([(all_ref, x_s, pairs * span, None)], in_sems, True)
        stores = Stream(
            [
                (rows_out, rows_s, pairs * count, None),
                (gate_out, gate_s, pairs * count, None),
                (up_out, up_s, pairs * count, None),
                (hidden_out, hidden_s, pairs * count, None),
                (mix_out, mix_s, pairs * span, None),
            ],
            out_sems,
            False,
        )

        def compute(slot):
            spans = [pl.ds(pair * span, span) for pair in range(pairs)]
            picks = [routed(x_s[slot, at, wide - 128 :], capacity) for at in spans]
            rows = jnp.concatenate(
                [contract(picks[k][0], x_s[slot, spans[k], :], 0, 0) for k in range(pairs)],
                axis=0,
            ).astype(low)
            rows_s[slot] = rows
            rows = rows[:, :width]
            gate_lin = contract(rows, gate_v[...], 1, 0) + gate_b_ref[...]
            up_lin = contract(rows, up_v[...], 1, 0) + up_b_ref[...]
            gate_s[slot] = gate_lin
            up_s[slot] = up_lin
            hidden = glu_units(gate_lin, up_lin).astype(low)
            hidden_s[slot] = hidden
            out = contract(hidden, down_v[...], 1, 0) + down_b_ref[...]
            for k in range(pairs):
                part = out[k * count : (k + 1) * count].astype(low)
                mix_s[slot, spans[k], :] = contract(picks[k][1], part, 1, 0).astype(low)

        gather = Gather(4, sent_ref, all_ref, sems)
        gather_and_compute(gather, held, loads, stores, compute)

    hbm = pl.BlockSpec(memory_space=pl.ANY)
    vmem = pl.BlockSpec(memory_space=pltpu.VMEM)
    return pl.pallas_call(
        kernel,
        out_shape=(
            jax.ShapeDtypeStruct((tokens, wide), low),
            jax.ShapeDtypeStruct((slot_rows, wide), low),
            jax.ShapeDtypeStruct((slot_rows, share), f32),
            jax.ShapeDtypeStruct((slot_rows, share), f32),
            jax.ShapeDtypeStruct((slot_rows, share), low),
            jax.ShapeDtypeStruct((tokens, width), low),
        ),
        in_specs=[hbm, hbm, hbm, hbm, vmem, vmem, vmem],
        out_specs=(hbm,) * 6,
        scratch_shapes=[
            pltpu.VMEM(gate_w.shape, low),
            pltpu.VMEM(up_w.shape, low),
            pltpu.VMEM(down_w.shape, low),
            two_of((pairs * span, wide), low),
            two_of((pairs * count, wide), low),
            two_of((pairs * count, share), f32),
            two_of((pairs * count, share), f32),
            two_of((pairs * count, share), low),
            two_of((pairs * span, width), low),
            pltpu.SemaphoreType.DMA((3,)),
            pltpu.SemaphoreType.DMA((2, 1)),
            pltpu.SemaphoreType.DMA((2, 5)),
            *gather_sems(4),
        ],
        compiler_params=pltpu.CompilerParams(
            collective_id=collective, has_side_effects=True, vmem_limit_bytes=60 * MIB
        ),
        name="expert_forward",
    )(sent, gate_w, up_w, down_w, gate_b, up_b, down_b)


def expert_backward(sent, all_normed, gate_w, up_w, down_w, gate_lin, up_lin, capacity, collective):
    low, f32 = jnp.bfloat16, jnp.float32
    block_rows = sent.shape[0]
    wide = all_normed.shape[1]
    width, share = gate_w.shape
    span = PAIR * block_rows
    pairs = STEP // PAIR
    count = PAIR * capacity
    tokens = 32 * block_rows
    slot_rows = 32 * capacity

    def kernel(
        sent_ref, normed_hbm, gate_hbm, up_hbm, down_hbm, gate_lin_hbm, up_lin_hbm,
        all_ref, rows_out, gate_out, up_out, tokens_out, down_sum, gate_sum, up_sum,
        gate_v, up_v, down_v, grad_s, cols_s, gate_s, up_s, rows_s, gate_gs, up_gs, tokens_s,
        held_sems, in_sems, out_sems, *sems,
    ):
        held = [
            pltpu.make_async_copy(source, target, held_sems.at[k])
            for k, (source, target) in enumerate(
                ((gate_hbm, gate_v), (up_hbm, up_v), (down_hbm, down_v))
            )
        ]
        loads = Stream(
            [
                (all_ref, grad_s, pairs * span, None),
                (normed_hbm, cols_s, pairs * span, pl.ds(wide - 128, 128)),
                (gate_lin_hbm, gate_s, pairs * count, None),
                (up_lin_hbm, up_s, pairs * count, None),
            ],
            in_sems,
            True,
        )
        stores = Stream(
            [
                (rows_out, rows_s, pairs * count, None),
                (gate_out, gate_gs, pairs * count, None),
                (up_out, up_gs, pairs * count, None),
                (tokens_out, tokens_s, pairs * span, None),
            ],
            out_sems,
            False,
        )
        down_sum[...] = jnp.zeros_like(down_sum)
        gate_sum[...] = jnp.zeros_like(gate_sum)
        up_sum[...] = jnp.zeros_like(up_sum)

        def compute(slot):
            spans = [pl.ds(pair * span, span) for pair in range(pairs)]
            picks = [routed(cols_s[slot, at, :], capacity) for at in spans]
            rows = jnp.concatenate(
                [contract(picks[k][1], grad_s[slot, spans[k], :], 0, 0) for k in range(pairs)],
                axis=0,
            ).astype(low)
            rows_s[slot, :, :width] = rows
            rows_s[slot, :, width:] = jnp.zeros((pairs * count, wide - width), low)
            down_sum[...] += jnp.sum(rows.astype(f32), axis=0, keepdims=True)
            grad_units = contract(rows, down_v[...], 1, 1)
            gate_tanh = jnp.tanh(gate_s[slot] / CLAMP_LIMIT)
            up_tanh = jnp.tanh(up_s[slot] / CLAMP_LIMIT)
            gated = CLAMP_LIMIT * gate_tanh
            lifted = CLAMP_LIMIT * up_tanh + 1.0
            part = jax.nn.sigmoid(GLU_ALPHA * gated)
            grad_up = (grad_units * gated * part * (1.0 - up_tanh * up_tanh)).astype(low)
            slope = part * (1.0 + GLU_ALPHA * gated * (1.0 - part))
            grad_gate = (grad_units * lifted * slope * (1.0 - gate_tanh * gate_tanh)).astype(low)
            gate_gs[slot] = grad_gate
            up_gs[slot] = grad_up
            gate_sum[...] += jnp.sum(grad_gate.astype(f32), axis=0, keepdims=True)
            up_sum[...] += jnp.sum(grad_up.astype(f32), axis=0, keepdims=True)
            copies = contract(grad_gate, gate_v[...], 1, 1) + contract(grad_up, up_v[...], 1, 1)
            for k in range(pairs):
                part = copies[k * count : (k + 1) * count].astype(low)
                tokens_s[slot, spans[k], :] = contract(picks[k][0], part, 1, 0).astype(low)

        gather = Gather(4, sent_ref, all_ref, sems)
        gather_and_compute(gather, held, loads, stores, compute)

    hbm = pl.BlockSpec(memory_space=pl.ANY)
    vmem = pl.BlockSpec(memory_space=pltpu.VMEM)
    return pl.pallas_call(
        kernel,
        out_shape=(
            jax.ShapeDtypeStruct((tokens, width), low),
            jax.ShapeDtypeStruct((slot_rows, wide), low),
            jax.ShapeDtypeStruct((slot_rows, share), low),
            jax.ShapeDtypeStruct((slot_rows, share), low),
            jax.ShapeDtypeStruct((tokens, width), low),
            jax.ShapeDtypeStruct((1, width), f32),
            jax.ShapeDtypeStruct((1, share), f32),
            jax.ShapeDtypeStruct((1, share), f32),
        ),
        in_specs=[hbm] * 7,
        out_specs=(hbm,) * 5 + (vmem,) * 3,
        scratch_shapes=[
            pltpu.VMEM(gate_w.shape, low),
            pltpu.VMEM(up_w.shape, low),
            pltpu.VMEM(down_w.shape, low),
            two_of((pairs * span, width), low),
            two_of((pairs * span, 128), low),
            two_of((pairs * count, share), f32),
            two_of((pairs * count, share), f32),
            two_of((pairs * count, wide), low),
            two_of((pairs * count, share), low),
            two_of((pairs * count, share), low),
            two_of((pairs * span, width), low),
            pltpu.SemaphoreType.DMA((3,)),
            pltpu.SemaphoreType.DMA((2, 4)),
            pltpu.SemaphoreType.DMA((2, 4)),
            *gather_sems(4),
        ],
        compiler_params=pltpu.CompilerParams(
            collective_id=collective, has_side_effects=True, vmem_limit_bytes=60 * MIB
        ),
        name="expert_backward",
    )(sent, all_normed, gate_w, up_w, down_w, gate_lin, up_lin)


def expert_weights(parts, rows_in, gate_grad, up_grad, collective):
    low, f32 = jnp.bfloat16, jnp.float32
    slot_rows, wide = rows_in.shape
    share = gate_grad.shape[1]
    block_rows, width = parts.shape[0] // 32, parts.shape[1]
    cut = 256
    whole, rest = width // cut, width % cut
    wide_rest = wide - whole * cut
    count = whole + 1

    def kernel(
        parts_ref, rows_hbm, gate_hbm, up_hbm, o_ref, gate_out, up_out,
        gate_v, up_v, in_s, gate_s, up_s, held_sems, in_sems, out_sems, *scratch,
    ):
        held = [
            pltpu.make_async_copy(gate_hbm, gate_v, held_sems.at[0]),
            pltpu.make_async_copy(up_hbm, up_v, held_sems.at[1]),
        ]
        for copy in held:
            copy.start()

        def load(chunk, columns):
            slot = lax.rem(chunk, 2)
            at = pl.ds(pl.multiple_of(chunk * cut, cut), columns)
            return pltpu.make_async_copy(
                rows_hbm.at[:, at], in_s.at[slot, :, pl.ds(0, columns)], in_sems.at[slot]
            )

        def store(chunk, rows, k):
            slot = lax.rem(chunk, 2)
            at = pl.ds(pl.multiple_of(chunk * cut, cut), rows)
            source, target = ((gate_s, gate_out), (up_s, up_out))[k]
            return pltpu.make_async_copy(
                source.at[slot, pl.ds(0, rows)], target.at[at], out_sems.at[slot, k]
            )

        def loads(chunk, act):
            pl.when(chunk < whole)(lambda: act(load(chunk, cut)))
            pl.when(chunk == whole)(lambda: act(load(chunk, wide_rest)))

        def stores(chunk, act):
            def do(rows):
                for k in range(2):
                    act(store(chunk, rows, k))

            pl.when(chunk < whole)(lambda: do(cut))
            pl.when(chunk == whole)(lambda: do(rest))

        def begin(copy):
            copy.start()

        def await_it(copy):
            copy.wait()

        def work(chunk):
            slot = lax.rem(chunk, 2)

            @pl.when(chunk == 0)
            def _():
                loads(0, begin)
                for copy in held:
                    copy.wait()

            pl.when(chunk + 1 < count)(lambda: loads(chunk + 1, begin))
            pl.when(chunk >= 2)(lambda: stores(chunk - 2, await_it))
            loads(chunk, await_it)
            turned_rows = in_s[slot].T
            gate_s[slot] = contract(turned_rows, gate_v[...], 1, 0)
            up_s[slot] = contract(turned_rows, up_v[...], 1, 0)
            stores(chunk, begin)

        Scatter(4, parts_ref, o_ref, scratch).run(work, count - 12)
        stores(count - 2, await_it)
        stores(count - 1, await_it)

    hbm = pl.BlockSpec(memory_space=pl.ANY)
    return pl.pallas_call(
        kernel,
        out_shape=(
            jax.ShapeDtypeStruct((block_rows, width), f32),
            jax.ShapeDtypeStruct((width, share), f32),
            jax.ShapeDtypeStruct((width, share), f32),
        ),
        in_specs=[hbm] * 4,
        out_specs=(hbm,) * 3,
        scratch_shapes=[
            pltpu.VMEM(gate_grad.shape, low),
            pltpu.VMEM(up_grad.shape, low),
            two_of((slot_rows, cut), low),
            two_of((cut, share), f32),
            two_of((cut, share), f32),
            pltpu.SemaphoreType.DMA((2,)),
            pltpu.SemaphoreType.DMA((2,)),
            pltpu.SemaphoreType.DMA((2, 2)),
            *scatter_scratch(4, block_rows, width, low),
        ],
        compiler_params=pltpu.CompilerParams(
            collective_id=collective, has_side_effects=True, vmem_limit_bytes=60 * MIB
        ),
        name="expert_weights",
    )(parts, rows_in, gate_grad, up_grad)


def product_kernel(left_ref, right_ref, out_ref):
    out_ref[...] = contract(left_ref[...], right_ref[...], 0, 0).astype(out_ref.dtype)


def product(left_t, right, name):
    depth, rows = left_t.shape
    columns = right.shape[1]
    return pl.pallas_call(
        product_kernel,
        grid=(rows // SPAN,),
        out_shape=jax.ShapeDtypeStruct((rows, columns), jnp.bfloat16),
        in_specs=[
            pl.BlockSpec((depth, SPAN), lambda i: (0, i)),
            pl.BlockSpec((depth, columns), lambda i: (0, 0), pipeline_mode=pl.Buffered(1)),
        ],
        out_specs=pl.BlockSpec((SPAN, columns), lambda i: (i, 0)),
        compiler_params=pltpu.CompilerParams(vmem_limit_bytes=40 * MIB),
        cost_estimate=pl.CostEstimate(
            flops=2 * depth * rows * columns, bytes_accessed=4 * rows * columns, transcendentals=0
        ),
        name=name,
    )(left_t, right)


def shards(
    layer_input, cotangent, gate_weights, routes, w_query, key_projection, value_projection, w_out,
    b_query, key_bias_vector, value_bias_vector, b_out, learned_sink_logits, gain_attn, gain_ffn,
    w_gate, w_up, w_down, b_gate, b_up, b_down,
):
    low = jnp.bfloat16
    ctx_n, z_n = lax.axis_size("ctx"), lax.axis_size("fsdp")
    ctx_at, z_at = lax.axis_index("ctx"), lax.axis_index("fsdp")
    tuned = ctx_n == 8 and z_n == 4
    width = layer_input.shape[-1]
    rows = layer_input.shape[0] * layer_input.shape[1]
    length = rows * ctx_n
    blocks = ctx_n * z_n
    capacity = max(2, rows * TOP * 17 // (16 * ctx_n))
    heads = QUERY_HEADS // ctx_n
    spread = ctx_n // KEY_VALUE_HEADS
    f32 = jnp.float32

    def gather_plane(value, call):
        if tuned:
            return gather_blocks(value, 1, call, f"gather_plane_{call}").reshape(length, width)
        return lax.all_gather(value, "ctx", axis=0, tiled=True)

    def scatter_plane(value, call):
        if tuned:
            return scatter_blocks(value, 1, call, f"scatter_plane_{call}")
        return lax.psum_scatter(value, "ctx", scatter_dimension=0, tiled=True).astype(f32)

    residual = layer_input.reshape(rows, width).astype(f32)
    grad_final = cotangent.reshape(rows, width)
    gain_attn_f, gain_ffn_f = gain_attn.astype(f32), gain_ffn.astype(f32)
    cosine, sine = rotary_tables(length)

    q_cols, k_cols = w_query.shape[1], key_projection.shape[1]
    own_rows = q_cols + 2 * k_cols
    padded = own_rows + 8
    biases = jnp.concatenate([b_query, key_bias_vector, value_bias_vector])
    own_weights = jnp.concatenate(
        [
            w_query.T,
            key_projection.T,
            value_projection.T,
            jnp.pad(biases[None, :], ((0, 7), (0, width - own_rows))),
        ],
        axis=0,
    )
    head_weights = lax.all_gather(own_weights, "fsdp", axis=0, tiled=True)
    out_weights = lax.all_gather(w_out, "fsdp", axis=0, tiled=True)

    token_routes = routes.reshape(rows, TOP)
    names = jnp.arange(ctx_n, dtype=jnp.int32)
    named = token_routes[:, :, None] == names[None, None, :]
    hits = jnp.sum(named.astype(f32), axis=1)
    gates = jnp.sum(
        jnp.where(named, gate_weights.reshape(rows, TOP)[:, :, None].astype(f32), 0.0), axis=1
    )
    earlier = (
        lax.broadcasted_iota(jnp.int32, (rows, rows), 0)
        > lax.broadcasted_iota(jnp.int32, (rows, rows), 1)
    ).astype(low)
    places = jnp.dot(earlier, hits.astype(low), preferred_element_type=f32)
    first_slot = (lax.rem(ctx_at, PAIR) * capacity).astype(f32) if tuned else 0.0
    places = jnp.where(hits > 0, places + first_slot, -1.0)
    slot_rows = blocks * capacity
    if not tuned:
        slots = jnp.arange(capacity, dtype=f32)[None, :, None]
        picked = places.T[:, None, :] == slots
        select = picked.astype(low)
        mixing = jnp.where(picked, gates.T[:, None, :], 0.0).astype(low)

    def exchanged(slot_values):
        moved = slot_values.reshape(ctx_n, capacity, width)
        return lax.all_to_all(moved, "ctx", split_axis=0, concat_axis=0, tiled=True)

    def to_slots(picks, token_rows):
        dims = (((2,), (0,)), ((), ()))
        moved = lax.dot_general(picks, token_rows, dims, preferred_element_type=f32).astype(low)
        moved = lax.all_gather(exchanged(moved), "fsdp", axis=0, tiled=True)
        return moved.reshape(slot_rows, width)

    def to_tokens(picks, slot_values):
        slot_values = exchanged(
            lax.psum_scatter(slot_values, "fsdp", scatter_dimension=0, tiled=True)
        )
        dims = (((1,), (1,)), ((0,), (0,)))
        moved = lax.dot_general(picks, slot_values, dims, preferred_element_type=f32)
        return jnp.sum(moved, axis=0)

    normed_own = norm_scale(residual, gain_attn_f).astype(low)
    normed_attn = gather_plane(normed_own, 1)
    lin = contract(head_weights, normed_attn, 1, 1).reshape(z_n, padded, length)
    head_bias = head_weights.reshape(z_n, padded, width)[:, own_rows, :own_rows].astype(f32)
    lin = lin[:, :own_rows] + head_bias[:, :, None]
    query_lin = lin[:, :q_cols].reshape(heads, HEAD_SIZE, length)
    kv_lin = jnp.stack([lin[:, q_cols : q_cols + k_cols], lin[:, q_cols + k_cols :]])
    kv_lin = kv_lin.reshape(2, z_n * k_cols, length)
    swap = [(i, i ^ 1) for i in range(ctx_n)]
    odd = lax.rem(ctx_at, 2) == 1
    if spread == 2:
        other = lax.ppermute(kv_lin, "ctx", swap)
        kv_lin = jnp.where(
            odd,
            jnp.concatenate([other, kv_lin], axis=1),
            jnp.concatenate([kv_lin, other], axis=1),
        )
    queries = turned(query_lin, cosine, sine).astype(low).reshape(heads * HEAD_SIZE, length)
    keys_t = turned(kv_lin[:1], cosine, sine)[0].astype(low)
    values_t = kv_lin[1].astype(low)
    keys, values = keys_t.T, values_t.T
    sinks = lax.dynamic_slice(learned_sink_logits.astype(f32), (ctx_at * heads,), (heads,))
    attended, log_sums = attend(sinks, queries, keys, values_t)
    branch_part = product(attended, out_weights, "branch")
    branch = scatter_plane(branch_part, 2) + b_out.astype(f32)
    middle = residual + branch
    normed_ffn = norm_scale(middle, gain_ffn_f).astype(low)

    gate_w, up_w, down_w = w_gate[0], w_up[0], w_down[0]
    share = b_down.shape[1]
    gate_b, up_b = b_gate.astype(f32), b_up.astype(f32)
    down_bias = lax.dynamic_update_slice(
        jnp.zeros((1, width), f32), b_down.astype(f32), (0, z_at * share)
    )
    if tuned:
        wide = -(-(width + 2 * ctx_n) // 128) * 128
        sent = jnp.concatenate(
            [
                normed_ffn,
                places.astype(low),
                gates.astype(low),
                jnp.zeros((rows, wide - width - 2 * ctx_n), low),
            ],
            axis=1,
        )
        all_normed, expert_in, gate_lin, up_lin, hidden_units, mix_part = expert_forward(
            sent, gate_w, up_w, down_w, gate_b, up_b, down_bias, capacity, 3
        )
        unused, grad_expert_out, grad_gate_lin, grad_up_lin, grad_normed_part, *grad_biases = (
            expert_backward(
                grad_final, all_normed, gate_w, up_w, down_w, gate_lin, up_lin, capacity, 4
            )
        )
        grad_b_down, grad_b_gate, grad_b_up = [value[0] for value in grad_biases]
        grad_normed_ffn, grad_w_gate, grad_w_up = expert_weights(
            grad_normed_part, expert_in, grad_gate_lin, grad_up_lin, 6
        )
        expert_mix = scatter_blocks(mix_part, 4, 5, "scatter_all_5")
    else:
        expert_in = to_slots(select, normed_ffn)
        gate_lin = contract(expert_in, gate_w, 1, 0) + gate_b
        up_lin = contract(expert_in, up_w, 1, 0) + up_b
        hidden_f, unit_back = jax.vjp(glu_units, gate_lin, up_lin)
        hidden_units = hidden_f.astype(low)
        expert_out = (contract(hidden_units, down_w, 1, 0) + down_bias).astype(low)
        expert_mix = to_tokens(mixing, expert_out)
        grad_expert_out = to_slots(mixing, grad_final)
        grad_units = contract(grad_expert_out, down_w, 1, 1)
        grad_gate_f, grad_up_f = unit_back(grad_units)
        grad_gate_lin, grad_up_lin = grad_gate_f.astype(low), grad_up_f.astype(low)
        grad_copy = contract(grad_gate_lin, gate_w, 1, 1) + contract(grad_up_lin, up_w, 1, 1)
        grad_normed_ffn = to_tokens(select, grad_copy.astype(low))
        grad_b_down = jnp.sum(grad_expert_out.astype(f32), axis=0)
        grad_b_gate = jnp.sum(grad_gate_lin.astype(f32), axis=0)
        grad_b_up = jnp.sum(grad_up_lin.astype(f32), axis=0)
        grad_w_gate = contract(expert_in, grad_gate_lin, 0, 0)
        grad_w_up = contract(expert_in, grad_up_lin, 0, 0)
    final_out = (middle + expert_mix).astype(low).reshape(layer_input.shape)
    grad_w_down = contract(hidden_units, grad_expert_out, 0, 0)[:, :width]
    grad_b_down = lax.dynamic_slice(grad_b_down, (z_at * share,), (share,))

    unused, norm_back = jax.vjp(norm_scale, middle, gain_ffn_f)
    grad_middle_part, grad_gain_ffn = norm_back(grad_normed_ffn)
    grad_middle = grad_final.astype(f32) + grad_middle_part
    grad_branch_own = grad_middle.astype(low)
    grad_branch = gather_plane(grad_branch_own, 7)
    grad_b_out = jnp.sum(grad_branch_own.astype(f32), axis=0)
    grad_attended = contract(out_weights, grad_branch, 1, 1).astype(low)
    grad_out_part = contract(attended, grad_branch, 1, 0).astype(low)
    grad_query, grad_keys, grad_values, grad_sink_parts = attend_back(
        sinks, queries, keys, keys_t, values, grad_attended, log_sums, cosine, sine
    )
    grad_kv = jnp.stack([turned(grad_keys.T[None], cosine, -sine)[0], grad_values.T])
    if spread == 2:
        grad_kv = grad_kv + lax.ppermute(grad_kv, "ctx", swap)
        halves = grad_kv.reshape(2, 2, HEAD_SIZE // 2, length)
        grad_kv = jnp.where(odd, halves[:, 1], halves[:, 0])
    grad_kv = grad_kv.astype(low).reshape(2, z_n, k_cols, length)
    grad_lin = jnp.concatenate(
        [
            grad_query.reshape(z_n, q_cols, length),
            grad_kv[0],
            grad_kv[1],
            jnp.zeros((z_n, padded - own_rows, length), low),
        ],
        axis=1,
    )
    grad_normed_part = product(grad_lin.reshape(z_n * padded, length), head_weights, "grad_normed")
    grad_normed_attn = scatter_plane(grad_normed_part, 8)
    grad_weights = contract(grad_lin.reshape(z_n * padded, length), normed_attn, 1, 0)
    grad_weights = grad_weights.reshape(z_n, padded, width)[:, :own_rows]
    grad_biases = jnp.sum(grad_lin[:, :own_rows].astype(f32), axis=2)
    grad_weights = jnp.concatenate(
        [
            grad_weights.astype(low),
            jnp.pad(grad_biases[:, None, :], ((0, 0), (0, 7), (0, width - own_rows))).astype(low),
        ],
        axis=1,
    ).reshape(z_n * padded, width)
    grad_w_out = lax.psum_scatter(grad_out_part, "fsdp", scatter_dimension=0, tiled=True).astype(f32)
    own_grads = lax.psum_scatter(grad_weights, "fsdp", scatter_dimension=0, tiled=True).astype(f32)
    grad_w_query = own_grads[:q_cols].T
    grad_w_key = own_grads[q_cols : q_cols + k_cols].T
    grad_w_value = own_grads[q_cols + k_cols : own_rows].T
    own_bias_grads = own_grads[own_rows, :own_rows]
    unused, norm_back = jax.vjp(norm_scale, residual, gain_attn_f)
    grad_residual_part, grad_gain_attn = norm_back(grad_normed_attn)
    input_grad = (grad_middle + grad_residual_part).reshape(layer_input.shape)
    grad_sinks = lax.dynamic_update_slice(
        jnp.zeros((QUERY_HEADS,), f32), jnp.sum(grad_sink_parts, axis=(1, 2)), (ctx_at * heads,)
    )
    sums = (grad_b_out, grad_gain_attn, grad_gain_ffn, grad_sinks)
    if tuned:
        joined = jnp.concatenate(sums)
        columns = -(-joined.shape[0] // (16 * 128)) * 128
        joined = jnp.pad(joined, (0, 16 * columns - joined.shape[0])).reshape(16, columns)
        joined = gather_blocks(joined, 4, 9, "gather_small").reshape(blocks, 16 * columns)
        joined = jnp.sum(joined, axis=0)
        cuts = (width, 2 * width, 3 * width, 3 * width + QUERY_HEADS)
        sums = [joined[at - value.shape[0] : at] for at, value in zip(cuts, sums)]
    else:
        sums = lax.psum(sums, ("ctx", "fsdp"))
    grad_b_out, grad_gain_attn, grad_gain_ffn, grad_sink_logits = sums
    return (
        final_out,
        input_grad,
        grad_w_query,
        grad_w_key,
        grad_w_value,
        grad_w_out,
        own_bias_grads[:q_cols],
        own_bias_grads[q_cols : q_cols + k_cols],
        own_bias_grads[q_cols + k_cols :],
        grad_b_out,
        grad_sink_logits,
        grad_gain_attn,
        grad_gain_ffn,
        grad_w_gate[None],
        grad_w_up[None],
        grad_w_down[None],
        grad_b_gate[None],
        grad_b_up[None],
        grad_b_down[None],
    )


def solution(mesh):
    return jax.shard_map(
        shards,
        mesh=mesh,
        in_specs=(
            P("fsdp", "ctx", None),
            P("fsdp", "ctx", None),
            P("fsdp", "ctx", None),
            P("fsdp", "ctx", None),
            P(None, ("ctx", "fsdp")),
            P(None, ("ctx", "fsdp")),
            P(None, ("ctx", "fsdp")),
            P(("ctx", "fsdp"), None),
            P(("ctx", "fsdp")),
            P(("ctx", "fsdp")),
            P(("ctx", "fsdp")),
            P(),
            P(),
            P(),
            P(),
            P("ctx", None, "fsdp"),
            P("ctx", None, "fsdp"),
            P("ctx", "fsdp", None),
            P("ctx", "fsdp"),
            P("ctx", "fsdp"),
            P("ctx", "fsdp"),
        ),
        out_specs=(
            P("fsdp", "ctx", None),
            P("fsdp", "ctx", None),
            P(None, ("ctx", "fsdp")),
            P(None, ("ctx", "fsdp")),
            P(None, ("ctx", "fsdp")),
            P(("ctx", "fsdp"), None),
            P(("ctx", "fsdp")),
            P(("ctx", "fsdp")),
            P(("ctx", "fsdp")),
            P(),
            P(),
            P(),
            P(),
            P("ctx", None, "fsdp"),
            P("ctx", None, "fsdp"),
            P("ctx", "fsdp", None),
            P("ctx", "fsdp"),
            P("ctx", "fsdp"),
            P("ctx", "fsdp"),
        ),
        check_vma=False,
    )
```

```python
import jax
import jax.numpy as jnp
from jax import lax
from jax.experimental import pallas as pl
from jax.experimental.pallas import tpu as pltpu
from jax.sharding import PartitionSpec as P

MESH = pl.DeviceIdType.MESH
MIB = 1 << 20


def remote(src, dst, send_sem, recv_sem, device):
    return pltpu.make_async_remote_copy(
        src_ref=src,
        dst_ref=dst,
        send_sem=send_sem,
        recv_sem=recv_sem,
        device_id=device,
        device_id_type=MESH,
    )


def neighbours():
    me = lax.axis_index("ctx")
    core = lax.rem(me, 2)
    x_at = lax.rem(me // 2, 2)
    y_at = me // 4
    return me, me + 1 - 2 * core, me + 2 - 4 * x_at, me + 4 - 8 * y_at, 2 - 4 * x_at


def greet(others, line, z_at):
    barrier = pltpu.get_barrier_semaphore()
    for other in others:
        pl.semaphore_signal(barrier, 1, device_id=(other, z_at), device_id_type=MESH)
    if line == 1:
        pl.semaphore_wait(barrier, len(others))
        return
    me = lax.axis_index("ctx")

    @pl.when(z_at > 0)
    def _():
        pl.semaphore_signal(barrier, 1, device_id=(me, z_at - 1), device_id_type=MESH)

    @pl.when(z_at < line - 1)
    def _():
        pl.semaphore_signal(barrier, 1, device_id=(me, z_at + 1), device_id_type=MESH)

    inner = (lax.rem(z_at, 3) + 1) // 2
    pl.semaphore_wait(barrier, len(others) + 1 + inner)


def gather_sems(line):
    return [
        pltpu.SemaphoreType.DMA,
        pltpu.SemaphoreType.DMA((line, 2)),
        pltpu.SemaphoreType.DMA((line,)),
        pltpu.SemaphoreType.DMA((line, 9)),
        pltpu.SemaphoreType.DMA((line, 9)),
    ]


class Gather:
    def __init__(self, line, x_ref, o_ref, sems):
        self.line, self.x_ref, self.o_ref = line, x_ref, o_ref
        self.own_sem, self.z_send, self.z_recv, self.p_send, self.p_recv = sems
        self.z_at = lax.axis_index("fsdp")
        self.me, self.mate, self.near_x, self.near_y, step_x = neighbours()
        self.across = self.near_y + step_x
        self.rows = x_ref.shape[0]
        self.half = self.rows // 2
        self.middle = (self.z_at == 1) | (self.z_at == 2)
        self.first_slot = self.z_at if line > 1 else 0

    def slot(self, order):
        z_at = self.z_at
        if self.line == 1:
            return 0
        second = z_at + 1 - 2 * lax.rem(z_at, 2)
        third = 2 - z_at // 2
        fourth = 3 - 3 * (z_at // 2)
        return jnp.where(
            order == 0, z_at, jnp.where(order == 1, second, jnp.where(order == 2, third, fourth))
        )

    def there(self, slot, place, part=None):
        start, count = (slot * 8 + place) * self.rows, self.rows
        if part is not None:
            start, count = start + part * self.half, self.half
        return self.o_ref.at[pl.ds(pl.multiple_of(start, self.half), count)]

    def z_copy(self, src_ref, slot, way, target):
        return remote(
            src_ref,
            self.there(slot, self.me),
            self.z_send.at[slot, way],
            self.z_recv.at[slot],
            (self.me, target),
        )

    def up(self):
        return self.z_copy(self.x_ref, self.z_at, 0, self.z_at + 1)

    def down(self):
        return self.z_copy(self.x_ref, self.z_at, 1, self.z_at - 1)

    def onward(self, order):
        slot = self.slot(order)
        target = jnp.where(order == 1, 3 - self.z_at, 3 * self.z_at - 3)
        return self.z_copy(self.there(slot, self.me), slot, 0, target)

    def copy(self, order, place, kind, device, part=None, src_ref=None):
        dst_ref = self.there(self.slot(order), place, part)
        return remote(
            dst_ref if src_ref is None else src_ref,
            dst_ref,
            self.p_send.at[order, kind],
            self.p_recv.at[order, kind],
            (device, self.z_at),
        )

    def out(self, order, src_ref=None):
        return [
            self.copy(order, self.me, 0, self.near_x, None, src_ref),
            self.copy(order, self.me, 1, self.near_y, None, src_ref),
            self.copy(order, self.me, 2, self.mate, None, src_ref),
        ]

    def passed(self, order, *which):
        places = (
            (self.near_x, 3, self.near_y, 0),
            (self.near_x, 5, self.mate, None),
            (self.near_y, 4, self.near_x, 1),
            (self.near_y, 6, self.mate, None),
            (self.across, 7, self.mate, 0),
            (self.across, 8, self.mate, 1),
        )
        return [self.copy(order, *places[k]) for k in which]

    def begin(self, met=False):
        line, z_at = self.line, self.z_at
        if not met:
            greet((self.mate, self.near_x, self.near_y), line, z_at)
        own = pltpu.make_async_copy(
            self.x_ref, self.there(self.first_slot, self.me), self.own_sem
        )
        own.start()
        if line > 1:
            self.begin_line()
        for copy in self.out(0, self.x_ref):
            copy.start()

    def begin_line(self):
        pl.when(self.z_at < self.line - 1)(lambda: self.up().start())
        pl.when(self.z_at > 0)(lambda: self.down().start())

    def own_block(self):
        pltpu.make_async_copy(
            self.x_ref, self.there(self.first_slot, self.me), self.own_sem
        ).wait()

    def from_line(self, order):
        slot = self.slot(order)
        self.z_copy(self.there(slot, self.me), slot, 0, self.z_at).wait_recv()

    def first(self, order):
        at_end = jnp.logical_not(self.middle)
        pl.when(at_end | (order == 1))(lambda: self.from_line(order))

        @pl.when(self.middle & (order == 1))
        def _():
            self.onward(1).start()
            self.from_line(2)
            self.onward(2).start()

        @pl.when(self.middle & (order == 2))
        def _():
            self.from_line(3)
            self.onward(3).start()

        for copy in self.out(order):
            copy.start()

    def second(self, order):
        to_y, mate_x, to_x, mate_y = self.passed(order, 0, 1, 2, 3)
        self.copy(order, self.near_x, 0, self.near_x).wait_recv()
        to_y.start()
        mate_x.start()
        self.copy(order, self.near_y, 1, self.near_y).wait_recv()
        to_x.start()
        mate_y.start()

    def near(self, order):
        step = self.mate - self.me
        self.copy(order, self.mate, 2, self.mate).wait_recv()
        self.copy(order, self.near_x + step, 5, self.mate).wait_recv()

    def third(self, order):
        step = self.mate - self.me
        top, low = self.passed(order, 4, 5)
        self.copy(order, self.across, 3, self.near_y, 0).wait_recv()
        top.start()
        self.copy(order, self.across, 4, self.near_x, 1).wait_recv()
        low.start()
        self.copy(order, self.near_y + step, 6, self.mate).wait_recv()
        self.copy(order, self.across + step, 7, self.mate, 0).wait_recv()
        self.copy(order, self.across + step, 8, self.mate, 1).wait_recv()

    def end(self, from_order=0):
        line, z_at = self.line, self.z_at

        def sent(order, carry):
            for copy in self.out(order) + self.passed(order, 0, 1, 2, 3, 4, 5):
                copy.wait_send()
            return carry

        lax.fori_loop(from_order, line, sent, 0)
        if line > 1:
            pl.when(z_at < line - 1)(lambda: self.up().wait_send())
            pl.when(z_at > 0)(lambda: self.down().wait_send())

            @pl.when(self.middle)
            def _():
                for order in range(1, line):
                    self.onward(order).wait_send()


def line_sems(line):
    return [
        pltpu.SemaphoreType.DMA,
        pltpu.SemaphoreType.DMA((line, 2)),
        pltpu.SemaphoreType.DMA((line,)),
    ]


class Line:
    def __init__(self, x_ref, o_ref, sems):
        self.x_ref, self.o_ref = x_ref, o_ref
        self.own_sem, self.sends, self.receives = sems
        self.me, self.z_at = lax.axis_index("ctx"), lax.axis_index("fsdp")
        self.middle = (self.z_at == 1) | (self.z_at == 2)
        self.slots = (
            self.z_at,
            self.z_at + 1 - 2 * lax.rem(self.z_at, 2),
            2 - self.z_at // 2,
            3 - 3 * (self.z_at // 2),
        )

    def there(self, slot):
        rows = self.x_ref.shape[0]
        return self.o_ref.at[pl.ds(pl.multiple_of(slot * rows, 16), rows)]

    def copy(self, src_ref, slot, way, target):
        return remote(
            src_ref,
            self.there(slot),
            self.sends.at[slot, way],
            self.receives.at[slot],
            (self.me, target),
        )

    def own(self):
        return pltpu.make_async_copy(self.x_ref, self.there(self.z_at), self.own_sem)

    def up(self):
        return self.copy(self.x_ref, self.z_at, 0, self.z_at + 1)

    def down(self):
        return self.copy(self.x_ref, self.z_at, 1, self.z_at - 1)

    def onward(self, order):
        slot = self.slots[order]
        target = 3 - self.z_at if order == 1 else 3 * self.z_at - 3
        return self.copy(self.there(slot), slot, 0, target)

    def begin(self):
        pl.when(self.z_at < 3)(lambda: self.up().start())
        pl.when(self.z_at > 0)(lambda: self.down().start())
        self.own().start()

    def arrive(self, order):
        slot = self.slots[order]
        self.copy(self.there(slot), slot, 0, self.z_at).wait_recv()

    def pass_on(self, *orders):
        @pl.when(self.middle)
        def _():
            for order in orders:
                self.arrive(order)
                self.onward(order).start()

    def rest(self):
        @pl.when(jnp.logical_not(self.middle))
        def _():
            for order in (1, 2, 3):
                self.arrive(order)

    def end(self):
        self.own().wait()
        pl.when(self.z_at < 3)(lambda: self.up().wait_send())
        pl.when(self.z_at > 0)(lambda: self.down().wait_send())

        @pl.when(self.middle)
        def _():
            for order in (1, 2, 3):
                self.onward(order).wait_send()


def gather_start(rows_own, grads_own, weights_own, collective):
    rows, width = rows_own.shape

    def kernel(rows_ref, grads_ref, weights_ref, all_rows, all_grads, all_weights, *sems):
        plane = Gather(1, rows_ref, all_rows, sems[:5])
        later = Gather(1, grads_ref, all_grads, sems[5:10])
        line = Line(weights_ref, all_weights, sems[10:])
        greet((plane.mate, plane.near_x, plane.near_y), 4, line.z_at)
        line.begin()
        plane.begin(True)
        plane.second(0)
        later.begin(True)
        line.pass_on(1, 2)
        plane.near(0)
        plane.third(0)
        later.second(0)
        line.pass_on(3)
        later.near(0)
        later.third(0)
        line.rest()
        for gather in (plane, later):
            gather.own_block()
            gather.end()
        line.end()

    hbm = pl.BlockSpec(memory_space=pl.ANY)
    return pl.pallas_call(
        kernel,
        out_shape=(
            jax.ShapeDtypeStruct((8 * rows, width), rows_own.dtype),
            jax.ShapeDtypeStruct((8 * rows, width), grads_own.dtype),
            jax.ShapeDtypeStruct((4 * weights_own.shape[0], width), weights_own.dtype),
        ),
        in_specs=[hbm] * 3,
        out_specs=(hbm,) * 3,
        scratch_shapes=[*gather_sems(1), *gather_sems(1), *line_sems(4)],
        compiler_params=pltpu.CompilerParams(collective_id=collective, has_side_effects=True),
        name="gather_start",
    )(rows_own, grads_own, weights_own)


def gather_blocks(x, line, collective, name):
    rows, width = x.shape

    def kernel(x_ref, o_ref, *sems):
        gather = Gather(line, x_ref, o_ref, sems)
        gather.begin()

        def body(order, carry):
            gather.second(order)
            if line > 1:
                pl.when(order + 1 < line)(lambda: gather.first(order + 1))
            gather.near(order)
            gather.third(order)
            return carry

        lax.fori_loop(0, line, body, 0)
        gather.own_block()
        gather.end()

    return pl.pallas_call(
        kernel,
        out_shape=jax.ShapeDtypeStruct((line * 8 * rows, width), x.dtype),
        in_specs=[pl.BlockSpec(memory_space=pl.ANY)],
        out_specs=pl.BlockSpec(memory_space=pl.ANY),
        scratch_shapes=gather_sems(line),
        compiler_params=pltpu.CompilerParams(collective_id=collective, has_side_effects=True),
        name=name,
    )(x)


CHUNK = 16


def add_rows(dst_ref, src_refs, start, count, out_ref=None):
    def body(i, carry):
        at = pl.ds(pl.multiple_of(start + i * CHUNK, CHUNK), CHUNK)
        value = dst_ref[at, :].astype(jnp.float32)
        for src_ref in src_refs:
            value = value + src_ref[at, :].astype(jnp.float32)
        to_ref = dst_ref if out_ref is None else out_ref
        to_ref[at, :] = value.astype(to_ref.dtype)
        return carry

    lax.fori_loop(0, count // CHUNK, body, 0)


class Scatter:
    def __init__(self, line, x_ref, o_ref, scratch):
        (
            self.mine, self.theirs, self.halves, self.from_x, self.from_y, self.from_z, self.total,
            self.load_sem, self.m_send, self.m_recv, self.p_send, self.p_recv, self.z_send,
            self.z_recv, self.out_sem,
        ) = scratch
        self.line, self.x_ref, self.o_ref = line, x_ref, o_ref
        self.z_at = lax.axis_index("fsdp")
        self.me, self.mate, self.near_x, self.near_y, step_x = neighbours()
        self.places = (self.near_y + step_x, self.near_x, self.near_y, self.me)
        self.rows = self.total.shape[0]
        self.half = self.rows // 2
        self.middle = (self.z_at == 1) | (self.z_at == 2)

    def slot(self, order):
        z_at = self.z_at
        if self.line == 1:
            return 0
        far, next_far, near = 3 - 3 * (z_at // 2), 2 - z_at // 2, z_at + 1 - 2 * lax.rem(z_at, 2)
        return jnp.where(
            order == 0, far, jnp.where(order == 1, next_far, jnp.where(order == 2, near, z_at))
        )

    def there(self, slot, place):
        return self.x_ref.at[pl.ds(pl.multiple_of((slot * 8 + place) * self.rows, 16), self.rows)]

    def give(self, order, k):
        return remote(
            self.there(self.slot(order), self.places[k] + self.mate - self.me),
            self.theirs.at[order, k],
            self.m_send.at[order, k],
            self.m_recv.at[order, k],
            (self.mate, self.z_at),
        )

    def load(self, order, k):
        return pltpu.make_async_copy(
            self.there(self.slot(order), self.places[k]),
            self.mine.at[order, k],
            self.load_sem.at[order, k],
        )

    def send(self, order, kind):
        top, low = pl.ds(0, self.half), pl.ds(self.half, self.half)
        k, part, to, device = (
            (0, top, self.halves, self.near_x),
            (0, low, self.halves, self.near_y),
            (1, top, self.from_x, self.near_x),
            (1, low, self.from_x, self.near_x),
            (2, low, self.from_y, self.near_y),
            (2, top, self.from_y, self.near_y),
        )[kind]
        return remote(
            self.mine.at[order, k, part],
            to.at[order, part],
            self.p_send.at[order, kind],
            self.p_recv.at[order, kind],
            (device, self.z_at),
        )

    def begin(self, met=False):
        if not met:
            greet((self.mate, self.near_x, self.near_y), self.line, self.z_at)

        def body(order, carry):
            for k in range(4):
                self.give(order, k).start()
                self.load(order, k).start()
            return carry

        lax.fori_loop(0, self.line, body, 0)

    def first(self, order):
        for k in range(4):
            self.give(order, k).wait_recv()
            self.load(order, k).wait()
            add_rows(self.mine.at[order, k], [self.theirs.at[order, k]], 0, self.rows)
            for kind in ((0, 1), (2,), (4,), ())[k]:
                self.send(order, kind).start()

    def second(self, order):
        self.send(order, 1).wait_recv()
        add_rows(self.mine.at[order, 1], [self.halves.at[order]], self.half, self.half)
        self.send(order, 3).start()
        self.send(order, 0).wait_recv()
        add_rows(self.mine.at[order, 2], [self.halves.at[order]], 0, self.half)
        self.send(order, 5).start()

    def third(self, order, out_ref=None):
        for kind in (2, 3, 4, 5):
            self.send(order, kind).wait_recv()
        sources = [self.from_x.at[order], self.from_y.at[order]]
        add_rows(self.mine.at[order, 3], sources, 0, self.rows, out_ref)

    def z_copy(self, order, slot_at, target):
        return remote(
            self.mine.at[order, 3],
            self.from_z.at[slot_at],
            self.z_send.at[order],
            self.z_recv.at[slot_at],
            (self.me, target),
        )

    def z_out(self, order):
        z_at, slot = self.z_at, self.slot(order)
        target = jnp.where(order == 2, slot, z_at + 1 - 2 * (z_at // 2))
        ends = jnp.where(target == slot, 1, 0)
        return self.z_copy(order, ends * (4 + (z_at - target + 1) // 2) + (1 - ends) * slot, target)

    def pass_on(self, order):
        slot = self.slot(order)
        self.z_copy(order, slot, self.z_at).wait_recv()
        add_rows(self.mine.at[order, 3], [self.from_z.at[slot]], 0, self.rows)
        self.z_out(order).start()

    def along(self, order):
        @pl.when((order < self.line - 1) & jnp.logical_not(self.middle))
        def _():
            self.z_out(order).start()

        pl.when((order == 1) & self.middle)(lambda: self.pass_on(0))

        @pl.when((order == 2) & self.middle)
        def _():
            self.pass_on(1)
            self.pass_on(2)

    def last(self):
        z_at, line = self.z_at, self.line
        pl.when(z_at > 0)(lambda: self.z_copy(line - 1, 4, z_at).wait_recv())
        pl.when(z_at < line - 1)(lambda: self.z_copy(line - 1, 5, z_at).wait_recv())
        mine = self.mine.at[line - 1, 3]
        below, above = self.from_z.at[4], self.from_z.at[5]
        pl.when(z_at == 0)(lambda: add_rows(mine, [above], 0, self.rows, self.total))
        pl.when(z_at == line - 1)(lambda: add_rows(mine, [below], 0, self.rows, self.total))
        pl.when(self.middle)(lambda: add_rows(mine, [below, above], 0, self.rows, self.total))

    def end(self):
        out = pltpu.make_async_copy(self.total, self.o_ref, self.out_sem)
        out.start()

        def sent(order, carry):
            for k in range(4):
                self.give(order, k).wait_send()
            for kind in range(6):
                self.send(order, kind).wait_send()
            if self.line > 1:
                pl.when(order < self.line - 1)(lambda: self.z_out(order).wait_send())
            return carry

        lax.fori_loop(0, self.line, sent, 0)
        out.wait()

    def run(self, work=None, extra=0, met=False):
        self.begin(met)
        self.first(0)
        if self.line == 1:
            self.second(0)
            self.third(0, self.total)
            self.end()
            return

        def body(step, carry):
            order, phase = step // 3, lax.rem(step, 3)

            @pl.when((phase == 0) & (order < self.line))
            def _():
                self.second(order)
                pl.when(order + 1 < self.line)(lambda: self.first(order + 1))

            pl.when((phase == 1) & (order < self.line))(lambda: self.third(order))
            pl.when((phase == 2) & (order < self.line))(lambda: self.along(order))
            if work is not None:
                work(step)
            return carry

        lax.fori_loop(0, 3 * self.line + extra, body, 0)
        self.last()
        self.end()


def scatter_scratch(line, rows, width, dtype):
    shard = (rows, width)
    return [
        pltpu.VMEM((line, 4) + shard, dtype),
        pltpu.VMEM((line, 4) + shard, dtype),
        pltpu.VMEM((line,) + shard, dtype),
        pltpu.VMEM((line,) + shard, dtype),
        pltpu.VMEM((line,) + shard, dtype),
        pltpu.VMEM((6 if line > 1 else 1,) + shard, dtype),
        pltpu.VMEM(shard, jnp.float32),
        pltpu.SemaphoreType.DMA((line, 4)),
        pltpu.SemaphoreType.DMA((line, 4)),
        pltpu.SemaphoreType.DMA((line, 4)),
        pltpu.SemaphoreType.DMA((line, 6)),
        pltpu.SemaphoreType.DMA((line, 6)),
        pltpu.SemaphoreType.DMA((line,)),
        pltpu.SemaphoreType.DMA((6,)),
        pltpu.SemaphoreType.DMA,
    ]


def scatter_blocks(x, line, collective, name):
    rows, width = x.shape[0] // (line * 8), x.shape[1]

    def kernel(x_ref, o_ref, *scratch):
        Scatter(line, x_ref, o_ref, scratch).run()

    return pl.pallas_call(
        kernel,
        out_shape=jax.ShapeDtypeStruct((rows, width), jnp.float32),
        in_specs=[pl.BlockSpec(memory_space=pl.ANY)],
        out_specs=pl.BlockSpec(memory_space=pl.ANY),
        scratch_shapes=scatter_scratch(line, rows, width, x.dtype),
        compiler_params=pltpu.CompilerParams(
            collective_id=collective, has_side_effects=True, vmem_limit_bytes=52 * MIB
        ),
        name=name,
    )(x)


QUERY_HEADS = 64
KEY_VALUE_HEADS = 8
HEAD_SIZE = 64
TOP = 4
EPSILON = 1e-05
THETA_BASE = 150000.0
CLAMP_LIMIT = 7.0
GLU_ALPHA = 1.702
MASK_FILL = -1e30
SPAN = 256
SCALE = HEAD_SIZE**-0.5


def contract(left, right, left_axis, right_axis):
    return lax.dot_general(
        left, right, (((left_axis,), (right_axis,)), ((), ())), preferred_element_type=jnp.float32
    )


def norm_scale(value_rows, gain_vec):
    return (
        value_rows
        * lax.rsqrt(jnp.mean(value_rows * value_rows, axis=-1, keepdims=True) + EPSILON)
        * gain_vec
    )


def soft_clamp(value_rows):
    return CLAMP_LIMIT * jnp.tanh(value_rows / CLAMP_LIMIT)


def glu_units(gate_lin, up_lin):
    gated = soft_clamp(gate_lin)
    return (soft_clamp(up_lin) + 1.0) * gated * jax.nn.sigmoid(GLU_ALPHA * gated)


def rotary_tables(length):
    half = HEAD_SIZE // 2
    inverse = THETA_BASE ** (-jnp.arange(half, dtype=jnp.float32) / half)
    angles = inverse[:, None] * jnp.arange(length, dtype=jnp.int32).astype(jnp.float32)[None, :]
    return jnp.cos(angles), jnp.sin(angles)


def turned(value, cosine, sine):
    half = HEAD_SIZE // 2
    first, second = value[:, :half], value[:, half:]
    return jnp.concatenate(
        [first * cosine - second * sine, second * cosine + first * sine], axis=1
    )


def diagonal(length):
    return lax.broadcasted_iota(jnp.int32, (length, length), 0) <= lax.broadcasted_iota(
        jnp.int32, (length, length), 1
    )


def masked_scores(key_rows, query_cols, count):
    scores = contract(key_rows, query_cols, 1, 0)
    edge = jnp.where(diagonal(SPAN), scores[count - SPAN :], MASK_FILL)
    if count == SPAN:
        return edge
    return jnp.concatenate([scores[: count - SPAN], edge], axis=0)


def attend_kernel(sink_ref, q_ref, k_ref, v_ref, out_ref, log_ref):
    sink = sink_ref[pl.program_id(0)]
    length = q_ref.shape[1]
    for start in range(0, length, SPAN):
        count = start + SPAN
        at = pl.ds(start, SPAN)
        query = q_ref[:, at] * jnp.bfloat16(SCALE)
        scores = masked_scores(k_ref[:count, :], query, count)
        row_top = jnp.maximum(jnp.max(scores, axis=0, keepdims=True), sink)
        weights = jnp.exp(scores - row_top)
        denominator = jnp.sum(weights, axis=0, keepdims=True) + jnp.exp(sink - row_top)
        probabilities = (weights / denominator).astype(jnp.bfloat16)
        out_ref[:, at] = contract(v_ref[:, :count], probabilities, 1, 0).astype(jnp.bfloat16)
        log_ref[0, :, at] = row_top + jnp.log(denominator)


def attend(sinks, queries, keys, values):
    heads, length = queries.shape[0] // HEAD_SIZE, queries.shape[1]
    per_head = pl.BlockSpec((HEAD_SIZE, length), lambda h: (h, 0))
    return pl.pallas_call(
        attend_kernel,
        grid=(heads,),
        out_shape=(
            jax.ShapeDtypeStruct(queries.shape, jnp.bfloat16),
            jax.ShapeDtypeStruct((heads, 1, length), jnp.float32),
        ),
        in_specs=[
            pl.BlockSpec(memory_space=pltpu.SMEM),
            per_head,
            pl.BlockSpec((length, HEAD_SIZE), lambda h: (0, 0)),
            pl.BlockSpec((HEAD_SIZE, length), lambda h: (0, 0)),
        ],
        out_specs=(per_head, pl.BlockSpec((1, 1, length), lambda h: (h, 0, 0))),
        compiler_params=pltpu.CompilerParams(vmem_limit_bytes=40 * MIB),
        cost_estimate=pl.CostEstimate(
            flops=heads * length * length * HEAD_SIZE * 4,
            bytes_accessed=heads * length * HEAD_SIZE * 4,
            transcendentals=heads * length * length,
        ),
        name="attend",
    )(sinks, queries, keys, values)


def attention(normed, weights, out_own, sinks, cosine, sine, collective):
    low, f32 = jnp.bfloat16, jnp.float32
    length, wide = normed.shape
    own_rows = weights.shape[0] // 4
    q_rows, width = out_own.shape
    kv_rows = (own_rows - q_rows) // 2
    heads = 4 * q_rows // HEAD_SIZE
    half = HEAD_SIZE // 2
    per_shard = q_rows // HEAD_SIZE
    block_rows = length // 8

    def kernel(
        sink_ref, normed_hbm, weights_hbm, out_ref, cos_ref, sin_ref,
        o_ref, all_out, q_ref, k_ref, kt_ref, v_ref, att_ref, log_ref,
        normed_v, weights_v, lin, vt_v, out_v, branch, held_sems, own_sem, z_send, z_recv, *scratch,
    ):
        held = [
            pltpu.make_async_copy(normed_hbm, normed_v, held_sems.at[0]),
            pltpu.make_async_copy(weights_hbm, weights_v, held_sems.at[1]),
        ]
        for copy in held:
            copy.start()
        line = Line(out_ref, all_out, (own_sem, z_send, z_recv))
        scatter = Scatter(1, branch, o_ref, scratch)
        greet((scatter.mate, scatter.near_x, scatter.near_y), 4, line.z_at)
        line.begin()
        for copy in held:
            copy.wait()

        def project(i, carry):
            at = pl.ds(pl.multiple_of(i * SPAN, SPAN), SPAN)
            lin[:, at] = contract(weights_v[...], normed_v[at, :], 1, 1)
            return carry

        lax.fori_loop(0, length // SPAN, project, 0)

        def turn(value):
            first, second = value[:half], value[half:]
            cosine, sine = cos_ref[...], sin_ref[...]
            return jnp.concatenate(
                [first * cosine - second * sine, second * cosine + first * sine], axis=0
            ).astype(low)

        def shards_of(offset):
            return jnp.concatenate(
                [
                    lin[z * own_rows + offset : z * own_rows + offset + kv_rows, :]
                    for z in range(4)
                ],
                axis=0,
            )

        keys_t = turn(shards_of(q_rows))
        values_t = shards_of(q_rows + kv_rows).astype(low)
        kt_ref[...] = keys_t
        vt_v[...] = values_t
        k_ref[...] = keys_t.T
        v_ref[...] = values_t.T

        def head(h, carry):
            pl.when(h == heads // 2)(lambda: line.pass_on(1, 2))
            start = (h // per_shard) * own_rows + lax.rem(h, per_shard) * HEAD_SIZE
            queries = turn(lin[pl.ds(pl.multiple_of(start, 16), HEAD_SIZE), :])
            rows = pl.ds(pl.multiple_of(h * HEAD_SIZE, HEAD_SIZE), HEAD_SIZE)
            q_ref[rows, :] = queries
            sink = sink_ref[h]
            for begin in range(0, length, SPAN):
                count = begin + SPAN
                query = queries[:, begin:count] * jnp.bfloat16(SCALE)
                scores = masked_scores(k_ref[:count, :], query, count)
                row_top = jnp.maximum(jnp.max(scores, axis=0, keepdims=True), sink)
                chances = jnp.exp(scores - row_top)
                denominator = jnp.sum(chances, axis=0, keepdims=True) + jnp.exp(sink - row_top)
                chances = (chances / denominator).astype(low)
                att_ref[rows, begin:count] = contract(vt_v[:, :count], chances, 1, 0).astype(low)
                log_ref[h, :, begin:count] = row_top + jnp.log(denominator)
            return carry

        lax.fori_loop(0, heads, head, 0)
        line.pass_on(3)
        line.rest()
        line.end()
        load = pltpu.make_async_copy(all_out, out_v, held_sems.at[0])
        load.start()
        load.wait()

        def give_back(i, carry):
            at = pl.ds(pl.multiple_of(i * SPAN, SPAN), SPAN)
            branch[at, :] = contract(att_ref[:, at], out_v[...], 0, 0).astype(low)
            return carry

        lax.fori_loop(0, length // SPAN, give_back, 0)
        scatter.run(met=True)

    hbm = pl.BlockSpec(memory_space=pl.ANY)
    vmem = pl.BlockSpec(memory_space=pltpu.VMEM)
    return pl.pallas_call(
        kernel,
        out_shape=(
            jax.ShapeDtypeStruct((block_rows, width), f32),
            jax.ShapeDtypeStruct((4 * q_rows, width), low),
            jax.ShapeDtypeStruct((4 * q_rows, length), low),
            jax.ShapeDtypeStruct((length, HEAD_SIZE), low),
            jax.ShapeDtypeStruct((HEAD_SIZE, length), low),
            jax.ShapeDtypeStruct((length, HEAD_SIZE), low),
            jax.ShapeDtypeStruct((4 * q_rows, length), low),
            jax.ShapeDtypeStruct((heads, 1, length), f32),
        ),
        in_specs=[pl.BlockSpec(memory_space=pltpu.SMEM), hbm, hbm, hbm, vmem, vmem],
        out_specs=(hbm, hbm) + (vmem,) * 6,
        scratch_shapes=[
            pltpu.VMEM(normed.shape, low),
            pltpu.VMEM(weights.shape, low),
            pltpu.VMEM((weights.shape[0], length), f32),
            pltpu.VMEM((HEAD_SIZE, length), low),
            pltpu.VMEM((4 * q_rows, width), low),
            pltpu.VMEM((length, width), low),
            pltpu.SemaphoreType.DMA((2,)),
            *line_sems(4),
            *scatter_scratch(1, block_rows, width, low),
        ],
        compiler_params=pltpu.CompilerParams(
            collective_id=collective, has_side_effects=True, vmem_limit_bytes=58 * MIB
        ),
        name="attention",
    )(sinks, normed, weights, out_own, cosine, sine)


def attend_back_kernel(
    sink_ref, q_ref, k_ref, kt_ref, v_ref, grad_ref, log_ref, cos_ref, sin_ref,
    dq_ref, dk_ref, dv_ref, dsink_ref,
):
    head = pl.program_id(0)
    sink = sink_ref[head]
    length = q_ref.shape[1]
    half = HEAD_SIZE // 2

    @pl.when(head == 0)
    def _():
        dk_ref[...] = jnp.zeros_like(dk_ref)
        dv_ref[...] = jnp.zeros_like(dv_ref)

    grad_sink = jnp.zeros((1, SPAN), jnp.float32)
    for start in range(0, length, SPAN):
        count = start + SPAN
        at = pl.ds(start, SPAN)
        query = q_ref[:, at] * jnp.bfloat16(SCALE)
        grad = grad_ref[:, at]
        log_sum = log_ref[0, :, at]
        probabilities = jnp.exp(masked_scores(k_ref[:count, :], query, count) - log_sum)
        grad_probs = contract(v_ref[:count, :], grad, 1, 0)
        inner_sum = jnp.sum(probabilities * grad_probs, axis=0, keepdims=True)
        grad_scores = (probabilities * (grad_probs - inner_sum)).astype(jnp.bfloat16)
        grad_query = contract(kt_ref[:, :count], grad_scores, 1, 0) * SCALE
        first, second = grad_query[:half], grad_query[half:]
        cosine, sine = cos_ref[:, at], sin_ref[:, at]
        dq_ref[:half, at] = (first * cosine + second * sine).astype(jnp.bfloat16)
        dq_ref[half:, at] = (second * cosine - first * sine).astype(jnp.bfloat16)
        dk_ref[:count, :] += contract(grad_scores, query, 1, 1)
        dv_ref[:count, :] += contract(probabilities.astype(jnp.bfloat16), grad, 1, 1)
        grad_sink = grad_sink - jnp.exp(sink - log_sum) * inner_sum
    dsink_ref[0] = grad_sink


def attend_back(sinks, queries, keys, keys_t, values, grads, log_sums, cosine, sine):
    heads, length = queries.shape[0] // HEAD_SIZE, queries.shape[1]
    per_head = pl.BlockSpec((HEAD_SIZE, length), lambda h: (h, 0))

    def whole(*shape):
        return pl.BlockSpec(shape, lambda h: (0,) * len(shape))

    return pl.pallas_call(
        attend_back_kernel,
        grid=(heads,),
        out_shape=(
            jax.ShapeDtypeStruct(queries.shape, jnp.bfloat16),
            jax.ShapeDtypeStruct((length, HEAD_SIZE), jnp.float32),
            jax.ShapeDtypeStruct((length, HEAD_SIZE), jnp.float32),
            jax.ShapeDtypeStruct((heads, 1, SPAN), jnp.float32),
        ),
        in_specs=[
            pl.BlockSpec(memory_space=pltpu.SMEM),
            per_head,
            whole(length, HEAD_SIZE),
            whole(HEAD_SIZE, length),
            whole(length, HEAD_SIZE),
            per_head,
            pl.BlockSpec((1, 1, length), lambda h: (h, 0, 0)),
            whole(HEAD_SIZE // 2, length),
            whole(HEAD_SIZE // 2, length),
        ],
        out_specs=(
            per_head,
            whole(length, HEAD_SIZE),
            whole(length, HEAD_SIZE),
            pl.BlockSpec((1, 1, SPAN), lambda h: (h, 0, 0)),
        ),
        compiler_params=pltpu.CompilerParams(vmem_limit_bytes=48 * MIB),
        cost_estimate=pl.CostEstimate(
            flops=heads * length * length * HEAD_SIZE * 10,
            bytes_accessed=heads * length * HEAD_SIZE * 8,
            transcendentals=heads * length * length,
        ),
        name="attend_back",
    )(sinks, queries, keys, keys_t, values, grads, log_sums, cosine, sine)


def attention_back(
    parts, sinks, queries, keys, keys_t, values, grads, log_sums, cosine, sine, own_rows, collective
):
    low, f32 = jnp.bfloat16, jnp.float32
    length = queries.shape[1]
    heads = queries.shape[0] // HEAD_SIZE
    half = HEAD_SIZE // 2
    block_rows, width = parts.shape[0] // 32, parts.shape[1]
    q_rows = queries.shape[0] // 4
    kv_rows = (own_rows - q_rows) // 2
    per_shard = q_rows // HEAD_SIZE
    spans = length // SPAN

    def kernel(
        sink_ref, parts_ref, q_ref, k_ref, kt_ref, v_ref, grad_ref, log_ref, cos_ref, sin_ref,
        o_ref, lin_ref, dsink_ref, dk_s, dv_s, *scratch,
    ):
        dk_s[...] = jnp.zeros_like(dk_s)
        dv_s[...] = jnp.zeros_like(dv_s)
        dsink_ref[...] = jnp.zeros_like(dsink_ref)

        def one(head, span):
            start, count = span * SPAN, span * SPAN + SPAN
            at = slice(start, count)
            rows = pl.ds(pl.multiple_of(head * HEAD_SIZE, HEAD_SIZE), HEAD_SIZE)
            query = q_ref[rows, at] * jnp.bfloat16(SCALE)
            grad = grad_ref[rows, at]
            log_sum = log_ref[head, :, at]
            chances = jnp.exp(masked_scores(k_ref[:count, :], query, count) - log_sum)
            grad_probs = contract(v_ref[:count, :], grad, 1, 0)
            inner_sum = jnp.sum(chances * grad_probs, axis=0, keepdims=True)
            grad_scores = (chances * (grad_probs - inner_sum)).astype(low)
            grad_query = contract(kt_ref[:, :count], grad_scores, 1, 0) * SCALE
            first, second = grad_query[:half], grad_query[half:]
            cosine, sine = cos_ref[:, at], sin_ref[:, at]
            place = (head // per_shard) * own_rows + lax.rem(head, per_shard) * HEAD_SIZE
            lin_ref[pl.ds(pl.multiple_of(place, 16), HEAD_SIZE), at] = jnp.concatenate(
                [first * cosine + second * sine, second * cosine - first * sine], axis=0
            ).astype(low)
            dk_s[:count, :] += contract(grad_scores, query, 1, 1)
            dv_s[:count, :] += contract(chances.astype(low), grad, 1, 1)
            dsink_ref[head] -= jnp.exp(sink_ref[head] - log_sum) * inner_sum

        def work(step):
            first_step = 0
            for span in reversed(range(spans)):
                at_once = max(1, 8 // (span + 1))
                count = -(-heads // at_once)
                here = (step >= first_step) & (step < first_step + count)

                @pl.when(here)
                def _():
                    begin = (step - first_step) * at_once

                    def body(head, carry):
                        pl.when(head < heads)(lambda: one(head, span))
                        return carry

                    lax.fori_loop(begin, begin + at_once, body, 0)

                first_step += count

        needed = sum(-(-heads // max(1, 8 // (span + 1))) for span in range(spans))
        Scatter(4, parts_ref, o_ref, scratch).run(work, max(0, needed - 12))
        grad_keys, grad_values = dk_s[...].T, dv_s[...].T
        first, second = grad_keys[:half], grad_keys[half:]
        cosine, sine = cos_ref[...], sin_ref[...]
        grad_keys = jnp.concatenate(
            [first * cosine + second * sine, second * cosine - first * sine], axis=0
        )
        for z in range(4):
            here = slice(z * kv_rows, (z + 1) * kv_rows)
            start = z * own_rows + q_rows
            lin_ref[start : start + kv_rows, :] = grad_keys[here].astype(low)
            lin_ref[start + kv_rows : start + 2 * kv_rows, :] = grad_values[here].astype(low)

    hbm = pl.BlockSpec(memory_space=pl.ANY)
    vmem = pl.BlockSpec(memory_space=pltpu.VMEM)
    return pl.pallas_call(
        kernel,
        out_shape=(
            jax.ShapeDtypeStruct((block_rows, width), f32),
            jax.ShapeDtypeStruct((4 * own_rows, length), low),
            jax.ShapeDtypeStruct((heads, 1, SPAN), f32),
        ),
        in_specs=[pl.BlockSpec(memory_space=pltpu.SMEM), hbm] + [vmem] * 8,
        out_specs=(hbm, vmem, vmem),
        scratch_shapes=[
            pltpu.VMEM((length, HEAD_SIZE), f32),
            pltpu.VMEM((length, HEAD_SIZE), f32),
            *scatter_scratch(4, block_rows, width, low),
        ],
        compiler_params=pltpu.CompilerParams(
            collective_id=collective, has_side_effects=True, vmem_limit_bytes=60 * MIB
        ),
        name="attention_back",
    )(sinks, parts, queries, keys, keys_t, values, grads, log_sums, cosine, sine)


PAIR = 2
STEP = 4


def routed(cols, capacity):
    expert = lax.axis_index("ctx")
    cols = cols.astype(jnp.float32)
    lane = lax.broadcasted_iota(jnp.int32, cols.shape, 1)
    place = jnp.sum(jnp.where(lane == 64 + expert, cols, 0.0), axis=1, keepdims=True)
    gate = jnp.sum(jnp.where(lane == 72 + expert, cols, 0.0), axis=1, keepdims=True)
    slot = lax.broadcasted_iota(jnp.int32, (cols.shape[0], PAIR * capacity), 1)
    picked = place.astype(jnp.int32) == slot
    return (
        jnp.where(picked, 1.0, 0.0).astype(jnp.bfloat16),
        jnp.where(picked, gate, 0.0).astype(jnp.bfloat16),
    )


class Stream:
    def __init__(self, arrays, sems, inward, first_sem=0):
        self.arrays, self.sems, self.inward, self.first_sem = arrays, sems, inward, first_sem

    def copies(self, slot, block):
        made = []
        for k, (array, slots, count, column) in enumerate(self.arrays):
            at = pl.ds(pl.multiple_of(block * count, 16), count)
            far = array.at[at] if column is None else array.at[at, column]
            pair = (far, slots.at[slot]) if self.inward else (slots.at[slot], far)
            made.append(pltpu.make_async_copy(*pair, self.sems.at[slot, self.first_sem + k]))
        return made

    def start(self, slot, block):
        for copy in self.copies(slot, block):
            copy.start()

    def wait(self, slot, block):
        for copy in self.copies(slot, block):
            copy.wait()


def two_of(shape, dtype):
    return pltpu.VMEM((2,) + shape, dtype)


def experts(sent, sent_grads, own_grads, gate_w, up_w, down_w, gate_b, up_b, down_b, capacity, collective):
    low, f32 = jnp.bfloat16, jnp.float32
    block_rows, wide = sent.shape
    share, width = gate_w.shape
    span = PAIR * block_rows
    pairs = STEP // PAIR
    count = PAIR * capacity
    tokens = 32 * block_rows
    slot_rows = 32 * capacity
    line = 4

    def kernel(
        sent_ref, sent_grads_ref, own_grads_ref, gate_hbm, up_hbm, down_hbm, gate_b_ref, up_b_ref, down_b_ref,
        all_ref, all_grads_ref, rows_out, gate_out, up_out, hidden_out, mix_out,
        grad_rows_out, gate_grad_out, up_grad_out, tokens_out, down_sum, gate_sum, up_sum,
        gate_v, up_v, down_v, x_s, rows_s, gate_s, up_s, hidden_s, mix_s, cols_s, gate_gs, up_gs,
        held_sems, in_sems, out_sems, *sems,
    ):
        held = [
            pltpu.make_async_copy(source, target, held_sems.at[k])
            for k, (source, target) in enumerate(
                ((gate_hbm, gate_v), (up_hbm, up_v), (down_hbm, down_v))
            )
        ]
        for copy in held:
            copy.start()
        forward_in = Stream([(all_ref, x_s, pairs * span, None)], in_sems, True)
        forward_out = Stream(
            [
                (rows_out, rows_s, pairs * count, None),
                (gate_out, gate_s, pairs * count, None),
                (up_out, up_s, pairs * count, None),
                (hidden_out, hidden_s, pairs * count, None),
                (mix_out, mix_s, pairs * span, None),
            ],
            out_sems,
            False,
        )
        kept = [
            (all_ref, cols_s, pairs * span, pl.ds(wide - 128, 128)),
            (gate_out, gate_s, pairs * count, None),
            (up_out, up_s, pairs * count, None),
        ]
        back_kept = Stream(kept, in_sems, True)
        back_own = Stream([(own_grads_ref, x_s, pairs * span, None)], in_sems, True, 3)
        back_far = Stream([(all_grads_ref, x_s, pairs * span, None)], in_sems, True, 3)
        back_out = Stream(
            [
                (grad_rows_out, rows_s, pairs * count, None),
                (gate_grad_out, gate_gs, pairs * count, None),
                (up_grad_out, up_gs, pairs * count, None),
                (tokens_out, mix_s, pairs * span, None),
            ],
            out_sems,
            False,
        )
        down_sum[...] = jnp.zeros_like(down_sum)
        gate_sum[...] = jnp.zeros_like(gate_sum)
        up_sum[...] = jnp.zeros_like(up_sum)
        spans = [pl.ds(pair * span, span) for pair in range(pairs)]

        def forward(slot):
            picks = [routed(x_s[slot, at, wide - 128 :], capacity) for at in spans]
            rows = jnp.concatenate(
                [contract(picks[k][0], x_s[slot, spans[k], :], 0, 0) for k in range(pairs)],
                axis=0,
            ).astype(low)
            rows_s[slot] = rows
            rows = rows[:, :width]
            gate_lin = contract(rows, gate_v[...], 1, 1) + gate_b_ref[...]
            up_lin = contract(rows, up_v[...], 1, 1) + up_b_ref[...]
            gate_s[slot] = gate_lin
            up_s[slot] = up_lin
            hidden = glu_units(gate_lin, up_lin).astype(low)
            hidden_s[slot] = hidden
            out = contract(hidden, down_v[...], 1, 0) + down_b_ref[...]
            for k in range(pairs):
                part = out[k * count : (k + 1) * count].astype(low)
                mix_s[slot, spans[k], :] = contract(picks[k][1], part, 1, 0).astype(low)

        def backward(slot):
            picks = [routed(cols_s[slot, at, :], capacity) for at in spans]
            rows = jnp.concatenate(
                [contract(picks[k][1], x_s[slot, spans[k], :], 0, 0) for k in range(pairs)],
                axis=0,
            ).astype(low)
            rows_s[slot] = rows
            rows = rows[:, :width]
            down_sum[...] += jnp.sum(rows.astype(f32), axis=0, keepdims=True)
            grad_units = contract(rows, down_v[...], 1, 1)
            gate_tanh = jnp.tanh(gate_s[slot] / CLAMP_LIMIT)
            up_tanh = jnp.tanh(up_s[slot] / CLAMP_LIMIT)
            gated = CLAMP_LIMIT * gate_tanh
            lifted = CLAMP_LIMIT * up_tanh + 1.0
            part = jax.nn.sigmoid(GLU_ALPHA * gated)
            grad_up = (grad_units * gated * part * (1.0 - up_tanh * up_tanh)).astype(low)
            slope = part * (1.0 + GLU_ALPHA * gated * (1.0 - part))
            grad_gate = (grad_units * lifted * slope * (1.0 - gate_tanh * gate_tanh)).astype(low)
            gate_gs[slot] = grad_gate
            up_gs[slot] = grad_up
            gate_sum[...] += jnp.sum(grad_gate.astype(f32), axis=0, keepdims=True)
            up_sum[...] += jnp.sum(grad_up.astype(f32), axis=0, keepdims=True)
            copies = contract(grad_gate, gate_v[...], 1, 0) + contract(grad_up, up_v[...], 1, 0)
            for k in range(pairs):
                part = copies[k * count : (k + 1) * count].astype(low)
                mix_s[slot, spans[k], :] = contract(picks[k][0], part, 1, 0).astype(low)

        ahead = Gather(line, sent_ref, all_ref, sems[:5])
        back = Gather(line, sent_grads_ref, all_grads_ref, sems[5:])
        y_at = ahead.me // 4

        def block(step):
            half = lax.rem(step, 2)
            return ahead.slot(step // 2) * 2 + (1 - half) * y_at + half * (1 - y_at)

        ahead.begin()

        def forward_step(step, carry):
            order, half = step // 2, lax.rem(step, 2)

            @pl.when(half == 0)
            def _():
                ahead.second(order)
                pl.when(order + 1 < line)(lambda: ahead.first(order + 1))
                pl.when(order == 1)(back.begin_line)
                pl.when(order == line - 1)(lambda: back.first(1))
                ahead.near(order)

            pl.when(half == 1)(lambda: ahead.third(order))

            @pl.when(step == 0)
            def _():
                ahead.own_block()
                for copy in held:
                    copy.wait()

            forward_in.start(half, block(step))
            pl.when(step >= 2)(lambda: forward_out.wait(half, block(step - 2)))
            forward_in.wait(half, block(step))
            forward(half)
            forward_out.start(half, block(step))
            return carry

        steps = 2 * line
        lax.fori_loop(0, steps, forward_step, 0)
        forward_out.wait(0, block(steps - 2))
        forward_out.wait(1, block(steps - 1))

        def grads_in(step, act):
            order, half = step // 2, lax.rem(step, 2)
            act(back_kept, half, block(step))
            pl.when(order == 0)(
                lambda: act(back_own, half, (1 - half) * y_at + half * (1 - y_at))
            )
            pl.when(order > 0)(lambda: act(back_far, half, block(step)))

        def backward_step(step, carry):
            order, half = step // 2, lax.rem(step, 2)

            @pl.when(half == 0)
            def _():
                @pl.when(order > 0)
                def _():
                    back.near(order)
                    back.third(order)

                grads_in(step, Stream.start)

            @pl.when(half == 1)
            def _():
                pl.when(order + 1 < line)(lambda: back.second(order + 1))
                pl.when(order + 2 < line)(lambda: back.first(order + 2))

            pl.when(half == 0)(lambda: grads_in(step + 1, Stream.start))
            pl.when(step >= 2)(lambda: back_out.wait(half, block(step - 2)))
            grads_in(step, Stream.wait)
            backward(half)
            back_out.start(half, block(step))
            return carry

        lax.fori_loop(0, steps, backward_step, 0)
        back_out.wait(0, block(steps - 2))
        back_out.wait(1, block(steps - 1))
        ahead.end()
        back.end(1)

    hbm = pl.BlockSpec(memory_space=pl.ANY)
    vmem = pl.BlockSpec(memory_space=pltpu.VMEM)

    def made(rows, columns, dtype=low):
        return jax.ShapeDtypeStruct((rows, columns), dtype)

    return pl.pallas_call(
        kernel,
        out_shape=(
            made(tokens, wide),
            made(tokens, wide),
            made(slot_rows, wide),
            made(slot_rows, share, f32),
            made(slot_rows, share, f32),
            made(slot_rows, share),
            made(tokens, width),
            made(slot_rows, wide),
            made(slot_rows, share),
            made(slot_rows, share),
            made(tokens, width),
            made(1, width, f32),
            made(1, share, f32),
            made(1, share, f32),
        ),
        in_specs=[hbm] * 6 + [vmem] * 3,
        out_specs=(hbm,) * 11 + (vmem,) * 3,
        scratch_shapes=[
            pltpu.VMEM(gate_w.shape, low),
            pltpu.VMEM(up_w.shape, low),
            pltpu.VMEM(down_w.shape, low),
            two_of((pairs * span, wide), low),
            two_of((pairs * count, wide), low),
            two_of((pairs * count, share), f32),
            two_of((pairs * count, share), f32),
            two_of((pairs * count, share), low),
            two_of((pairs * span, width), low),
            two_of((pairs * span, 128), low),
            two_of((pairs * count, share), low),
            two_of((pairs * count, share), low),
            pltpu.SemaphoreType.DMA((3,)),
            pltpu.SemaphoreType.DMA((2, 4)),
            pltpu.SemaphoreType.DMA((2, 5)),
            *gather_sems(line),
            *gather_sems(line),
        ],
        compiler_params=pltpu.CompilerParams(
            collective_id=collective, has_side_effects=True, vmem_limit_bytes=60 * MIB
        ),
        name="experts",
    )(sent, sent_grads, own_grads, gate_w, up_w, down_w, gate_b, up_b, down_b)


def expert_weights(parts, rows_in, gate_grad, up_grad, collective):
    low, f32 = jnp.bfloat16, jnp.float32
    slot_rows, wide = rows_in.shape
    share = gate_grad.shape[1]
    block_rows, width = parts.shape[0] // 32, parts.shape[1]
    cut = 256
    whole, rest = wide // cut, wide % cut
    count = whole + 1

    def kernel(
        parts_ref, rows_hbm, gate_hbm, up_hbm, o_ref, gate_out, up_out,
        stage, gate_t, up_t, in_s, gate_s, up_s, held_sem, in_sems, out_sems, *scratch,
    ):
        first = pltpu.make_async_copy(gate_hbm, stage, held_sem)
        first.start()

        def load(chunk, columns):
            slot = lax.rem(chunk, 2)
            at = pl.ds(pl.multiple_of(chunk * cut, cut), columns)
            return pltpu.make_async_copy(
                rows_hbm.at[:, at], in_s.at[slot, :, pl.ds(0, columns)], in_sems.at[slot]
            )

        def store(chunk, columns, k):
            slot = lax.rem(chunk, 2)
            at = pl.ds(pl.multiple_of(chunk * cut, cut), columns)
            source, target = ((gate_s, gate_out), (up_s, up_out))[k]
            return pltpu.make_async_copy(
                source.at[slot, :, pl.ds(0, columns)], target.at[:, at], out_sems.at[slot, k]
            )

        def loads(chunk, act):
            pl.when(chunk < whole)(lambda: act(load(chunk, cut)))
            pl.when(chunk == whole)(lambda: act(load(chunk, rest)))

        def stores(chunk, act):
            def do(columns):
                for k in range(2):
                    act(store(chunk, columns, k))

            pl.when(chunk < whole)(lambda: do(cut))
            pl.when(chunk == whole)(lambda: do(rest))

        def begin(copy):
            copy.start()

        def await_it(copy):
            copy.wait()

        def work(chunk):
            slot = lax.rem(chunk, 2)

            @pl.when(chunk == 0)
            def _():
                loads(0, begin)
                first.wait()
                gate_t[...] = stage[...].T
                later = pltpu.make_async_copy(up_hbm, stage, held_sem)
                later.start()
                later.wait()
                up_t[...] = stage[...].T

            pl.when(chunk + 1 < count)(lambda: loads(chunk + 1, begin))
            pl.when(chunk >= 2)(lambda: stores(chunk - 2, await_it))
            loads(chunk, await_it)
            gate_s[slot] = contract(gate_t[...], in_s[slot], 1, 0)
            up_s[slot] = contract(up_t[...], in_s[slot], 1, 0)
            stores(chunk, begin)

        Scatter(4, parts_ref, o_ref, scratch).run(work, count - 12)
        stores(count - 2, await_it)
        stores(count - 1, await_it)

    hbm = pl.BlockSpec(memory_space=pl.ANY)
    return pl.pallas_call(
        kernel,
        out_shape=(
            jax.ShapeDtypeStruct((block_rows, width), f32),
            jax.ShapeDtypeStruct((share, wide), f32),
            jax.ShapeDtypeStruct((share, wide), f32),
        ),
        in_specs=[hbm] * 4,
        out_specs=(hbm,) * 3,
        scratch_shapes=[
            pltpu.VMEM(gate_grad.shape, low),
            pltpu.VMEM(gate_grad.shape[::-1], low),
            pltpu.VMEM(gate_grad.shape[::-1], low),
            two_of((slot_rows, cut), low),
            two_of((share, cut), f32),
            two_of((share, cut), f32),
            pltpu.SemaphoreType.DMA,
            pltpu.SemaphoreType.DMA((2,)),
            pltpu.SemaphoreType.DMA((2, 2)),
            *scatter_scratch(4, block_rows, width, low),
        ],
        compiler_params=pltpu.CompilerParams(
            collective_id=collective, has_side_effects=True, vmem_limit_bytes=60 * MIB
        ),
        name="expert_weights",
    )(parts, rows_in, gate_grad, up_grad)


def product_kernel(left_ref, right_ref, out_ref):
    right = right_ref[:, : out_ref.shape[1]]
    out_ref[...] = contract(left_ref[...], right, 0, 0).astype(out_ref.dtype)


def product(left_t, right, name, columns=None):
    depth, rows = left_t.shape
    columns = columns or right.shape[1]
    return pl.pallas_call(
        product_kernel,
        grid=(rows // SPAN,),
        out_shape=jax.ShapeDtypeStruct((rows, columns), jnp.bfloat16),
        in_specs=[
            pl.BlockSpec((depth, SPAN), lambda i: (0, i)),
            pl.BlockSpec(right.shape, lambda i: (0, 0), pipeline_mode=pl.Buffered(1)),
        ],
        out_specs=pl.BlockSpec((SPAN, columns), lambda i: (i, 0)),
        compiler_params=pltpu.CompilerParams(vmem_limit_bytes=40 * MIB),
        cost_estimate=pl.CostEstimate(
            flops=2 * depth * rows * columns, bytes_accessed=4 * rows * columns, transcendentals=0
        ),
        name=name,
    )(left_t, right)


def input_back(grad_lin, weights, normed, width, collective, small):
    low, f32 = jnp.bfloat16, jnp.float32
    depth, length = grad_lin.shape
    block_rows = length // 8
    wide = normed.shape[1]
    columns = small.shape[1]
    gain_columns = -(-wide // (16 * 128)) * 128

    def kernel(
        lin_ref, weights_ref, normed_hbm, small_ref, o_ref, all_sums,
        normed_v, part, found_v, sums_v, sem, *scratch,
    ):
        gather = Gather(4, sums_v, all_sums, scratch[:5])
        scatter = Scatter(1, part, o_ref, scratch[5:])
        load = pltpu.make_async_copy(normed_hbm, normed_v, sem)
        load.start()
        greet((gather.mate, gather.near_x, gather.near_y), 4, gather.z_at)
        found_v[...] = jnp.zeros_like(found_v)
        load.wait()

        def body(i, carry):
            at = pl.ds(pl.multiple_of(i * SPAN, SPAN), SPAN)
            value = contract(lin_ref[:, at], weights_ref[...], 0, 0)
            part[at, :] = value[:, :width].astype(low)
            found = value * normed_v[at, :].astype(f32)
            found_v[...] += jnp.sum(found, axis=0, keepdims=True)
            return carry

        lax.fori_loop(0, length // SPAN, body, 0)
        scatter.begin(True)
        sums_v[:, :columns] = small_ref[...]
        sums_v[:, columns:] = jnp.zeros((16, gain_columns), f32)
        for k in range(wide // 128):
            row, lane = k // (gain_columns // 128), k % (gain_columns // 128) * 128
            sums_v[row : row + 1, columns + lane : columns + lane + 128] = found_v[
                :, k * 128 : (k + 1) * 128
            ]
        gather.begin(True)
        scatter.first(0)
        gather.second(0)
        gather.first(1)
        scatter.second(0)
        gather.near(0)
        gather.third(0)
        for order in (1, 2, 3):
            gather.second(order)
            if order < 3:
                gather.first(order + 1)
            gather.near(order)
            gather.third(order)
        scatter.third(0, scatter.total)
        scatter.end()
        gather.own_block()
        gather.end()

    hbm = pl.BlockSpec(memory_space=pl.ANY)
    vmem = pl.BlockSpec(memory_space=pltpu.VMEM)
    return pl.pallas_call(
        kernel,
        out_shape=(
            jax.ShapeDtypeStruct((block_rows, width), f32),
            jax.ShapeDtypeStruct((32 * 16, columns + gain_columns), f32),
        ),
        in_specs=[vmem, vmem, hbm, vmem],
        out_specs=(hbm,) * 2,
        scratch_shapes=[
            pltpu.VMEM((length, wide), low),
            pltpu.VMEM((length, width), low),
            pltpu.VMEM((1, wide), f32),
            pltpu.VMEM((16, columns + gain_columns), f32),
            pltpu.SemaphoreType.DMA,
            *gather_sems(4),
            *scatter_scratch(1, block_rows, width, low),
        ],
        compiler_params=pltpu.CompilerParams(
            collective_id=collective, has_side_effects=True, vmem_limit_bytes=58 * MIB
        ),
        name="input_back",
    )(grad_lin, weights, normed, small)


def shards(
    layer_input, cotangent, gate_weights, routes, w_query, key_projection, value_projection, w_out,
    b_query, key_bias_vector, value_bias_vector, b_out, learned_sink_logits, gain_attn, gain_ffn,
    w_gate, w_up, w_down, b_gate, b_up, b_down,
):
    low = jnp.bfloat16
    ctx_n, z_n = lax.axis_size("ctx"), lax.axis_size("fsdp")
    ctx_at, z_at = lax.axis_index("ctx"), lax.axis_index("fsdp")
    tuned = ctx_n == 8 and z_n == 4
    width = layer_input.shape[-1]
    rows = layer_input.shape[0] * layer_input.shape[1]
    length = rows * ctx_n
    blocks = ctx_n * z_n
    capacity = max(2, rows * TOP * 17 // (16 * ctx_n))
    heads = QUERY_HEADS // ctx_n
    spread = ctx_n // KEY_VALUE_HEADS
    f32 = jnp.float32

    def gather_plane(value, call):
        if tuned:
            return gather_blocks(value, 1, call, f"gather_plane_{call}")
        return lax.all_gather(value, "ctx", axis=0, tiled=True)

    def scatter_plane(value, call):
        if tuned:
            return scatter_blocks(value, 1, call, f"scatter_plane_{call}")
        return lax.psum_scatter(value, "ctx", scatter_dimension=0, tiled=True).astype(f32)

    residual = layer_input.reshape(rows, width).astype(f32)
    grad_final = cotangent.reshape(rows, width)
    gain_attn_f, gain_ffn_f = gain_attn.astype(f32), gain_ffn.astype(f32)
    cosine, sine = rotary_tables(length)

    q_cols, k_cols = w_query.shape[1], key_projection.shape[1]
    own_rows = q_cols + 2 * k_cols
    wide = -(-(width + 2 * ctx_n) // 128) * 128
    biases = jnp.concatenate([b_query, key_bias_vector, value_bias_vector])
    own_weights = jnp.concatenate([w_query, key_projection, value_projection], axis=1).T
    own_weights = jnp.concatenate(
        [own_weights, biases[:, None], jnp.zeros((own_rows, wide - width - 1), low)], axis=1
    )
    ones = jnp.concatenate(
        [jnp.ones((rows, 1), low), jnp.zeros((rows, wide - width - 1), low)], axis=1
    )

    token_routes = routes.reshape(rows, TOP)
    names = jnp.arange(ctx_n, dtype=jnp.int32)
    named = token_routes[:, :, None] == names[None, None, :]
    hits = jnp.sum(named.astype(f32), axis=1)
    gates = jnp.sum(
        jnp.where(named, gate_weights.reshape(rows, TOP)[:, :, None].astype(f32), 0.0), axis=1
    )
    earlier = (
        lax.broadcasted_iota(jnp.int32, (rows, rows), 0)
        > lax.broadcasted_iota(jnp.int32, (rows, rows), 1)
    ).astype(low)
    places = jnp.dot(earlier, hits.astype(low), preferred_element_type=f32)
    first_slot = (lax.rem(ctx_at, PAIR) * capacity).astype(f32) if tuned else 0.0
    places = jnp.where(hits > 0, places + first_slot, -1.0)
    slot_rows = blocks * capacity
    if not tuned:
        slots = jnp.arange(capacity, dtype=f32)[None, :, None]
        picked = places.T[:, None, :] == slots
        select = picked.astype(low)
        mixing = jnp.where(picked, gates.T[:, None, :], 0.0).astype(low)

    def exchanged(slot_values):
        moved = slot_values.reshape(ctx_n, capacity, width)
        return lax.all_to_all(moved, "ctx", split_axis=0, concat_axis=0, tiled=True)

    def to_slots(picks, token_rows):
        dims = (((2,), (0,)), ((), ()))
        moved = lax.dot_general(picks, token_rows, dims, preferred_element_type=f32).astype(low)
        moved = lax.all_gather(exchanged(moved), "fsdp", axis=0, tiled=True)
        return moved.reshape(slot_rows, width)

    def to_tokens(picks, slot_values):
        slot_values = exchanged(
            lax.psum_scatter(slot_values, "fsdp", scatter_dimension=0, tiled=True)
        )
        dims = (((1,), (1,)), ((0,), (0,)))
        moved = lax.dot_general(picks, slot_values, dims, preferred_element_type=f32)
        return jnp.sum(moved, axis=0)

    normed_own = jnp.concatenate([norm_scale(residual, gain_attn_f).astype(low), ones], axis=1)
    sinks = lax.dynamic_slice(learned_sink_logits.astype(f32), (ctx_at * heads,), (heads,))
    swap = [(i, i ^ 1) for i in range(ctx_n)]
    odd = lax.rem(ctx_at, 2) == 1
    if tuned:
        sent_grads = jnp.pad(grad_final, ((0, 0), (0, wide - width)))
        normed_attn, own_grads, head_weights = gather_start(normed_own, sent_grads, own_weights, 1)
        branch, out_weights, queries, keys, keys_t, values, attended, log_sums = attention(
            normed_attn, head_weights, w_out, sinks, cosine, sine, 2
        )
    else:
        normed_attn = lax.all_gather(normed_own, "ctx", axis=0, tiled=True)
        head_weights = lax.all_gather(own_weights, "fsdp", axis=0, tiled=True)
        out_weights = lax.all_gather(w_out, "fsdp", axis=0, tiled=True)
        lin = contract(head_weights, normed_attn, 1, 1).reshape(z_n, own_rows, length)
        query_lin = lin[:, :q_cols].reshape(heads, HEAD_SIZE, length)
        kv_lin = jnp.stack([lin[:, q_cols : q_cols + k_cols], lin[:, q_cols + k_cols :]])
        kv_lin = kv_lin.reshape(2, z_n * k_cols, length)
        if spread == 2:
            other = lax.ppermute(kv_lin, "ctx", swap)
            kv_lin = jnp.where(
                odd,
                jnp.concatenate([other, kv_lin], axis=1),
                jnp.concatenate([kv_lin, other], axis=1),
            )
        queries = turned(query_lin, cosine, sine).astype(low).reshape(heads * HEAD_SIZE, length)
        keys_t = turned(kv_lin[:1], cosine, sine)[0].astype(low)
        values_t = kv_lin[1].astype(low)
        keys, values = keys_t.T, values_t.T
        attended, log_sums = attend(sinks, queries, keys, values_t)
        branch = scatter_plane(product(attended, out_weights, "branch"), 2)
    middle = residual + branch + b_out.astype(f32)
    normed_ffn = norm_scale(middle, gain_ffn_f).astype(low)

    gate_w, up_w, down_w = w_gate[0].T, w_up[0].T, w_down[0]
    share = b_down.shape[1]
    gate_b, up_b = b_gate.astype(f32), b_up.astype(f32)
    down_bias = lax.dynamic_update_slice(
        jnp.zeros((1, width), f32), b_down.astype(f32), (0, z_at * share)
    )
    if tuned:
        sent = jnp.concatenate(
            [
                normed_ffn,
                places.astype(low),
                gates.astype(low),
                jnp.zeros((rows, wide - width - 2 * ctx_n), low),
            ],
            axis=1,
        )
        made = experts(
            sent, sent_grads, own_grads, gate_w, up_w, down_w, gate_b, up_b, down_bias, capacity, 3
        )
        expert_in, hidden_units, mix_part = made[2], made[5], made[6]
        grad_expert_out, grad_gate_lin, grad_up_lin, grad_normed_part = made[7:11]
        grad_biases = made[11:]
        grad_b_down, grad_b_gate, grad_b_up = [value[0] for value in grad_biases]
        grad_normed_ffn, grad_w_gate, grad_w_up = expert_weights(
            grad_normed_part, expert_in, grad_gate_lin, grad_up_lin, 6
        )
    else:
        expert_in = to_slots(select, normed_ffn)
        gate_lin = contract(expert_in, gate_w, 1, 1) + gate_b
        up_lin = contract(expert_in, up_w, 1, 1) + up_b
        hidden_f, unit_back = jax.vjp(glu_units, gate_lin, up_lin)
        hidden_units = hidden_f.astype(low)
        expert_out = (contract(hidden_units, down_w, 1, 0) + down_bias).astype(low)
        expert_mix = to_tokens(mixing, expert_out)
        grad_expert_out = to_slots(mixing, grad_final)
        grad_units = contract(grad_expert_out, down_w, 1, 1)
        grad_gate_f, grad_up_f = unit_back(grad_units)
        grad_gate_lin, grad_up_lin = grad_gate_f.astype(low), grad_up_f.astype(low)
        grad_copy = contract(grad_gate_lin, gate_w, 1, 0) + contract(grad_up_lin, up_w, 1, 0)
        grad_normed_ffn = to_tokens(select, grad_copy.astype(low))
        grad_b_down = jnp.sum(grad_expert_out.astype(f32), axis=0)
        grad_b_gate = jnp.sum(grad_gate_lin.astype(f32), axis=0)
        grad_b_up = jnp.sum(grad_up_lin.astype(f32), axis=0)
        grad_w_gate = contract(grad_gate_lin, expert_in, 0, 0)
        grad_w_up = contract(grad_up_lin, expert_in, 0, 0)
    grad_w_down = contract(hidden_units, grad_expert_out, 0, 0)[:, :width]
    grad_b_down = lax.dynamic_slice(grad_b_down, (z_at * share,), (share,))

    unused, norm_back = jax.vjp(norm_scale, middle, gain_ffn_f)
    grad_middle_part, grad_gain_ffn = norm_back(grad_normed_ffn)
    grad_middle = grad_final.astype(f32) + grad_middle_part
    grad_branch_own = grad_middle.astype(low)
    grad_branch = gather_plane(grad_branch_own, 7)
    grad_b_out = jnp.sum(grad_branch_own.astype(f32), axis=0)
    grad_attended = contract(out_weights, grad_branch, 1, 1).astype(low)
    grad_out_part = contract(attended, grad_branch, 1, 0).astype(low)
    if tuned:
        expert_mix, grad_lin, grad_sink_parts = attention_back(
            mix_part, sinks, queries, keys, keys_t, values, grad_attended, log_sums, cosine, sine,
            own_rows, 5,
        )
    else:
        grad_query, grad_keys, grad_values, grad_sink_parts = attend_back(
            sinks, queries, keys, keys_t, values, grad_attended, log_sums, cosine, sine
        )
        grad_kv = jnp.stack([turned(grad_keys.T[None], cosine, -sine)[0], grad_values.T])
        if spread == 2:
            grad_kv = grad_kv + lax.ppermute(grad_kv, "ctx", swap)
            halves = grad_kv.reshape(2, 2, HEAD_SIZE // 2, length)
            grad_kv = jnp.where(odd, halves[:, 1], halves[:, 0])
        grad_kv = grad_kv.astype(low).reshape(2, z_n, k_cols, length)
        grad_lin = jnp.concatenate(
            [grad_query.reshape(z_n, q_cols, length), grad_kv[0], grad_kv[1]], axis=1
        ).reshape(z_n * own_rows, length)
    final_out = (middle + expert_mix).astype(low).reshape(layer_input.shape)
    grad_weights = contract(grad_lin, normed_attn, 1, 0).astype(low)
    grad_w_out = lax.psum_scatter(grad_out_part, "fsdp", scatter_dimension=0, tiled=True).astype(f32)
    own_grads = lax.psum_scatter(grad_weights, "fsdp", scatter_dimension=0, tiled=True).astype(f32)
    grad_w_query = own_grads[:q_cols, :width].T
    grad_w_key = own_grads[q_cols : q_cols + k_cols, :width].T
    grad_w_value = own_grads[q_cols + k_cols :, :width].T
    own_bias_grads = own_grads[:, width]
    grad_sinks = lax.dynamic_update_slice(
        jnp.zeros((QUERY_HEADS,), f32), jnp.sum(grad_sink_parts, axis=(1, 2)), (ctx_at * heads,)
    )
    sums = (grad_b_out, grad_gain_ffn, grad_sinks)
    if tuned:
        joined = jnp.concatenate(sums)
        columns = -(-joined.shape[0] // (16 * 128)) * 128
        joined = jnp.pad(joined, (0, 16 * columns - joined.shape[0])).reshape(16, columns)
        grad_normed_attn, joined = input_back(
            grad_lin, head_weights, normed_attn, width, 8, joined
        )
        joined = jnp.sum(joined.reshape(blocks, 16, -1), axis=0)
        grad_gain_attn = joined[:, columns:].reshape(-1)[:width] / gain_attn_f
        joined = joined[:, :columns].reshape(-1)
        cuts = (width, 2 * width, 2 * width + QUERY_HEADS)
        sums = [joined[at - value.shape[0] : at] for at, value in zip(cuts, sums)]
    else:
        grad_normed_part = product(grad_lin, head_weights, "grad_normed", width)
        grad_normed_attn = scatter_plane(grad_normed_part, 8)
    unused, norm_back = jax.vjp(norm_scale, residual, gain_attn_f)
    grad_residual_part, own_gain = norm_back(grad_normed_attn)
    input_grad = (grad_middle + grad_residual_part).reshape(layer_input.shape)
    if not tuned:
        *sums, grad_gain_attn = lax.psum((*sums, own_gain), ("ctx", "fsdp"))
    grad_b_out, grad_gain_ffn, grad_sink_logits = sums
    return (
        final_out,
        input_grad,
        grad_w_query,
        grad_w_key,
        grad_w_value,
        grad_w_out,
        own_bias_grads[:q_cols],
        own_bias_grads[q_cols : q_cols + k_cols],
        own_bias_grads[q_cols + k_cols :],
        grad_b_out,
        grad_sink_logits,
        grad_gain_attn,
        grad_gain_ffn,
        grad_w_gate[:, :width].T[None],
        grad_w_up[:, :width].T[None],
        grad_w_down[None],
        grad_b_gate[None],
        grad_b_up[None],
        grad_b_down[None],
    )


def solution(mesh):
    return jax.shard_map(
        shards,
        mesh=mesh,
        in_specs=(
            P("fsdp", "ctx", None),
            P("fsdp", "ctx", None),
            P("fsdp", "ctx", None),
            P("fsdp", "ctx", None),
            P(None, ("ctx", "fsdp")),
            P(None, ("ctx", "fsdp")),
            P(None, ("ctx", "fsdp")),
            P(("ctx", "fsdp"), None),
            P(("ctx", "fsdp")),
            P(("ctx", "fsdp")),
            P(("ctx", "fsdp")),
            P(),
            P(),
            P(),
            P(),
            P("ctx", None, "fsdp"),
            P("ctx", None, "fsdp"),
            P("ctx", "fsdp", None),
            P("ctx", "fsdp"),
            P("ctx", "fsdp"),
            P("ctx", "fsdp"),
        ),
        out_specs=(
            P("fsdp", "ctx", None),
            P("fsdp", "ctx", None),
            P(None, ("ctx", "fsdp")),
            P(None, ("ctx", "fsdp")),
            P(None, ("ctx", "fsdp")),
            P(("ctx", "fsdp"), None),
            P(("ctx", "fsdp")),
            P(("ctx", "fsdp")),
            P(("ctx", "fsdp")),
            P(),
            P(),
            P(),
            P(),
            P("ctx", None, "fsdp"),
            P("ctx", None, "fsdp"),
            P("ctx", "fsdp", None),
            P("ctx", "fsdp"),
            P("ctx", "fsdp"),
            P("ctx", "fsdp"),
        ),
        check_vma=False,
    )
```

```python
import jax
import jax.numpy as jnp
from jax import lax
from jax.experimental import pallas as pl
from jax.experimental.pallas import tpu as pltpu
from jax.sharding import PartitionSpec as P

MESH = pl.DeviceIdType.MESH
MIB = 1 << 20


def remote(src, dst, send_sem, recv_sem, device):
    return pltpu.make_async_remote_copy(
        src_ref=src,
        dst_ref=dst,
        send_sem=send_sem,
        recv_sem=recv_sem,
        device_id=device,
        device_id_type=MESH,
    )


def neighbours():
    me = lax.axis_index("ctx")
    core = lax.rem(me, 2)
    x_at = lax.rem(me // 2, 2)
    y_at = me // 4
    return me, me + 1 - 2 * core, me + 2 - 4 * x_at, me + 4 - 8 * y_at, 2 - 4 * x_at


def greet(others, line, z_at):
    barrier = pltpu.get_barrier_semaphore()
    for other in others:
        pl.semaphore_signal(barrier, 1, device_id=(other, z_at), device_id_type=MESH)
    if line == 1:
        pl.semaphore_wait(barrier, len(others))
        return
    me = lax.axis_index("ctx")

    @pl.when(z_at > 0)
    def _():
        pl.semaphore_signal(barrier, 1, device_id=(me, z_at - 1), device_id_type=MESH)

    @pl.when(z_at < line - 1)
    def _():
        pl.semaphore_signal(barrier, 1, device_id=(me, z_at + 1), device_id_type=MESH)

    inner = (lax.rem(z_at, 3) + 1) // 2
    pl.semaphore_wait(barrier, len(others) + 1 + inner)


def gather_sems(line):
    return [
        pltpu.SemaphoreType.DMA,
        pltpu.SemaphoreType.DMA((line, 2)),
        pltpu.SemaphoreType.DMA((line,)),
        pltpu.SemaphoreType.DMA((line, 9)),
        pltpu.SemaphoreType.DMA((line, 9)),
    ]


class Gather:
    def __init__(self, line, x_ref, o_ref, sems):
        self.line, self.x_ref, self.o_ref = line, x_ref, o_ref
        self.own_sem, self.z_send, self.z_recv, self.p_send, self.p_recv = sems
        self.z_at = lax.axis_index("fsdp")
        self.me, self.mate, self.near_x, self.near_y, step_x = neighbours()
        self.across = self.near_y + step_x
        self.rows = x_ref.shape[0]
        self.half = self.rows // 2
        self.middle = (self.z_at == 1) | (self.z_at == 2)
        self.first_slot = self.z_at if line > 1 else 0

    def slot(self, order):
        z_at = self.z_at
        if self.line == 1:
            return 0
        second = z_at + 1 - 2 * lax.rem(z_at, 2)
        third = 2 - z_at // 2
        fourth = 3 - 3 * (z_at // 2)
        return jnp.where(
            order == 0, z_at, jnp.where(order == 1, second, jnp.where(order == 2, third, fourth))
        )

    def there(self, slot, place, part=None):
        start, count = (slot * 8 + place) * self.rows, self.rows
        if part is not None:
            start, count = start + part * self.half, self.half
        return self.o_ref.at[pl.ds(pl.multiple_of(start, self.half), count)]

    def z_copy(self, src_ref, slot, way, target):
        return remote(
            src_ref,
            self.there(slot, self.me),
            self.z_send.at[slot, way],
            self.z_recv.at[slot],
            (self.me, target),
        )

    def up(self):
        return self.z_copy(self.x_ref, self.z_at, 0, self.z_at + 1)

    def down(self):
        return self.z_copy(self.x_ref, self.z_at, 1, self.z_at - 1)

    def onward(self, order):
        slot = self.slot(order)
        target = jnp.where(order == 1, 3 - self.z_at, 3 * self.z_at - 3)
        return self.z_copy(self.there(slot, self.me), slot, 0, target)

    def copy(self, order, place, kind, device, part=None, src_ref=None):
        dst_ref = self.there(self.slot(order), place, part)
        return remote(
            dst_ref if src_ref is None else src_ref,
            dst_ref,
            self.p_send.at[order, kind],
            self.p_recv.at[order, kind],
            (device, self.z_at),
        )

    def out(self, order, src_ref=None):
        return [
            self.copy(order, self.me, 0, self.near_x, None, src_ref),
            self.copy(order, self.me, 1, self.near_y, None, src_ref),
            self.copy(order, self.me, 2, self.mate, None, src_ref),
        ]

    def passed(self, order, *which):
        places = (
            (self.near_x, 3, self.near_y, 0),
            (self.near_x, 5, self.mate, None),
            (self.near_y, 4, self.near_x, 1),
            (self.near_y, 6, self.mate, None),
            (self.across, 7, self.mate, 0),
            (self.across, 8, self.mate, 1),
        )
        return [self.copy(order, *places[k]) for k in which]

    def begin(self, met=False):
        line, z_at = self.line, self.z_at
        if not met:
            greet((self.mate, self.near_x, self.near_y), line, z_at)
        own = pltpu.make_async_copy(
            self.x_ref, self.there(self.first_slot, self.me), self.own_sem
        )
        own.start()
        if line > 1:
            self.begin_line()
        for copy in self.out(0, self.x_ref):
            copy.start()

    def begin_line(self):
        pl.when(self.z_at < self.line - 1)(lambda: self.up().start())
        pl.when(self.z_at > 0)(lambda: self.down().start())

    def own_block(self):
        pltpu.make_async_copy(
            self.x_ref, self.there(self.first_slot, self.me), self.own_sem
        ).wait()

    def from_line(self, order):
        slot = self.slot(order)
        self.z_copy(self.there(slot, self.me), slot, 0, self.z_at).wait_recv()

    def first(self, order):
        at_end = jnp.logical_not(self.middle)
        pl.when(at_end | (order == 1))(lambda: self.from_line(order))

        @pl.when(self.middle & (order == 1))
        def _():
            self.onward(1).start()
            self.from_line(2)
            self.onward(2).start()

        @pl.when(self.middle & (order == 2))
        def _():
            self.from_line(3)
            self.onward(3).start()

        for copy in self.out(order):
            copy.start()

    def second(self, order):
        to_y, mate_x, to_x, mate_y = self.passed(order, 0, 1, 2, 3)
        self.copy(order, self.near_x, 0, self.near_x).wait_recv()
        to_y.start()
        mate_x.start()
        self.copy(order, self.near_y, 1, self.near_y).wait_recv()
        to_x.start()
        mate_y.start()

    def near(self, order):
        step = self.mate - self.me
        self.copy(order, self.mate, 2, self.mate).wait_recv()
        self.copy(order, self.near_x + step, 5, self.mate).wait_recv()

    def third(self, order):
        step = self.mate - self.me
        top, low = self.passed(order, 4, 5)
        self.copy(order, self.across, 3, self.near_y, 0).wait_recv()
        top.start()
        self.copy(order, self.across, 4, self.near_x, 1).wait_recv()
        low.start()
        self.copy(order, self.near_y + step, 6, self.mate).wait_recv()
        self.copy(order, self.across + step, 7, self.mate, 0).wait_recv()
        self.copy(order, self.across + step, 8, self.mate, 1).wait_recv()

    def end(self, from_order=0):
        line, z_at = self.line, self.z_at

        def sent(order, carry):
            for copy in self.out(order) + self.passed(order, 0, 1, 2, 3, 4, 5):
                copy.wait_send()
            return carry

        lax.fori_loop(from_order, line, sent, 0)
        if line > 1:
            pl.when(z_at < line - 1)(lambda: self.up().wait_send())
            pl.when(z_at > 0)(lambda: self.down().wait_send())

            @pl.when(self.middle)
            def _():
                for order in range(1, line):
                    self.onward(order).wait_send()


def line_sems(line):
    return [
        pltpu.SemaphoreType.DMA,
        pltpu.SemaphoreType.DMA((line, 2)),
        pltpu.SemaphoreType.DMA((line,)),
    ]


class Line:
    def __init__(self, x_ref, o_ref, sems):
        self.x_ref, self.o_ref = x_ref, o_ref
        self.own_sem, self.sends, self.receives = sems
        self.me, self.z_at = lax.axis_index("ctx"), lax.axis_index("fsdp")
        self.middle = (self.z_at == 1) | (self.z_at == 2)
        self.slots = (
            self.z_at,
            self.z_at + 1 - 2 * lax.rem(self.z_at, 2),
            2 - self.z_at // 2,
            3 - 3 * (self.z_at // 2),
        )

    def there(self, slot):
        rows = self.x_ref.shape[0]
        return self.o_ref.at[pl.ds(pl.multiple_of(slot * rows, 16), rows)]

    def copy(self, src_ref, slot, way, target):
        return remote(
            src_ref,
            self.there(slot),
            self.sends.at[slot, way],
            self.receives.at[slot],
            (self.me, target),
        )

    def own(self):
        return pltpu.make_async_copy(self.x_ref, self.there(self.z_at), self.own_sem)

    def up(self):
        return self.copy(self.x_ref, self.z_at, 0, self.z_at + 1)

    def down(self):
        return self.copy(self.x_ref, self.z_at, 1, self.z_at - 1)

    def onward(self, order):
        slot = self.slots[order]
        target = 3 - self.z_at if order == 1 else 3 * self.z_at - 3
        return self.copy(self.there(slot), slot, 0, target)

    def begin(self):
        pl.when(self.z_at < 3)(lambda: self.up().start())
        pl.when(self.z_at > 0)(lambda: self.down().start())
        self.own().start()

    def arrive(self, order):
        slot = self.slots[order]
        self.copy(self.there(slot), slot, 0, self.z_at).wait_recv()

    def pass_on(self, *orders):
        @pl.when(self.middle)
        def _():
            for order in orders:
                self.arrive(order)
                self.onward(order).start()

    def rest(self):
        @pl.when(jnp.logical_not(self.middle))
        def _():
            for order in (1, 2, 3):
                self.arrive(order)

    def end(self):
        self.own().wait()
        pl.when(self.z_at < 3)(lambda: self.up().wait_send())
        pl.when(self.z_at > 0)(lambda: self.down().wait_send())

        @pl.when(self.middle)
        def _():
            for order in (1, 2, 3):
                self.onward(order).wait_send()


def gather_blocks(x, line, collective, name):
    rows, width = x.shape

    def kernel(x_ref, o_ref, *sems):
        gather = Gather(line, x_ref, o_ref, sems)
        gather.begin()

        def body(order, carry):
            gather.second(order)
            if line > 1:
                pl.when(order + 1 < line)(lambda: gather.first(order + 1))
            gather.near(order)
            gather.third(order)
            return carry

        lax.fori_loop(0, line, body, 0)
        gather.own_block()
        gather.end()

    return pl.pallas_call(
        kernel,
        out_shape=jax.ShapeDtypeStruct((line * 8 * rows, width), x.dtype),
        in_specs=[pl.BlockSpec(memory_space=pl.ANY)],
        out_specs=pl.BlockSpec(memory_space=pl.ANY),
        scratch_shapes=gather_sems(line),
        compiler_params=pltpu.CompilerParams(collective_id=collective, has_side_effects=True),
        name=name,
    )(x)


CHUNK = 16


def add_rows(dst_ref, src_refs, start, count, out_ref=None):
    def body(i, carry):
        at = pl.ds(pl.multiple_of(start + i * CHUNK, CHUNK), CHUNK)
        value = dst_ref[at, :].astype(jnp.float32)
        for src_ref in src_refs:
            value = value + src_ref[at, :].astype(jnp.float32)
        to_ref = dst_ref if out_ref is None else out_ref
        to_ref[at, :] = value.astype(to_ref.dtype)
        return carry

    lax.fori_loop(0, count // CHUNK, body, 0)


class Scatter:
    def __init__(self, line, x_ref, o_ref, scratch, columns=None):
        self.columns = columns
        (
            self.mine, self.theirs, self.halves, self.from_x, self.from_y, self.from_z, self.total,
            self.load_sem, self.m_send, self.m_recv, self.p_send, self.p_recv, self.z_send,
            self.z_recv, self.out_sem,
        ) = scratch
        self.line, self.x_ref, self.o_ref = line, x_ref, o_ref
        self.z_at = lax.axis_index("fsdp")
        self.me, self.mate, self.near_x, self.near_y, step_x = neighbours()
        self.places = (self.near_y + step_x, self.near_x, self.near_y, self.me)
        self.rows = self.total.shape[0]
        self.half = self.rows // 2
        self.middle = (self.z_at == 1) | (self.z_at == 2)

    def slot(self, order):
        z_at = self.z_at
        if self.line == 1:
            return 0
        far, next_far, near = 3 - 3 * (z_at // 2), 2 - z_at // 2, z_at + 1 - 2 * lax.rem(z_at, 2)
        return jnp.where(
            order == 0, far, jnp.where(order == 1, next_far, jnp.where(order == 2, near, z_at))
        )

    def there(self, slot, place):
        at = pl.ds(pl.multiple_of((slot * 8 + place) * self.rows, 16), self.rows)
        return self.x_ref.at[at] if self.columns is None else self.x_ref.at[at, self.columns]

    def give(self, order, k):
        return remote(
            self.there(self.slot(order), self.places[k] + self.mate - self.me),
            self.theirs.at[order, k],
            self.m_send.at[order, k],
            self.m_recv.at[order, k],
            (self.mate, self.z_at),
        )

    def load(self, order, k):
        return pltpu.make_async_copy(
            self.there(self.slot(order), self.places[k]),
            self.mine.at[order, k],
            self.load_sem.at[order, k],
        )

    def send(self, order, kind):
        top, low = pl.ds(0, self.half), pl.ds(self.half, self.half)
        k, part, to, device = (
            (0, top, self.halves, self.near_x),
            (0, low, self.halves, self.near_y),
            (1, top, self.from_x, self.near_x),
            (1, low, self.from_x, self.near_x),
            (2, low, self.from_y, self.near_y),
            (2, top, self.from_y, self.near_y),
        )[kind]
        return remote(
            self.mine.at[order, k, part],
            to.at[order, part],
            self.p_send.at[order, kind],
            self.p_recv.at[order, kind],
            (device, self.z_at),
        )

    def begin(self, met=False):
        if not met:
            greet((self.mate, self.near_x, self.near_y), self.line, self.z_at)

        def body(order, carry):
            for k in range(4):
                self.start_part(order, k)
            return carry

        lax.fori_loop(0, self.line, body, 0)

    def start_part(self, order, k):
        self.give(order, k).start()
        self.load(order, k).start()

    def produce(self, make):
        for k in range(4):
            make(self.places[k] // 2)
            self.start_part(0, k)

    def first(self, order):
        for k in range(4):
            self.give(order, k).wait_recv()
            self.load(order, k).wait()
            add_rows(self.mine.at[order, k], [self.theirs.at[order, k]], 0, self.rows)
            for kind in ((0, 1), (2,), (4,), ())[k]:
                self.send(order, kind).start()

    def second(self, order):
        self.send(order, 1).wait_recv()
        add_rows(self.mine.at[order, 1], [self.halves.at[order]], self.half, self.half)
        self.send(order, 3).start()
        self.send(order, 0).wait_recv()
        add_rows(self.mine.at[order, 2], [self.halves.at[order]], 0, self.half)
        self.send(order, 5).start()

    def third(self, order, out_ref=None):
        for kind in (2, 3, 4, 5):
            self.send(order, kind).wait_recv()
        sources = [self.from_x.at[order], self.from_y.at[order]]
        add_rows(self.mine.at[order, 3], sources, 0, self.rows, out_ref)

    def z_copy(self, order, slot_at, target):
        return remote(
            self.mine.at[order, 3],
            self.from_z.at[slot_at],
            self.z_send.at[order],
            self.z_recv.at[slot_at],
            (self.me, target),
        )

    def z_out(self, order):
        z_at, slot = self.z_at, self.slot(order)
        target = jnp.where(order == 2, slot, z_at + 1 - 2 * (z_at // 2))
        ends = jnp.where(target == slot, 1, 0)
        return self.z_copy(order, ends * (4 + (z_at - target + 1) // 2) + (1 - ends) * slot, target)

    def pass_on(self, order):
        slot = self.slot(order)
        self.z_copy(order, slot, self.z_at).wait_recv()
        add_rows(self.mine.at[order, 3], [self.from_z.at[slot]], 0, self.rows)
        self.z_out(order).start()

    def along(self, order):
        @pl.when((order < self.line - 1) & jnp.logical_not(self.middle))
        def _():
            self.z_out(order).start()

        pl.when((order == 1) & self.middle)(lambda: self.pass_on(0))

        @pl.when((order == 2) & self.middle)
        def _():
            self.pass_on(1)
            self.pass_on(2)

    def last(self):
        z_at, line = self.z_at, self.line
        pl.when(z_at > 0)(lambda: self.z_copy(line - 1, 4, z_at).wait_recv())
        pl.when(z_at < line - 1)(lambda: self.z_copy(line - 1, 5, z_at).wait_recv())
        mine = self.mine.at[line - 1, 3]
        below, above = self.from_z.at[4], self.from_z.at[5]
        pl.when(z_at == 0)(lambda: add_rows(mine, [above], 0, self.rows, self.total))
        pl.when(z_at == line - 1)(lambda: add_rows(mine, [below], 0, self.rows, self.total))
        pl.when(self.middle)(lambda: add_rows(mine, [below, above], 0, self.rows, self.total))

    def end(self):
        out = pltpu.make_async_copy(self.total, self.o_ref, self.out_sem)
        out.start()

        def sent(order, carry):
            for k in range(4):
                self.give(order, k).wait_send()
            for kind in range(6):
                self.send(order, kind).wait_send()
            if self.line > 1:
                pl.when(order < self.line - 1)(lambda: self.z_out(order).wait_send())
            return carry

        lax.fori_loop(0, self.line, sent, 0)
        out.wait()

    def plane_sum(self):
        self.first(0)
        self.second(0)
        self.third(0, self.total)
        self.end()

    def run(self, work=None, extra=0, met=False, begun=False):
        if not begun:
            self.begin(met)
        if self.line == 1:
            self.plane_sum()
            return
        if not begun:
            self.first(0)

        def body(step, carry):
            order, phase = step // 3, lax.rem(step, 3)

            @pl.when((phase == 0) & (order < self.line))
            def _():
                self.second(order)
                pl.when(order + 1 < self.line)(lambda: self.first(order + 1))

            pl.when((phase == 1) & (order < self.line))(lambda: self.third(order))
            pl.when((phase == 2) & (order < self.line))(lambda: self.along(order))
            if work is not None:
                work(step)
            return carry

        lax.fori_loop(0, 3 * self.line + extra, body, 0)
        self.last()
        self.end()


def scatter_scratch(line, rows, width, dtype):
    shard = (rows, width)
    return [
        pltpu.VMEM((line, 4) + shard, dtype),
        pltpu.VMEM((line, 4) + shard, dtype),
        pltpu.VMEM((line,) + shard, dtype),
        pltpu.VMEM((line,) + shard, dtype),
        pltpu.VMEM((line,) + shard, dtype),
        pltpu.VMEM((6 if line > 1 else 1,) + shard, dtype),
        pltpu.VMEM(shard, jnp.float32),
        pltpu.SemaphoreType.DMA((line, 4)),
        pltpu.SemaphoreType.DMA((line, 4)),
        pltpu.SemaphoreType.DMA((line, 4)),
        pltpu.SemaphoreType.DMA((line, 6)),
        pltpu.SemaphoreType.DMA((line, 6)),
        pltpu.SemaphoreType.DMA((line,)),
        pltpu.SemaphoreType.DMA((6,)),
        pltpu.SemaphoreType.DMA,
    ]


def scatter_blocks(x, line, collective, name):
    rows, width = x.shape[0] // (line * 8), x.shape[1]

    def kernel(x_ref, o_ref, *scratch):
        Scatter(line, x_ref, o_ref, scratch).run()

    return pl.pallas_call(
        kernel,
        out_shape=jax.ShapeDtypeStruct((rows, width), jnp.float32),
        in_specs=[pl.BlockSpec(memory_space=pl.ANY)],
        out_specs=pl.BlockSpec(memory_space=pl.ANY),
        scratch_shapes=scatter_scratch(line, rows, width, x.dtype),
        compiler_params=pltpu.CompilerParams(
            collective_id=collective, has_side_effects=True, vmem_limit_bytes=52 * MIB
        ),
        name=name,
    )(x)


QUERY_HEADS = 64
KEY_VALUE_HEADS = 8
HEAD_SIZE = 64
TOP = 4
EPSILON = 1e-05
THETA_BASE = 150000.0
CLAMP_LIMIT = 7.0
GLU_ALPHA = 1.702
MASK_FILL = -1e30
SPAN = 256
SCALE = HEAD_SIZE**-0.5


def contract(left, right, left_axis, right_axis):
    return lax.dot_general(
        left, right, (((left_axis,), (right_axis,)), ((), ())), preferred_element_type=jnp.float32
    )


def norm_scale(value_rows, gain_vec):
    return (
        value_rows
        * lax.rsqrt(jnp.mean(value_rows * value_rows, axis=-1, keepdims=True) + EPSILON)
        * gain_vec
    )


def soft_clamp(value_rows):
    return CLAMP_LIMIT * jnp.tanh(value_rows / CLAMP_LIMIT)


def glu_units(gate_lin, up_lin):
    gated = soft_clamp(gate_lin)
    return (soft_clamp(up_lin) + 1.0) * gated * jax.nn.sigmoid(GLU_ALPHA * gated)


def rotary_tables(length):
    half = HEAD_SIZE // 2
    inverse = THETA_BASE ** (-jnp.arange(half, dtype=jnp.float32) / half)
    angles = inverse[:, None] * jnp.arange(length, dtype=jnp.int32).astype(jnp.float32)[None, :]
    return jnp.cos(angles), jnp.sin(angles)


def turned(value, cosine, sine):
    half = HEAD_SIZE // 2
    first, second = value[:, :half], value[:, half:]
    return jnp.concatenate(
        [first * cosine - second * sine, second * cosine + first * sine], axis=1
    )


def diagonal(length):
    return lax.broadcasted_iota(jnp.int32, (length, length), 0) <= lax.broadcasted_iota(
        jnp.int32, (length, length), 1
    )


def masked_scores(key_rows, query_cols, count):
    scores = contract(key_rows, query_cols, 1, 0)
    edge = jnp.where(diagonal(SPAN), scores[count - SPAN :], MASK_FILL)
    if count == SPAN:
        return edge
    return jnp.concatenate([scores[: count - SPAN], edge], axis=0)


def attend_kernel(sink_ref, q_ref, k_ref, v_ref, out_ref, log_ref):
    sink = sink_ref[pl.program_id(0)]
    length = q_ref.shape[1]
    for start in range(0, length, SPAN):
        count = start + SPAN
        at = pl.ds(start, SPAN)
        query = q_ref[:, at] * jnp.bfloat16(SCALE)
        scores = masked_scores(k_ref[:count, :], query, count)
        row_top = jnp.maximum(jnp.max(scores, axis=0, keepdims=True), sink)
        weights = jnp.exp(scores - row_top)
        denominator = jnp.sum(weights, axis=0, keepdims=True) + jnp.exp(sink - row_top)
        probabilities = (weights / denominator).astype(jnp.bfloat16)
        out_ref[:, at] = contract(v_ref[:, :count], probabilities, 1, 0).astype(jnp.bfloat16)
        log_ref[0, :, at] = row_top + jnp.log(denominator)


def attend(sinks, queries, keys, values):
    heads, length = queries.shape[0] // HEAD_SIZE, queries.shape[1]
    per_head = pl.BlockSpec((HEAD_SIZE, length), lambda h: (h, 0))
    return pl.pallas_call(
        attend_kernel,
        grid=(heads,),
        out_shape=(
            jax.ShapeDtypeStruct(queries.shape, jnp.bfloat16),
            jax.ShapeDtypeStruct((heads, 1, length), jnp.float32),
        ),
        in_specs=[
            pl.BlockSpec(memory_space=pltpu.SMEM),
            per_head,
            pl.BlockSpec((length, HEAD_SIZE), lambda h: (0, 0)),
            pl.BlockSpec((HEAD_SIZE, length), lambda h: (0, 0)),
        ],
        out_specs=(per_head, pl.BlockSpec((1, 1, length), lambda h: (h, 0, 0))),
        compiler_params=pltpu.CompilerParams(vmem_limit_bytes=40 * MIB),
        cost_estimate=pl.CostEstimate(
            flops=heads * length * length * HEAD_SIZE * 4,
            bytes_accessed=heads * length * HEAD_SIZE * 4,
            transcendentals=heads * length * length,
        ),
        name="attend",
    )(sinks, queries, keys, values)


def attention(rows_own, grads_own, weights_own, out_own, sinks, cosine, sine, collective):
    low, f32 = jnp.bfloat16, jnp.float32
    block_rows, wide = rows_own.shape
    length = 8 * block_rows
    own_rows = weights_own.shape[0]
    q_rows, width = out_own.shape
    kv_rows = (own_rows - q_rows) // 2
    heads = 4 * q_rows // HEAD_SIZE
    half = HEAD_SIZE // 2
    per_shard = q_rows // HEAD_SIZE

    def kernel(
        sink_ref, rows_ref, grads_ref, weights_ref, out_ref, cos_ref, sin_ref,
        o_ref, all_rows, all_grads, all_weights, all_out, q_ref, k_ref, kt_ref, v_ref, att_ref, log_ref,
        normed_v, weights_v, lin, vt_v, out_v, branch, held_sems, *scratch,
    ):
        plane = Gather(1, rows_ref, all_rows, scratch[:5])
        later = Gather(1, grads_ref, all_grads, scratch[5:10])
        heads_line = Line(weights_ref, all_weights, scratch[10:13])
        line = Line(out_ref, all_out, scratch[13:16])
        scatter = Scatter(1, branch, o_ref, scratch[16:])
        load_rows = pltpu.make_async_copy(all_rows, normed_v, held_sems.at[0])
        load_weights = pltpu.make_async_copy(all_weights, weights_v, held_sems.at[1])
        greet((plane.mate, plane.near_x, plane.near_y), 4, line.z_at)
        heads_line.begin()
        plane.begin(True)
        heads_line.pass_on(1, 2)
        plane.second(0)
        later.begin(True)
        line.begin()
        plane.near(0)
        plane.third(0)
        plane.own_block()
        load_rows.start()
        heads_line.pass_on(3)
        later.second(0)
        later.near(0)
        later.third(0)
        later.own_block()
        heads_line.rest()
        heads_line.end()
        load_weights.start()
        load_rows.wait()
        load_weights.wait()

        def project(i, carry):
            at = pl.ds(pl.multiple_of(i * SPAN, SPAN), SPAN)
            lin[:, at] = contract(weights_v[...], normed_v[at, :], 1, 1)
            return carry

        lax.fori_loop(0, length // SPAN, project, 0)
        line.pass_on(1, 2)

        def turn(value):
            first, second = value[:half], value[half:]
            cosine, sine = cos_ref[...], sin_ref[...]
            return jnp.concatenate(
                [first * cosine - second * sine, second * cosine + first * sine], axis=0
            ).astype(low)

        def shards_of(offset):
            return jnp.concatenate(
                [
                    lin[z * own_rows + offset : z * own_rows + offset + kv_rows, :]
                    for z in range(4)
                ],
                axis=0,
            )

        keys_t = turn(shards_of(q_rows))
        values_t = shards_of(q_rows + kv_rows).astype(low)
        kt_ref[...] = keys_t
        vt_v[...] = values_t
        k_ref[...] = keys_t.T
        v_ref[...] = values_t.T

        def head(h, carry):
            pl.when(h == heads // 2)(lambda: line.pass_on(3))
            start = (h // per_shard) * own_rows + lax.rem(h, per_shard) * HEAD_SIZE
            queries = turn(lin[pl.ds(pl.multiple_of(start, 16), HEAD_SIZE), :])
            rows = pl.ds(pl.multiple_of(h * HEAD_SIZE, HEAD_SIZE), HEAD_SIZE)
            q_ref[rows, :] = queries
            sink = sink_ref[h]
            for begin in range(0, length, SPAN):
                count = begin + SPAN
                query = queries[:, begin:count] * jnp.bfloat16(SCALE)
                scores = masked_scores(k_ref[:count, :], query, count)
                row_top = jnp.maximum(jnp.max(scores, axis=0, keepdims=True), sink)
                chances = jnp.exp(scores - row_top)
                denominator = jnp.sum(chances, axis=0, keepdims=True) + jnp.exp(sink - row_top)
                chances = (chances / denominator).astype(low)
                att_ref[rows, begin:count] = contract(vt_v[:, :count], chances, 1, 0).astype(low)
                log_ref[h, :, begin:count] = row_top + jnp.log(denominator)
            return carry

        lax.fori_loop(0, heads, head, 0)
        line.rest()
        line.end()
        load = pltpu.make_async_copy(all_out, out_v, held_sems.at[0])
        load.start()
        load.wait()

        def give_back(chip):
            at = pl.ds(pl.multiple_of(chip * SPAN, SPAN), SPAN)
            branch[at, :] = contract(att_ref[:, at], out_v[...], 0, 0).astype(low)

        scatter.produce(give_back)
        scatter.plane_sum()
        plane.end()
        later.end()

    hbm = pl.BlockSpec(memory_space=pl.ANY)
    vmem = pl.BlockSpec(memory_space=pltpu.VMEM)
    return pl.pallas_call(
        kernel,
        out_shape=(
            jax.ShapeDtypeStruct((block_rows, width), f32),
            jax.ShapeDtypeStruct((length, wide), low),
            jax.ShapeDtypeStruct((length, wide), low),
            jax.ShapeDtypeStruct((4 * own_rows, wide), low),
            jax.ShapeDtypeStruct((4 * q_rows, width), low),
            jax.ShapeDtypeStruct((4 * q_rows, length), low),
            jax.ShapeDtypeStruct((length, HEAD_SIZE), low),
            jax.ShapeDtypeStruct((HEAD_SIZE, length), low),
            jax.ShapeDtypeStruct((length, HEAD_SIZE), low),
            jax.ShapeDtypeStruct((4 * q_rows, length), low),
            jax.ShapeDtypeStruct((heads, 1, length), f32),
        ),
        in_specs=[pl.BlockSpec(memory_space=pltpu.SMEM), hbm, hbm, hbm, hbm, vmem, vmem],
        out_specs=(hbm,) * 5 + (vmem,) * 6,
        scratch_shapes=[
            pltpu.VMEM((length, wide), low),
            pltpu.VMEM((4 * own_rows, wide), low),
            pltpu.VMEM((4 * own_rows, length), f32),
            pltpu.VMEM((HEAD_SIZE, length), low),
            pltpu.VMEM((4 * q_rows, width), low),
            pltpu.VMEM((length, width), low),
            pltpu.SemaphoreType.DMA((2,)),
            *gather_sems(1),
            *gather_sems(1),
            *line_sems(4),
            *line_sems(4),
            *scatter_scratch(1, block_rows, width, low),
        ],
        compiler_params=pltpu.CompilerParams(
            collective_id=collective, has_side_effects=True, vmem_limit_bytes=58 * MIB
        ),
        name="attention",
    )(sinks, rows_own, grads_own, weights_own, out_own, cosine, sine)


def attend_back_kernel(
    sink_ref, q_ref, k_ref, kt_ref, v_ref, grad_ref, log_ref, cos_ref, sin_ref,
    dq_ref, dk_ref, dv_ref, dsink_ref,
):
    head = pl.program_id(0)
    sink = sink_ref[head]
    length = q_ref.shape[1]
    half = HEAD_SIZE // 2

    @pl.when(head == 0)
    def _():
        dk_ref[...] = jnp.zeros_like(dk_ref)
        dv_ref[...] = jnp.zeros_like(dv_ref)

    grad_sink = jnp.zeros((1, SPAN), jnp.float32)
    for start in range(0, length, SPAN):
        count = start + SPAN
        at = pl.ds(start, SPAN)
        query = q_ref[:, at] * jnp.bfloat16(SCALE)
        grad = grad_ref[:, at]
        log_sum = log_ref[0, :, at]
        probabilities = jnp.exp(masked_scores(k_ref[:count, :], query, count) - log_sum)
        grad_probs = contract(v_ref[:count, :], grad, 1, 0)
        inner_sum = jnp.sum(probabilities * grad_probs, axis=0, keepdims=True)
        grad_scores = (probabilities * (grad_probs - inner_sum)).astype(jnp.bfloat16)
        grad_query = contract(kt_ref[:, :count], grad_scores, 1, 0) * SCALE
        first, second = grad_query[:half], grad_query[half:]
        cosine, sine = cos_ref[:, at], sin_ref[:, at]
        dq_ref[:half, at] = (first * cosine + second * sine).astype(jnp.bfloat16)
        dq_ref[half:, at] = (second * cosine - first * sine).astype(jnp.bfloat16)
        dk_ref[:count, :] += contract(grad_scores, query, 1, 1)
        dv_ref[:count, :] += contract(probabilities.astype(jnp.bfloat16), grad, 1, 1)
        grad_sink = grad_sink - jnp.exp(sink - log_sum) * inner_sum
    dsink_ref[0] = grad_sink


def attend_back(sinks, queries, keys, keys_t, values, grads, log_sums, cosine, sine):
    heads, length = queries.shape[0] // HEAD_SIZE, queries.shape[1]
    per_head = pl.BlockSpec((HEAD_SIZE, length), lambda h: (h, 0))

    def whole(*shape):
        return pl.BlockSpec(shape, lambda h: (0,) * len(shape))

    return pl.pallas_call(
        attend_back_kernel,
        grid=(heads,),
        out_shape=(
            jax.ShapeDtypeStruct(queries.shape, jnp.bfloat16),
            jax.ShapeDtypeStruct((length, HEAD_SIZE), jnp.float32),
            jax.ShapeDtypeStruct((length, HEAD_SIZE), jnp.float32),
            jax.ShapeDtypeStruct((heads, 1, SPAN), jnp.float32),
        ),
        in_specs=[
            pl.BlockSpec(memory_space=pltpu.SMEM),
            per_head,
            whole(length, HEAD_SIZE),
            whole(HEAD_SIZE, length),
            whole(length, HEAD_SIZE),
            per_head,
            pl.BlockSpec((1, 1, length), lambda h: (h, 0, 0)),
            whole(HEAD_SIZE // 2, length),
            whole(HEAD_SIZE // 2, length),
        ],
        out_specs=(
            per_head,
            whole(length, HEAD_SIZE),
            whole(length, HEAD_SIZE),
            pl.BlockSpec((1, 1, SPAN), lambda h: (h, 0, 0)),
        ),
        compiler_params=pltpu.CompilerParams(vmem_limit_bytes=48 * MIB),
        cost_estimate=pl.CostEstimate(
            flops=heads * length * length * HEAD_SIZE * 10,
            bytes_accessed=heads * length * HEAD_SIZE * 8,
            transcendentals=heads * length * length,
        ),
        name="attend_back",
    )(sinks, queries, keys, keys_t, values, grads, log_sums, cosine, sine)


def branch_back(parts, columns, grad_own, out_weights, attended, collective):
    low, f32 = jnp.bfloat16, jnp.float32
    block_rows, width = grad_own.shape
    depth, length = attended.shape
    cut = 512

    def kernel(
        parts_ref, grad_ref, out_ref, att_ref, o_ref, grad_att, grad_out, all_grads, *scratch
    ):
        gather = Gather(1, grad_ref, all_grads, scratch[:5])
        scatter = Scatter(4, parts_ref, o_ref, scratch[5:], pl.ds(0, columns))
        greet((gather.mate, gather.near_x, gather.near_y), 4, gather.z_at)
        gather.begin(True)
        scatter.begin(True)
        gather.second(0)
        scatter.first(0)
        gather.near(0)
        gather.third(0)
        gather.own_block()

        def work(step):
            for i in range(length // SPAN):

                @pl.when(step == i)
                def _():
                    at = slice(i * SPAN, (i + 1) * SPAN)
                    grad_att[:, at] = contract(out_ref[...], all_grads[at, :], 1, 1).astype(low)

            for i in range(-(-width // cut)):

                @pl.when(step == i + length // SPAN)
                def _():
                    at = slice(i * cut, min(width, (i + 1) * cut))
                    grad_out[:, at] = contract(att_ref[...], all_grads[:, at], 1, 0).astype(low)

        steps = length // SPAN + -(-width // cut)
        scatter.run(work, max(0, steps - 12), begun=True)
        gather.end()

    hbm = pl.BlockSpec(memory_space=pl.ANY)
    vmem = pl.BlockSpec(memory_space=pltpu.VMEM)
    return pl.pallas_call(
        kernel,
        out_shape=(
            jax.ShapeDtypeStruct((block_rows, columns), f32),
            jax.ShapeDtypeStruct((depth, length), low),
            jax.ShapeDtypeStruct((depth, width), low),
        ),
        in_specs=[hbm, hbm, vmem, vmem],
        out_specs=(hbm, vmem, vmem),
        scratch_shapes=[
            pltpu.VMEM((length, width), low),
            *gather_sems(1),
            *scatter_scratch(4, block_rows, columns, low),
        ],
        compiler_params=pltpu.CompilerParams(
            collective_id=collective, has_side_effects=True, vmem_limit_bytes=56 * MIB
        ),
        name="branch_back",
    )(parts, grad_own, out_weights, attended)


def attention_back(
    parts, first_column, sinks, queries, keys, keys_t, values, grads, log_sums, cosine, sine, normed,
    own_rows, collective,
):
    low, f32 = jnp.bfloat16, jnp.float32
    length = queries.shape[1]
    heads = queries.shape[0] // HEAD_SIZE
    half = HEAD_SIZE // 2
    block_rows, columns = parts.shape[0] // 32, parts.shape[1] - first_column
    q_rows = queries.shape[0] // 4
    kv_rows = (own_rows - q_rows) // 2
    per_shard = q_rows // HEAD_SIZE
    spans = length // SPAN

    def kernel(
        sink_ref, parts_ref, q_ref, k_ref, kt_ref, v_ref, grad_ref, log_ref, cos_ref, sin_ref, normed_hbm,
        o_ref, lin_ref, weights_ref, dsink_ref, dk_s, dv_s, normed_v, normed_sem, *scratch,
    ):
        load = pltpu.make_async_copy(normed_hbm, normed_v, normed_sem)
        load.start()
        dk_s[...] = jnp.zeros_like(dk_s)
        dv_s[...] = jnp.zeros_like(dv_s)
        dsink_ref[...] = jnp.zeros_like(dsink_ref)

        def one(head, span):
            start, count = span * SPAN, span * SPAN + SPAN
            at = slice(start, count)
            rows = pl.ds(pl.multiple_of(head * HEAD_SIZE, HEAD_SIZE), HEAD_SIZE)
            query = q_ref[rows, at] * jnp.bfloat16(SCALE)
            grad = grad_ref[rows, at]
            log_sum = log_ref[head, :, at]
            chances = jnp.exp(masked_scores(k_ref[:count, :], query, count) - log_sum)
            grad_probs = contract(v_ref[:count, :], grad, 1, 0)
            inner_sum = jnp.sum(chances * grad_probs, axis=0, keepdims=True)
            grad_scores = (chances * (grad_probs - inner_sum)).astype(low)
            grad_query = contract(kt_ref[:, :count], grad_scores, 1, 0) * SCALE
            first, second = grad_query[:half], grad_query[half:]
            cosine, sine = cos_ref[:, at], sin_ref[:, at]
            place = (head // per_shard) * own_rows + lax.rem(head, per_shard) * HEAD_SIZE
            lin_ref[pl.ds(pl.multiple_of(place, 16), HEAD_SIZE), at] = jnp.concatenate(
                [first * cosine + second * sine, second * cosine - first * sine], axis=0
            ).astype(low)
            dk_s[:count, :] += contract(grad_scores, query, 1, 1)
            dv_s[:count, :] += contract(chances.astype(low), grad, 1, 1)
            dsink_ref[head] -= jnp.exp(sink_ref[head] - log_sum) * inner_sum

        def finish():
            grad_keys, grad_values = dk_s[...].T, dv_s[...].T
            first, second = grad_keys[:half], grad_keys[half:]
            cosine, sine = cos_ref[...], sin_ref[...]
            grad_keys = jnp.concatenate(
                [first * cosine + second * sine, second * cosine - first * sine], axis=0
            )
            for z in range(4):
                here = slice(z * kv_rows, (z + 1) * kv_rows)
                start = z * own_rows + q_rows
                lin_ref[start : start + kv_rows, :] = grad_keys[here].astype(low)
                lin_ref[start + kv_rows : start + 2 * kv_rows, :] = grad_values[here].astype(low)
            load.wait()

        wide = normed.shape[1]
        cut = 512

        def work(step):
            first_step = 0
            for span in reversed(range(spans)):
                at_once = max(1, 16 // (span + 1))
                count = -(-heads // at_once)
                here = (step >= first_step) & (step < first_step + count)

                @pl.when(here)
                def _():
                    begin = (step - first_step) * at_once

                    def body(head, carry):
                        pl.when(head < heads)(lambda: one(head, span))
                        return carry

                    lax.fori_loop(begin, begin + at_once, body, 0)

                first_step += count
            pl.when(step == first_step)(finish)
            for i in range(-(-wide // cut)):

                @pl.when(step == first_step + i)
                def _():
                    at = slice(i * cut, min(wide, (i + 1) * cut))
                    weights_ref[:, at] = contract(lin_ref[...], normed_v[:, at], 1, 0).astype(low)

        needed = sum(-(-heads // max(1, 16 // (span + 1))) for span in range(spans))
        needed += -(-wide // cut)
        late = pl.ds(first_column, columns)
        Scatter(4, parts_ref, o_ref, scratch, late).run(work, max(0, needed - 12))

    hbm = pl.BlockSpec(memory_space=pl.ANY)
    vmem = pl.BlockSpec(memory_space=pltpu.VMEM)
    return pl.pallas_call(
        kernel,
        out_shape=(
            jax.ShapeDtypeStruct((block_rows, columns), f32),
            jax.ShapeDtypeStruct((4 * own_rows, length), low),
            jax.ShapeDtypeStruct((4 * own_rows, normed.shape[1]), low),
            jax.ShapeDtypeStruct((heads, 1, SPAN), f32),
        ),
        in_specs=[pl.BlockSpec(memory_space=pltpu.SMEM), hbm] + [vmem] * 8 + [hbm],
        out_specs=(hbm, vmem, vmem, vmem),
        scratch_shapes=[
            pltpu.VMEM((length, HEAD_SIZE), f32),
            pltpu.VMEM((length, HEAD_SIZE), f32),
            pltpu.VMEM(normed.shape, low),
            pltpu.SemaphoreType.DMA,
            *scatter_scratch(4, block_rows, columns, low),
        ],
        compiler_params=pltpu.CompilerParams(
            collective_id=collective, has_side_effects=True, vmem_limit_bytes=60 * MIB
        ),
        name="attention_back",
    )(sinks, parts, queries, keys, keys_t, values, grads, log_sums, cosine, sine, normed)


PAIR = 2
STEP = 4


def routed(cols, capacity):
    expert = lax.axis_index("ctx")
    cols = cols.astype(jnp.float32)
    lane = lax.broadcasted_iota(jnp.int32, cols.shape, 1)
    place = jnp.sum(jnp.where(lane == 64 + expert, cols, 0.0), axis=1, keepdims=True)
    gate = jnp.sum(jnp.where(lane == 72 + expert, cols, 0.0), axis=1, keepdims=True)
    slot = lax.broadcasted_iota(jnp.int32, (cols.shape[0], PAIR * capacity), 1)
    picked = place.astype(jnp.int32) == slot
    return (
        jnp.where(picked, 1.0, 0.0).astype(jnp.bfloat16),
        jnp.where(picked, gate, 0.0).astype(jnp.bfloat16),
    )


class Stream:
    def __init__(self, arrays, sems, inward, first_sem=0):
        self.arrays, self.sems, self.inward, self.first_sem = arrays, sems, inward, first_sem

    def copies(self, slot, block):
        made = []
        for k, (array, slots, count, column) in enumerate(self.arrays):
            at = pl.ds(pl.multiple_of(block * count, 16), count)
            far = array.at[at] if column is None else array.at[at, column]
            pair = (far, slots.at[slot]) if self.inward else (slots.at[slot], far)
            made.append(pltpu.make_async_copy(*pair, self.sems.at[slot, self.first_sem + k]))
        return made

    def start(self, slot, block):
        for copy in self.copies(slot, block):
            copy.start()

    def wait(self, slot, block):
        for copy in self.copies(slot, block):
            copy.wait()


def two_of(shape, dtype):
    return pltpu.VMEM((2,) + shape, dtype)


def experts(sent, sent_grads, own_grads, gate_w, up_w, down_w, gate_b, up_b, down_b, capacity, collective):
    low, f32 = jnp.bfloat16, jnp.float32
    block_rows, wide = sent.shape
    share, width = gate_w.shape
    span = PAIR * block_rows
    pairs = STEP // PAIR
    count = PAIR * capacity
    tokens = 32 * block_rows
    slot_rows = 32 * capacity
    line = 4

    def kernel(
        sent_ref, sent_grads_ref, own_grads_ref, gate_hbm, up_hbm, down_hbm, gate_b_ref, up_b_ref, down_b_ref,
        all_ref, all_grads_ref, rows_out, gate_out, up_out, hidden_out, mix_out,
        grad_rows_out, gate_grad_out, up_grad_out, tokens_out, down_sum, gate_sum, up_sum,
        gate_v, up_v, down_v, x_s, rows_s, gate_s, up_s, hidden_s, mix_s, cols_s, gate_gs, up_gs,
        held_sems, in_sems, out_sems, *sems,
    ):
        held = [
            pltpu.make_async_copy(source, target, held_sems.at[k])
            for k, (source, target) in enumerate(
                ((gate_hbm, gate_v), (up_hbm, up_v), (down_hbm, down_v))
            )
        ]
        for copy in held:
            copy.start()
        forward_in = Stream([(all_ref, x_s, pairs * span, None)], in_sems, True)
        forward_out = Stream(
            [
                (rows_out, rows_s, pairs * count, None),
                (gate_out, gate_s, pairs * count, None),
                (up_out, up_s, pairs * count, None),
                (hidden_out, hidden_s, pairs * count, None),
                (mix_out, mix_s, pairs * span, None),
            ],
            out_sems,
            False,
        )
        kept = [
            (all_ref, cols_s, pairs * span, pl.ds(wide - 128, 128)),
            (gate_out, gate_s, pairs * count, None),
            (up_out, up_s, pairs * count, None),
        ]
        back_kept = Stream(kept, in_sems, True)
        back_own = Stream([(own_grads_ref, x_s, pairs * span, None)], in_sems, True, 3)
        back_far = Stream([(all_grads_ref, x_s, pairs * span, None)], in_sems, True, 3)
        back_out = Stream(
            [
                (grad_rows_out, rows_s, pairs * count, None),
                (gate_grad_out, gate_gs, pairs * count, None),
                (up_grad_out, up_gs, pairs * count, None),
                (tokens_out, mix_s, pairs * span, None),
            ],
            out_sems,
            False,
        )
        down_sum[...] = jnp.zeros_like(down_sum)
        gate_sum[...] = jnp.zeros_like(gate_sum)
        up_sum[...] = jnp.zeros_like(up_sum)
        for slot in range(2):
            mix_s[slot, :, width:] = jnp.zeros((pairs * span, wide - width), low)
        spans = [pl.ds(pair * span, span) for pair in range(pairs)]

        def forward(slot):
            picks = [routed(x_s[slot, at, wide - 128 :], capacity) for at in spans]
            rows = jnp.concatenate(
                [contract(picks[k][0], x_s[slot, spans[k], :], 0, 0) for k in range(pairs)],
                axis=0,
            ).astype(low)
            rows_s[slot] = rows
            rows = rows[:, :width]
            gate_lin = contract(rows, gate_v[...], 1, 1) + gate_b_ref[...]
            up_lin = contract(rows, up_v[...], 1, 1) + up_b_ref[...]
            gate_s[slot] = gate_lin
            up_s[slot] = up_lin
            hidden = glu_units(gate_lin, up_lin).astype(low)
            hidden_s[slot] = hidden
            out = contract(hidden, down_v[...], 1, 0) + down_b_ref[...]
            for k in range(pairs):
                part = out[k * count : (k + 1) * count].astype(low)
                mix_s[slot, spans[k], :width] = contract(picks[k][1], part, 1, 0).astype(low)

        def backward(slot):
            picks = [routed(cols_s[slot, at, :], capacity) for at in spans]
            rows = jnp.concatenate(
                [contract(picks[k][1], x_s[slot, spans[k], :], 0, 0) for k in range(pairs)],
                axis=0,
            ).astype(low)
            rows_s[slot] = rows
            rows = rows[:, :width]
            down_sum[...] += jnp.sum(rows.astype(f32), axis=0, keepdims=True)
            grad_units = contract(rows, down_v[...], 1, 1)
            gate_tanh = jnp.tanh(gate_s[slot] / CLAMP_LIMIT)
            up_tanh = jnp.tanh(up_s[slot] / CLAMP_LIMIT)
            gated = CLAMP_LIMIT * gate_tanh
            lifted = CLAMP_LIMIT * up_tanh + 1.0
            part = jax.nn.sigmoid(GLU_ALPHA * gated)
            grad_up = (grad_units * gated * part * (1.0 - up_tanh * up_tanh)).astype(low)
            slope = part * (1.0 + GLU_ALPHA * gated * (1.0 - part))
            grad_gate = (grad_units * lifted * slope * (1.0 - gate_tanh * gate_tanh)).astype(low)
            gate_gs[slot] = grad_gate
            up_gs[slot] = grad_up
            gate_sum[...] += jnp.sum(grad_gate.astype(f32), axis=0, keepdims=True)
            up_sum[...] += jnp.sum(grad_up.astype(f32), axis=0, keepdims=True)
            copies = contract(grad_gate, gate_v[...], 1, 0) + contract(grad_up, up_v[...], 1, 0)
            for k in range(pairs):
                part = copies[k * count : (k + 1) * count].astype(low)
                mix_s[slot, spans[k], :width] = contract(picks[k][0], part, 1, 0).astype(low)

        ahead = Gather(line, sent_ref, all_ref, sems[:5])
        back = Gather(line, sent_grads_ref, all_grads_ref, sems[5:])
        y_at = ahead.me // 4

        def block(step):
            half = lax.rem(step, 2)
            return ahead.slot(step // 2) * 2 + (1 - half) * y_at + half * (1 - y_at)

        ahead.begin()

        def forward_step(step, carry):
            order, half = step // 2, lax.rem(step, 2)

            @pl.when(half == 0)
            def _():
                ahead.second(order)
                pl.when(order + 1 < line)(lambda: ahead.first(order + 1))
                pl.when(order == 1)(back.begin_line)
                pl.when(order == line - 1)(lambda: back.first(1))
                ahead.near(order)

            pl.when(half == 1)(lambda: ahead.third(order))

            @pl.when(step == 0)
            def _():
                ahead.own_block()
                for copy in held:
                    copy.wait()

            forward_in.start(half, block(step))
            pl.when(step >= 2)(lambda: forward_out.wait(half, block(step - 2)))
            forward_in.wait(half, block(step))
            forward(half)
            forward_out.start(half, block(step))
            return carry

        steps = 2 * line
        lax.fori_loop(0, steps, forward_step, 0)
        forward_out.wait(0, block(steps - 2))
        forward_out.wait(1, block(steps - 1))

        def grads_in(step, act):
            order, half = step // 2, lax.rem(step, 2)
            act(back_kept, half, block(step))
            pl.when(order == 0)(
                lambda: act(back_own, half, (1 - half) * y_at + half * (1 - y_at))
            )
            pl.when(order > 0)(lambda: act(back_far, half, block(step)))

        def backward_step(step, carry):
            order, half = step // 2, lax.rem(step, 2)

            @pl.when(half == 0)
            def _():
                @pl.when(order > 0)
                def _():
                    back.near(order)
                    back.third(order)

                grads_in(step, Stream.start)

            @pl.when(half == 1)
            def _():
                pl.when(order + 1 < line)(lambda: back.second(order + 1))
                pl.when(order + 2 < line)(lambda: back.first(order + 2))

            pl.when(half == 0)(lambda: grads_in(step + 1, Stream.start))
            pl.when(step >= 2)(lambda: back_out.wait(half, block(step - 2)))
            grads_in(step, Stream.wait)
            backward(half)
            back_out.start(half, block(step))
            return carry

        lax.fori_loop(0, steps, backward_step, 0)
        back_out.wait(0, block(steps - 2))
        back_out.wait(1, block(steps - 1))
        ahead.end()
        back.end(1)

    hbm = pl.BlockSpec(memory_space=pl.ANY)
    vmem = pl.BlockSpec(memory_space=pltpu.VMEM)

    def made(rows, columns, dtype=low):
        return jax.ShapeDtypeStruct((rows, columns), dtype)

    return pl.pallas_call(
        kernel,
        out_shape=(
            made(tokens, wide),
            made(tokens, wide),
            made(slot_rows, wide),
            made(slot_rows, share, f32),
            made(slot_rows, share, f32),
            made(slot_rows, share),
            made(tokens, wide),
            made(slot_rows, wide),
            made(slot_rows, share),
            made(slot_rows, share),
            made(tokens, wide),
            made(1, width, f32),
            made(1, share, f32),
            made(1, share, f32),
        ),
        in_specs=[hbm] * 6 + [vmem] * 3,
        out_specs=(hbm,) * 11 + (vmem,) * 3,
        scratch_shapes=[
            pltpu.VMEM(gate_w.shape, low),
            pltpu.VMEM(up_w.shape, low),
            pltpu.VMEM(down_w.shape, low),
            two_of((pairs * span, wide), low),
            two_of((pairs * count, wide), low),
            two_of((pairs * count, share), f32),
            two_of((pairs * count, share), f32),
            two_of((pairs * count, share), low),
            two_of((pairs * span, wide), low),
            two_of((pairs * span, 128), low),
            two_of((pairs * count, share), low),
            two_of((pairs * count, share), low),
            pltpu.SemaphoreType.DMA((3,)),
            pltpu.SemaphoreType.DMA((2, 4)),
            pltpu.SemaphoreType.DMA((2, 5)),
            *gather_sems(line),
            *gather_sems(line),
        ],
        compiler_params=pltpu.CompilerParams(
            collective_id=collective, has_side_effects=True, vmem_limit_bytes=60 * MIB
        ),
        name="experts",
    )(sent, sent_grads, own_grads, gate_w, up_w, down_w, gate_b, up_b, down_b)


def expert_weights(parts, rows_in, gate_grad, up_grad, rows_grad, hidden, collective):
    low, f32 = jnp.bfloat16, jnp.float32
    slot_rows, wide = rows_in.shape
    share = gate_grad.shape[1]
    block_rows, width = parts.shape[0] // 32, parts.shape[1]
    cut = 256
    whole, rest = wide // cut, wide % cut
    count = whole + 1

    def kernel(
        parts_ref, rows_hbm, gate_hbm, up_hbm, grad_hbm, hidden_hbm, o_ref, gate_out, up_out, down_out,
        stage, first_t, second_t, in_s, first_s, second_s, held_sem, in_sems, out_sems, *scratch,
    ):
        def held(source):
            return pltpu.make_async_copy(source, stage, held_sem)

        held(gate_hbm).start()

        def begin(copy):
            copy.start()

        def await_it(copy):
            copy.wait()

        def by_width(index, act):
            pl.when((index >= 0) & (index < whole))(lambda: act(cut))
            pl.when(index == whole)(lambda: act(rest))

        def loads(chunk, act):
            slot = lax.rem(chunk, 2)
            for source, index in ((rows_hbm, chunk), (grad_hbm, chunk - count)):

                def one(columns):
                    at = pl.ds(pl.multiple_of(index * cut, cut), columns)
                    here = in_s.at[slot, :, pl.ds(0, columns)]
                    act(pltpu.make_async_copy(source.at[:, at], here, in_sems.at[slot]))

                by_width(index, one)

        def stores(chunk, act):
            slot = lax.rem(chunk, 2)
            for targets, index in (
                (((first_s, gate_out), (second_s, up_out)), chunk),
                (((first_s, down_out),), chunk - count),
            ):

                def one(columns):
                    at = pl.ds(pl.multiple_of(index * cut, cut), columns)
                    for k, (source, target) in enumerate(targets):
                        here = source.at[slot, :, pl.ds(0, columns)]
                        act(pltpu.make_async_copy(here, target.at[:, at], out_sems.at[slot, k]))

                by_width(index, one)

        def work(chunk):
            slot = lax.rem(chunk, 2)

            @pl.when(chunk == 0)
            def _():
                loads(0, begin)
                held(gate_hbm).wait()
                first_t[...] = stage[...].T
                held(up_hbm).start()
                held(up_hbm).wait()
                second_t[...] = stage[...].T
                held(hidden_hbm).start()

            @pl.when(chunk == count)
            def _():
                held(hidden_hbm).wait()
                first_t[...] = stage[...].T

            pl.when(chunk + 1 < 2 * count)(lambda: loads(chunk + 1, begin))
            pl.when(chunk >= 2)(lambda: stores(chunk - 2, await_it))
            loads(chunk, await_it)
            first_s[slot] = contract(first_t[...], in_s[slot], 1, 0).astype(low)

            @pl.when(chunk < count)
            def _():
                second_s[slot] = contract(second_t[...], in_s[slot], 1, 0).astype(low)

            stores(chunk, begin)

        def works(step):
            def body(chunk, carry):
                work(chunk)
                return carry

            lax.fori_loop(2 * step, 2 * step + 2, body, 0)

        Scatter(4, parts_ref, o_ref, scratch).run(works, count - 12)
        stores(2 * count - 2, await_it)
        stores(2 * count - 1, await_it)

    hbm = pl.BlockSpec(memory_space=pl.ANY)
    return pl.pallas_call(
        kernel,
        out_shape=(
            jax.ShapeDtypeStruct((block_rows, width), f32),
            jax.ShapeDtypeStruct((share, wide), low),
            jax.ShapeDtypeStruct((share, wide), low),
            jax.ShapeDtypeStruct((share, wide), low),
        ),
        in_specs=[hbm] * 6,
        out_specs=(hbm,) * 4,
        scratch_shapes=[
            pltpu.VMEM(gate_grad.shape, low),
            pltpu.VMEM(gate_grad.shape[::-1], low),
            pltpu.VMEM(gate_grad.shape[::-1], low),
            two_of((slot_rows, cut), low),
            two_of((share, cut), low),
            two_of((share, cut), low),
            pltpu.SemaphoreType.DMA,
            pltpu.SemaphoreType.DMA((2,)),
            pltpu.SemaphoreType.DMA((2, 2)),
            *scatter_scratch(4, block_rows, width, low),
        ],
        compiler_params=pltpu.CompilerParams(
            collective_id=collective, has_side_effects=True, vmem_limit_bytes=60 * MIB
        ),
        name="expert_weights",
    )(parts, rows_in, gate_grad, up_grad, rows_grad, hidden)


def product_kernel(left_ref, right_ref, out_ref):
    right = right_ref[:, : out_ref.shape[1]]
    out_ref[...] = contract(left_ref[...], right, 0, 0).astype(out_ref.dtype)


def product(left_t, right, name, columns=None):
    depth, rows = left_t.shape
    columns = columns or right.shape[1]
    return pl.pallas_call(
        product_kernel,
        grid=(rows // SPAN,),
        out_shape=jax.ShapeDtypeStruct((rows, columns), jnp.bfloat16),
        in_specs=[
            pl.BlockSpec((depth, SPAN), lambda i: (0, i)),
            pl.BlockSpec(right.shape, lambda i: (0, 0), pipeline_mode=pl.Buffered(1)),
        ],
        out_specs=pl.BlockSpec((SPAN, columns), lambda i: (i, 0)),
        compiler_params=pltpu.CompilerParams(vmem_limit_bytes=40 * MIB),
        cost_estimate=pl.CostEstimate(
            flops=2 * depth * rows * columns, bytes_accessed=4 * rows * columns, transcendentals=0
        ),
        name=name,
    )(left_t, right)


def input_back(grad_lin, weights, normed, width, collective, small):
    low, f32 = jnp.bfloat16, jnp.float32
    depth, length = grad_lin.shape
    block_rows = length // 8
    wide = normed.shape[1]
    columns = small.shape[1]
    gain_columns = -(-wide // (16 * 128)) * 128

    def kernel(
        lin_ref, weights_ref, normed_hbm, small_ref, o_ref, all_sums,
        normed_v, part, found_v, sums_v, sem, *scratch,
    ):
        gather = Gather(4, sums_v, all_sums, scratch[:5])
        scatter = Scatter(1, part, o_ref, scratch[5:])
        load = pltpu.make_async_copy(normed_hbm, normed_v, sem)
        load.start()
        greet((gather.mate, gather.near_x, gather.near_y), 4, gather.z_at)
        found_v[...] = jnp.zeros_like(found_v)
        load.wait()

        def make(chip):
            at = pl.ds(pl.multiple_of(chip * SPAN, SPAN), SPAN)
            value = contract(lin_ref[:, at], weights_ref[...], 0, 0)
            part[at, :] = value[:, :width].astype(low)
            found = value * normed_v[at, :].astype(f32)
            found_v[...] += jnp.sum(found, axis=0, keepdims=True)

        scatter.produce(make)
        sums_v[:, :columns] = small_ref[...]
        sums_v[:, columns:] = jnp.zeros((16, gain_columns), f32)
        for k in range(wide // 128):
            row, lane = k // (gain_columns // 128), k % (gain_columns // 128) * 128
            sums_v[row : row + 1, columns + lane : columns + lane + 128] = found_v[
                :, k * 128 : (k + 1) * 128
            ]
        gather.begin(True)
        scatter.first(0)
        for order in (1, 2, 3):
            gather.first(order)
        for order in range(4):
            gather.second(order)
        scatter.second(0)
        for order in range(4):
            gather.near(order)
            gather.third(order)
        scatter.third(0, scatter.total)
        scatter.end()
        gather.own_block()
        gather.end()

    hbm = pl.BlockSpec(memory_space=pl.ANY)
    vmem = pl.BlockSpec(memory_space=pltpu.VMEM)
    return pl.pallas_call(
        kernel,
        out_shape=(
            jax.ShapeDtypeStruct((block_rows, width), f32),
            jax.ShapeDtypeStruct((32 * 16, columns + gain_columns), f32),
        ),
        in_specs=[vmem, vmem, hbm, vmem],
        out_specs=(hbm,) * 2,
        scratch_shapes=[
            pltpu.VMEM((length, wide), low),
            pltpu.VMEM((length, width), low),
            pltpu.VMEM((1, wide), f32),
            pltpu.VMEM((16, columns + gain_columns), f32),
            pltpu.SemaphoreType.DMA,
            *gather_sems(4),
            *scatter_scratch(1, block_rows, width, low),
        ],
        compiler_params=pltpu.CompilerParams(
            collective_id=collective, has_side_effects=True, vmem_limit_bytes=58 * MIB
        ),
        name="input_back",
    )(grad_lin, weights, normed, small)


def shards(
    layer_input, cotangent, gate_weights, routes, w_query, key_projection, value_projection, w_out,
    b_query, key_bias_vector, value_bias_vector, b_out, learned_sink_logits, gain_attn, gain_ffn,
    w_gate, w_up, w_down, b_gate, b_up, b_down,
):
    low = jnp.bfloat16
    ctx_n, z_n = lax.axis_size("ctx"), lax.axis_size("fsdp")
    ctx_at, z_at = lax.axis_index("ctx"), lax.axis_index("fsdp")
    tuned = ctx_n == 8 and z_n == 4
    width = layer_input.shape[-1]
    rows = layer_input.shape[0] * layer_input.shape[1]
    length = rows * ctx_n
    blocks = ctx_n * z_n
    capacity = max(2, rows * TOP * 17 // (16 * ctx_n))
    heads = QUERY_HEADS // ctx_n
    spread = ctx_n // KEY_VALUE_HEADS
    f32 = jnp.float32

    def gather_plane(value, call):
        if tuned:
            return gather_blocks(value, 1, call, f"gather_plane_{call}")
        return lax.all_gather(value, "ctx", axis=0, tiled=True)

    def scatter_plane(value, call):
        if tuned:
            return scatter_blocks(value, 1, call, f"scatter_plane_{call}")
        return lax.psum_scatter(value, "ctx", scatter_dimension=0, tiled=True).astype(f32)

    residual = layer_input.reshape(rows, width).astype(f32)
    grad_final = cotangent.reshape(rows, width)
    gain_attn_f, gain_ffn_f = gain_attn.astype(f32), gain_ffn.astype(f32)
    cosine, sine = rotary_tables(length)

    q_cols, k_cols = w_query.shape[1], key_projection.shape[1]
    own_rows = q_cols + 2 * k_cols
    wide = -(-(width + 2 * ctx_n) // 128) * 128
    biases = jnp.concatenate([b_query, key_bias_vector, value_bias_vector])
    own_weights = jnp.concatenate([w_query, key_projection, value_projection], axis=1).T
    own_weights = jnp.concatenate(
        [own_weights, biases[:, None], jnp.zeros((own_rows, wide - width - 1), low)], axis=1
    )
    ones = jnp.concatenate(
        [jnp.ones((rows, 1), low), jnp.zeros((rows, wide - width - 1), low)], axis=1
    )

    token_routes = routes.reshape(rows, TOP)
    names = jnp.arange(ctx_n, dtype=jnp.int32)
    named = token_routes[:, :, None] == names[None, None, :]
    hits = jnp.sum(named.astype(f32), axis=1)
    gates = jnp.sum(
        jnp.where(named, gate_weights.reshape(rows, TOP)[:, :, None].astype(f32), 0.0), axis=1
    )
    earlier = (
        lax.broadcasted_iota(jnp.int32, (rows, rows), 0)
        > lax.broadcasted_iota(jnp.int32, (rows, rows), 1)
    ).astype(low)
    places = jnp.dot(earlier, hits.astype(low), preferred_element_type=f32)
    first_slot = (lax.rem(ctx_at, PAIR) * capacity).astype(f32) if tuned else 0.0
    places = jnp.where(hits > 0, places + first_slot, -1.0)
    slot_rows = blocks * capacity
    if not tuned:
        slots = jnp.arange(capacity, dtype=f32)[None, :, None]
        picked = places.T[:, None, :] == slots
        select = picked.astype(low)
        mixing = jnp.where(picked, gates.T[:, None, :], 0.0).astype(low)

    def exchanged(slot_values):
        moved = slot_values.reshape(ctx_n, capacity, width)
        return lax.all_to_all(moved, "ctx", split_axis=0, concat_axis=0, tiled=True)

    def to_slots(picks, token_rows):
        dims = (((2,), (0,)), ((), ()))
        moved = lax.dot_general(picks, token_rows, dims, preferred_element_type=f32).astype(low)
        moved = lax.all_gather(exchanged(moved), "fsdp", axis=0, tiled=True)
        return moved.reshape(slot_rows, width)

    def to_tokens(picks, slot_values):
        slot_values = exchanged(
            lax.psum_scatter(slot_values, "fsdp", scatter_dimension=0, tiled=True)
        )
        dims = (((1,), (1,)), ((0,), (0,)))
        moved = lax.dot_general(picks, slot_values, dims, preferred_element_type=f32)
        return jnp.sum(moved, axis=0)

    normed_own = jnp.concatenate([norm_scale(residual, gain_attn_f).astype(low), ones], axis=1)
    sinks = lax.dynamic_slice(learned_sink_logits.astype(f32), (ctx_at * heads,), (heads,))
    swap = [(i, i ^ 1) for i in range(ctx_n)]
    odd = lax.rem(ctx_at, 2) == 1
    if tuned:
        sent_grads = jnp.pad(grad_final, ((0, 0), (0, wide - width)))
        branch, normed_attn, own_grads, head_weights, out_weights, *kept = attention(
            normed_own, sent_grads, own_weights, w_out, sinks, cosine, sine, 1
        )
        queries, keys, keys_t, values, attended, log_sums = kept
    else:
        normed_attn = lax.all_gather(normed_own, "ctx", axis=0, tiled=True)
        head_weights = lax.all_gather(own_weights, "fsdp", axis=0, tiled=True)
        out_weights = lax.all_gather(w_out, "fsdp", axis=0, tiled=True)
        lin = contract(head_weights, normed_attn, 1, 1).reshape(z_n, own_rows, length)
        query_lin = lin[:, :q_cols].reshape(heads, HEAD_SIZE, length)
        kv_lin = jnp.stack([lin[:, q_cols : q_cols + k_cols], lin[:, q_cols + k_cols :]])
        kv_lin = kv_lin.reshape(2, z_n * k_cols, length)
        if spread == 2:
            other = lax.ppermute(kv_lin, "ctx", swap)
            kv_lin = jnp.where(
                odd,
                jnp.concatenate([other, kv_lin], axis=1),
                jnp.concatenate([kv_lin, other], axis=1),
            )
        queries = turned(query_lin, cosine, sine).astype(low).reshape(heads * HEAD_SIZE, length)
        keys_t = turned(kv_lin[:1], cosine, sine)[0].astype(low)
        values_t = kv_lin[1].astype(low)
        keys, values = keys_t.T, values_t.T
        attended, log_sums = attend(sinks, queries, keys, values_t)
        branch = scatter_plane(product(attended, out_weights, "branch"), 2)
    middle = residual + branch + b_out.astype(f32)
    normed_ffn = norm_scale(middle, gain_ffn_f).astype(low)

    gate_w, up_w, down_w = w_gate[0].T, w_up[0].T, w_down[0]
    share = b_down.shape[1]
    gate_b, up_b = b_gate.astype(f32), b_up.astype(f32)
    down_bias = lax.dynamic_update_slice(
        jnp.zeros((1, width), f32), b_down.astype(f32), (0, z_at * share)
    )
    if tuned:
        sent = jnp.concatenate(
            [
                normed_ffn,
                places.astype(low),
                gates.astype(low),
                jnp.zeros((rows, wide - width - 2 * ctx_n), low),
            ],
            axis=1,
        )
        made = experts(
            sent, sent_grads, own_grads, gate_w, up_w, down_w, gate_b, up_b, down_bias, capacity, 3
        )
        expert_in, hidden_units, mix_part = made[2], made[5], made[6]
        grad_expert_out, grad_gate_lin, grad_up_lin, grad_normed_part = made[7:11]
        grad_biases = made[11:]
        grad_b_down, grad_b_gate, grad_b_up = [value[0] for value in grad_biases]
        grad_normed_ffn, grad_w_gate, grad_w_up, grad_w_down = expert_weights(
            grad_normed_part, expert_in, grad_gate_lin, grad_up_lin, grad_expert_out, hidden_units, 6
        )
        grad_normed_ffn = grad_normed_ffn[:, :width]
    else:
        expert_in = to_slots(select, normed_ffn)
        gate_lin = contract(expert_in, gate_w, 1, 1) + gate_b
        up_lin = contract(expert_in, up_w, 1, 1) + up_b
        hidden_f, unit_back = jax.vjp(glu_units, gate_lin, up_lin)
        hidden_units = hidden_f.astype(low)
        expert_out = (contract(hidden_units, down_w, 1, 0) + down_bias).astype(low)
        expert_mix = to_tokens(mixing, expert_out)
        grad_expert_out = to_slots(mixing, grad_final)
        grad_units = contract(grad_expert_out, down_w, 1, 1)
        grad_gate_f, grad_up_f = unit_back(grad_units)
        grad_gate_lin, grad_up_lin = grad_gate_f.astype(low), grad_up_f.astype(low)
        grad_copy = contract(grad_gate_lin, gate_w, 1, 0) + contract(grad_up_lin, up_w, 1, 0)
        grad_normed_ffn = to_tokens(select, grad_copy.astype(low))
        grad_b_down = jnp.sum(grad_expert_out.astype(f32), axis=0)
        grad_b_gate = jnp.sum(grad_gate_lin.astype(f32), axis=0)
        grad_b_up = jnp.sum(grad_up_lin.astype(f32), axis=0)
        grad_w_gate = contract(grad_gate_lin, expert_in, 0, 0)
        grad_w_up = contract(grad_up_lin, expert_in, 0, 0)
        grad_w_down = contract(hidden_units, grad_expert_out, 0, 0)
    grad_b_down = lax.dynamic_slice(grad_b_down, (z_at * share,), (share,))

    unused, norm_back = jax.vjp(norm_scale, middle, gain_ffn_f)
    grad_middle_part, grad_gain_ffn = norm_back(grad_normed_ffn)
    grad_middle = grad_final.astype(f32) + grad_middle_part
    grad_branch_own = grad_middle.astype(low)
    grad_b_out = jnp.sum(grad_branch_own.astype(f32), axis=0)
    if tuned:
        early = 768
        first_mix, grad_attended, grad_out_part = branch_back(
            mix_part, early, grad_branch_own, out_weights, attended, 7
        )
        late_mix, grad_lin, grad_weights, grad_sink_parts = attention_back(
            mix_part, early, sinks, queries, keys, keys_t, values, grad_attended, log_sums, cosine,
            sine, normed_attn, own_rows, 5,
        )
        expert_mix = jnp.concatenate([first_mix, late_mix[:, : width - early]], axis=1)
    else:
        grad_branch = lax.all_gather(grad_branch_own, "ctx", axis=0, tiled=True)
        grad_attended = contract(out_weights, grad_branch, 1, 1).astype(low)
        grad_out_part = contract(attended, grad_branch, 1, 0).astype(low)
        grad_query, grad_keys, grad_values, grad_sink_parts = attend_back(
            sinks, queries, keys, keys_t, values, grad_attended, log_sums, cosine, sine
        )
        grad_kv = jnp.stack([turned(grad_keys.T[None], cosine, -sine)[0], grad_values.T])
        if spread == 2:
            grad_kv = grad_kv + lax.ppermute(grad_kv, "ctx", swap)
            halves = grad_kv.reshape(2, 2, HEAD_SIZE // 2, length)
            grad_kv = jnp.where(odd, halves[:, 1], halves[:, 0])
        grad_kv = grad_kv.astype(low).reshape(2, z_n, k_cols, length)
        grad_lin = jnp.concatenate(
            [grad_query.reshape(z_n, q_cols, length), grad_kv[0], grad_kv[1]], axis=1
        ).reshape(z_n * own_rows, length)
        grad_weights = contract(grad_lin, normed_attn, 1, 0).astype(low)
    final_out = (middle + expert_mix).astype(low).reshape(layer_input.shape)
    grad_w_out = lax.psum_scatter(grad_out_part, "fsdp", scatter_dimension=0, tiled=True).astype(f32)
    own_grads = lax.psum_scatter(grad_weights, "fsdp", scatter_dimension=0, tiled=True).astype(f32)
    grad_w_query = own_grads[:q_cols, :width].T
    grad_w_key = own_grads[q_cols : q_cols + k_cols, :width].T
    grad_w_value = own_grads[q_cols + k_cols :, :width].T
    own_bias_grads = own_grads[:, width]
    grad_sinks = lax.dynamic_update_slice(
        jnp.zeros((QUERY_HEADS,), f32), jnp.sum(grad_sink_parts, axis=(1, 2)), (ctx_at * heads,)
    )
    sums = (grad_b_out, grad_gain_ffn, grad_sinks)
    if tuned:
        joined = jnp.concatenate(sums)
        columns = -(-joined.shape[0] // (16 * 128)) * 128
        joined = jnp.pad(joined, (0, 16 * columns - joined.shape[0])).reshape(16, columns)
        grad_normed_attn, joined = input_back(
            grad_lin, head_weights, normed_attn, width, 8, joined
        )
        joined = jnp.sum(joined.reshape(blocks, 16, -1), axis=0)
        grad_gain_attn = joined[:, columns:].reshape(-1)[:width] / gain_attn_f
        joined = joined[:, :columns].reshape(-1)
        cuts = (width, 2 * width, 2 * width + QUERY_HEADS)
        sums = [joined[at - value.shape[0] : at] for at, value in zip(cuts, sums)]
    else:
        grad_normed_part = product(grad_lin, head_weights, "grad_normed", width)
        grad_normed_attn = scatter_plane(grad_normed_part, 8)
    unused, norm_back = jax.vjp(norm_scale, residual, gain_attn_f)
    grad_residual_part, own_gain = norm_back(grad_normed_attn)
    input_grad = (grad_middle + grad_residual_part).reshape(layer_input.shape)
    if not tuned:
        *sums, grad_gain_attn = lax.psum((*sums, own_gain), ("ctx", "fsdp"))
    grad_b_out, grad_gain_ffn, grad_sink_logits = sums
    return (
        final_out,
        input_grad,
        grad_w_query,
        grad_w_key,
        grad_w_value,
        grad_w_out,
        own_bias_grads[:q_cols],
        own_bias_grads[q_cols : q_cols + k_cols],
        own_bias_grads[q_cols + k_cols :],
        grad_b_out,
        grad_sink_logits,
        grad_gain_attn,
        grad_gain_ffn,
        grad_w_gate[:, :width].astype(f32).T[None],
        grad_w_up[:, :width].astype(f32).T[None],
        grad_w_down[:, :width].astype(f32)[None],
        grad_b_gate[None],
        grad_b_up[None],
        grad_b_down[None],
    )


def solution(mesh):
    return jax.shard_map(
        shards,
        mesh=mesh,
        in_specs=(
            P("fsdp", "ctx", None),
            P("fsdp", "ctx", None),
            P("fsdp", "ctx", None),
            P("fsdp", "ctx", None),
            P(None, ("ctx", "fsdp")),
            P(None, ("ctx", "fsdp")),
            P(None, ("ctx", "fsdp")),
            P(("ctx", "fsdp"), None),
            P(("ctx", "fsdp")),
            P(("ctx", "fsdp")),
            P(("ctx", "fsdp")),
            P(),
            P(),
            P(),
            P(),
            P("ctx", None, "fsdp"),
            P("ctx", None, "fsdp"),
            P("ctx", "fsdp", None),
            P("ctx", "fsdp"),
            P("ctx", "fsdp"),
            P("ctx", "fsdp"),
        ),
        out_specs=(
            P("fsdp", "ctx", None),
            P("fsdp", "ctx", None),
            P(None, ("ctx", "fsdp")),
            P(None, ("ctx", "fsdp")),
            P(None, ("ctx", "fsdp")),
            P(("ctx", "fsdp"), None),
            P(("ctx", "fsdp")),
            P(("ctx", "fsdp")),
            P(("ctx", "fsdp")),
            P(),
            P(),
            P(),
            P(),
            P("ctx", None, "fsdp"),
            P("ctx", None, "fsdp"),
            P("ctx", "fsdp", None),
            P("ctx", "fsdp"),
            P("ctx", "fsdp"),
            P("ctx", "fsdp"),
        ),
        check_vma=False,
    )
```

```python
import jax
import jax.numpy as jnp
from jax import lax
from jax.experimental import pallas as pl
from jax.experimental.pallas import tpu as pltpu
from jax.sharding import PartitionSpec as P

MESH = pl.DeviceIdType.MESH
MIB = 1 << 20


def remote(src, dst, send_sem, recv_sem, device):
    return pltpu.make_async_remote_copy(
        src_ref=src,
        dst_ref=dst,
        send_sem=send_sem,
        recv_sem=recv_sem,
        device_id=device,
        device_id_type=MESH,
    )


def neighbours():
    me = lax.axis_index("ctx")
    core = lax.rem(me, 2)
    x_at = lax.rem(me // 2, 2)
    y_at = me // 4
    return me, me + 1 - 2 * core, me + 2 - 4 * x_at, me + 4 - 8 * y_at, 2 - 4 * x_at


def greet(others, line, z_at):
    barrier = pltpu.get_barrier_semaphore()
    for other in others:
        pl.semaphore_signal(barrier, 1, device_id=(other, z_at), device_id_type=MESH)
    if line == 1:
        pl.semaphore_wait(barrier, len(others))
        return
    me = lax.axis_index("ctx")

    @pl.when(z_at > 0)
    def _():
        pl.semaphore_signal(barrier, 1, device_id=(me, z_at - 1), device_id_type=MESH)

    @pl.when(z_at < line - 1)
    def _():
        pl.semaphore_signal(barrier, 1, device_id=(me, z_at + 1), device_id_type=MESH)

    inner = (lax.rem(z_at, 3) + 1) // 2
    pl.semaphore_wait(barrier, len(others) + 1 + inner)


def gather_sems(line, tail=0):
    sems = [
        pltpu.SemaphoreType.DMA,
        pltpu.SemaphoreType.DMA((line, 2)),
        pltpu.SemaphoreType.DMA((line,)),
        pltpu.SemaphoreType.DMA((line, 9)),
        pltpu.SemaphoreType.DMA((line, 9)),
    ]
    if tail:
        sems += [
            pltpu.SemaphoreType.DMA((line, 2, 4)),
            pltpu.SemaphoreType.DMA((line, 4)),
            pltpu.SemaphoreType.DMA((line, 4)),
            pltpu.SemaphoreType.DMA((line, 4)),
        ]
    return sems


class Gather:
    def __init__(self, line, x_ref, o_ref, sems, tail=0, own_blocks=None):
        self.line, self.x_ref, self.o_ref, self.tail = line, x_ref, o_ref, tail
        self.own_sem, self.z_send, self.z_recv, self.p_send, self.p_recv = sems[:5]
        if tail:
            self.t_send, self.t_recv, self.q_send, self.q_recv = sems[5:]
        self.own_blocks = own_blocks
        self.z_at = lax.axis_index("fsdp")
        self.me, self.mate, self.near_x, self.near_y, step_x = neighbours()
        self.across = self.near_y + step_x
        self.places = (self.me, self.near_x, self.near_y, self.across)
        self.rows = x_ref.shape[0]
        self.half = self.rows // 2
        self.middle = (self.z_at == 1) | (self.z_at == 2)
        self.first_slot = self.z_at if line > 1 else 0

    def slot(self, order):
        z_at = self.z_at
        if self.line == 1:
            return 0
        second = z_at + 1 - 2 * lax.rem(z_at, 2)
        third = 2 - z_at // 2
        fourth = 3 - 3 * (z_at // 2)
        return jnp.where(
            order == 0, z_at, jnp.where(order == 1, second, jnp.where(order == 2, third, fourth))
        )

    def each(self, order, act):
        if not self.tail:
            act(True)
        elif isinstance(order, int):
            act(order == 0)
        else:
            pl.when(order == 0)(lambda: act(True))
            pl.when(order > 0)(lambda: act(False))

    def span(self, part, whole):
        count = self.rows if whole else self.rows - self.tail
        return ((0, count), (0, self.half), (self.half, count - self.half))[part]

    def there(self, slot, place, start, count):
        at = (slot * 8 + place) * self.rows + start
        return self.o_ref.at[pl.ds(pl.multiple_of(at, 8), count)]

    def z_copy(self, src_ref, slot, way, target):
        return remote(
            src_ref,
            self.there(slot, self.me, *self.span(0, False)),
            self.z_send.at[slot, way],
            self.z_recv.at[slot],
            (self.me, target),
        )

    def own_main(self):
        start, count = self.span(0, False)
        return self.x_ref.at[pl.ds(start, count)]

    def up(self):
        return self.z_copy(self.own_main(), self.z_at, 0, self.z_at + 1)

    def down(self):
        return self.z_copy(self.own_main(), self.z_at, 1, self.z_at - 1)

    def beyond(self, order):
        return jnp.where(order == 1, 3 - self.z_at, 3 * self.z_at - 3)

    def onward(self, order):
        slot = self.slot(order)
        main = self.there(slot, self.me, *self.span(0, False))
        return self.z_copy(main, slot, 0, self.beyond(order))

    def copy(self, order, place, kind, device, part, whole, src_ref=None):
        dst_ref = self.there(self.slot(order), place, *self.span(part, whole))
        return remote(
            dst_ref if src_ref is None else src_ref,
            dst_ref,
            self.p_send.at[order, kind],
            self.p_recv.at[order, kind],
            (device, self.z_at),
        )

    def out(self, order, whole, src_ref=None):
        return [
            self.copy(order, self.me, 0, self.near_x, 0, whole, src_ref),
            self.copy(order, self.me, 1, self.near_y, 0, whole, src_ref),
            self.copy(order, self.me, 2, self.mate, 0, whole, src_ref),
        ]

    def passed(self, order, whole, *which):
        places = (
            (self.near_x, 3, self.near_y, 1),
            (self.near_x, 5, self.mate, 0),
            (self.near_y, 4, self.near_x, 2),
            (self.near_y, 6, self.mate, 0),
            (self.across, 7, self.mate, 1),
            (self.across, 8, self.mate, 2),
        )
        return [self.copy(order, *places[k], whole) for k in which]

    def begin(self, met=False):
        line, z_at = self.line, self.z_at
        if not met:
            greet((self.mate, self.near_x, self.near_y), line, z_at)
        self.own_copy().start()
        if line > 1:
            self.begin_line()
        for copy in self.out(0, True, self.x_ref):
            copy.start()

    def begin_line(self):
        pl.when(self.z_at < self.line - 1)(lambda: self.up().start())
        pl.when(self.z_at > 0)(lambda: self.down().start())

    def own_copy(self):
        return pltpu.make_async_copy(
            self.x_ref, self.there(self.first_slot, self.me, 0, self.rows), self.own_sem
        )

    def own_block(self):
        self.own_copy().wait()

    def from_line(self, order):
        slot = self.slot(order)
        main = self.there(slot, self.me, *self.span(0, False))
        self.z_copy(main, slot, 0, self.z_at).wait_recv()

    def first(self, order):
        at_end = jnp.logical_not(self.middle)
        pl.when(at_end | (order == 1))(lambda: self.from_line(order))

        @pl.when(self.middle & (order == 1))
        def _():
            self.onward(1).start()
            self.from_line(2)
            self.onward(2).start()

        @pl.when(self.middle & (order == 2))
        def _():
            self.from_line(3)
            self.onward(3).start()

        for copy in self.out(order, False):
            copy.start()

    def second(self, order):
        def act(whole):
            to_y, mate_x, to_x, mate_y = self.passed(order, whole, 0, 1, 2, 3)
            self.copy(order, self.near_x, 0, self.near_x, 0, whole).wait_recv()
            to_y.start()
            mate_x.start()
            self.copy(order, self.near_y, 1, self.near_y, 0, whole).wait_recv()
            to_x.start()
            mate_y.start()

        self.each(order, act)

    def tail_copy(self, slot, k, way, target, own=False):
        start = self.rows - self.tail
        dst_ref = self.there(slot, self.places[k], start, self.tail)
        src_ref = dst_ref
        if own and self.own_blocks is not None:
            at = pl.multiple_of(self.places[k] * self.rows + start, 8)
            src_ref = self.own_blocks.at[pl.ds(at, self.tail)]
        return remote(
            src_ref,
            dst_ref,
            self.t_send.at[slot, way, k],
            self.t_recv.at[slot, k],
            (self.me, target),
        )

    def own_tails(self, act):
        z_at = self.z_at
        for k in range(4):
            pl.when(z_at < self.line - 1)(lambda: act(self.tail_copy(z_at, k, 0, z_at + 1, True)))
            pl.when(z_at > 0)(lambda: act(self.tail_copy(z_at, k, 1, z_at - 1, True)))

    def send_tails(self):
        self.own_tails(lambda copy: copy.start())

    def tails_on(self, order):
        return [self.tail_copy(self.slot(order), k, 0, self.beyond(order)) for k in range(4)]

    def tail_to_mate(self, order, k, place):
        ref = self.there(self.slot(order), place, self.rows - self.tail, self.tail)
        return remote(
            ref, ref, self.q_send.at[order, k], self.q_recv.at[order, k], (self.mate, self.z_at)
        )

    def tails(self, order):
        def arrive(one):
            for k in range(4):
                self.tail_copy(self.slot(one), k, 0, self.z_at).wait_recv()

        def on(one):
            for copy in self.tails_on(one):
                copy.start()

        pl.when(jnp.logical_not(self.middle) | (order == 1))(lambda: arrive(order))

        @pl.when(self.middle & (order == 1))
        def _():
            on(1)
            arrive(2)
            on(2)

        @pl.when(self.middle & (order == 2))
        def _():
            arrive(3)
            on(3)

        for k in range(4):
            self.tail_to_mate(order, k, self.places[k]).start()

    def mates_tails(self, order, *which):
        if self.tail:

            @pl.when(order > 0)
            def _():
                for k in which:
                    place = self.places[k] + self.mate - self.me
                    self.tail_to_mate(order, k, place).wait_recv()

    def near(self, order):
        step = self.mate - self.me

        def act(whole):
            self.copy(order, self.mate, 2, self.mate, 0, whole).wait_recv()
            self.copy(order, self.near_x + step, 5, self.mate, 0, whole).wait_recv()

        self.each(order, act)
        self.mates_tails(order, 0, 1)

    def third(self, order):
        step = self.mate - self.me

        def act(whole):
            top, low = self.passed(order, whole, 4, 5)
            self.copy(order, self.across, 3, self.near_y, 1, whole).wait_recv()
            top.start()
            self.copy(order, self.across, 4, self.near_x, 2, whole).wait_recv()
            low.start()
            self.copy(order, self.near_y + step, 6, self.mate, 0, whole).wait_recv()
            self.copy(order, self.across + step, 7, self.mate, 1, whole).wait_recv()
            self.copy(order, self.across + step, 8, self.mate, 2, whole).wait_recv()

        self.each(order, act)
        self.mates_tails(order, 2, 3)

    def end(self, from_order=0):
        line, z_at = self.line, self.z_at

        def sent(order, carry):
            def act(whole):
                for copy in self.out(order, whole) + self.passed(order, whole, 0, 1, 2, 3, 4, 5):
                    copy.wait_send()

            self.each(order, act)
            return carry

        lax.fori_loop(from_order, line, sent, 0)
        if line > 1:
            pl.when(z_at < line - 1)(lambda: self.up().wait_send())
            pl.when(z_at > 0)(lambda: self.down().wait_send())

            @pl.when(self.middle)
            def _():
                for order in range(1, line):
                    self.onward(order).wait_send()

        if self.tail:
            self.own_tails(lambda copy: copy.wait_send())
            for order in range(1, line):
                for k in range(4):
                    self.tail_to_mate(order, k, self.places[k]).wait_send()

            @pl.when(self.middle)
            def _():
                for order in range(1, line):
                    for copy in self.tails_on(order):
                        copy.wait_send()


def line_sems(line):
    return [
        pltpu.SemaphoreType.DMA,
        pltpu.SemaphoreType.DMA((line, 2)),
        pltpu.SemaphoreType.DMA((line,)),
    ]


class Line:
    def __init__(self, x_ref, o_ref, sems):
        self.x_ref, self.o_ref = x_ref, o_ref
        self.own_sem, self.sends, self.receives = sems
        self.me, self.z_at = lax.axis_index("ctx"), lax.axis_index("fsdp")
        self.middle = (self.z_at == 1) | (self.z_at == 2)
        self.slots = (
            self.z_at,
            self.z_at + 1 - 2 * lax.rem(self.z_at, 2),
            2 - self.z_at // 2,
            3 - 3 * (self.z_at // 2),
        )

    def there(self, slot):
        rows = self.x_ref.shape[0]
        return self.o_ref.at[pl.ds(pl.multiple_of(slot * rows, 16), rows)]

    def copy(self, src_ref, slot, way, target):
        return remote(
            src_ref,
            self.there(slot),
            self.sends.at[slot, way],
            self.receives.at[slot],
            (self.me, target),
        )

    def own(self):
        return pltpu.make_async_copy(self.x_ref, self.there(self.z_at), self.own_sem)

    def up(self):
        return self.copy(self.x_ref, self.z_at, 0, self.z_at + 1)

    def down(self):
        return self.copy(self.x_ref, self.z_at, 1, self.z_at - 1)

    def onward(self, order):
        slot = self.slots[order]
        target = 3 - self.z_at if order == 1 else 3 * self.z_at - 3
        return self.copy(self.there(slot), slot, 0, target)

    def begin(self):
        pl.when(self.z_at < 3)(lambda: self.up().start())
        pl.when(self.z_at > 0)(lambda: self.down().start())
        self.own().start()

    def arrive(self, order):
        slot = self.slots[order]
        self.copy(self.there(slot), slot, 0, self.z_at).wait_recv()

    def pass_on(self, *orders):
        @pl.when(self.middle)
        def _():
            for order in orders:
                self.arrive(order)
                self.onward(order).start()

    def rest(self):
        @pl.when(jnp.logical_not(self.middle))
        def _():
            for order in (1, 2, 3):
                self.arrive(order)

    def end(self):
        self.own().wait()
        pl.when(self.z_at < 3)(lambda: self.up().wait_send())
        pl.when(self.z_at > 0)(lambda: self.down().wait_send())

        @pl.when(self.middle)
        def _():
            for order in (1, 2, 3):
                self.onward(order).wait_send()


def gather_blocks(x, line, collective, name):
    rows, width = x.shape

    def kernel(x_ref, o_ref, *sems):
        gather = Gather(line, x_ref, o_ref, sems)
        gather.begin()

        def body(order, carry):
            gather.second(order)
            if line > 1:
                pl.when(order + 1 < line)(lambda: gather.first(order + 1))
            gather.near(order)
            gather.third(order)
            return carry

        lax.fori_loop(0, line, body, 0)
        gather.own_block()
        gather.end()

    return pl.pallas_call(
        kernel,
        out_shape=jax.ShapeDtypeStruct((line * 8 * rows, width), x.dtype),
        in_specs=[pl.BlockSpec(memory_space=pl.ANY)],
        out_specs=pl.BlockSpec(memory_space=pl.ANY),
        scratch_shapes=gather_sems(line),
        compiler_params=pltpu.CompilerParams(collective_id=collective, has_side_effects=True),
        name=name,
    )(x)


CHUNK = 16


def add_rows(dst_ref, src_refs, start, count, out_ref=None):
    def body(i, carry):
        at = pl.ds(pl.multiple_of(start + i * CHUNK, CHUNK), CHUNK)
        value = dst_ref[at, :].astype(jnp.float32)
        for src_ref in src_refs:
            value = value + src_ref[at, :].astype(jnp.float32)
        to_ref = dst_ref if out_ref is None else out_ref
        to_ref[at, :] = value.astype(to_ref.dtype)
        return carry

    lax.fori_loop(0, count // CHUNK, body, 0)


class Scatter:
    def __init__(self, line, x_ref, o_ref, scratch, columns=None):
        self.columns = columns
        (
            self.mine, self.theirs, self.halves, self.from_x, self.from_y, self.from_z, self.total,
            self.load_sem, self.m_send, self.m_recv, self.p_send, self.p_recv, self.z_send,
            self.z_recv, self.out_sem, *rest,
        ) = scratch
        self.tail = 0
        if rest:
            self.from_t, self.t_send, self.t_recv = rest
            self.tail = self.from_t.shape[2]
        self.line, self.x_ref, self.o_ref = line, x_ref, o_ref
        self.z_at = lax.axis_index("fsdp")
        self.me, self.mate, self.near_x, self.near_y, step_x = neighbours()
        self.places = (self.near_y + step_x, self.near_x, self.near_y, self.me)
        self.rows = self.total.shape[0]
        self.half = self.rows // 2
        self.main = self.rows - self.tail
        self.middle = (self.z_at == 1) | (self.z_at == 2)

    def slot(self, order):
        z_at = self.z_at
        if self.line == 1:
            return 0
        far, next_far, near = 3 - 3 * (z_at // 2), 2 - z_at // 2, z_at + 1 - 2 * lax.rem(z_at, 2)
        return jnp.where(
            order == 0, far, jnp.where(order == 1, next_far, jnp.where(order == 2, near, z_at))
        )

    def each(self, order, act):
        if not self.tail:
            act(self.rows)
        elif isinstance(order, int):
            act(self.rows if order == self.line - 1 else self.main)
        else:
            pl.when(order == self.line - 1)(lambda: act(self.rows))
            pl.when(order < self.line - 1)(lambda: act(self.main))

    def there(self, slot, place):
        at = pl.ds(pl.multiple_of((slot * 8 + place) * self.rows, 16), self.rows)
        return self.x_ref.at[at] if self.columns is None else self.x_ref.at[at, self.columns]

    def give(self, order, k):
        return remote(
            self.there(self.slot(order), self.places[k] + self.mate - self.me),
            self.theirs.at[order, k],
            self.m_send.at[order, k],
            self.m_recv.at[order, k],
            (self.mate, self.z_at),
        )

    def load(self, order, k):
        return pltpu.make_async_copy(
            self.there(self.slot(order), self.places[k]),
            self.mine.at[order, k],
            self.load_sem.at[order, k],
        )

    def send(self, order, kind, count):
        top, low = pl.ds(0, self.half), pl.ds(self.half, count - self.half)
        k, part, to, device = (
            (0, top, self.halves, self.near_x),
            (0, low, self.halves, self.near_y),
            (1, top, self.from_x, self.near_x),
            (1, low, self.from_x, self.near_x),
            (2, low, self.from_y, self.near_y),
            (2, top, self.from_y, self.near_y),
        )[kind]
        return remote(
            self.mine.at[order, k, part],
            to.at[order, part],
            self.p_send.at[order, kind],
            self.p_recv.at[order, kind],
            (device, self.z_at),
        )

    def begin(self, met=False):
        if not met:
            greet((self.mate, self.near_x, self.near_y), self.line, self.z_at)

        def body(order, carry):
            for k in range(4):
                self.start_part(order, k)
            return carry

        lax.fori_loop(0, self.line, body, 0)

    def start_part(self, order, k):
        self.give(order, k).start()
        self.load(order, k).start()

    def produce(self, make):
        for k in range(4):
            make(self.places[k] // 2)
            self.start_part(0, k)

    def tail_copy(self, order, k, index, target):
        return remote(
            self.mine.at[order, k, pl.ds(self.main, self.tail)],
            self.from_t.at[index, k],
            self.t_send.at[order, k],
            self.t_recv.at[index, k],
            (self.me, target),
        )

    def toward(self, order):
        return jnp.where(order == 2, self.slot(order), self.z_at + 1 - 2 * (self.z_at // 2))

    def tails_out(self, order):
        slot, target = self.slot(order), self.toward(order)
        above = jnp.where((target == slot) & (self.z_at > target), 1, 0)
        index = above * 4 + (1 - above) * slot
        return [self.tail_copy(order, k, index, target) for k in range(4)]

    def tails_on(self, order):
        slot = self.slot(order)
        copies = self.tails_out(order)
        for k in range(4):
            self.tail_copy(order, k, slot, self.z_at).wait_recv()
            add_rows(self.mine.at[order, k, pl.ds(self.main, self.tail)], [self.from_t.at[slot, k]], 0, self.tail)
            copies[k].start()

    def tails_in(self, order, k):
        z_at = self.z_at
        mine = self.mine.at[order, k, pl.ds(self.main, self.tail)]

        @pl.when(z_at > 0)
        def _():
            self.tail_copy(order, k, z_at, z_at).wait_recv()
            add_rows(mine, [self.from_t.at[z_at, k]], 0, self.tail)

        @pl.when(z_at < self.line - 1)
        def _():
            self.tail_copy(order, k, 4, z_at).wait_recv()
            add_rows(mine, [self.from_t.at[4, k]], 0, self.tail)

    def first(self, order):
        for k in range(4):
            self.give(order, k).wait_recv()
            self.load(order, k).wait()
            add_rows(self.mine.at[order, k], [self.theirs.at[order, k]], 0, self.rows)
            if self.tail:
                pl.when(order == self.line - 1)(lambda: self.tails_in(order, k))

            def act(count):
                for kind in ((0, 1), (2,), (4,), ())[k]:
                    self.send(order, kind, count).start()

            self.each(order, act)
        if self.tail:

            @pl.when((order < self.line - 1) & jnp.logical_not(self.middle))
            def _():
                for copy in self.tails_out(order):
                    copy.start()

    def second(self, order):
        def act(count):
            self.send(order, 1, count).wait_recv()
            low = count - self.half
            add_rows(self.mine.at[order, 1], [self.halves.at[order]], self.half, low)
            self.send(order, 3, count).start()
            self.send(order, 0, count).wait_recv()
            add_rows(self.mine.at[order, 2], [self.halves.at[order]], 0, self.half)
            self.send(order, 5, count).start()

        self.each(order, act)

    def third(self, order, out_ref=None):
        sources = [self.from_x.at[order], self.from_y.at[order]]

        def act(count):
            for kind in (2, 3, 4, 5):
                self.send(order, kind, count).wait_recv()
            add_rows(self.mine.at[order, 3], sources, 0, count, out_ref)

        self.each(order, act)

    def z_copy(self, order, slot_at, target):
        at = pl.ds(0, self.main)
        return remote(
            self.mine.at[order, 3, at],
            self.from_z.at[slot_at, at],
            self.z_send.at[order],
            self.z_recv.at[slot_at],
            (self.me, target),
        )

    def z_out(self, order):
        z_at, slot, target = self.z_at, self.slot(order), self.toward(order)
        ends = jnp.where(target == slot, 1, 0)
        return self.z_copy(order, ends * (4 + (z_at - target + 1) // 2) + (1 - ends) * slot, target)

    def pass_on(self, order):
        slot = self.slot(order)
        self.z_copy(order, slot, self.z_at).wait_recv()
        add_rows(self.mine.at[order, 3], [self.from_z.at[slot]], 0, self.main)
        self.z_out(order).start()

    def along(self, order):
        @pl.when((order < self.line - 1) & jnp.logical_not(self.middle))
        def _():
            self.z_out(order).start()

        if self.tail:
            pl.when((order == 0) & self.middle)(lambda: self.tails_on(0))

            @pl.when((order == 1) & self.middle)
            def _():
                self.tails_on(1)
                self.tails_on(2)

        pl.when((order == 1) & self.middle)(lambda: self.pass_on(0))

        @pl.when((order == 2) & self.middle)
        def _():
            self.pass_on(1)
            self.pass_on(2)

    def last(self):
        z_at, line = self.z_at, self.line
        pl.when(z_at > 0)(lambda: self.z_copy(line - 1, 4, z_at).wait_recv())
        pl.when(z_at < line - 1)(lambda: self.z_copy(line - 1, 5, z_at).wait_recv())
        mine = self.mine.at[line - 1, 3]
        below, above = self.from_z.at[4], self.from_z.at[5]
        pl.when(z_at == 0)(lambda: add_rows(mine, [above], 0, self.main, self.total))
        pl.when(z_at == line - 1)(lambda: add_rows(mine, [below], 0, self.main, self.total))
        pl.when(self.middle)(lambda: add_rows(mine, [below, above], 0, self.main, self.total))
        if self.tail:
            add_rows(mine, [], self.main, self.tail, self.total)

    def end(self):
        out = pltpu.make_async_copy(self.total, self.o_ref, self.out_sem)
        out.start()

        def sent(order, carry):
            def act(count):
                for kind in range(6):
                    self.send(order, kind, count).wait_send()

            for k in range(4):
                self.give(order, k).wait_send()
            self.each(order, act)
            if self.line > 1:

                @pl.when(order < self.line - 1)
                def _():
                    self.z_out(order).wait_send()
                    if self.tail:
                        for copy in self.tails_out(order):
                            copy.wait_send()

            return carry

        lax.fori_loop(0, self.line, sent, 0)
        out.wait()

    def plane_sum(self):
        self.first(0)
        self.second(0)
        self.third(0, self.total)
        self.end()

    def run(self, work=None, extra=0, met=False, begun=False):
        if not begun:
            self.begin(met)
        if self.line == 1:
            self.plane_sum()
            return
        if not begun:
            self.first(0)

        def body(step, carry):
            order, phase = step // 3, lax.rem(step, 3)

            @pl.when((phase == 0) & (order < self.line))
            def _():
                self.second(order)
                pl.when(order + 1 < self.line)(lambda: self.first(order + 1))

            pl.when((phase == 1) & (order < self.line))(lambda: self.third(order))
            pl.when((phase == 2) & (order < self.line))(lambda: self.along(order))
            if work is not None:
                work(step)
            return carry

        lax.fori_loop(0, 3 * self.line + extra, body, 0)
        self.last()
        self.end()


TAIL = 16


def scatter_scratch(line, rows, width, dtype, tail=TAIL):
    shard = (rows, width)
    made = [
        pltpu.VMEM((line, 4) + shard, dtype),
        pltpu.VMEM((line, 4) + shard, dtype),
        pltpu.VMEM((line,) + shard, dtype),
        pltpu.VMEM((line,) + shard, dtype),
        pltpu.VMEM((line,) + shard, dtype),
        pltpu.VMEM((6 if line > 1 else 1,) + shard, dtype),
        pltpu.VMEM(shard, jnp.float32),
        pltpu.SemaphoreType.DMA((line, 4)),
        pltpu.SemaphoreType.DMA((line, 4)),
        pltpu.SemaphoreType.DMA((line, 4)),
        pltpu.SemaphoreType.DMA((line, 6)),
        pltpu.SemaphoreType.DMA((line, 6)),
        pltpu.SemaphoreType.DMA((line,)),
        pltpu.SemaphoreType.DMA((6,)),
        pltpu.SemaphoreType.DMA,
    ]
    if line > 1 and tail:
        made += [
            pltpu.VMEM((5, 4, tail, width), dtype),
            pltpu.SemaphoreType.DMA((line, 4)),
            pltpu.SemaphoreType.DMA((5, 4)),
        ]
    return made


def scatter_blocks(x, line, collective, name):
    rows, width = x.shape[0] // (line * 8), x.shape[1]

    def kernel(x_ref, o_ref, *scratch):
        Scatter(line, x_ref, o_ref, scratch).run()

    return pl.pallas_call(
        kernel,
        out_shape=jax.ShapeDtypeStruct((rows, width), jnp.float32),
        in_specs=[pl.BlockSpec(memory_space=pl.ANY)],
        out_specs=pl.BlockSpec(memory_space=pl.ANY),
        scratch_shapes=scatter_scratch(line, rows, width, x.dtype),
        compiler_params=pltpu.CompilerParams(
            collective_id=collective, has_side_effects=True, vmem_limit_bytes=52 * MIB
        ),
        name=name,
    )(x)


QUERY_HEADS = 64
KEY_VALUE_HEADS = 8
HEAD_SIZE = 64
TOP = 4
EPSILON = 1e-05
THETA_BASE = 150000.0
CLAMP_LIMIT = 7.0
GLU_ALPHA = 1.702
MASK_FILL = -1e30
SPAN = 256
SCALE = HEAD_SIZE**-0.5


def contract(left, right, left_axis, right_axis):
    return lax.dot_general(
        left, right, (((left_axis,), (right_axis,)), ((), ())), preferred_element_type=jnp.float32
    )


def norm_scale(value_rows, gain_vec):
    return (
        value_rows
        * lax.rsqrt(jnp.mean(value_rows * value_rows, axis=-1, keepdims=True) + EPSILON)
        * gain_vec
    )


def soft_clamp(value_rows):
    return CLAMP_LIMIT * jnp.tanh(value_rows / CLAMP_LIMIT)


def glu_units(gate_lin, up_lin):
    gated = soft_clamp(gate_lin)
    return (soft_clamp(up_lin) + 1.0) * gated * jax.nn.sigmoid(GLU_ALPHA * gated)


def rotary_tables(length):
    half = HEAD_SIZE // 2
    inverse = THETA_BASE ** (-jnp.arange(half, dtype=jnp.float32) / half)
    angles = inverse[:, None] * jnp.arange(length, dtype=jnp.int32).astype(jnp.float32)[None, :]
    return jnp.cos(angles), jnp.sin(angles)


def turned(value, cosine, sine):
    half = HEAD_SIZE // 2
    first, second = value[:, :half], value[:, half:]
    return jnp.concatenate(
        [first * cosine - second * sine, second * cosine + first * sine], axis=1
    )


def diagonal(length):
    return lax.broadcasted_iota(jnp.int32, (length, length), 0) <= lax.broadcasted_iota(
        jnp.int32, (length, length), 1
    )


def masked_scores(key_rows, query_cols, count):
    scores = contract(key_rows, query_cols, 1, 0)
    edge = jnp.where(diagonal(SPAN), scores[count - SPAN :], MASK_FILL)
    if count == SPAN:
        return edge
    return jnp.concatenate([scores[: count - SPAN], edge], axis=0)


def attend_kernel(sink_ref, q_ref, k_ref, v_ref, out_ref, log_ref):
    sink = sink_ref[pl.program_id(0)]
    length = q_ref.shape[1]
    for start in range(0, length, SPAN):
        count = start + SPAN
        at = pl.ds(start, SPAN)
        query = q_ref[:, at] * jnp.bfloat16(SCALE)
        scores = masked_scores(k_ref[:count, :], query, count)
        row_top = jnp.maximum(jnp.max(scores, axis=0, keepdims=True), sink)
        weights = jnp.exp(scores - row_top)
        denominator = jnp.sum(weights, axis=0, keepdims=True) + jnp.exp(sink - row_top)
        probabilities = (weights / denominator).astype(jnp.bfloat16)
        out_ref[:, at] = contract(v_ref[:, :count], probabilities, 1, 0).astype(jnp.bfloat16)
        log_ref[0, :, at] = row_top + jnp.log(denominator)


def attend(sinks, queries, keys, values):
    heads, length = queries.shape[0] // HEAD_SIZE, queries.shape[1]
    per_head = pl.BlockSpec((HEAD_SIZE, length), lambda h: (h, 0))
    return pl.pallas_call(
        attend_kernel,
        grid=(heads,),
        out_shape=(
            jax.ShapeDtypeStruct(queries.shape, jnp.bfloat16),
            jax.ShapeDtypeStruct((heads, 1, length), jnp.float32),
        ),
        in_specs=[
            pl.BlockSpec(memory_space=pltpu.SMEM),
            per_head,
            pl.BlockSpec((length, HEAD_SIZE), lambda h: (0, 0)),
            pl.BlockSpec((HEAD_SIZE, length), lambda h: (0, 0)),
        ],
        out_specs=(per_head, pl.BlockSpec((1, 1, length), lambda h: (h, 0, 0))),
        compiler_params=pltpu.CompilerParams(vmem_limit_bytes=40 * MIB),
        cost_estimate=pl.CostEstimate(
            flops=heads * length * length * HEAD_SIZE * 4,
            bytes_accessed=heads * length * HEAD_SIZE * 4,
            transcendentals=heads * length * length,
        ),
        name="attend",
    )(sinks, queries, keys, values)


def attention(rows_own, grads_own, weights_own, out_own, sinks, cosine, sine, collective):
    low, f32 = jnp.bfloat16, jnp.float32
    block_rows, wide = rows_own.shape
    length = 8 * block_rows
    own_rows = weights_own.shape[0]
    q_rows, width = out_own.shape
    kv_rows = (own_rows - q_rows) // 2
    heads = 4 * q_rows // HEAD_SIZE
    half = HEAD_SIZE // 2
    per_shard = q_rows // HEAD_SIZE

    def kernel(
        sink_ref, rows_ref, grads_ref, weights_ref, out_ref, cos_ref, sin_ref,
        o_ref, all_rows, all_grads, all_weights, all_out, q_ref, k_ref, kt_ref, v_ref, att_ref, log_ref,
        normed_v, weights_v, lin, vt_v, out_v, branch, held_sems, *scratch,
    ):
        plane = Gather(1, rows_ref, all_rows, scratch[:5])
        later = Gather(1, grads_ref, all_grads, scratch[5:10])
        heads_line = Line(weights_ref, all_weights, scratch[10:13])
        line = Line(out_ref, all_out, scratch[13:16])
        scatter = Scatter(1, branch, o_ref, scratch[16:])
        load_rows = pltpu.make_async_copy(all_rows, normed_v, held_sems.at[0])
        load_weights = pltpu.make_async_copy(all_weights, weights_v, held_sems.at[1])
        greet((plane.mate, plane.near_x, plane.near_y), 4, line.z_at)
        heads_line.begin()
        plane.begin(True)
        heads_line.pass_on(1, 2)
        plane.second(0)
        later.begin(True)
        line.begin()
        plane.near(0)
        plane.third(0)
        plane.own_block()
        load_rows.start()
        heads_line.pass_on(3)
        later.second(0)
        later.near(0)
        later.third(0)
        later.own_block()
        heads_line.rest()
        heads_line.end()
        load_weights.start()
        load_rows.wait()
        load_weights.wait()

        def project(i, carry):
            at = pl.ds(pl.multiple_of(i * SPAN, SPAN), SPAN)
            lin[:, at] = contract(weights_v[...], normed_v[at, :], 1, 1)
            return carry

        lax.fori_loop(0, length // SPAN, project, 0)
        line.pass_on(1, 2)

        def turn(value):
            first, second = value[:half], value[half:]
            cosine, sine = cos_ref[...], sin_ref[...]
            return jnp.concatenate(
                [first * cosine - second * sine, second * cosine + first * sine], axis=0
            ).astype(low)

        def shards_of(offset):
            return jnp.concatenate(
                [
                    lin[z * own_rows + offset : z * own_rows + offset + kv_rows, :]
                    for z in range(4)
                ],
                axis=0,
            )

        keys_t = turn(shards_of(q_rows))
        values_t = shards_of(q_rows + kv_rows).astype(low)
        kt_ref[...] = keys_t
        vt_v[...] = values_t
        k_ref[...] = keys_t.T
        v_ref[...] = values_t.T

        def head(h, carry):
            pl.when(h == heads // 2)(lambda: line.pass_on(3))
            start = (h // per_shard) * own_rows + lax.rem(h, per_shard) * HEAD_SIZE
            queries = turn(lin[pl.ds(pl.multiple_of(start, 16), HEAD_SIZE), :])
            rows = pl.ds(pl.multiple_of(h * HEAD_SIZE, HEAD_SIZE), HEAD_SIZE)
            q_ref[rows, :] = queries
            sink = sink_ref[h]
            for begin in range(0, length, SPAN):
                count = begin + SPAN
                query = queries[:, begin:count] * jnp.bfloat16(SCALE)
                scores = masked_scores(k_ref[:count, :], query, count)
                row_top = jnp.maximum(jnp.max(scores, axis=0, keepdims=True), sink)
                chances = jnp.exp(scores - row_top)
                denominator = jnp.sum(chances, axis=0, keepdims=True) + jnp.exp(sink - row_top)
                chances = (chances / denominator).astype(low)
                att_ref[rows, begin:count] = contract(vt_v[:, :count], chances, 1, 0).astype(low)
                log_ref[h, :, begin:count] = row_top + jnp.log(denominator)
            return carry

        lax.fori_loop(0, heads, head, 0)
        line.rest()
        line.end()
        load = pltpu.make_async_copy(all_out, out_v, held_sems.at[0])
        load.start()
        load.wait()

        def give_back(chip):
            at = pl.ds(pl.multiple_of(chip * SPAN, SPAN), SPAN)
            branch[at, :] = contract(att_ref[:, at], out_v[...], 0, 0).astype(low)

        scatter.produce(give_back)
        scatter.plane_sum()
        plane.end()
        later.end()

    hbm = pl.BlockSpec(memory_space=pl.ANY)
    vmem = pl.BlockSpec(memory_space=pltpu.VMEM)
    return pl.pallas_call(
        kernel,
        out_shape=(
            jax.ShapeDtypeStruct((block_rows, width), f32),
            jax.ShapeDtypeStruct((length, wide), low),
            jax.ShapeDtypeStruct((length, wide), low),
            jax.ShapeDtypeStruct((4 * own_rows, wide), low),
            jax.ShapeDtypeStruct((4 * q_rows, width), low),
            jax.ShapeDtypeStruct((4 * q_rows, length), low),
            jax.ShapeDtypeStruct((length, HEAD_SIZE), low),
            jax.ShapeDtypeStruct((HEAD_SIZE, length), low),
            jax.ShapeDtypeStruct((length, HEAD_SIZE), low),
            jax.ShapeDtypeStruct((4 * q_rows, length), low),
            jax.ShapeDtypeStruct((heads, 1, length), f32),
        ),
        in_specs=[pl.BlockSpec(memory_space=pltpu.SMEM), hbm, hbm, hbm, hbm, vmem, vmem],
        out_specs=(hbm,) * 5 + (vmem,) * 6,
        scratch_shapes=[
            pltpu.VMEM((length, wide), low),
            pltpu.VMEM((4 * own_rows, wide), low),
            pltpu.VMEM((4 * own_rows, length), f32),
            pltpu.VMEM((HEAD_SIZE, length), low),
            pltpu.VMEM((4 * q_rows, width), low),
            pltpu.VMEM((length, width), low),
            pltpu.SemaphoreType.DMA((2,)),
            *gather_sems(1),
            *gather_sems(1),
            *line_sems(4),
            *line_sems(4),
            *scatter_scratch(1, block_rows, width, low),
        ],
        compiler_params=pltpu.CompilerParams(
            collective_id=collective, has_side_effects=True, vmem_limit_bytes=58 * MIB
        ),
        name="attention",
    )(sinks, rows_own, grads_own, weights_own, out_own, cosine, sine)


def attend_back_kernel(
    sink_ref, q_ref, k_ref, kt_ref, v_ref, grad_ref, log_ref, cos_ref, sin_ref,
    dq_ref, dk_ref, dv_ref, dsink_ref,
):
    head = pl.program_id(0)
    sink = sink_ref[head]
    length = q_ref.shape[1]
    half = HEAD_SIZE // 2

    @pl.when(head == 0)
    def _():
        dk_ref[...] = jnp.zeros_like(dk_ref)
        dv_ref[...] = jnp.zeros_like(dv_ref)

    grad_sink = jnp.zeros((1, SPAN), jnp.float32)
    for start in range(0, length, SPAN):
        count = start + SPAN
        at = pl.ds(start, SPAN)
        query = q_ref[:, at] * jnp.bfloat16(SCALE)
        grad = grad_ref[:, at]
        log_sum = log_ref[0, :, at]
        probabilities = jnp.exp(masked_scores(k_ref[:count, :], query, count) - log_sum)
        grad_probs = contract(v_ref[:count, :], grad, 1, 0)
        inner_sum = jnp.sum(probabilities * grad_probs, axis=0, keepdims=True)
        grad_scores = (probabilities * (grad_probs - inner_sum)).astype(jnp.bfloat16)
        grad_query = contract(kt_ref[:, :count], grad_scores, 1, 0) * SCALE
        first, second = grad_query[:half], grad_query[half:]
        cosine, sine = cos_ref[:, at], sin_ref[:, at]
        dq_ref[:half, at] = (first * cosine + second * sine).astype(jnp.bfloat16)
        dq_ref[half:, at] = (second * cosine - first * sine).astype(jnp.bfloat16)
        dk_ref[:count, :] += contract(grad_scores, query, 1, 1)
        dv_ref[:count, :] += contract(probabilities.astype(jnp.bfloat16), grad, 1, 1)
        grad_sink = grad_sink - jnp.exp(sink - log_sum) * inner_sum
    dsink_ref[0] = grad_sink


def attend_back(sinks, queries, keys, keys_t, values, grads, log_sums, cosine, sine):
    heads, length = queries.shape[0] // HEAD_SIZE, queries.shape[1]
    per_head = pl.BlockSpec((HEAD_SIZE, length), lambda h: (h, 0))

    def whole(*shape):
        return pl.BlockSpec(shape, lambda h: (0,) * len(shape))

    return pl.pallas_call(
        attend_back_kernel,
        grid=(heads,),
        out_shape=(
            jax.ShapeDtypeStruct(queries.shape, jnp.bfloat16),
            jax.ShapeDtypeStruct((length, HEAD_SIZE), jnp.float32),
            jax.ShapeDtypeStruct((length, HEAD_SIZE), jnp.float32),
            jax.ShapeDtypeStruct((heads, 1, SPAN), jnp.float32),
        ),
        in_specs=[
            pl.BlockSpec(memory_space=pltpu.SMEM),
            per_head,
            whole(length, HEAD_SIZE),
            whole(HEAD_SIZE, length),
            whole(length, HEAD_SIZE),
            per_head,
            pl.BlockSpec((1, 1, length), lambda h: (h, 0, 0)),
            whole(HEAD_SIZE // 2, length),
            whole(HEAD_SIZE // 2, length),
        ],
        out_specs=(
            per_head,
            whole(length, HEAD_SIZE),
            whole(length, HEAD_SIZE),
            pl.BlockSpec((1, 1, SPAN), lambda h: (h, 0, 0)),
        ),
        compiler_params=pltpu.CompilerParams(vmem_limit_bytes=48 * MIB),
        cost_estimate=pl.CostEstimate(
            flops=heads * length * length * HEAD_SIZE * 10,
            bytes_accessed=heads * length * HEAD_SIZE * 8,
            transcendentals=heads * length * length,
        ),
        name="attend_back",
    )(sinks, queries, keys, keys_t, values, grads, log_sums, cosine, sine)


def branch_back(parts, columns, grad_own, out_weights, attended, collective):
    low, f32 = jnp.bfloat16, jnp.float32
    block_rows, width = grad_own.shape
    depth, length = attended.shape
    cut = 512

    def kernel(
        parts_ref, grad_ref, out_ref, att_ref, o_ref, grad_att, grad_out, all_grads, *scratch
    ):
        gather = Gather(1, grad_ref, all_grads, scratch[:5])
        scatter = Scatter(4, parts_ref, o_ref, scratch[5:], pl.ds(0, columns))
        greet((gather.mate, gather.near_x, gather.near_y), 4, gather.z_at)
        gather.begin(True)
        scatter.begin(True)
        gather.second(0)
        scatter.first(0)
        gather.near(0)
        gather.third(0)
        gather.own_block()

        def work(step):
            for i in range(length // SPAN):

                @pl.when(step == i)
                def _():
                    at = slice(i * SPAN, (i + 1) * SPAN)
                    grad_att[:, at] = contract(out_ref[...], all_grads[at, :], 1, 1).astype(low)

            for i in range(-(-width // cut)):

                @pl.when(step == i + length // SPAN)
                def _():
                    at = slice(i * cut, min(width, (i + 1) * cut))
                    grad_out[:, at] = contract(att_ref[...], all_grads[:, at], 1, 0).astype(low)

        steps = length // SPAN + -(-width // cut)
        scatter.run(work, max(0, steps - 12), begun=True)
        gather.end()

    hbm = pl.BlockSpec(memory_space=pl.ANY)
    vmem = pl.BlockSpec(memory_space=pltpu.VMEM)
    return pl.pallas_call(
        kernel,
        out_shape=(
            jax.ShapeDtypeStruct((block_rows, columns), f32),
            jax.ShapeDtypeStruct((depth, length), low),
            jax.ShapeDtypeStruct((depth, width), low),
        ),
        in_specs=[hbm, hbm, vmem, vmem],
        out_specs=(hbm, vmem, vmem),
        scratch_shapes=[
            pltpu.VMEM((length, width), low),
            *gather_sems(1),
            *scatter_scratch(4, block_rows, columns, low),
        ],
        compiler_params=pltpu.CompilerParams(
            collective_id=collective, has_side_effects=True, vmem_limit_bytes=56 * MIB
        ),
        name="branch_back",
    )(parts, grad_own, out_weights, attended)


def attention_back(
    parts, first_column, sinks, queries, keys, keys_t, values, grads, log_sums, cosine, sine, normed,
    own_rows, collective,
):
    low, f32 = jnp.bfloat16, jnp.float32
    length = queries.shape[1]
    heads = queries.shape[0] // HEAD_SIZE
    half = HEAD_SIZE // 2
    block_rows, columns = parts.shape[0] // 32, parts.shape[1] - first_column
    q_rows = queries.shape[0] // 4
    kv_rows = (own_rows - q_rows) // 2
    per_shard = q_rows // HEAD_SIZE
    spans = length // SPAN

    def kernel(
        sink_ref, parts_ref, q_ref, k_ref, kt_ref, v_ref, grad_ref, log_ref, cos_ref, sin_ref, normed_hbm,
        o_ref, lin_ref, weights_ref, dsink_ref, dk_s, dv_s, normed_v, normed_sem, *scratch,
    ):
        load = pltpu.make_async_copy(normed_hbm, normed_v, normed_sem)
        load.start()
        dk_s[...] = jnp.zeros_like(dk_s)
        dv_s[...] = jnp.zeros_like(dv_s)
        dsink_ref[...] = jnp.zeros_like(dsink_ref)

        def one(head, span):
            start, count = span * SPAN, span * SPAN + SPAN
            at = slice(start, count)
            rows = pl.ds(pl.multiple_of(head * HEAD_SIZE, HEAD_SIZE), HEAD_SIZE)
            query = q_ref[rows, at] * jnp.bfloat16(SCALE)
            grad = grad_ref[rows, at]
            log_sum = log_ref[head, :, at]
            chances = jnp.exp(masked_scores(k_ref[:count, :], query, count) - log_sum)
            grad_probs = contract(v_ref[:count, :], grad, 1, 0)
            inner_sum = jnp.sum(chances * grad_probs, axis=0, keepdims=True)
            grad_scores = (chances * (grad_probs - inner_sum)).astype(low)
            grad_query = contract(kt_ref[:, :count], grad_scores, 1, 0) * SCALE
            first, second = grad_query[:half], grad_query[half:]
            cosine, sine = cos_ref[:, at], sin_ref[:, at]
            place = (head // per_shard) * own_rows + lax.rem(head, per_shard) * HEAD_SIZE
            lin_ref[pl.ds(pl.multiple_of(place, 16), HEAD_SIZE), at] = jnp.concatenate(
                [first * cosine + second * sine, second * cosine - first * sine], axis=0
            ).astype(low)
            dk_s[:count, :] += contract(grad_scores, query, 1, 1)
            dv_s[:count, :] += contract(chances.astype(low), grad, 1, 1)
            dsink_ref[head] -= jnp.exp(sink_ref[head] - log_sum) * inner_sum

        def finish():
            grad_keys, grad_values = dk_s[...].T, dv_s[...].T
            first, second = grad_keys[:half], grad_keys[half:]
            cosine, sine = cos_ref[...], sin_ref[...]
            grad_keys = jnp.concatenate(
                [first * cosine + second * sine, second * cosine - first * sine], axis=0
            )
            for z in range(4):
                here = slice(z * kv_rows, (z + 1) * kv_rows)
                start = z * own_rows + q_rows
                lin_ref[start : start + kv_rows, :] = grad_keys[here].astype(low)
                lin_ref[start + kv_rows : start + 2 * kv_rows, :] = grad_values[here].astype(low)
            load.wait()

        wide = normed.shape[1]
        cut = 512

        def work(step):
            first_step = 0
            for span in reversed(range(spans)):
                at_once = max(1, 16 // (span + 1))
                count = -(-heads // at_once)
                here = (step >= first_step) & (step < first_step + count)

                @pl.when(here)
                def _():
                    begin = (step - first_step) * at_once

                    def body(head, carry):
                        pl.when(head < heads)(lambda: one(head, span))
                        return carry

                    lax.fori_loop(begin, begin + at_once, body, 0)

                first_step += count
            pl.when(step == first_step)(finish)
            for i in range(-(-wide // cut)):

                @pl.when(step == first_step + i)
                def _():
                    at = slice(i * cut, min(wide, (i + 1) * cut))
                    weights_ref[:, at] = contract(lin_ref[...], normed_v[:, at], 1, 0).astype(low)

        needed = sum(-(-heads // max(1, 16 // (span + 1))) for span in range(spans))
        needed += -(-wide // cut)
        late = pl.ds(first_column, columns)
        Scatter(4, parts_ref, o_ref, scratch, late).run(work, max(0, needed - 12))

    hbm = pl.BlockSpec(memory_space=pl.ANY)
    vmem = pl.BlockSpec(memory_space=pltpu.VMEM)
    return pl.pallas_call(
        kernel,
        out_shape=(
            jax.ShapeDtypeStruct((block_rows, columns), f32),
            jax.ShapeDtypeStruct((4 * own_rows, length), low),
            jax.ShapeDtypeStruct((4 * own_rows, normed.shape[1]), low),
            jax.ShapeDtypeStruct((heads, 1, SPAN), f32),
        ),
        in_specs=[pl.BlockSpec(memory_space=pltpu.SMEM), hbm] + [vmem] * 8 + [hbm],
        out_specs=(hbm, vmem, vmem, vmem),
        scratch_shapes=[
            pltpu.VMEM((length, HEAD_SIZE), f32),
            pltpu.VMEM((length, HEAD_SIZE), f32),
            pltpu.VMEM(normed.shape, low),
            pltpu.SemaphoreType.DMA,
            *scatter_scratch(4, block_rows, columns, low, 0),
        ],
        compiler_params=pltpu.CompilerParams(
            collective_id=collective, has_side_effects=True, vmem_limit_bytes=60 * MIB
        ),
        name="attention_back",
    )(sinks, parts, queries, keys, keys_t, values, grads, log_sums, cosine, sine, normed)


PAIR = 2
STEP = 4


def routed(cols, capacity):
    expert = lax.axis_index("ctx")
    cols = cols.astype(jnp.float32)
    lane = lax.broadcasted_iota(jnp.int32, cols.shape, 1)
    place = jnp.sum(jnp.where(lane == 64 + expert, cols, 0.0), axis=1, keepdims=True)
    gate = jnp.sum(jnp.where(lane == 72 + expert, cols, 0.0), axis=1, keepdims=True)
    slot = lax.broadcasted_iota(jnp.int32, (cols.shape[0], PAIR * capacity), 1)
    picked = place.astype(jnp.int32) == slot
    return (
        jnp.where(picked, 1.0, 0.0).astype(jnp.bfloat16),
        jnp.where(picked, gate, 0.0).astype(jnp.bfloat16),
    )


class Stream:
    def __init__(self, arrays, sems, inward, first_sem=0):
        self.arrays, self.sems, self.inward, self.first_sem = arrays, sems, inward, first_sem

    def copies(self, slot, block):
        made = []
        for k, (array, slots, count, column) in enumerate(self.arrays):
            at = pl.ds(pl.multiple_of(block * count, 16), count)
            far = array.at[at] if column is None else array.at[at, column]
            pair = (far, slots.at[slot]) if self.inward else (slots.at[slot], far)
            made.append(pltpu.make_async_copy(*pair, self.sems.at[slot, self.first_sem + k]))
        return made

    def start(self, slot, block):
        for copy in self.copies(slot, block):
            copy.start()

    def wait(self, slot, block):
        for copy in self.copies(slot, block):
            copy.wait()


def two_of(shape, dtype):
    return pltpu.VMEM((2,) + shape, dtype)


def experts(sent, sent_grads, own_grads, gate_w, up_w, down_w, gate_b, up_b, down_b, capacity, collective):
    low, f32 = jnp.bfloat16, jnp.float32
    block_rows, wide = sent.shape
    share, width = gate_w.shape
    span = PAIR * block_rows
    pairs = STEP // PAIR
    count = PAIR * capacity
    tokens = 32 * block_rows
    slot_rows = 32 * capacity
    line = 4

    def kernel(
        sent_ref, sent_grads_ref, own_grads_ref, gate_hbm, up_hbm, down_hbm, gate_b_ref, up_b_ref, down_b_ref,
        all_ref, all_grads_ref, rows_out, gate_out, up_out, hidden_out, mix_out,
        grad_rows_out, gate_grad_out, up_grad_out, tokens_out, down_sum, gate_sum, up_sum,
        gate_v, up_v, down_v, x_s, rows_s, gate_s, up_s, hidden_s, mix_s, cols_s, gate_gs, up_gs,
        held_sems, in_sems, out_sems, *sems,
    ):
        held = [
            pltpu.make_async_copy(source, target, held_sems.at[k])
            for k, (source, target) in enumerate(
                ((gate_hbm, gate_v), (up_hbm, up_v), (down_hbm, down_v))
            )
        ]
        for copy in held:
            copy.start()
        forward_in = Stream([(all_ref, x_s, pairs * span, None)], in_sems, True)
        forward_out = Stream(
            [
                (rows_out, rows_s, pairs * count, None),
                (gate_out, gate_s, pairs * count, None),
                (up_out, up_s, pairs * count, None),
                (hidden_out, hidden_s, pairs * count, None),
                (mix_out, mix_s, pairs * span, None),
            ],
            out_sems,
            False,
        )
        kept = [
            (all_ref, cols_s, pairs * span, pl.ds(wide - 128, 128)),
            (gate_out, gate_s, pairs * count, None),
            (up_out, up_s, pairs * count, None),
        ]
        back_kept = Stream(kept, in_sems, True)
        back_own = Stream([(own_grads_ref, x_s, pairs * span, None)], in_sems, True, 3)
        back_far = Stream([(all_grads_ref, x_s, pairs * span, None)], in_sems, True, 3)
        back_out = Stream(
            [
                (grad_rows_out, rows_s, pairs * count, None),
                (gate_grad_out, gate_gs, pairs * count, None),
                (up_grad_out, up_gs, pairs * count, None),
                (tokens_out, mix_s, pairs * span, None),
            ],
            out_sems,
            False,
        )
        down_sum[...] = jnp.zeros_like(down_sum)
        gate_sum[...] = jnp.zeros_like(gate_sum)
        up_sum[...] = jnp.zeros_like(up_sum)
        for slot in range(2):
            mix_s[slot, :, width:] = jnp.zeros((pairs * span, wide - width), low)
        spans = [pl.ds(pair * span, span) for pair in range(pairs)]

        def forward(slot):
            picks = [routed(x_s[slot, at, wide - 128 :], capacity) for at in spans]
            rows = jnp.concatenate(
                [contract(picks[k][0], x_s[slot, spans[k], :], 0, 0) for k in range(pairs)],
                axis=0,
            ).astype(low)
            rows_s[slot] = rows
            rows = rows[:, :width]
            gate_lin = contract(rows, gate_v[...], 1, 1) + gate_b_ref[...]
            up_lin = contract(rows, up_v[...], 1, 1) + up_b_ref[...]
            gate_s[slot] = gate_lin
            up_s[slot] = up_lin
            hidden = glu_units(gate_lin, up_lin).astype(low)
            hidden_s[slot] = hidden
            out = contract(hidden, down_v[...], 1, 0) + down_b_ref[...]
            for k in range(pairs):
                part = out[k * count : (k + 1) * count].astype(low)
                mix_s[slot, spans[k], :width] = contract(picks[k][1], part, 1, 0).astype(low)

        def backward(slot):
            picks = [routed(cols_s[slot, at, :], capacity) for at in spans]
            rows = jnp.concatenate(
                [contract(picks[k][1], x_s[slot, spans[k], :], 0, 0) for k in range(pairs)],
                axis=0,
            ).astype(low)
            rows_s[slot] = rows
            rows = rows[:, :width]
            down_sum[...] += jnp.sum(rows.astype(f32), axis=0, keepdims=True)
            grad_units = contract(rows, down_v[...], 1, 1)
            gate_tanh = jnp.tanh(gate_s[slot] / CLAMP_LIMIT)
            up_tanh = jnp.tanh(up_s[slot] / CLAMP_LIMIT)
            gated = CLAMP_LIMIT * gate_tanh
            lifted = CLAMP_LIMIT * up_tanh + 1.0
            part = jax.nn.sigmoid(GLU_ALPHA * gated)
            grad_up = (grad_units * gated * part * (1.0 - up_tanh * up_tanh)).astype(low)
            slope = part * (1.0 + GLU_ALPHA * gated * (1.0 - part))
            grad_gate = (grad_units * lifted * slope * (1.0 - gate_tanh * gate_tanh)).astype(low)
            gate_gs[slot] = grad_gate
            up_gs[slot] = grad_up
            gate_sum[...] += jnp.sum(grad_gate.astype(f32), axis=0, keepdims=True)
            up_sum[...] += jnp.sum(grad_up.astype(f32), axis=0, keepdims=True)
            copies = contract(grad_gate, gate_v[...], 1, 0) + contract(grad_up, up_v[...], 1, 0)
            for k in range(pairs):
                part = copies[k * count : (k + 1) * count].astype(low)
                mix_s[slot, spans[k], :width] = contract(picks[k][0], part, 1, 0).astype(low)

        ahead = Gather(line, sent_ref, all_ref, sems[:9], TAIL)
        back = Gather(line, sent_grads_ref, all_grads_ref, sems[9:], TAIL, own_grads_ref)
        y_at = ahead.me // 4

        def block(step):
            half = lax.rem(step, 2)
            return ahead.slot(step // 2) * 2 + (1 - half) * y_at + half * (1 - y_at)

        ahead.begin()

        steps = 2 * line

        def forward_order(order, carry):
            @pl.when(order < line)
            def _():
                ahead.second(order)
                pl.when(order + 1 < line)(lambda: ahead.first(order + 1))
                pl.when(order > 0)(lambda: ahead.tails(order))
                pl.when(order == 1)(back.begin_line)
                pl.when(order == 2)(back.send_tails)
                pl.when(order == line - 1)(lambda: back.first(1))
                ahead.near(order)

                @pl.when(order == 0)
                def _():
                    ahead.own_block()
                    for copy in held:
                        copy.wait()

                forward_in.start(0, block(2 * order))

            def half_plane(step, carry):
                slot = lax.rem(step, 2)
                forward_in.wait(slot, block(step))
                pl.when(step >= 2)(lambda: forward_out.wait(slot, block(step - 2)))
                forward(slot)
                forward_out.start(slot, block(step))
                return carry

            lax.fori_loop(
                jnp.maximum(2 * order - 1, 0), jnp.minimum(2 * order + 1, steps), half_plane, 0
            )

            @pl.when(order < line)
            def _():
                ahead.third(order)
                pl.when(order == 0)(ahead.send_tails)
                forward_in.start(1, block(2 * order + 1))

            return carry

        lax.fori_loop(0, line + 1, forward_order, 0)
        back.second(1)
        back.first(2)
        forward_out.wait(0, block(steps - 2))
        forward_out.wait(1, block(steps - 1))

        def grads_in(step, act):
            order, half = step // 2, lax.rem(step, 2)
            act(back_kept, half, block(step))
            pl.when(order == 0)(
                lambda: act(back_own, half, (1 - half) * y_at + half * (1 - y_at))
            )
            pl.when(order > 0)(lambda: act(back_far, half, block(step)))

        def backward_step(step, carry):
            order, half = step // 2, lax.rem(step, 2)
            pl.when(half == 1)(lambda: grads_in(step, Stream.start))

            @pl.when(step > 0)
            def _():
                slot = 1 - half
                pl.when(step >= 3)(lambda: back_out.wait(slot, block(step - 3)))
                grads_in(step - 1, Stream.wait)
                backward(slot)
                back_out.start(slot, block(step - 1))

            @pl.when((half == 0) & (order < line))
            def _():
                @pl.when(order > 0)
                def _():
                    back.tails(order)
                    back.near(order)
                    back.third(order)

                grads_in(step, Stream.start)

            @pl.when((half == 1) & (order > 0))
            def _():
                pl.when(order + 1 < line)(lambda: back.second(order + 1))
                pl.when(order + 2 < line)(lambda: back.first(order + 2))

            return carry

        lax.fori_loop(0, steps + 1, backward_step, 0)
        back_out.wait(0, block(steps - 2))
        back_out.wait(1, block(steps - 1))
        ahead.end()
        back.end(1)

    hbm = pl.BlockSpec(memory_space=pl.ANY)
    vmem = pl.BlockSpec(memory_space=pltpu.VMEM)

    def made(rows, columns, dtype=low):
        return jax.ShapeDtypeStruct((rows, columns), dtype)

    return pl.pallas_call(
        kernel,
        out_shape=(
            made(tokens, wide),
            made(tokens, wide),
            made(slot_rows, wide),
            made(slot_rows, share, f32),
            made(slot_rows, share, f32),
            made(slot_rows, share),
            made(tokens, wide),
            made(slot_rows, wide),
            made(slot_rows, share),
            made(slot_rows, share),
            made(tokens, wide),
            made(1, width, f32),
            made(1, share, f32),
            made(1, share, f32),
        ),
        in_specs=[hbm] * 6 + [vmem] * 3,
        out_specs=(hbm,) * 11 + (vmem,) * 3,
        scratch_shapes=[
            pltpu.VMEM(gate_w.shape, low),
            pltpu.VMEM(up_w.shape, low),
            pltpu.VMEM(down_w.shape, low),
            two_of((pairs * span, wide), low),
            two_of((pairs * count, wide), low),
            two_of((pairs * count, share), f32),
            two_of((pairs * count, share), f32),
            two_of((pairs * count, share), low),
            two_of((pairs * span, wide), low),
            two_of((pairs * span, 128), low),
            two_of((pairs * count, share), low),
            two_of((pairs * count, share), low),
            pltpu.SemaphoreType.DMA((3,)),
            pltpu.SemaphoreType.DMA((2, 4)),
            pltpu.SemaphoreType.DMA((2, 5)),
            *gather_sems(line, TAIL),
            *gather_sems(line, TAIL),
        ],
        compiler_params=pltpu.CompilerParams(
            collective_id=collective, has_side_effects=True, vmem_limit_bytes=60 * MIB
        ),
        name="experts",
    )(sent, sent_grads, own_grads, gate_w, up_w, down_w, gate_b, up_b, down_b)


def expert_weights(parts, rows_in, gate_grad, up_grad, rows_grad, hidden, collective):
    low, f32 = jnp.bfloat16, jnp.float32
    slot_rows, wide = rows_in.shape
    share = gate_grad.shape[1]
    block_rows, width = parts.shape[0] // 32, parts.shape[1]
    cut = 256
    whole, rest = wide // cut, wide % cut
    count = whole + 1

    def kernel(
        parts_ref, rows_hbm, gate_hbm, up_hbm, grad_hbm, hidden_hbm, o_ref, gate_out, up_out, down_out,
        stage, first_t, second_t, in_s, first_s, second_s, held_sem, in_sems, out_sems, *scratch,
    ):
        def held(source):
            return pltpu.make_async_copy(source, stage, held_sem)

        held(gate_hbm).start()

        def begin(copy):
            copy.start()

        def await_it(copy):
            copy.wait()

        def by_width(index, act):
            pl.when((index >= 0) & (index < whole))(lambda: act(cut))
            pl.when(index == whole)(lambda: act(rest))

        def loads(chunk, act):
            slot = lax.rem(chunk, 2)
            for source, index in ((rows_hbm, chunk), (grad_hbm, chunk - count)):

                def one(columns):
                    at = pl.ds(pl.multiple_of(index * cut, cut), columns)
                    here = in_s.at[slot, :, pl.ds(0, columns)]
                    act(pltpu.make_async_copy(source.at[:, at], here, in_sems.at[slot]))

                by_width(index, one)

        def stores(chunk, act):
            slot = lax.rem(chunk, 2)
            for targets, index in (
                (((first_s, gate_out), (second_s, up_out)), chunk),
                (((first_s, down_out),), chunk - count),
            ):

                def one(columns):
                    at = pl.ds(pl.multiple_of(index * cut, cut), columns)
                    for k, (source, target) in enumerate(targets):
                        here = source.at[slot, :, pl.ds(0, columns)]
                        act(pltpu.make_async_copy(here, target.at[:, at], out_sems.at[slot, k]))

                by_width(index, one)

        def work(chunk):
            slot = lax.rem(chunk, 2)

            @pl.when(chunk == 0)
            def _():
                loads(0, begin)
                held(gate_hbm).wait()
                first_t[...] = stage[...].T
                held(up_hbm).start()
                held(up_hbm).wait()
                second_t[...] = stage[...].T
                held(hidden_hbm).start()

            @pl.when(chunk == count)
            def _():
                held(hidden_hbm).wait()
                first_t[...] = stage[...].T

            pl.when(chunk + 1 < 2 * count)(lambda: loads(chunk + 1, begin))
            pl.when(chunk >= 2)(lambda: stores(chunk - 2, await_it))
            loads(chunk, await_it)
            first_s[slot] = contract(first_t[...], in_s[slot], 1, 0).astype(low)

            @pl.when(chunk < count)
            def _():
                second_s[slot] = contract(second_t[...], in_s[slot], 1, 0).astype(low)

            stores(chunk, begin)

        def works(step):
            def body(chunk, carry):
                work(chunk)
                return carry

            lax.fori_loop(2 * step, 2 * step + 2, body, 0)

        Scatter(4, parts_ref, o_ref, scratch).run(works, count - 12)
        stores(2 * count - 2, await_it)
        stores(2 * count - 1, await_it)

    hbm = pl.BlockSpec(memory_space=pl.ANY)
    return pl.pallas_call(
        kernel,
        out_shape=(
            jax.ShapeDtypeStruct((block_rows, width), f32),
            jax.ShapeDtypeStruct((share, wide), low),
            jax.ShapeDtypeStruct((share, wide), low),
            jax.ShapeDtypeStruct((share, wide), low),
        ),
        in_specs=[hbm] * 6,
        out_specs=(hbm,) * 4,
        scratch_shapes=[
            pltpu.VMEM(gate_grad.shape, low),
            pltpu.VMEM(gate_grad.shape[::-1], low),
            pltpu.VMEM(gate_grad.shape[::-1], low),
            two_of((slot_rows, cut), low),
            two_of((share, cut), low),
            two_of((share, cut), low),
            pltpu.SemaphoreType.DMA,
            pltpu.SemaphoreType.DMA((2,)),
            pltpu.SemaphoreType.DMA((2, 2)),
            *scatter_scratch(4, block_rows, width, low),
        ],
        compiler_params=pltpu.CompilerParams(
            collective_id=collective, has_side_effects=True, vmem_limit_bytes=60 * MIB
        ),
        name="expert_weights",
    )(parts, rows_in, gate_grad, up_grad, rows_grad, hidden)


def product_kernel(left_ref, right_ref, out_ref):
    right = right_ref[:, : out_ref.shape[1]]
    out_ref[...] = contract(left_ref[...], right, 0, 0).astype(out_ref.dtype)


def product(left_t, right, name, columns=None):
    depth, rows = left_t.shape
    columns = columns or right.shape[1]
    return pl.pallas_call(
        product_kernel,
        grid=(rows // SPAN,),
        out_shape=jax.ShapeDtypeStruct((rows, columns), jnp.bfloat16),
        in_specs=[
            pl.BlockSpec((depth, SPAN), lambda i: (0, i)),
            pl.BlockSpec(right.shape, lambda i: (0, 0), pipeline_mode=pl.Buffered(1)),
        ],
        out_specs=pl.BlockSpec((SPAN, columns), lambda i: (i, 0)),
        compiler_params=pltpu.CompilerParams(vmem_limit_bytes=40 * MIB),
        cost_estimate=pl.CostEstimate(
            flops=2 * depth * rows * columns, bytes_accessed=4 * rows * columns, transcendentals=0
        ),
        name=name,
    )(left_t, right)


def input_back(grad_lin, weights, normed, width, collective, small):
    low, f32 = jnp.bfloat16, jnp.float32
    depth, length = grad_lin.shape
    block_rows = length // 8
    wide = normed.shape[1]
    columns = small.shape[1]
    gain_columns = -(-wide // (16 * 128)) * 128

    def kernel(
        lin_ref, weights_ref, normed_hbm, small_ref, o_ref, all_sums,
        normed_v, part, found_v, sums_v, sem, *scratch,
    ):
        gather = Gather(4, sums_v, all_sums, scratch[:5])
        scatter = Scatter(1, part, o_ref, scratch[5:])
        load = pltpu.make_async_copy(normed_hbm, normed_v, sem)
        load.start()
        greet((gather.mate, gather.near_x, gather.near_y), 4, gather.z_at)
        found_v[...] = jnp.zeros_like(found_v)
        load.wait()

        def make(chip):
            at = pl.ds(pl.multiple_of(chip * SPAN, SPAN), SPAN)
            value = contract(lin_ref[:, at], weights_ref[...], 0, 0)
            part[at, :] = value[:, :width].astype(low)
            found = value * normed_v[at, :].astype(f32)
            found_v[...] += jnp.sum(found, axis=0, keepdims=True)

        scatter.produce(make)
        sums_v[:, :columns] = small_ref[...]
        sums_v[:, columns:] = jnp.zeros((16, gain_columns), f32)
        for k in range(wide // 128):
            row, lane = k // (gain_columns // 128), k % (gain_columns // 128) * 128
            sums_v[row : row + 1, columns + lane : columns + lane + 128] = found_v[
                :, k * 128 : (k + 1) * 128
            ]
        gather.begin(True)
        scatter.first(0)
        for order in (1, 2, 3):
            gather.first(order)
        for order in range(4):
            gather.second(order)
        scatter.second(0)
        for order in range(4):
            gather.near(order)
            gather.third(order)
        scatter.third(0, scatter.total)
        scatter.end()
        gather.own_block()
        gather.end()

    hbm = pl.BlockSpec(memory_space=pl.ANY)
    vmem = pl.BlockSpec(memory_space=pltpu.VMEM)
    return pl.pallas_call(
        kernel,
        out_shape=(
            jax.ShapeDtypeStruct((block_rows, width), f32),
            jax.ShapeDtypeStruct((32 * 16, columns + gain_columns), f32),
        ),
        in_specs=[vmem, vmem, hbm, vmem],
        out_specs=(hbm,) * 2,
        scratch_shapes=[
            pltpu.VMEM((length, wide), low),
            pltpu.VMEM((length, width), low),
            pltpu.VMEM((1, wide), f32),
            pltpu.VMEM((16, columns + gain_columns), f32),
            pltpu.SemaphoreType.DMA,
            *gather_sems(4),
            *scatter_scratch(1, block_rows, width, low),
        ],
        compiler_params=pltpu.CompilerParams(
            collective_id=collective, has_side_effects=True, vmem_limit_bytes=58 * MIB
        ),
        name="input_back",
    )(grad_lin, weights, normed, small)


def shards(
    layer_input, cotangent, gate_weights, routes, w_query, key_projection, value_projection, w_out,
    b_query, key_bias_vector, value_bias_vector, b_out, learned_sink_logits, gain_attn, gain_ffn,
    w_gate, w_up, w_down, b_gate, b_up, b_down,
):
    low = jnp.bfloat16
    ctx_n, z_n = lax.axis_size("ctx"), lax.axis_size("fsdp")
    ctx_at, z_at = lax.axis_index("ctx"), lax.axis_index("fsdp")
    tuned = ctx_n == 8 and z_n == 4
    width = layer_input.shape[-1]
    rows = layer_input.shape[0] * layer_input.shape[1]
    length = rows * ctx_n
    blocks = ctx_n * z_n
    capacity = max(2, rows * TOP * 17 // (16 * ctx_n))
    heads = QUERY_HEADS // ctx_n
    spread = ctx_n // KEY_VALUE_HEADS
    f32 = jnp.float32

    def gather_plane(value, call):
        if tuned:
            return gather_blocks(value, 1, call, f"gather_plane_{call}")
        return lax.all_gather(value, "ctx", axis=0, tiled=True)

    def scatter_plane(value, call):
        if tuned:
            return scatter_blocks(value, 1, call, f"scatter_plane_{call}")
        return lax.psum_scatter(value, "ctx", scatter_dimension=0, tiled=True).astype(f32)

    residual = layer_input.reshape(rows, width).astype(f32)
    grad_final = cotangent.reshape(rows, width)
    gain_attn_f, gain_ffn_f = gain_attn.astype(f32), gain_ffn.astype(f32)
    cosine, sine = rotary_tables(length)

    q_cols, k_cols = w_query.shape[1], key_projection.shape[1]
    own_rows = q_cols + 2 * k_cols
    wide = -(-(width + 2 * ctx_n) // 128) * 128
    biases = jnp.concatenate([b_query, key_bias_vector, value_bias_vector])
    own_weights = jnp.concatenate([w_query, key_projection, value_projection], axis=1).T
    own_weights = jnp.concatenate(
        [own_weights, biases[:, None], jnp.zeros((own_rows, wide - width - 1), low)], axis=1
    )
    ones = jnp.concatenate(
        [jnp.ones((rows, 1), low), jnp.zeros((rows, wide - width - 1), low)], axis=1
    )

    token_routes = routes.reshape(rows, TOP)
    names = jnp.arange(ctx_n, dtype=jnp.int32)
    named = token_routes[:, :, None] == names[None, None, :]
    hits = jnp.sum(named.astype(f32), axis=1)
    gates = jnp.sum(
        jnp.where(named, gate_weights.reshape(rows, TOP)[:, :, None].astype(f32), 0.0), axis=1
    )
    earlier = (
        lax.broadcasted_iota(jnp.int32, (rows, rows), 0)
        > lax.broadcasted_iota(jnp.int32, (rows, rows), 1)
    ).astype(low)
    places = jnp.dot(earlier, hits.astype(low), preferred_element_type=f32)
    first_slot = (lax.rem(ctx_at, PAIR) * capacity).astype(f32) if tuned else 0.0
    places = jnp.where(hits > 0, places + first_slot, -1.0)
    slot_rows = blocks * capacity
    if not tuned:
        slots = jnp.arange(capacity, dtype=f32)[None, :, None]
        picked = places.T[:, None, :] == slots
        select = picked.astype(low)
        mixing = jnp.where(picked, gates.T[:, None, :], 0.0).astype(low)

    def exchanged(slot_values):
        moved = slot_values.reshape(ctx_n, capacity, width)
        return lax.all_to_all(moved, "ctx", split_axis=0, concat_axis=0, tiled=True)

    def to_slots(picks, token_rows):
        dims = (((2,), (0,)), ((), ()))
        moved = lax.dot_general(picks, token_rows, dims, preferred_element_type=f32).astype(low)
        moved = lax.all_gather(exchanged(moved), "fsdp", axis=0, tiled=True)
        return moved.reshape(slot_rows, width)

    def to_tokens(picks, slot_values):
        slot_values = exchanged(
            lax.psum_scatter(slot_values, "fsdp", scatter_dimension=0, tiled=True)
        )
        dims = (((1,), (1,)), ((0,), (0,)))
        moved = lax.dot_general(picks, slot_values, dims, preferred_element_type=f32)
        return jnp.sum(moved, axis=0)

    normed_own = jnp.concatenate([norm_scale(residual, gain_attn_f).astype(low), ones], axis=1)
    sinks = lax.dynamic_slice(learned_sink_logits.astype(f32), (ctx_at * heads,), (heads,))
    swap = [(i, i ^ 1) for i in range(ctx_n)]
    odd = lax.rem(ctx_at, 2) == 1
    if tuned:
        sent_grads = jnp.pad(grad_final, ((0, 0), (0, wide - width)))
        branch, normed_attn, own_grads, head_weights, out_weights, *kept = attention(
            normed_own, sent_grads, own_weights, w_out, sinks, cosine, sine, 1
        )
        queries, keys, keys_t, values, attended, log_sums = kept
    else:
        normed_attn = lax.all_gather(normed_own, "ctx", axis=0, tiled=True)
        head_weights = lax.all_gather(own_weights, "fsdp", axis=0, tiled=True)
        out_weights = lax.all_gather(w_out, "fsdp", axis=0, tiled=True)
        lin = contract(head_weights, normed_attn, 1, 1).reshape(z_n, own_rows, length)
        query_lin = lin[:, :q_cols].reshape(heads, HEAD_SIZE, length)
        kv_lin = jnp.stack([lin[:, q_cols : q_cols + k_cols], lin[:, q_cols + k_cols :]])
        kv_lin = kv_lin.reshape(2, z_n * k_cols, length)
        if spread == 2:
            other = lax.ppermute(kv_lin, "ctx", swap)
            kv_lin = jnp.where(
                odd,
                jnp.concatenate([other, kv_lin], axis=1),
                jnp.concatenate([kv_lin, other], axis=1),
            )
        queries = turned(query_lin, cosine, sine).astype(low).reshape(heads * HEAD_SIZE, length)
        keys_t = turned(kv_lin[:1], cosine, sine)[0].astype(low)
        values_t = kv_lin[1].astype(low)
        keys, values = keys_t.T, values_t.T
        attended, log_sums = attend(sinks, queries, keys, values_t)
        branch = scatter_plane(product(attended, out_weights, "branch"), 2)
    middle = residual + branch + b_out.astype(f32)
    normed_ffn = norm_scale(middle, gain_ffn_f).astype(low)

    gate_w, up_w, down_w = w_gate[0].T, w_up[0].T, w_down[0]
    share = b_down.shape[1]
    gate_b, up_b = b_gate.astype(f32), b_up.astype(f32)
    down_bias = lax.dynamic_update_slice(
        jnp.zeros((1, width), f32), b_down.astype(f32), (0, z_at * share)
    )
    if tuned:
        sent = jnp.concatenate(
            [
                normed_ffn,
                places.astype(low),
                gates.astype(low),
                jnp.zeros((rows, wide - width - 2 * ctx_n), low),
            ],
            axis=1,
        )
        made = experts(
            sent, sent_grads, own_grads, gate_w, up_w, down_w, gate_b, up_b, down_bias, capacity, 3
        )
        expert_in, hidden_units, mix_part = made[2], made[5], made[6]
        grad_expert_out, grad_gate_lin, grad_up_lin, grad_normed_part = made[7:11]
        grad_biases = made[11:]
        grad_b_down, grad_b_gate, grad_b_up = [value[0] for value in grad_biases]
        grad_normed_ffn, grad_w_gate, grad_w_up, grad_w_down = expert_weights(
            grad_normed_part, expert_in, grad_gate_lin, grad_up_lin, grad_expert_out, hidden_units, 6
        )
        grad_normed_ffn = grad_normed_ffn[:, :width]
    else:
        expert_in = to_slots(select, normed_ffn)
        gate_lin = contract(expert_in, gate_w, 1, 1) + gate_b
        up_lin = contract(expert_in, up_w, 1, 1) + up_b
        hidden_f, unit_back = jax.vjp(glu_units, gate_lin, up_lin)
        hidden_units = hidden_f.astype(low)
        expert_out = (contract(hidden_units, down_w, 1, 0) + down_bias).astype(low)
        expert_mix = to_tokens(mixing, expert_out)
        grad_expert_out = to_slots(mixing, grad_final)
        grad_units = contract(grad_expert_out, down_w, 1, 1)
        grad_gate_f, grad_up_f = unit_back(grad_units)
        grad_gate_lin, grad_up_lin = grad_gate_f.astype(low), grad_up_f.astype(low)
        grad_copy = contract(grad_gate_lin, gate_w, 1, 0) + contract(grad_up_lin, up_w, 1, 0)
        grad_normed_ffn = to_tokens(select, grad_copy.astype(low))
        grad_b_down = jnp.sum(grad_expert_out.astype(f32), axis=0)
        grad_b_gate = jnp.sum(grad_gate_lin.astype(f32), axis=0)
        grad_b_up = jnp.sum(grad_up_lin.astype(f32), axis=0)
        grad_w_gate = contract(grad_gate_lin, expert_in, 0, 0)
        grad_w_up = contract(grad_up_lin, expert_in, 0, 0)
        grad_w_down = contract(hidden_units, grad_expert_out, 0, 0)
    grad_b_down = lax.dynamic_slice(grad_b_down, (z_at * share,), (share,))

    unused, norm_back = jax.vjp(norm_scale, middle, gain_ffn_f)
    grad_middle_part, grad_gain_ffn = norm_back(grad_normed_ffn)
    grad_middle = grad_final.astype(f32) + grad_middle_part
    grad_branch_own = grad_middle.astype(low)
    grad_b_out = jnp.sum(grad_branch_own.astype(f32), axis=0)
    if tuned:
        early = 1536
        first_mix, grad_attended, grad_out_part = branch_back(
            mix_part, early, grad_branch_own, out_weights, attended, 7
        )
        late_mix, grad_lin, grad_weights, grad_sink_parts = attention_back(
            mix_part, early, sinks, queries, keys, keys_t, values, grad_attended, log_sums, cosine,
            sine, normed_attn, own_rows, 5,
        )
        expert_mix = jnp.concatenate([first_mix, late_mix[:, : width - early]], axis=1)
    else:
        grad_branch = lax.all_gather(grad_branch_own, "ctx", axis=0, tiled=True)
        grad_attended = contract(out_weights, grad_branch, 1, 1).astype(low)
        grad_out_part = contract(attended, grad_branch, 1, 0).astype(low)
        grad_query, grad_keys, grad_values, grad_sink_parts = attend_back(
            sinks, queries, keys, keys_t, values, grad_attended, log_sums, cosine, sine
        )
        grad_kv = jnp.stack([turned(grad_keys.T[None], cosine, -sine)[0], grad_values.T])
        if spread == 2:
            grad_kv = grad_kv + lax.ppermute(grad_kv, "ctx", swap)
            halves = grad_kv.reshape(2, 2, HEAD_SIZE // 2, length)
            grad_kv = jnp.where(odd, halves[:, 1], halves[:, 0])
        grad_kv = grad_kv.astype(low).reshape(2, z_n, k_cols, length)
        grad_lin = jnp.concatenate(
            [grad_query.reshape(z_n, q_cols, length), grad_kv[0], grad_kv[1]], axis=1
        ).reshape(z_n * own_rows, length)
        grad_weights = contract(grad_lin, normed_attn, 1, 0).astype(low)
    final_out = (middle + expert_mix).astype(low).reshape(layer_input.shape)
    grad_w_out = lax.psum_scatter(grad_out_part, "fsdp", scatter_dimension=0, tiled=True).astype(f32)
    own_grads = lax.psum_scatter(grad_weights, "fsdp", scatter_dimension=0, tiled=True).astype(f32)
    grad_w_query = own_grads[:q_cols, :width].T
    grad_w_key = own_grads[q_cols : q_cols + k_cols, :width].T
    grad_w_value = own_grads[q_cols + k_cols :, :width].T
    own_bias_grads = own_grads[:, width]
    grad_sinks = lax.dynamic_update_slice(
        jnp.zeros((QUERY_HEADS,), f32), jnp.sum(grad_sink_parts, axis=(1, 2)), (ctx_at * heads,)
    )
    sums = (grad_b_out, grad_gain_ffn, grad_sinks)
    if tuned:
        joined = jnp.concatenate(sums)
        columns = -(-joined.shape[0] // (16 * 128)) * 128
        joined = jnp.pad(joined, (0, 16 * columns - joined.shape[0])).reshape(16, columns)
        grad_normed_attn, joined = input_back(
            grad_lin, head_weights, normed_attn, width, 8, joined
        )
        joined = jnp.sum(joined.reshape(blocks, 16, -1), axis=0)
        grad_gain_attn = joined[:, columns:].reshape(-1)[:width] / gain_attn_f
        joined = joined[:, :columns].reshape(-1)
        cuts = (width, 2 * width, 2 * width + QUERY_HEADS)
        sums = [joined[at - value.shape[0] : at] for at, value in zip(cuts, sums)]
    else:
        grad_normed_part = product(grad_lin, head_weights, "grad_normed", width)
        grad_normed_attn = scatter_plane(grad_normed_part, 8)
    unused, norm_back = jax.vjp(norm_scale, residual, gain_attn_f)
    grad_residual_part, own_gain = norm_back(grad_normed_attn)
    input_grad = (grad_middle + grad_residual_part).reshape(layer_input.shape)
    if not tuned:
        *sums, grad_gain_attn = lax.psum((*sums, own_gain), ("ctx", "fsdp"))
    grad_b_out, grad_gain_ffn, grad_sink_logits = sums
    return (
        final_out,
        input_grad,
        grad_w_query,
        grad_w_key,
        grad_w_value,
        grad_w_out,
        own_bias_grads[:q_cols],
        own_bias_grads[q_cols : q_cols + k_cols],
        own_bias_grads[q_cols + k_cols :],
        grad_b_out,
        grad_sink_logits,
        grad_gain_attn,
        grad_gain_ffn,
        grad_w_gate[:, :width].astype(f32).T[None],
        grad_w_up[:, :width].astype(f32).T[None],
        grad_w_down[:, :width].astype(f32)[None],
        grad_b_gate[None],
        grad_b_up[None],
        grad_b_down[None],
    )


def solution(mesh):
    return jax.shard_map(
        shards,
        mesh=mesh,
        in_specs=(
            P("fsdp", "ctx", None),
            P("fsdp", "ctx", None),
            P("fsdp", "ctx", None),
            P("fsdp", "ctx", None),
            P(None, ("ctx", "fsdp")),
            P(None, ("ctx", "fsdp")),
            P(None, ("ctx", "fsdp")),
            P(("ctx", "fsdp"), None),
            P(("ctx", "fsdp")),
            P(("ctx", "fsdp")),
            P(("ctx", "fsdp")),
            P(),
            P(),
            P(),
            P(),
            P("ctx", None, "fsdp"),
            P("ctx", None, "fsdp"),
            P("ctx", "fsdp", None),
            P("ctx", "fsdp"),
            P("ctx", "fsdp"),
            P("ctx", "fsdp"),
        ),
        out_specs=(
            P("fsdp", "ctx", None),
            P("fsdp", "ctx", None),
            P(None, ("ctx", "fsdp")),
            P(None, ("ctx", "fsdp")),
            P(None, ("ctx", "fsdp")),
            P(("ctx", "fsdp"), None),
            P(("ctx", "fsdp")),
            P(("ctx", "fsdp")),
            P(("ctx", "fsdp")),
            P(),
            P(),
            P(),
            P(),
            P("ctx", None, "fsdp"),
            P("ctx", None, "fsdp"),
            P("ctx", "fsdp", None),
            P("ctx", "fsdp"),
            P("ctx", "fsdp"),
            P("ctx", "fsdp"),
        ),
        check_vma=False,
    )
```

```python
import jax
import jax.numpy as jnp
import numpy as np
from jax import lax
from jax.experimental import pallas as pl
from jax.experimental.pallas import tpu as pltpu
from jax.sharding import PartitionSpec as P

MESH = pl.DeviceIdType.MESH
MIB = 1 << 20


def remote(src, dst, send_sem, recv_sem, device):
    return pltpu.make_async_remote_copy(
        src_ref=src,
        dst_ref=dst,
        send_sem=send_sem,
        recv_sem=recv_sem,
        device_id=device,
        device_id_type=MESH,
    )


def neighbours():
    me = lax.axis_index("ctx")
    core = lax.rem(me, 2)
    x_at = lax.rem(me // 2, 2)
    y_at = me // 4
    return me, me + 1 - 2 * core, me + 2 - 4 * x_at, me + 4 - 8 * y_at, 2 - 4 * x_at


def greet(others, line, z_at):
    barrier = pltpu.get_barrier_semaphore()
    for other in others:
        pl.semaphore_signal(barrier, 1, device_id=(other, z_at), device_id_type=MESH)
    if line == 1:
        pl.semaphore_wait(barrier, len(others))
        return
    me = lax.axis_index("ctx")

    @pl.when(z_at > 0)
    def _():
        pl.semaphore_signal(barrier, 1, device_id=(me, z_at - 1), device_id_type=MESH)

    @pl.when(z_at < line - 1)
    def _():
        pl.semaphore_signal(barrier, 1, device_id=(me, z_at + 1), device_id_type=MESH)

    inner = (lax.rem(z_at, 3) + 1) // 2
    pl.semaphore_wait(barrier, len(others) + 1 + inner)


def gather_sems(line, tail=0):
    sems = [
        pltpu.SemaphoreType.DMA,
        pltpu.SemaphoreType.DMA((line, 2)),
        pltpu.SemaphoreType.DMA((line,)),
        pltpu.SemaphoreType.DMA((line, 9)),
        pltpu.SemaphoreType.DMA((line, 9)),
    ]
    if tail:
        sems += [
            pltpu.SemaphoreType.DMA((line, 2, 4)),
            pltpu.SemaphoreType.DMA((line, 4)),
            pltpu.SemaphoreType.DMA((line, 4)),
            pltpu.SemaphoreType.DMA((line, 4)),
        ]
    return sems


class Gather:
    def __init__(self, line, x_ref, o_ref, sems, tail=0, own_blocks=None):
        self.line, self.x_ref, self.o_ref, self.tail = line, x_ref, o_ref, tail
        self.own_sem, self.z_send, self.z_recv, self.p_send, self.p_recv = sems[:5]
        if tail:
            self.t_send, self.t_recv, self.q_send, self.q_recv = sems[5:]
        self.own_blocks = own_blocks
        self.z_at = lax.axis_index("fsdp")
        self.me, self.mate, self.near_x, self.near_y, step_x = neighbours()
        self.across = self.near_y + step_x
        self.places = (self.me, self.near_x, self.near_y, self.across)
        self.rows = x_ref.shape[0]
        self.half = self.rows // 2
        self.middle = (self.z_at == 1) | (self.z_at == 2)
        self.first_slot = self.z_at if line > 1 else 0

    def slot(self, order):
        z_at = self.z_at
        if self.line == 1:
            return 0
        second = z_at + 1 - 2 * lax.rem(z_at, 2)
        third = 2 - z_at // 2
        fourth = 3 - 3 * (z_at // 2)
        return jnp.where(
            order == 0, z_at, jnp.where(order == 1, second, jnp.where(order == 2, third, fourth))
        )

    def each(self, order, act):
        if not self.tail:
            act(True)
        elif isinstance(order, int):
            act(order == 0)
        else:
            pl.when(order == 0)(lambda: act(True))
            pl.when(order > 0)(lambda: act(False))

    def span(self, part, whole):
        count = self.rows if whole else self.rows - self.tail
        return ((0, count), (0, self.half), (self.half, count - self.half))[part]

    def there(self, slot, place, start, count):
        at = (slot * 8 + place) * self.rows + start
        return self.o_ref.at[pl.ds(pl.multiple_of(at, 8), count)]

    def z_copy(self, src_ref, slot, way, target):
        return remote(
            src_ref,
            self.there(slot, self.me, *self.span(0, False)),
            self.z_send.at[slot, way],
            self.z_recv.at[slot],
            (self.me, target),
        )

    def own_main(self):
        start, count = self.span(0, False)
        return self.x_ref.at[pl.ds(start, count)]

    def up(self):
        return self.z_copy(self.own_main(), self.z_at, 0, self.z_at + 1)

    def down(self):
        return self.z_copy(self.own_main(), self.z_at, 1, self.z_at - 1)

    def beyond(self, order):
        return jnp.where(order == 1, 3 - self.z_at, 3 * self.z_at - 3)

    def onward(self, order):
        slot = self.slot(order)
        main = self.there(slot, self.me, *self.span(0, False))
        return self.z_copy(main, slot, 0, self.beyond(order))

    def copy(self, order, place, kind, device, part, whole, src_ref=None):
        dst_ref = self.there(self.slot(order), place, *self.span(part, whole))
        return remote(
            dst_ref if src_ref is None else src_ref,
            dst_ref,
            self.p_send.at[order, kind],
            self.p_recv.at[order, kind],
            (device, self.z_at),
        )

    def out(self, order, whole, src_ref=None):
        return [
            self.copy(order, self.me, 0, self.near_x, 0, whole, src_ref),
            self.copy(order, self.me, 1, self.near_y, 0, whole, src_ref),
            self.copy(order, self.me, 2, self.mate, 0, whole, src_ref),
        ]

    def passed(self, order, whole, *which):
        places = (
            (self.near_x, 3, self.near_y, 1),
            (self.near_x, 5, self.mate, 0),
            (self.near_y, 4, self.near_x, 2),
            (self.near_y, 6, self.mate, 0),
            (self.across, 7, self.mate, 1),
            (self.across, 8, self.mate, 2),
        )
        return [self.copy(order, *places[k], whole) for k in which]

    def begin(self, met=False):
        line, z_at = self.line, self.z_at
        if not met:
            greet((self.mate, self.near_x, self.near_y), line, z_at)
        self.own_copy().start()
        if line > 1:
            self.begin_line()
        for copy in self.out(0, True, self.x_ref):
            copy.start()

    def begin_line(self):
        pl.when(self.z_at < self.line - 1)(lambda: self.up().start())
        pl.when(self.z_at > 0)(lambda: self.down().start())

    def own_copy(self):
        return pltpu.make_async_copy(
            self.x_ref, self.there(self.first_slot, self.me, 0, self.rows), self.own_sem
        )

    def own_block(self):
        self.own_copy().wait()

    def from_line(self, order):
        slot = self.slot(order)
        main = self.there(slot, self.me, *self.span(0, False))
        self.z_copy(main, slot, 0, self.z_at).wait_recv()

    def first(self, order):
        at_end = jnp.logical_not(self.middle)
        pl.when(at_end | (order == 1))(lambda: self.from_line(order))

        @pl.when(self.middle & (order == 1))
        def _():
            self.onward(1).start()
            self.from_line(2)
            self.onward(2).start()

        @pl.when(self.middle & (order == 2))
        def _():
            self.from_line(3)
            self.onward(3).start()

        for copy in self.out(order, False):
            copy.start()

    def second(self, order):
        def act(whole):
            to_y, mate_x, to_x, mate_y = self.passed(order, whole, 0, 1, 2, 3)
            self.copy(order, self.near_x, 0, self.near_x, 0, whole).wait_recv()
            to_y.start()
            mate_x.start()
            self.copy(order, self.near_y, 1, self.near_y, 0, whole).wait_recv()
            to_x.start()
            mate_y.start()

        self.each(order, act)

    def tail_copy(self, slot, k, way, target, own=False):
        start = self.rows - self.tail
        dst_ref = self.there(slot, self.places[k], start, self.tail)
        src_ref = dst_ref
        if own and self.own_blocks is not None:
            at = pl.multiple_of(self.places[k] * self.rows + start, 8)
            src_ref = self.own_blocks.at[pl.ds(at, self.tail)]
        return remote(
            src_ref,
            dst_ref,
            self.t_send.at[slot, way, k],
            self.t_recv.at[slot, k],
            (self.me, target),
        )

    def own_tails(self, act):
        z_at = self.z_at
        for k in range(4):
            pl.when(z_at < self.line - 1)(lambda: act(self.tail_copy(z_at, k, 0, z_at + 1, True)))
            pl.when(z_at > 0)(lambda: act(self.tail_copy(z_at, k, 1, z_at - 1, True)))

    def send_tails(self):
        self.own_tails(lambda copy: copy.start())

    def tails_on(self, order):
        return [self.tail_copy(self.slot(order), k, 0, self.beyond(order)) for k in range(4)]

    def tail_to_mate(self, order, k, place):
        ref = self.there(self.slot(order), place, self.rows - self.tail, self.tail)
        return remote(
            ref, ref, self.q_send.at[order, k], self.q_recv.at[order, k], (self.mate, self.z_at)
        )

    def tails(self, order):
        def arrive(one):
            for k in range(4):
                self.tail_copy(self.slot(one), k, 0, self.z_at).wait_recv()

        def on(one):
            for copy in self.tails_on(one):
                copy.start()

        pl.when(jnp.logical_not(self.middle) | (order == 1))(lambda: arrive(order))

        @pl.when(self.middle & (order == 1))
        def _():
            on(1)
            arrive(2)
            on(2)

        @pl.when(self.middle & (order == 2))
        def _():
            arrive(3)
            on(3)

        for k in range(4):
            self.tail_to_mate(order, k, self.places[k]).start()

    def mates_tails(self, order, *which):
        if self.tail:

            @pl.when(order > 0)
            def _():
                for k in which:
                    place = self.places[k] + self.mate - self.me
                    self.tail_to_mate(order, k, place).wait_recv()

    def near(self, order):
        step = self.mate - self.me

        def act(whole):
            self.copy(order, self.mate, 2, self.mate, 0, whole).wait_recv()
            self.copy(order, self.near_x + step, 5, self.mate, 0, whole).wait_recv()

        self.each(order, act)
        self.mates_tails(order, 0, 1)

    def third(self, order):
        step = self.mate - self.me

        def act(whole):
            top, low = self.passed(order, whole, 4, 5)
            self.copy(order, self.across, 3, self.near_y, 1, whole).wait_recv()
            top.start()
            self.copy(order, self.across, 4, self.near_x, 2, whole).wait_recv()
            low.start()
            self.copy(order, self.near_y + step, 6, self.mate, 0, whole).wait_recv()
            self.copy(order, self.across + step, 7, self.mate, 1, whole).wait_recv()
            self.copy(order, self.across + step, 8, self.mate, 2, whole).wait_recv()

        self.each(order, act)
        self.mates_tails(order, 2, 3)

    def end(self, from_order=0):
        line, z_at = self.line, self.z_at

        def sent(order, carry):
            def act(whole):
                for copy in self.out(order, whole) + self.passed(order, whole, 0, 1, 2, 3, 4, 5):
                    copy.wait_send()

            self.each(order, act)
            return carry

        lax.fori_loop(from_order, line, sent, 0)
        if line > 1:
            pl.when(z_at < line - 1)(lambda: self.up().wait_send())
            pl.when(z_at > 0)(lambda: self.down().wait_send())

            @pl.when(self.middle)
            def _():
                for order in range(1, line):
                    self.onward(order).wait_send()

        if self.tail:
            self.own_tails(lambda copy: copy.wait_send())
            for order in range(1, line):
                for k in range(4):
                    self.tail_to_mate(order, k, self.places[k]).wait_send()

            @pl.when(self.middle)
            def _():
                for order in range(1, line):
                    for copy in self.tails_on(order):
                        copy.wait_send()


def line_sems(line):
    return [
        pltpu.SemaphoreType.DMA,
        pltpu.SemaphoreType.DMA((line, 2)),
        pltpu.SemaphoreType.DMA((line,)),
    ]


class Line:
    def __init__(self, x_ref, o_ref, sems):
        self.x_ref, self.o_ref = x_ref, o_ref
        self.own_sem, self.sends, self.receives = sems
        self.me, self.z_at = lax.axis_index("ctx"), lax.axis_index("fsdp")
        self.middle = (self.z_at == 1) | (self.z_at == 2)
        self.slots = (
            self.z_at,
            self.z_at + 1 - 2 * lax.rem(self.z_at, 2),
            2 - self.z_at // 2,
            3 - 3 * (self.z_at // 2),
        )

    def there(self, slot):
        rows = self.x_ref.shape[0]
        return self.o_ref.at[pl.ds(pl.multiple_of(slot * rows, 16), rows)]

    def copy(self, src_ref, slot, way, target):
        return remote(
            src_ref,
            self.there(slot),
            self.sends.at[slot, way],
            self.receives.at[slot],
            (self.me, target),
        )

    def own(self):
        return pltpu.make_async_copy(self.x_ref, self.there(self.z_at), self.own_sem)

    def up(self):
        return self.copy(self.x_ref, self.z_at, 0, self.z_at + 1)

    def down(self):
        return self.copy(self.x_ref, self.z_at, 1, self.z_at - 1)

    def onward(self, order):
        slot = self.slots[order]
        target = 3 - self.z_at if order == 1 else 3 * self.z_at - 3
        return self.copy(self.there(slot), slot, 0, target)

    def begin(self):
        pl.when(self.z_at < 3)(lambda: self.up().start())
        pl.when(self.z_at > 0)(lambda: self.down().start())
        self.own().start()

    def arrive(self, order):
        slot = self.slots[order]
        self.copy(self.there(slot), slot, 0, self.z_at).wait_recv()

    def pass_on(self, *orders):
        @pl.when(self.middle)
        def _():
            for order in orders:
                self.arrive(order)
                self.onward(order).start()

    def rest(self):
        @pl.when(jnp.logical_not(self.middle))
        def _():
            for order in (1, 2, 3):
                self.arrive(order)

    def end(self):
        self.own().wait()
        pl.when(self.z_at < 3)(lambda: self.up().wait_send())
        pl.when(self.z_at > 0)(lambda: self.down().wait_send())

        @pl.when(self.middle)
        def _():
            for order in (1, 2, 3):
                self.onward(order).wait_send()


def gather_blocks(x, line, collective, name):
    rows, width = x.shape

    def kernel(x_ref, o_ref, *sems):
        gather = Gather(line, x_ref, o_ref, sems)
        gather.begin()

        def body(order, carry):
            gather.second(order)
            if line > 1:
                pl.when(order + 1 < line)(lambda: gather.first(order + 1))
            gather.near(order)
            gather.third(order)
            return carry

        lax.fori_loop(0, line, body, 0)
        gather.own_block()
        gather.end()

    return pl.pallas_call(
        kernel,
        out_shape=jax.ShapeDtypeStruct((line * 8 * rows, width), x.dtype),
        in_specs=[pl.BlockSpec(memory_space=pl.ANY)],
        out_specs=pl.BlockSpec(memory_space=pl.ANY),
        scratch_shapes=gather_sems(line),
        compiler_params=pltpu.CompilerParams(collective_id=collective, has_side_effects=True),
        name=name,
    )(x)


CHUNK = 16


def add_rows(dst_ref, src_refs, start, count, out_ref=None):
    def body(i, carry):
        at = pl.ds(pl.multiple_of(start + i * CHUNK, CHUNK), CHUNK)
        value = dst_ref[at, :].astype(jnp.float32)
        for src_ref in src_refs:
            value = value + src_ref[at, :].astype(jnp.float32)
        to_ref = dst_ref if out_ref is None else out_ref
        to_ref[at, :] = value.astype(to_ref.dtype)
        return carry

    lax.fori_loop(0, count // CHUNK, body, 0)


class Scatter:
    def __init__(self, line, x_ref, o_ref, scratch, columns=None):
        self.columns = columns
        (
            self.mine, self.theirs, self.halves, self.from_x, self.from_y, self.from_z, self.total,
            self.load_sem, self.m_send, self.m_recv, self.p_send, self.p_recv, self.z_send,
            self.z_recv, self.out_sem, *rest,
        ) = scratch
        self.tail = 0
        if rest:
            self.from_t, self.t_send, self.t_recv = rest
            self.tail = self.from_t.shape[2]
        self.line, self.x_ref, self.o_ref = line, x_ref, o_ref
        self.z_at = lax.axis_index("fsdp")
        self.me, self.mate, self.near_x, self.near_y, step_x = neighbours()
        self.places = (self.near_y + step_x, self.near_x, self.near_y, self.me)
        self.rows = self.total.shape[0]
        self.half = self.rows // 2
        self.main = self.rows - self.tail
        self.middle = (self.z_at == 1) | (self.z_at == 2)

    def slot(self, order):
        z_at = self.z_at
        if self.line == 1:
            return 0
        far, next_far, near = 3 - 3 * (z_at // 2), 2 - z_at // 2, z_at + 1 - 2 * lax.rem(z_at, 2)
        return jnp.where(
            order == 0, far, jnp.where(order == 1, next_far, jnp.where(order == 2, near, z_at))
        )

    def each(self, order, act):
        if not self.tail:
            act(self.rows)
        elif isinstance(order, int):
            act(self.rows if order == self.line - 1 else self.main)
        else:
            pl.when(order == self.line - 1)(lambda: act(self.rows))
            pl.when(order < self.line - 1)(lambda: act(self.main))

    def there(self, slot, place):
        at = pl.ds(pl.multiple_of((slot * 8 + place) * self.rows, 16), self.rows)
        return self.x_ref.at[at] if self.columns is None else self.x_ref.at[at, self.columns]

    def give(self, order, k):
        return remote(
            self.there(self.slot(order), self.places[k] + self.mate - self.me),
            self.theirs.at[order, k],
            self.m_send.at[order, k],
            self.m_recv.at[order, k],
            (self.mate, self.z_at),
        )

    def load(self, order, k):
        return pltpu.make_async_copy(
            self.there(self.slot(order), self.places[k]),
            self.mine.at[order, k],
            self.load_sem.at[order, k],
        )

    def send(self, order, kind, count):
        top, low = pl.ds(0, self.half), pl.ds(self.half, count - self.half)
        k, part, to, device = (
            (0, top, self.halves, self.near_x),
            (0, low, self.halves, self.near_y),
            (1, top, self.from_x, self.near_x),
            (1, low, self.from_x, self.near_x),
            (2, low, self.from_y, self.near_y),
            (2, top, self.from_y, self.near_y),
        )[kind]
        return remote(
            self.mine.at[order, k, part],
            to.at[order, part],
            self.p_send.at[order, kind],
            self.p_recv.at[order, kind],
            (device, self.z_at),
        )

    def begin(self, met=False):
        if not met:
            greet((self.mate, self.near_x, self.near_y), self.line, self.z_at)

        def body(order, carry):
            for k in range(4):
                self.start_part(order, k)
            return carry

        lax.fori_loop(0, self.line, body, 0)

    def start_part(self, order, k):
        self.give(order, k).start()
        self.load(order, k).start()

    def produce(self, make):
        for k in range(4):
            make(self.places[k] // 2)
            self.start_part(0, k)
            if k > 0:
                self.part(0, k - 1)
        self.part(0, 3)

    def tail_copy(self, order, k, index, target):
        return remote(
            self.mine.at[order, k, pl.ds(self.main, self.tail)],
            self.from_t.at[index, k],
            self.t_send.at[order, k],
            self.t_recv.at[index, k],
            (self.me, target),
        )

    def toward(self, order):
        return jnp.where(order == 2, self.slot(order), self.z_at + 1 - 2 * (self.z_at // 2))

    def tails_out(self, order):
        slot, target = self.slot(order), self.toward(order)
        above = jnp.where((target == slot) & (self.z_at > target), 1, 0)
        index = above * 4 + (1 - above) * slot
        return [self.tail_copy(order, k, index, target) for k in range(4)]

    def tails_on(self, order):
        slot = self.slot(order)
        copies = self.tails_out(order)
        for k in range(4):
            self.tail_copy(order, k, slot, self.z_at).wait_recv()
            add_rows(self.mine.at[order, k, pl.ds(self.main, self.tail)], [self.from_t.at[slot, k]], 0, self.tail)
            copies[k].start()

    def tails_in(self, order, k):
        z_at = self.z_at
        mine = self.mine.at[order, k, pl.ds(self.main, self.tail)]

        @pl.when(z_at > 0)
        def _():
            self.tail_copy(order, k, z_at, z_at).wait_recv()
            add_rows(mine, [self.from_t.at[z_at, k]], 0, self.tail)

        @pl.when(z_at < self.line - 1)
        def _():
            self.tail_copy(order, k, 4, z_at).wait_recv()
            add_rows(mine, [self.from_t.at[4, k]], 0, self.tail)

    def part(self, order, k):
        self.give(order, k).wait_recv()
        self.load(order, k).wait()
        add_rows(self.mine.at[order, k], [self.theirs.at[order, k]], 0, self.rows)
        if self.tail:
            pl.when(order == self.line - 1)(lambda: self.tails_in(order, k))

        def act(count):
            for kind in ((0, 1), (2,), (4,), ())[k]:
                self.send(order, kind, count).start()

        self.each(order, act)

    def first(self, order):
        for k in range(4):
            self.part(order, k)
        if self.tail:

            @pl.when((order < self.line - 1) & jnp.logical_not(self.middle))
            def _():
                for copy in self.tails_out(order):
                    copy.start()

    def second(self, order):
        def act(count):
            self.send(order, 1, count).wait_recv()
            low = count - self.half
            add_rows(self.mine.at[order, 1], [self.halves.at[order]], self.half, low)
            self.send(order, 3, count).start()
            self.send(order, 0, count).wait_recv()
            add_rows(self.mine.at[order, 2], [self.halves.at[order]], 0, self.half)
            self.send(order, 5, count).start()

        self.each(order, act)

    def third(self, order, out_ref=None):
        sources = [self.from_x.at[order], self.from_y.at[order]]

        def act(count):
            for kind in (2, 3, 4, 5):
                self.send(order, kind, count).wait_recv()
            add_rows(self.mine.at[order, 3], sources, 0, count, out_ref)

        self.each(order, act)

    def z_copy(self, order, slot_at, target):
        at = pl.ds(0, self.main)
        return remote(
            self.mine.at[order, 3, at],
            self.from_z.at[slot_at, at],
            self.z_send.at[order],
            self.z_recv.at[slot_at],
            (self.me, target),
        )

    def z_out(self, order):
        z_at, slot, target = self.z_at, self.slot(order), self.toward(order)
        ends = jnp.where(target == slot, 1, 0)
        return self.z_copy(order, ends * (4 + (z_at - target + 1) // 2) + (1 - ends) * slot, target)

    def pass_on(self, order):
        slot = self.slot(order)
        self.z_copy(order, slot, self.z_at).wait_recv()
        add_rows(self.mine.at[order, 3], [self.from_z.at[slot]], 0, self.main)
        self.z_out(order).start()

    def along(self, order):
        @pl.when((order < self.line - 1) & jnp.logical_not(self.middle))
        def _():
            self.z_out(order).start()

        if self.tail:
            pl.when((order == 0) & self.middle)(lambda: self.tails_on(0))

            @pl.when((order == 1) & self.middle)
            def _():
                self.tails_on(1)
                self.tails_on(2)

        pl.when((order == 1) & self.middle)(lambda: self.pass_on(0))

        @pl.when((order == 2) & self.middle)
        def _():
            self.pass_on(1)
            self.pass_on(2)

    def last(self):
        z_at, line = self.z_at, self.line
        pl.when(z_at > 0)(lambda: self.z_copy(line - 1, 4, z_at).wait_recv())
        pl.when(z_at < line - 1)(lambda: self.z_copy(line - 1, 5, z_at).wait_recv())
        mine = self.mine.at[line - 1, 3]
        below, above = self.from_z.at[4], self.from_z.at[5]
        pl.when(z_at == 0)(lambda: add_rows(mine, [above], 0, self.main, self.total))
        pl.when(z_at == line - 1)(lambda: add_rows(mine, [below], 0, self.main, self.total))
        pl.when(self.middle)(lambda: add_rows(mine, [below, above], 0, self.main, self.total))
        if self.tail:
            add_rows(mine, [], self.main, self.tail, self.total)

    def end(self):
        out = pltpu.make_async_copy(self.total, self.o_ref, self.out_sem)
        out.start()

        def sent(order, carry):
            def act(count):
                for kind in range(6):
                    self.send(order, kind, count).wait_send()

            for k in range(4):
                self.give(order, k).wait_send()
            self.each(order, act)
            if self.line > 1:

                @pl.when(order < self.line - 1)
                def _():
                    self.z_out(order).wait_send()
                    if self.tail:
                        for copy in self.tails_out(order):
                            copy.wait_send()

            return carry

        lax.fori_loop(0, self.line, sent, 0)
        out.wait()

    def plane_sum(self, make=None):
        if make is None:
            self.first(0)
        else:
            self.produce(make)
        self.second(0)
        self.third(0, self.total)
        self.end()

    def run(self, work=None, extra=0, met=False, begun=False):
        if not begun:
            self.begin(met)
        if self.line == 1:
            self.plane_sum()
            return
        if not begun:
            self.first(0)

        def body(step, carry):
            order, phase = step // 3, lax.rem(step, 3)

            @pl.when((phase == 0) & (order < self.line))
            def _():
                self.second(order)
                pl.when(order + 1 < self.line)(lambda: self.first(order + 1))

            pl.when((phase == 1) & (order < self.line))(lambda: self.third(order))
            pl.when((phase == 2) & (order < self.line))(lambda: self.along(order))
            if work is not None:
                work(step)
            return carry

        lax.fori_loop(0, 3 * self.line + extra, body, 0)
        self.last()
        self.end()


TAIL = 16


def scatter_scratch(line, rows, width, dtype, tail=TAIL):
    shard = (rows, width)
    made = [
        pltpu.VMEM((line, 4) + shard, dtype),
        pltpu.VMEM((line, 4) + shard, dtype),
        pltpu.VMEM((line,) + shard, dtype),
        pltpu.VMEM((line,) + shard, dtype),
        pltpu.VMEM((line,) + shard, dtype),
        pltpu.VMEM((6 if line > 1 else 1,) + shard, dtype),
        pltpu.VMEM(shard, jnp.float32),
        pltpu.SemaphoreType.DMA((line, 4)),
        pltpu.SemaphoreType.DMA((line, 4)),
        pltpu.SemaphoreType.DMA((line, 4)),
        pltpu.SemaphoreType.DMA((line, 6)),
        pltpu.SemaphoreType.DMA((line, 6)),
        pltpu.SemaphoreType.DMA((line,)),
        pltpu.SemaphoreType.DMA((6,)),
        pltpu.SemaphoreType.DMA,
    ]
    if line > 1 and tail:
        made += [
            pltpu.VMEM((5, 4, tail, width), dtype),
            pltpu.SemaphoreType.DMA((line, 4)),
            pltpu.SemaphoreType.DMA((5, 4)),
        ]
    return made


def scatter_blocks(x, line, collective, name):
    rows, width = x.shape[0] // (line * 8), x.shape[1]

    def kernel(x_ref, o_ref, *scratch):
        Scatter(line, x_ref, o_ref, scratch).run()

    return pl.pallas_call(
        kernel,
        out_shape=jax.ShapeDtypeStruct((rows, width), jnp.float32),
        in_specs=[pl.BlockSpec(memory_space=pl.ANY)],
        out_specs=pl.BlockSpec(memory_space=pl.ANY),
        scratch_shapes=scatter_scratch(line, rows, width, x.dtype),
        compiler_params=pltpu.CompilerParams(
            collective_id=collective, has_side_effects=True, vmem_limit_bytes=52 * MIB
        ),
        name=name,
    )(x)


QUERY_HEADS = 64
KEY_VALUE_HEADS = 8
HEAD_SIZE = 64
TOP = 4
EPSILON = 1e-05
THETA_BASE = 150000.0
CLAMP_LIMIT = 7.0
GLU_ALPHA = 1.702
MASK_FILL = -1e30
SPAN = 256
SCALE = HEAD_SIZE**-0.5


def contract(left, right, left_axis, right_axis):
    return lax.dot_general(
        left, right, (((left_axis,), (right_axis,)), ((), ())), preferred_element_type=jnp.float32
    )


def norm_scale(value_rows, gain_vec):
    return (
        value_rows
        * lax.rsqrt(jnp.mean(value_rows * value_rows, axis=-1, keepdims=True) + EPSILON)
        * gain_vec
    )


def soft_clamp(value_rows):
    return CLAMP_LIMIT * jnp.tanh(value_rows / CLAMP_LIMIT)


def glu_units(gate_lin, up_lin):
    gated = soft_clamp(gate_lin)
    return (soft_clamp(up_lin) + 1.0) * gated * jax.nn.sigmoid(GLU_ALPHA * gated)


def rotary_tables(length):
    half = HEAD_SIZE // 2
    inverse = np.float32(THETA_BASE) ** (-np.arange(half, dtype=np.float32) / np.float32(half))
    angles = inverse[:, None] * np.arange(length, dtype=np.float32)[None, :]
    return jnp.asarray(np.cos(angles)), jnp.asarray(np.sin(angles))


def turned(value, cosine, sine):
    half = HEAD_SIZE // 2
    first, second = value[:, :half], value[:, half:]
    return jnp.concatenate(
        [first * cosine - second * sine, second * cosine + first * sine], axis=1
    )


def diagonal(length):
    return lax.broadcasted_iota(jnp.int32, (length, length), 0) <= lax.broadcasted_iota(
        jnp.int32, (length, length), 1
    )


def masked_scores(key_rows, query_cols, count):
    scores = contract(key_rows, query_cols, 1, 0)
    edge = jnp.where(diagonal(SPAN), scores[count - SPAN :], MASK_FILL)
    if count == SPAN:
        return edge
    return jnp.concatenate([scores[: count - SPAN], edge], axis=0)


def attend_kernel(sink_ref, q_ref, k_ref, v_ref, out_ref, log_ref):
    sink = sink_ref[pl.program_id(0)]
    length = q_ref.shape[1]
    for start in range(0, length, SPAN):
        count = start + SPAN
        at = pl.ds(start, SPAN)
        query = q_ref[:, at] * jnp.bfloat16(SCALE)
        scores = masked_scores(k_ref[:count, :], query, count)
        row_top = jnp.maximum(jnp.max(scores, axis=0, keepdims=True), sink)
        weights = jnp.exp(scores - row_top)
        denominator = jnp.sum(weights, axis=0, keepdims=True) + jnp.exp(sink - row_top)
        probabilities = (weights / denominator).astype(jnp.bfloat16)
        out_ref[:, at] = contract(v_ref[:, :count], probabilities, 1, 0).astype(jnp.bfloat16)
        log_ref[0, :, at] = row_top + jnp.log(denominator)


def attend(sinks, queries, keys, values):
    heads, length = queries.shape[0] // HEAD_SIZE, queries.shape[1]
    per_head = pl.BlockSpec((HEAD_SIZE, length), lambda h: (h, 0))
    return pl.pallas_call(
        attend_kernel,
        grid=(heads,),
        out_shape=(
            jax.ShapeDtypeStruct(queries.shape, jnp.bfloat16),
            jax.ShapeDtypeStruct((heads, 1, length), jnp.float32),
        ),
        in_specs=[
            pl.BlockSpec(memory_space=pltpu.SMEM),
            per_head,
            pl.BlockSpec((length, HEAD_SIZE), lambda h: (0, 0)),
            pl.BlockSpec((HEAD_SIZE, length), lambda h: (0, 0)),
        ],
        out_specs=(per_head, pl.BlockSpec((1, 1, length), lambda h: (h, 0, 0))),
        compiler_params=pltpu.CompilerParams(vmem_limit_bytes=40 * MIB),
        cost_estimate=pl.CostEstimate(
            flops=heads * length * length * HEAD_SIZE * 4,
            bytes_accessed=heads * length * HEAD_SIZE * 4,
            transcendentals=heads * length * length,
        ),
        name="attend",
    )(sinks, queries, keys, values)


def attention(rows_own, grads_own, weights_own, out_own, sinks, cosine, sine, collective):
    low, f32 = jnp.bfloat16, jnp.float32
    block_rows, wide = rows_own.shape
    length = 8 * block_rows
    own_rows = weights_own.shape[0]
    q_rows, width = out_own.shape
    kv_rows = (own_rows - q_rows) // 2
    heads = 4 * q_rows // HEAD_SIZE
    half = HEAD_SIZE // 2
    per_shard = q_rows // HEAD_SIZE

    def kernel(
        sink_ref, rows_ref, grads_ref, weights_ref, out_ref, cos_ref, sin_ref,
        o_ref, all_rows, all_grads, all_weights, all_out, q_ref, k_ref, kt_ref, v_ref, att_ref, log_ref,
        normed_v, weights_v, lin, vt_v, out_v, branch, held_sems, *scratch,
    ):
        plane = Gather(1, rows_ref, all_rows, scratch[:5])
        later = Gather(1, grads_ref, all_grads, scratch[5:10])
        heads_line = Line(weights_ref, all_weights, scratch[10:13])
        line = Line(out_ref, all_out, scratch[13:16])
        scatter = Scatter(1, branch, o_ref, scratch[16:])
        load_rows = pltpu.make_async_copy(all_rows, normed_v, held_sems.at[0])
        load_weights = pltpu.make_async_copy(all_weights, weights_v, held_sems.at[1])
        greet((plane.mate, plane.near_x, plane.near_y), 4, line.z_at)
        heads_line.begin()
        plane.begin(True)
        heads_line.pass_on(1, 2)
        plane.second(0)
        later.begin(True)
        line.begin()
        plane.near(0)
        plane.third(0)
        plane.own_block()
        load_rows.start()
        heads_line.pass_on(3)
        later.second(0)
        later.near(0)
        later.third(0)
        later.own_block()
        heads_line.rest()
        heads_line.end()
        load_weights.start()
        load_rows.wait()
        load_weights.wait()

        def project(i, carry):
            at = pl.ds(pl.multiple_of(i * SPAN, SPAN), SPAN)
            lin[:, at] = contract(weights_v[...], normed_v[at, :], 1, 1)
            return carry

        lax.fori_loop(0, length // SPAN, project, 0)
        line.pass_on(1, 2)

        def turn(value):
            first, second = value[:half], value[half:]
            cosine, sine = cos_ref[...], sin_ref[...]
            return jnp.concatenate(
                [first * cosine - second * sine, second * cosine + first * sine], axis=0
            ).astype(low)

        def shards_of(offset):
            return jnp.concatenate(
                [
                    lin[z * own_rows + offset : z * own_rows + offset + kv_rows, :]
                    for z in range(4)
                ],
                axis=0,
            )

        keys_t = turn(shards_of(q_rows))
        values_t = shards_of(q_rows + kv_rows).astype(low)
        kt_ref[...] = keys_t
        vt_v[...] = values_t
        k_ref[...] = keys_t.T
        v_ref[...] = values_t.T

        def head(h, carry):
            pl.when(h == heads // 2)(lambda: line.pass_on(3))
            start = (h // per_shard) * own_rows + lax.rem(h, per_shard) * HEAD_SIZE
            queries = turn(lin[pl.ds(pl.multiple_of(start, 16), HEAD_SIZE), :])
            rows = pl.ds(pl.multiple_of(h * HEAD_SIZE, HEAD_SIZE), HEAD_SIZE)
            q_ref[rows, :] = queries
            sink = sink_ref[h]
            for begin in range(0, length, SPAN):
                count = begin + SPAN
                query = queries[:, begin:count] * jnp.bfloat16(SCALE)
                scores = masked_scores(k_ref[:count, :], query, count)
                row_top = jnp.maximum(jnp.max(scores, axis=0, keepdims=True), sink)
                chances = jnp.exp(scores - row_top)
                denominator = jnp.sum(chances, axis=0, keepdims=True) + jnp.exp(sink - row_top)
                chances = (chances / denominator).astype(low)
                att_ref[rows, begin:count] = contract(vt_v[:, :count], chances, 1, 0).astype(low)
                log_ref[h, :, begin:count] = row_top + jnp.log(denominator)
            return carry

        lax.fori_loop(0, heads, head, 0)
        line.rest()
        line.end()
        load = pltpu.make_async_copy(all_out, out_v, held_sems.at[0])
        load.start()
        load.wait()

        def give_back(chip):
            at = pl.ds(pl.multiple_of(chip * SPAN, SPAN), SPAN)
            branch[at, :] = contract(att_ref[:, at], out_v[...], 0, 0).astype(low)

        scatter.plane_sum(give_back)
        plane.end()
        later.end()

    hbm = pl.BlockSpec(memory_space=pl.ANY)
    vmem = pl.BlockSpec(memory_space=pltpu.VMEM)
    return pl.pallas_call(
        kernel,
        out_shape=(
            jax.ShapeDtypeStruct((block_rows, width), f32),
            jax.ShapeDtypeStruct((length, wide), low),
            jax.ShapeDtypeStruct((length, wide), low),
            jax.ShapeDtypeStruct((4 * own_rows, wide), low),
            jax.ShapeDtypeStruct((4 * q_rows, width), low),
            jax.ShapeDtypeStruct((4 * q_rows, length), low),
            jax.ShapeDtypeStruct((length, HEAD_SIZE), low),
            jax.ShapeDtypeStruct((HEAD_SIZE, length), low),
            jax.ShapeDtypeStruct((length, HEAD_SIZE), low),
            jax.ShapeDtypeStruct((4 * q_rows, length), low),
            jax.ShapeDtypeStruct((heads, 1, length), f32),
        ),
        in_specs=[pl.BlockSpec(memory_space=pltpu.SMEM), hbm, hbm, hbm, hbm, vmem, vmem],
        out_specs=(hbm,) * 5 + (vmem,) * 6,
        scratch_shapes=[
            pltpu.VMEM((length, wide), low),
            pltpu.VMEM((4 * own_rows, wide), low),
            pltpu.VMEM((4 * own_rows, length), f32),
            pltpu.VMEM((HEAD_SIZE, length), low),
            pltpu.VMEM((4 * q_rows, width), low),
            pltpu.VMEM((length, width), low),
            pltpu.SemaphoreType.DMA((2,)),
            *gather_sems(1),
            *gather_sems(1),
            *line_sems(4),
            *line_sems(4),
            *scatter_scratch(1, block_rows, width, low),
        ],
        compiler_params=pltpu.CompilerParams(
            collective_id=collective, has_side_effects=True, vmem_limit_bytes=58 * MIB
        ),
        name="attention",
    )(sinks, rows_own, grads_own, weights_own, out_own, cosine, sine)


def attend_back_kernel(
    sink_ref, q_ref, k_ref, kt_ref, v_ref, grad_ref, log_ref, cos_ref, sin_ref,
    dq_ref, dk_ref, dv_ref, dsink_ref,
):
    head = pl.program_id(0)
    sink = sink_ref[head]
    length = q_ref.shape[1]
    half = HEAD_SIZE // 2

    @pl.when(head == 0)
    def _():
        dk_ref[...] = jnp.zeros_like(dk_ref)
        dv_ref[...] = jnp.zeros_like(dv_ref)

    grad_sink = jnp.zeros((1, SPAN), jnp.float32)
    for start in range(0, length, SPAN):
        count = start + SPAN
        at = pl.ds(start, SPAN)
        query = q_ref[:, at] * jnp.bfloat16(SCALE)
        grad = grad_ref[:, at]
        log_sum = log_ref[0, :, at]
        probabilities = jnp.exp(masked_scores(k_ref[:count, :], query, count) - log_sum)
        grad_probs = contract(v_ref[:count, :], grad, 1, 0)
        inner_sum = jnp.sum(probabilities * grad_probs, axis=0, keepdims=True)
        grad_scores = (probabilities * (grad_probs - inner_sum)).astype(jnp.bfloat16)
        grad_query = contract(kt_ref[:, :count], grad_scores, 1, 0) * SCALE
        first, second = grad_query[:half], grad_query[half:]
        cosine, sine = cos_ref[:, at], sin_ref[:, at]
        dq_ref[:half, at] = (first * cosine + second * sine).astype(jnp.bfloat16)
        dq_ref[half:, at] = (second * cosine - first * sine).astype(jnp.bfloat16)
        dk_ref[:count, :] += contract(grad_scores, query, 1, 1)
        dv_ref[:count, :] += contract(probabilities.astype(jnp.bfloat16), grad, 1, 1)
        grad_sink = grad_sink - jnp.exp(sink - log_sum) * inner_sum
    dsink_ref[0] = grad_sink


def attend_back(sinks, queries, keys, keys_t, values, grads, log_sums, cosine, sine):
    heads, length = queries.shape[0] // HEAD_SIZE, queries.shape[1]
    per_head = pl.BlockSpec((HEAD_SIZE, length), lambda h: (h, 0))

    def whole(*shape):
        return pl.BlockSpec(shape, lambda h: (0,) * len(shape))

    return pl.pallas_call(
        attend_back_kernel,
        grid=(heads,),
        out_shape=(
            jax.ShapeDtypeStruct(queries.shape, jnp.bfloat16),
            jax.ShapeDtypeStruct((length, HEAD_SIZE), jnp.float32),
            jax.ShapeDtypeStruct((length, HEAD_SIZE), jnp.float32),
            jax.ShapeDtypeStruct((heads, 1, SPAN), jnp.float32),
        ),
        in_specs=[
            pl.BlockSpec(memory_space=pltpu.SMEM),
            per_head,
            whole(length, HEAD_SIZE),
            whole(HEAD_SIZE, length),
            whole(length, HEAD_SIZE),
            per_head,
            pl.BlockSpec((1, 1, length), lambda h: (h, 0, 0)),
            whole(HEAD_SIZE // 2, length),
            whole(HEAD_SIZE // 2, length),
        ],
        out_specs=(
            per_head,
            whole(length, HEAD_SIZE),
            whole(length, HEAD_SIZE),
            pl.BlockSpec((1, 1, SPAN), lambda h: (h, 0, 0)),
        ),
        compiler_params=pltpu.CompilerParams(vmem_limit_bytes=48 * MIB),
        cost_estimate=pl.CostEstimate(
            flops=heads * length * length * HEAD_SIZE * 10,
            bytes_accessed=heads * length * HEAD_SIZE * 8,
            transcendentals=heads * length * length,
        ),
        name="attend_back",
    )(sinks, queries, keys, keys_t, values, grads, log_sums, cosine, sine)


def branch_back(parts, columns, grad_own, out_weights, attended, collective):
    low, f32 = jnp.bfloat16, jnp.float32
    block_rows, width = grad_own.shape
    depth, length = attended.shape
    cut = 512

    def kernel(
        parts_ref, grad_ref, out_ref, att_ref, o_ref, grad_att, grad_out, all_grads, *scratch
    ):
        gather = Gather(1, grad_ref, all_grads, scratch[:5])
        scatter = Scatter(4, parts_ref, o_ref, scratch[5:], pl.ds(0, columns))
        greet((gather.mate, gather.near_x, gather.near_y), 4, gather.z_at)
        gather.begin(True)
        scatter.begin(True)
        gather.second(0)
        scatter.first(0)
        gather.near(0)
        gather.third(0)
        gather.own_block()

        def work(step):
            for i in range(length // SPAN):

                @pl.when(step == i)
                def _():
                    at = slice(i * SPAN, (i + 1) * SPAN)
                    grad_att[:, at] = contract(out_ref[...], all_grads[at, :], 1, 1).astype(low)

            for i in range(-(-width // cut)):

                @pl.when(step == i + length // SPAN)
                def _():
                    at = slice(i * cut, min(width, (i + 1) * cut))
                    grad_out[:, at] = contract(att_ref[...], all_grads[:, at], 1, 0).astype(low)

        steps = length // SPAN + -(-width // cut)
        scatter.run(work, max(0, steps - 12), begun=True)
        gather.end()

    hbm = pl.BlockSpec(memory_space=pl.ANY)
    vmem = pl.BlockSpec(memory_space=pltpu.VMEM)
    return pl.pallas_call(
        kernel,
        out_shape=(
            jax.ShapeDtypeStruct((block_rows, columns), f32),
            jax.ShapeDtypeStruct((depth, length), low),
            jax.ShapeDtypeStruct((depth, width), low),
        ),
        in_specs=[hbm, hbm, vmem, vmem],
        out_specs=(hbm, vmem, vmem),
        scratch_shapes=[
            pltpu.VMEM((length, width), low),
            *gather_sems(1),
            *scatter_scratch(4, block_rows, columns, low),
        ],
        compiler_params=pltpu.CompilerParams(
            collective_id=collective, has_side_effects=True, vmem_limit_bytes=56 * MIB
        ),
        name="branch_back",
    )(parts, grad_own, out_weights, attended)


def attention_back(
    parts, first_column, sinks, queries, keys, keys_t, values, grads, log_sums, cosine, sine, normed,
    own_rows, collective,
):
    low, f32 = jnp.bfloat16, jnp.float32
    length = queries.shape[1]
    heads = queries.shape[0] // HEAD_SIZE
    half = HEAD_SIZE // 2
    block_rows, columns = parts.shape[0] // 32, parts.shape[1] - first_column
    q_rows = queries.shape[0] // 4
    kv_rows = (own_rows - q_rows) // 2
    per_shard = q_rows // HEAD_SIZE
    spans = length // SPAN

    def kernel(
        sink_ref, parts_ref, q_ref, k_ref, kt_ref, v_ref, grad_ref, log_ref, cos_ref, sin_ref, normed_hbm,
        o_ref, lin_ref, weights_ref, dsink_ref, dk_s, dv_s, normed_v, normed_sem, *scratch,
    ):
        load = pltpu.make_async_copy(normed_hbm, normed_v, normed_sem)
        load.start()
        dk_s[...] = jnp.zeros_like(dk_s)
        dv_s[...] = jnp.zeros_like(dv_s)
        dsink_ref[...] = jnp.zeros_like(dsink_ref)

        def one(head, span):
            start, count = span * SPAN, span * SPAN + SPAN
            at = slice(start, count)
            rows = pl.ds(pl.multiple_of(head * HEAD_SIZE, HEAD_SIZE), HEAD_SIZE)
            query = q_ref[rows, at] * jnp.bfloat16(SCALE)
            grad = grad_ref[rows, at]
            log_sum = log_ref[head, :, at]
            chances = jnp.exp(masked_scores(k_ref[:count, :], query, count) - log_sum)
            grad_probs = contract(v_ref[:count, :], grad, 1, 0)
            inner_sum = jnp.sum(chances * grad_probs, axis=0, keepdims=True)
            grad_scores = (chances * (grad_probs - inner_sum)).astype(low)
            grad_query = contract(kt_ref[:, :count], grad_scores, 1, 0) * SCALE
            first, second = grad_query[:half], grad_query[half:]
            cosine, sine = cos_ref[:, at], sin_ref[:, at]
            place = (head // per_shard) * own_rows + lax.rem(head, per_shard) * HEAD_SIZE
            lin_ref[pl.ds(pl.multiple_of(place, 16), HEAD_SIZE), at] = jnp.concatenate(
                [first * cosine + second * sine, second * cosine - first * sine], axis=0
            ).astype(low)
            dk_s[:count, :] += contract(grad_scores, query, 1, 1)
            dv_s[:count, :] += contract(chances.astype(low), grad, 1, 1)
            dsink_ref[head] -= jnp.exp(sink_ref[head] - log_sum) * inner_sum

        def finish():
            grad_keys, grad_values = dk_s[...].T, dv_s[...].T
            first, second = grad_keys[:half], grad_keys[half:]
            cosine, sine = cos_ref[...], sin_ref[...]
            grad_keys = jnp.concatenate(
                [first * cosine + second * sine, second * cosine - first * sine], axis=0
            )
            for z in range(4):
                here = slice(z * kv_rows, (z + 1) * kv_rows)
                start = z * own_rows + q_rows
                lin_ref[start : start + kv_rows, :] = grad_keys[here].astype(low)
                lin_ref[start + kv_rows : start + 2 * kv_rows, :] = grad_values[here].astype(low)
            load.wait()

        wide = normed.shape[1]
        cut = 512

        def work(step):
            first_step = 0
            for span in reversed(range(spans)):
                at_once = max(1, 16 // (span + 1))
                count = -(-heads // at_once)
                here = (step >= first_step) & (step < first_step + count)

                @pl.when(here)
                def _():
                    begin = (step - first_step) * at_once

                    def body(head, carry):
                        pl.when(head < heads)(lambda: one(head, span))
                        return carry

                    lax.fori_loop(begin, begin + at_once, body, 0)

                first_step += count
            pl.when(step == first_step)(finish)
            for i in range(-(-wide // cut)):

                @pl.when(step == first_step + i)
                def _():
                    at = slice(i * cut, min(wide, (i + 1) * cut))
                    weights_ref[:, at] = contract(lin_ref[...], normed_v[:, at], 1, 0).astype(low)

        needed = sum(-(-heads // max(1, 16 // (span + 1))) for span in range(spans))
        needed += -(-wide // cut)
        late = pl.ds(first_column, columns)
        Scatter(4, parts_ref, o_ref, scratch, late).run(work, max(0, needed - 12))

    hbm = pl.BlockSpec(memory_space=pl.ANY)
    vmem = pl.BlockSpec(memory_space=pltpu.VMEM)
    return pl.pallas_call(
        kernel,
        out_shape=(
            jax.ShapeDtypeStruct((block_rows, columns), f32),
            jax.ShapeDtypeStruct((4 * own_rows, length), low),
            jax.ShapeDtypeStruct((4 * own_rows, normed.shape[1]), low),
            jax.ShapeDtypeStruct((heads, 1, SPAN), f32),
        ),
        in_specs=[pl.BlockSpec(memory_space=pltpu.SMEM), hbm] + [vmem] * 8 + [hbm],
        out_specs=(hbm, vmem, vmem, vmem),
        scratch_shapes=[
            pltpu.VMEM((length, HEAD_SIZE), f32),
            pltpu.VMEM((length, HEAD_SIZE), f32),
            pltpu.VMEM(normed.shape, low),
            pltpu.SemaphoreType.DMA,
            *scatter_scratch(4, block_rows, columns, low, 0),
        ],
        compiler_params=pltpu.CompilerParams(
            collective_id=collective, has_side_effects=True, vmem_limit_bytes=60 * MIB
        ),
        name="attention_back",
    )(sinks, parts, queries, keys, keys_t, values, grads, log_sums, cosine, sine, normed)


PAIR = 2
STEP = 4


def routed(cols, capacity):
    expert = lax.axis_index("ctx")
    cols = cols.astype(jnp.float32)
    lane = lax.broadcasted_iota(jnp.int32, cols.shape, 1)
    place = jnp.sum(jnp.where(lane == 64 + expert, cols, 0.0), axis=1, keepdims=True)
    gate = jnp.sum(jnp.where(lane == 72 + expert, cols, 0.0), axis=1, keepdims=True)
    slot = lax.broadcasted_iota(jnp.int32, (cols.shape[0], PAIR * capacity), 1)
    picked = place.astype(jnp.int32) == slot
    return (
        jnp.where(picked, 1.0, 0.0).astype(jnp.bfloat16),
        jnp.where(picked, gate, 0.0).astype(jnp.bfloat16),
    )


class Stream:
    def __init__(self, arrays, sems, inward, first_sem=0):
        self.arrays, self.sems, self.inward, self.first_sem = arrays, sems, inward, first_sem

    def copies(self, slot, block):
        made = []
        for k, (array, slots, count, column) in enumerate(self.arrays):
            at = pl.ds(pl.multiple_of(block * count, 16), count)
            far = array.at[at] if column is None else array.at[at, column]
            pair = (far, slots.at[slot]) if self.inward else (slots.at[slot], far)
            made.append(pltpu.make_async_copy(*pair, self.sems.at[slot, self.first_sem + k]))
        return made

    def start(self, slot, block):
        for copy in self.copies(slot, block):
            copy.start()

    def wait(self, slot, block):
        for copy in self.copies(slot, block):
            copy.wait()


def two_of(shape, dtype):
    return pltpu.VMEM((2,) + shape, dtype)


def experts(sent, sent_grads, own_grads, gate_w, up_w, down_w, gate_b, up_b, down_b, capacity, collective):
    low, f32 = jnp.bfloat16, jnp.float32
    block_rows, wide = sent.shape
    share, width = gate_w.shape
    pad_share = -(-share // 128) * 128
    span = PAIR * block_rows
    pairs = STEP // PAIR
    count = PAIR * capacity
    tokens = 32 * block_rows
    slot_rows = 32 * capacity
    line = 4

    def kernel(
        sent_ref, sent_grads_ref, own_grads_ref, gate_hbm, up_hbm, down_hbm, gate_b_ref, up_b_ref, down_b_ref,
        all_ref, all_grads_ref, rows_out, gate_out, up_out, hidden_out, mix_out,
        grad_rows_out, gate_grad_out, up_grad_out, tokens_out, down_sum, gate_sum, up_sum,
        pair_v, down_v, x_s, rows_s, gate_s, up_s, hidden_s, mix_s, cols_s, gate_gs, up_gs,
        held_sems, in_sems, out_sems, *sems,
    ):
        held = [
            pltpu.make_async_copy(source, target, held_sems.at[k])
            for k, (source, target) in enumerate(
                (
                    (gate_hbm, pair_v.at[pl.ds(0, share)]),
                    (up_hbm, pair_v.at[pl.ds(pad_share, share)]),
                    (down_hbm, down_v),
                )
            )
        ]
        for copy in held:
            copy.start()
        pad = jnp.zeros((pairs * count, pad_share - share), low)
        for k in range(2):
            pair_v[k * pad_share + share : (k + 1) * pad_share, :] = jnp.zeros(
                (pad_share - share, width), low
            )
        forward_in = Stream([(all_ref, x_s, pairs * span, None)], in_sems, True)
        forward_out = Stream(
            [
                (rows_out, rows_s, pairs * count, None),
                (gate_out, gate_s, pairs * count, None),
                (up_out, up_s, pairs * count, None),
                (hidden_out, hidden_s, pairs * count, None),
                (mix_out, mix_s, pairs * span, None),
            ],
            out_sems,
            False,
        )
        kept = [
            (all_ref, cols_s, pairs * span, pl.ds(wide - 128, 128)),
            (gate_out, gate_s, pairs * count, None),
            (up_out, up_s, pairs * count, None),
        ]
        back_kept = Stream(kept, in_sems, True)
        back_own = Stream([(own_grads_ref, x_s, pairs * span, None)], in_sems, True, 3)
        back_far = Stream([(all_grads_ref, x_s, pairs * span, None)], in_sems, True, 3)
        back_out = Stream(
            [
                (grad_rows_out, rows_s, pairs * count, None),
                (gate_grad_out, gate_gs, pairs * count, None),
                (up_grad_out, up_gs, pairs * count, None),
                (tokens_out, mix_s, pairs * span, None),
            ],
            out_sems,
            False,
        )
        down_sum[...] = jnp.zeros_like(down_sum)
        gate_sum[...] = jnp.zeros_like(gate_sum)
        up_sum[...] = jnp.zeros_like(up_sum)
        for slot in range(2):
            mix_s[slot, :, width:] = jnp.zeros((pairs * span, wide - width), low)
        spans = [pl.ds(pair * span, span) for pair in range(pairs)]

        def forward(slot):
            picks = [routed(x_s[slot, at, wide - 128 :], capacity) for at in spans]
            rows = jnp.concatenate(
                [contract(picks[k][0], x_s[slot, spans[k], :], 0, 0) for k in range(pairs)],
                axis=0,
            ).astype(low)
            rows_s[slot] = rows
            rows = rows[:, :width]
            gate_lin = contract(rows, pair_v[:share, :], 1, 1) + gate_b_ref[...].astype(f32)
            up_lin = contract(rows, pair_v[pad_share : pad_share + share, :], 1, 1) + up_b_ref[...].astype(f32)
            gate_s[slot] = gate_lin
            up_s[slot] = up_lin
            hidden = glu_units(gate_lin, up_lin).astype(low)
            hidden_s[slot] = hidden
            out = contract(hidden, down_v[...], 1, 0) + down_b_ref[...]
            for k in range(pairs):
                part = out[k * count : (k + 1) * count].astype(low)
                mix_s[slot, spans[k], :width] = contract(picks[k][1], part, 1, 0).astype(low)

        def backward(slot):
            picks = [routed(cols_s[slot, at, :], capacity) for at in spans]
            rows = jnp.concatenate(
                [contract(picks[k][1], x_s[slot, spans[k], :], 0, 0) for k in range(pairs)],
                axis=0,
            ).astype(low)
            rows_s[slot] = rows
            rows = rows[:, :width]
            down_sum[...] += jnp.sum(rows.astype(f32), axis=0, keepdims=True)
            grad_units = contract(rows, down_v[...], 1, 1)
            gate_tanh = jnp.tanh(gate_s[slot] / CLAMP_LIMIT)
            up_tanh = jnp.tanh(up_s[slot] / CLAMP_LIMIT)
            gated = CLAMP_LIMIT * gate_tanh
            lifted = CLAMP_LIMIT * up_tanh + 1.0
            part = jax.nn.sigmoid(GLU_ALPHA * gated)
            grad_up = (grad_units * gated * part * (1.0 - up_tanh * up_tanh)).astype(low)
            slope = part * (1.0 + GLU_ALPHA * gated * (1.0 - part))
            grad_gate = (grad_units * lifted * slope * (1.0 - gate_tanh * gate_tanh)).astype(low)
            gate_gs[slot] = grad_gate
            up_gs[slot] = grad_up
            gate_sum[...] += jnp.sum(grad_gate.astype(f32), axis=0, keepdims=True)
            up_sum[...] += jnp.sum(grad_up.astype(f32), axis=0, keepdims=True)
            both = jnp.concatenate([grad_gate, pad, grad_up, pad], axis=1)
            copies = contract(both, pair_v[...], 1, 0)
            for k in range(pairs):
                part = copies[k * count : (k + 1) * count].astype(low)
                mix_s[slot, spans[k], :width] = contract(picks[k][0], part, 1, 0).astype(low)

        ahead = Gather(line, sent_ref, all_ref, sems[:9], TAIL)
        back = Gather(line, sent_grads_ref, all_grads_ref, sems[9:], TAIL, own_grads_ref)
        y_at = ahead.me // 4

        def block(step):
            half = lax.rem(step, 2)
            return ahead.slot(step // 2) * 2 + (1 - half) * y_at + half * (1 - y_at)

        ahead.begin()

        steps = 2 * line

        def forward_order(order, carry):
            @pl.when(order < line)
            def _():
                ahead.second(order)
                pl.when(order + 1 < line)(lambda: ahead.first(order + 1))
                pl.when(order > 0)(lambda: ahead.tails(order))
                pl.when(order == 1)(back.begin_line)
                pl.when(order == 2)(back.send_tails)
                pl.when(order == line - 1)(lambda: back.first(1))
                ahead.near(order)

                @pl.when(order == 0)
                def _():
                    ahead.own_block()
                    for copy in held:
                        copy.wait()

                forward_in.start(0, block(2 * order))

            def half_plane(step, carry):
                slot = lax.rem(step, 2)
                forward_in.wait(slot, block(step))
                pl.when(step >= 2)(lambda: forward_out.wait(slot, block(step - 2)))
                forward(slot)
                forward_out.start(slot, block(step))
                return carry

            lax.fori_loop(
                jnp.maximum(2 * order - 1, 0), jnp.minimum(2 * order + 1, steps), half_plane, 0
            )

            @pl.when(order < line)
            def _():
                ahead.third(order)
                pl.when(order == 0)(ahead.send_tails)
                forward_in.start(1, block(2 * order + 1))

            return carry

        lax.fori_loop(0, line + 1, forward_order, 0)
        back.second(1)
        back.first(2)
        forward_out.wait(0, block(steps - 2))
        forward_out.wait(1, block(steps - 1))

        def grads_in(step, act):
            order, half = step // 2, lax.rem(step, 2)
            act(back_kept, half, block(step))
            pl.when(order == 0)(
                lambda: act(back_own, half, (1 - half) * y_at + half * (1 - y_at))
            )
            pl.when(order > 0)(lambda: act(back_far, half, block(step)))

        def backward_step(step, carry):
            order, half = step // 2, lax.rem(step, 2)
            pl.when(half == 1)(lambda: grads_in(step, Stream.start))

            @pl.when(step > 0)
            def _():
                slot = 1 - half
                pl.when(step >= 3)(lambda: back_out.wait(slot, block(step - 3)))
                grads_in(step - 1, Stream.wait)
                backward(slot)
                back_out.start(slot, block(step - 1))

            @pl.when((half == 0) & (order < line))
            def _():
                @pl.when(order > 0)
                def _():
                    back.tails(order)
                    back.near(order)
                    back.third(order)

                grads_in(step, Stream.start)

            @pl.when((half == 1) & (order > 0))
            def _():
                pl.when(order + 1 < line)(lambda: back.second(order + 1))
                pl.when(order + 2 < line)(lambda: back.first(order + 2))

            return carry

        lax.fori_loop(0, steps + 1, backward_step, 0)
        back_out.wait(0, block(steps - 2))
        back_out.wait(1, block(steps - 1))
        ahead.end()
        back.end(1)

    hbm = pl.BlockSpec(memory_space=pl.ANY)
    vmem = pl.BlockSpec(memory_space=pltpu.VMEM)

    def made(rows, columns, dtype=low):
        return jax.ShapeDtypeStruct((rows, columns), dtype)

    return pl.pallas_call(
        kernel,
        out_shape=(
            made(tokens, wide),
            made(tokens, wide),
            made(slot_rows, wide),
            made(slot_rows, share, f32),
            made(slot_rows, share, f32),
            made(slot_rows, share),
            made(tokens, wide),
            made(slot_rows, wide),
            made(slot_rows, share),
            made(slot_rows, share),
            made(tokens, wide),
            made(1, width, f32),
            made(1, share, f32),
            made(1, share, f32),
        ),
        in_specs=[hbm] * 6 + [vmem] * 3,
        out_specs=(hbm,) * 11 + (vmem,) * 3,
        scratch_shapes=[
            pltpu.VMEM((2 * pad_share, width), low),
            pltpu.VMEM(down_w.shape, low),
            two_of((pairs * span, wide), low),
            two_of((pairs * count, wide), low),
            two_of((pairs * count, share), f32),
            two_of((pairs * count, share), f32),
            two_of((pairs * count, share), low),
            two_of((pairs * span, wide), low),
            two_of((pairs * span, 128), low),
            two_of((pairs * count, share), low),
            two_of((pairs * count, share), low),
            pltpu.SemaphoreType.DMA((3,)),
            pltpu.SemaphoreType.DMA((2, 4)),
            pltpu.SemaphoreType.DMA((2, 5)),
            *gather_sems(line, TAIL),
            *gather_sems(line, TAIL),
        ],
        compiler_params=pltpu.CompilerParams(
            collective_id=collective, has_side_effects=True, vmem_limit_bytes=60 * MIB
        ),
        name="experts",
    )(sent, sent_grads, own_grads, gate_w, up_w, down_w, gate_b, up_b, down_b)


def expert_weights(parts, rows_in, gate_grad, up_grad, rows_grad, hidden, collective):
    low, f32 = jnp.bfloat16, jnp.float32
    slot_rows, wide = rows_in.shape
    share = gate_grad.shape[1]
    block_rows, width = parts.shape[0] // 32, parts.shape[1]
    cut = 256
    whole, rest = wide // cut, wide % cut
    count = whole + 1

    def kernel(
        parts_ref, rows_hbm, gate_hbm, up_hbm, grad_hbm, hidden_hbm, o_ref, gate_out, up_out, down_out,
        stage, first_t, second_t, in_s, first_s, second_s, held_sem, in_sems, out_sems, *scratch,
    ):
        def held(source):
            return pltpu.make_async_copy(source, stage, held_sem)

        held(gate_hbm).start()

        def begin(copy):
            copy.start()

        def await_it(copy):
            copy.wait()

        def by_width(index, act):
            pl.when((index >= 0) & (index < whole))(lambda: act(cut))
            pl.when(index == whole)(lambda: act(rest))

        def loads(chunk, act):
            slot = lax.rem(chunk, 2)
            for source, index in ((rows_hbm, chunk), (grad_hbm, chunk - count)):

                def one(columns):
                    at = pl.ds(pl.multiple_of(index * cut, cut), columns)
                    here = in_s.at[slot, :, pl.ds(0, columns)]
                    act(pltpu.make_async_copy(source.at[:, at], here, in_sems.at[slot]))

                by_width(index, one)

        def stores(chunk, act):
            slot = lax.rem(chunk, 2)
            for targets, index in (
                (((first_s, gate_out), (second_s, up_out)), chunk),
                (((first_s, down_out),), chunk - count),
            ):

                def one(columns):
                    at = pl.ds(pl.multiple_of(index * cut, cut), columns)
                    for k, (source, target) in enumerate(targets):
                        here = source.at[slot, :, pl.ds(0, columns)]
                        act(pltpu.make_async_copy(here, target.at[:, at], out_sems.at[slot, k]))

                by_width(index, one)

        def work(chunk):
            slot = lax.rem(chunk, 2)

            @pl.when(chunk == 0)
            def _():
                loads(0, begin)
                held(gate_hbm).wait()
                first_t[...] = stage[...].T
                held(up_hbm).start()
                held(up_hbm).wait()
                second_t[...] = stage[...].T
                held(hidden_hbm).start()

            @pl.when(chunk == count)
            def _():
                held(hidden_hbm).wait()
                first_t[...] = stage[...].T

            pl.when(chunk + 1 < 2 * count)(lambda: loads(chunk + 1, begin))
            pl.when(chunk >= 2)(lambda: stores(chunk - 2, await_it))
            loads(chunk, await_it)
            first_s[slot] = contract(first_t[...], in_s[slot], 1, 0).astype(low)

            @pl.when(chunk < count)
            def _():
                second_s[slot] = contract(second_t[...], in_s[slot], 1, 0).astype(low)

            stores(chunk, begin)

        def works(step):
            def body(chunk, carry):
                work(chunk)
                return carry

            lax.fori_loop(2 * step, 2 * step + 2, body, 0)

        Scatter(4, parts_ref, o_ref, scratch).run(works, count - 12)
        stores(2 * count - 2, await_it)
        stores(2 * count - 1, await_it)

    hbm = pl.BlockSpec(memory_space=pl.ANY)
    return pl.pallas_call(
        kernel,
        out_shape=(
            jax.ShapeDtypeStruct((block_rows, width), f32),
            jax.ShapeDtypeStruct((share, wide), low),
            jax.ShapeDtypeStruct((share, wide), low),
            jax.ShapeDtypeStruct((share, wide), low),
        ),
        in_specs=[hbm] * 6,
        out_specs=(hbm,) * 4,
        scratch_shapes=[
            pltpu.VMEM(gate_grad.shape, low),
            pltpu.VMEM(gate_grad.shape[::-1], low),
            pltpu.VMEM(gate_grad.shape[::-1], low),
            two_of((slot_rows, cut), low),
            two_of((share, cut), low),
            two_of((share, cut), low),
            pltpu.SemaphoreType.DMA,
            pltpu.SemaphoreType.DMA((2,)),
            pltpu.SemaphoreType.DMA((2, 2)),
            *scatter_scratch(4, block_rows, width, low),
        ],
        compiler_params=pltpu.CompilerParams(
            collective_id=collective, has_side_effects=True, vmem_limit_bytes=60 * MIB
        ),
        name="expert_weights",
    )(parts, rows_in, gate_grad, up_grad, rows_grad, hidden)


def product_kernel(left_ref, right_ref, out_ref):
    right = right_ref[:, : out_ref.shape[1]]
    out_ref[...] = contract(left_ref[...], right, 0, 0).astype(out_ref.dtype)


def product(left_t, right, name, columns=None):
    depth, rows = left_t.shape
    columns = columns or right.shape[1]
    return pl.pallas_call(
        product_kernel,
        grid=(rows // SPAN,),
        out_shape=jax.ShapeDtypeStruct((rows, columns), jnp.bfloat16),
        in_specs=[
            pl.BlockSpec((depth, SPAN), lambda i: (0, i)),
            pl.BlockSpec(right.shape, lambda i: (0, 0), pipeline_mode=pl.Buffered(1)),
        ],
        out_specs=pl.BlockSpec((SPAN, columns), lambda i: (i, 0)),
        compiler_params=pltpu.CompilerParams(vmem_limit_bytes=40 * MIB),
        cost_estimate=pl.CostEstimate(
            flops=2 * depth * rows * columns, bytes_accessed=4 * rows * columns, transcendentals=0
        ),
        name=name,
    )(left_t, right)


def finish_kernel(
    width, grads_ref, out_grads_ref, query_ref, key_ref, value_ref, bias_ref, out_ref
):
    grads = grads_ref[...].astype(jnp.float32)
    q_rows = query_ref.shape[1]
    kv_rows = key_ref.shape[0]
    query_ref[...] = grads[:q_rows, :width].T
    key_ref[...] = grads[q_rows : q_rows + kv_rows, :width]
    value_ref[...] = grads[q_rows + kv_rows :, :width]
    lane = width // 128 * 128
    bias_ref[...] = grads[:, lane : lane + 128].T[width - lane : width - lane + 1, :]
    out_ref[...] = out_grads_ref[...].astype(jnp.float32).T


def finished(grads, out_grads, q_rows):
    rows = grads.shape[0]
    width = out_grads.shape[1]
    kv_rows = (rows - q_rows) // 2
    vmem = pl.BlockSpec(memory_space=pltpu.VMEM)
    return pl.pallas_call(
        lambda *refs: finish_kernel(width, *refs),
        out_shape=tuple(
            jax.ShapeDtypeStruct(shape, jnp.float32)
            for shape in (
                (width, q_rows), (kv_rows, width), (kv_rows, width), (1, rows), (width, out_grads.shape[0]),
            )
        ),
        in_specs=[vmem] * 2,
        out_specs=(vmem,) * 5,
        compiler_params=pltpu.CompilerParams(vmem_limit_bytes=32 * MIB),
        name="finished",
    )(grads, out_grads)


def input_back(grad_lin, weights, normed, rows_in, gain, grad_rows, collective, small):
    low, f32 = jnp.bfloat16, jnp.float32
    depth, length = grad_lin.shape
    block_rows, width = rows_in.shape
    wide = normed.shape[1]
    columns = small.shape[1]
    gain_columns = -(-wide // (16 * 128)) * 128

    def kernel(
        lin_ref, weights_ref, normed_hbm, small_ref, rows_ref, gain_ref, grad_ref, o_ref, all_sums,
        result_ref,
        normed_v, part, found_v, sums_v, grad_v, sem, *scratch,
    ):
        gather = Gather(4, sums_v, all_sums, scratch[:5])
        scatter = Scatter(1, part, o_ref, scratch[5:])
        loads = []
        for k in range(4):
            at = pl.ds(pl.multiple_of(scatter.places[k] // 2 * SPAN, SPAN), SPAN)
            loads.append(pltpu.make_async_copy(normed_hbm.at[at], normed_v.at[at], sem.at[k]))
            loads[k].start()
        greet((gather.mate, gather.near_x, gather.near_y), 4, gather.z_at)
        found_v[...] = jnp.zeros_like(found_v)

        def make(chip):
            at = pl.ds(pl.multiple_of(chip * SPAN, SPAN), SPAN)
            value = contract(lin_ref[:, at], weights_ref[...], 0, 0)
            part[at, :] = value[:, :width].astype(low)
            loads.pop(0).wait()
            found = value * normed_v[at, :].astype(f32)
            found_v[...] += jnp.sum(found, axis=0, keepdims=True)

        scatter.produce(make)
        sums_v[:, :columns] = small_ref[...]
        sums_v[:, columns:] = jnp.zeros((16, gain_columns), f32)
        for k in range(wide // 128):
            row, lane = k // (gain_columns // 128), k % (gain_columns // 128) * 128
            sums_v[row : row + 1, columns + lane : columns + lane + 128] = found_v[
                :, k * 128 : (k + 1) * 128
            ]
        gather.begin(True)
        for order in (1, 2, 3):
            gather.first(order)
        for order in range(4):
            gather.second(order)
        scatter.second(0)
        for order in range(4):
            gather.near(order)
            gather.third(order)
        scatter.third(0, scatter.total)

        def through_norm(i, carry):
            at = pl.ds(pl.multiple_of(i * CHUNK, CHUNK), CHUNK)
            value = rows_ref[at, :].astype(f32)
            scale = lax.rsqrt(jnp.mean(value * value, axis=-1, keepdims=True) + EPSILON)
            grad = scatter.total[at, :] * gain_ref[...]
            inner = jnp.mean(grad * value, axis=-1, keepdims=True)
            grad_v[at, :] = (
                grad_ref[at, :] + grad * scale - value * (scale * scale * scale * inner)
            )
            return carry

        lax.fori_loop(0, block_rows // CHUNK, through_norm, 0)
        result_ref[...] = grad_v[...].T
        scatter.end()
        gather.own_block()
        gather.end()

    hbm = pl.BlockSpec(memory_space=pl.ANY)
    vmem = pl.BlockSpec(memory_space=pltpu.VMEM)
    return pl.pallas_call(
        kernel,
        out_shape=(
            jax.ShapeDtypeStruct((block_rows, width), f32),
            jax.ShapeDtypeStruct((32 * 16, columns + gain_columns), f32),
            jax.ShapeDtypeStruct((width, block_rows), f32),
        ),
        in_specs=[vmem, vmem, hbm] + [vmem] * 4,
        out_specs=(hbm, hbm, vmem),
        scratch_shapes=[
            pltpu.VMEM((length, wide), low),
            pltpu.VMEM((length, width), low),
            pltpu.VMEM((1, wide), f32),
            pltpu.VMEM((16, columns + gain_columns), f32),
            pltpu.VMEM((block_rows, width), f32),
            pltpu.SemaphoreType.DMA((4,)),
            *gather_sems(4),
            *scatter_scratch(1, block_rows, width, low),
        ],
        compiler_params=pltpu.CompilerParams(
            collective_id=collective, has_side_effects=True, vmem_limit_bytes=58 * MIB
        ),
        name="input_back",
    )(grad_lin, weights, normed, small, rows_in, gain, grad_rows)


def shards(
    layer_input, cotangent, gate_weights, routes, w_query, key_projection, value_projection, w_out,
    b_query, key_bias_vector, value_bias_vector, b_out, learned_sink_logits, gain_attn, gain_ffn,
    w_gate, w_up, w_down, b_gate, b_up, b_down,
):
    low = jnp.bfloat16
    ctx_n, z_n = lax.axis_size("ctx"), lax.axis_size("fsdp")
    ctx_at, z_at = lax.axis_index("ctx"), lax.axis_index("fsdp")
    tuned = ctx_n == 8 and z_n == 4
    width = layer_input.shape[-1]
    rows = layer_input.shape[0] * layer_input.shape[1]
    length = rows * ctx_n
    blocks = ctx_n * z_n
    capacity = max(2, rows * TOP * 17 // (16 * ctx_n))
    heads = QUERY_HEADS // ctx_n
    spread = ctx_n // KEY_VALUE_HEADS
    f32 = jnp.float32

    def gather_plane(value, call):
        if tuned:
            return gather_blocks(value, 1, call, f"gather_plane_{call}")
        return lax.all_gather(value, "ctx", axis=0, tiled=True)

    def scatter_plane(value, call):
        if tuned:
            return scatter_blocks(value, 1, call, f"scatter_plane_{call}")
        return lax.psum_scatter(value, "ctx", scatter_dimension=0, tiled=True).astype(f32)

    residual = layer_input.reshape(rows, width).astype(f32)
    grad_final = cotangent.reshape(rows, width)
    gain_attn_f, gain_ffn_f = gain_attn.astype(f32), gain_ffn.astype(f32)
    cosine, sine = rotary_tables(length)

    q_cols, k_cols = w_query.shape[1], key_projection.shape[1]
    own_rows = q_cols + 2 * k_cols
    wide = -(-(width + 2 * ctx_n) // 128) * 128
    biases = jnp.concatenate([b_query, key_bias_vector, value_bias_vector])
    own_weights = jnp.concatenate([w_query, key_projection, value_projection], axis=1).T
    own_weights = jnp.concatenate(
        [own_weights, biases[:, None], jnp.zeros((own_rows, wide - width - 1), low)], axis=1
    )
    ones = jnp.concatenate(
        [jnp.ones((rows, 1), low), jnp.zeros((rows, wide - width - 1), low)], axis=1
    )

    token_routes = routes.reshape(rows, TOP)
    names = jnp.arange(ctx_n, dtype=jnp.int32)
    named = token_routes[:, :, None] == names[None, None, :]
    hits = jnp.sum(named.astype(f32), axis=1)
    gates = jnp.sum(
        jnp.where(named, gate_weights.reshape(rows, TOP)[:, :, None].astype(f32), 0.0), axis=1
    )
    earlier = (
        lax.broadcasted_iota(jnp.int32, (rows, rows), 0)
        > lax.broadcasted_iota(jnp.int32, (rows, rows), 1)
    ).astype(low)
    places = jnp.dot(earlier, hits.astype(low), preferred_element_type=f32)
    first_slot = (lax.rem(ctx_at, PAIR) * capacity).astype(f32) if tuned else 0.0
    places = jnp.where(hits > 0, places + first_slot, -1.0)
    slot_rows = blocks * capacity
    if not tuned:
        slots = jnp.arange(capacity, dtype=f32)[None, :, None]
        picked = places.T[:, None, :] == slots
        select = picked.astype(low)
        mixing = jnp.where(picked, gates.T[:, None, :], 0.0).astype(low)

    def exchanged(slot_values):
        moved = slot_values.reshape(ctx_n, capacity, width)
        return lax.all_to_all(moved, "ctx", split_axis=0, concat_axis=0, tiled=True)

    def to_slots(picks, token_rows):
        dims = (((2,), (0,)), ((), ()))
        moved = lax.dot_general(picks, token_rows, dims, preferred_element_type=f32).astype(low)
        moved = lax.all_gather(exchanged(moved), "fsdp", axis=0, tiled=True)
        return moved.reshape(slot_rows, width)

    def to_tokens(picks, slot_values):
        slot_values = exchanged(
            lax.psum_scatter(slot_values, "fsdp", scatter_dimension=0, tiled=True)
        )
        dims = (((1,), (1,)), ((0,), (0,)))
        moved = lax.dot_general(picks, slot_values, dims, preferred_element_type=f32)
        return jnp.sum(moved, axis=0)

    normed_own = jnp.concatenate([norm_scale(residual, gain_attn_f).astype(low), ones], axis=1)
    sinks = lax.dynamic_slice(learned_sink_logits.astype(f32), (ctx_at * heads,), (heads,))
    swap = [(i, i ^ 1) for i in range(ctx_n)]
    odd = lax.rem(ctx_at, 2) == 1
    if tuned:
        sent_grads = jnp.pad(grad_final, ((0, 0), (0, wide - width)))
        branch, normed_attn, own_grads, head_weights, out_weights, *kept = attention(
            normed_own, sent_grads, own_weights, w_out, sinks, cosine, sine, 1
        )
        queries, keys, keys_t, values, attended, log_sums = kept
    else:
        normed_attn = lax.all_gather(normed_own, "ctx", axis=0, tiled=True)
        head_weights = lax.all_gather(own_weights, "fsdp", axis=0, tiled=True)
        out_weights = lax.all_gather(w_out, "fsdp", axis=0, tiled=True)
        lin = contract(head_weights, normed_attn, 1, 1).reshape(z_n, own_rows, length)
        query_lin = lin[:, :q_cols].reshape(heads, HEAD_SIZE, length)
        kv_lin = jnp.stack([lin[:, q_cols : q_cols + k_cols], lin[:, q_cols + k_cols :]])
        kv_lin = kv_lin.reshape(2, z_n * k_cols, length)
        if spread == 2:
            other = lax.ppermute(kv_lin, "ctx", swap)
            kv_lin = jnp.where(
                odd,
                jnp.concatenate([other, kv_lin], axis=1),
                jnp.concatenate([kv_lin, other], axis=1),
            )
        queries = turned(query_lin, cosine, sine).astype(low).reshape(heads * HEAD_SIZE, length)
        keys_t = turned(kv_lin[:1], cosine, sine)[0].astype(low)
        values_t = kv_lin[1].astype(low)
        keys, values = keys_t.T, values_t.T
        attended, log_sums = attend(sinks, queries, keys, values_t)
        branch = scatter_plane(product(attended, out_weights, "branch"), 2)
    middle = residual + branch + b_out.astype(f32)
    normed_ffn = norm_scale(middle, gain_ffn_f).astype(low)

    gate_w, up_w, down_w = w_gate[0].T, w_up[0].T, w_down[0]
    share = b_down.shape[1]
    down_bias = lax.dynamic_update_slice(
        jnp.zeros((1, width), f32), b_down.astype(f32), (0, z_at * share)
    )
    if tuned:
        sent = jnp.concatenate(
            [
                normed_ffn,
                places.astype(low),
                gates.astype(low),
                jnp.zeros((rows, wide - width - 2 * ctx_n), low),
            ],
            axis=1,
        )
        made = experts(
            sent, sent_grads, own_grads, gate_w, up_w, down_w, b_gate, b_up, down_bias, capacity, 3
        )
        expert_in, hidden_units, mix_part = made[2], made[5], made[6]
        grad_expert_out, grad_gate_lin, grad_up_lin, grad_normed_part = made[7:11]
        grad_biases = made[11:]
        grad_b_down, grad_b_gate, grad_b_up = [value[0] for value in grad_biases]
        grad_normed_ffn, grad_w_gate, grad_w_up, grad_w_down = expert_weights(
            grad_normed_part, expert_in, grad_gate_lin, grad_up_lin, grad_expert_out, hidden_units, 6
        )
        grad_normed_ffn = grad_normed_ffn[:, :width]
    else:
        expert_in = to_slots(select, normed_ffn)
        gate_lin = contract(expert_in, gate_w, 1, 1) + b_gate.astype(f32)
        up_lin = contract(expert_in, up_w, 1, 1) + b_up.astype(f32)
        hidden_f, unit_back = jax.vjp(glu_units, gate_lin, up_lin)
        hidden_units = hidden_f.astype(low)
        expert_out = (contract(hidden_units, down_w, 1, 0) + down_bias).astype(low)
        expert_mix = to_tokens(mixing, expert_out)
        grad_expert_out = to_slots(mixing, grad_final)
        grad_units = contract(grad_expert_out, down_w, 1, 1)
        grad_gate_f, grad_up_f = unit_back(grad_units)
        grad_gate_lin, grad_up_lin = grad_gate_f.astype(low), grad_up_f.astype(low)
        grad_copy = contract(grad_gate_lin, gate_w, 1, 0) + contract(grad_up_lin, up_w, 1, 0)
        grad_normed_ffn = to_tokens(select, grad_copy.astype(low))
        grad_b_down = jnp.sum(grad_expert_out.astype(f32), axis=0)
        grad_b_gate = jnp.sum(grad_gate_lin.astype(f32), axis=0)
        grad_b_up = jnp.sum(grad_up_lin.astype(f32), axis=0)
        grad_w_gate = contract(grad_gate_lin, expert_in, 0, 0)
        grad_w_up = contract(grad_up_lin, expert_in, 0, 0)
        grad_w_down = contract(hidden_units, grad_expert_out, 0, 0)
    grad_b_down = lax.dynamic_slice(grad_b_down, (z_at * share,), (share,))

    unused, norm_back = jax.vjp(norm_scale, middle, gain_ffn_f)
    grad_middle_part, grad_gain_ffn = norm_back(grad_normed_ffn)
    grad_middle = grad_final.astype(f32) + grad_middle_part
    grad_branch_own = grad_middle.astype(low)
    grad_b_out = jnp.sum(grad_branch_own.astype(f32), axis=0)
    if tuned:
        early = 1536
        first_mix, grad_attended, grad_out_part = branch_back(
            mix_part, early, grad_branch_own, out_weights, attended, 7
        )
        late_mix, grad_lin, grad_weights, grad_sink_parts = attention_back(
            mix_part, early, sinks, queries, keys, keys_t, values, grad_attended, log_sums, cosine,
            sine, normed_attn, own_rows, 5,
        )
        expert_mix = jnp.concatenate([first_mix, late_mix[:, : width - early]], axis=1)
    else:
        grad_branch = lax.all_gather(grad_branch_own, "ctx", axis=0, tiled=True)
        grad_attended = contract(out_weights, grad_branch, 1, 1).astype(low)
        grad_out_part = contract(attended, grad_branch, 1, 0).astype(low)
        grad_query, grad_keys, grad_values, grad_sink_parts = attend_back(
            sinks, queries, keys, keys_t, values, grad_attended, log_sums, cosine, sine
        )
        grad_kv = jnp.stack([turned(grad_keys.T[None], cosine, -sine)[0], grad_values.T])
        if spread == 2:
            grad_kv = grad_kv + lax.ppermute(grad_kv, "ctx", swap)
            halves = grad_kv.reshape(2, 2, HEAD_SIZE // 2, length)
            grad_kv = jnp.where(odd, halves[:, 1], halves[:, 0])
        grad_kv = grad_kv.astype(low).reshape(2, z_n, k_cols, length)
        grad_lin = jnp.concatenate(
            [grad_query.reshape(z_n, q_cols, length), grad_kv[0], grad_kv[1]], axis=1
        ).reshape(z_n * own_rows, length)
        grad_weights = contract(grad_lin, normed_attn, 1, 0).astype(low)
    final_out = (middle + expert_mix).astype(low).reshape(layer_input.shape)
    own_out_grads = lax.psum_scatter(grad_out_part, "fsdp", scatter_dimension=0, tiled=True)
    own_grads = lax.psum_scatter(grad_weights, "fsdp", scatter_dimension=0, tiled=True)
    if tuned:
        grad_w_query, grad_w_key, grad_w_value, own_bias_grads, grad_w_out = finished(
            own_grads, own_out_grads, q_cols
        )
        own_bias_grads, grad_w_out = own_bias_grads[0], grad_w_out.T
    else:
        own_grads = own_grads.astype(f32)
        grad_w_out = own_out_grads.astype(f32)
        grad_w_query = own_grads[:q_cols, :width].T
        grad_w_key = own_grads[q_cols : q_cols + k_cols, :width]
        grad_w_value = own_grads[q_cols + k_cols :, :width]
        own_bias_grads = own_grads[:, width]
    grad_w_key, grad_w_value = grad_w_key.T, grad_w_value.T
    grad_sinks = lax.dynamic_update_slice(
        jnp.zeros((QUERY_HEADS,), f32), jnp.sum(grad_sink_parts, axis=(1, 2)), (ctx_at * heads,)
    )
    sums = (grad_b_out, grad_gain_ffn, grad_sinks)
    if tuned:
        joined = jnp.concatenate(sums)
        columns = -(-joined.shape[0] // (16 * 128)) * 128
        joined = jnp.pad(joined, (0, 16 * columns - joined.shape[0])).reshape(16, columns)
        unused, joined, input_grad = input_back(
            grad_lin, head_weights, normed_attn, layer_input.reshape(rows, width),
            gain_attn_f.reshape(1, width), grad_middle, 8, joined,
        )
        input_grad = input_grad.T.reshape(layer_input.shape)
        joined = jnp.sum(joined.reshape(blocks, 16, -1), axis=0)
        grad_gain_attn = joined[:, columns:].reshape(-1)[:width] / gain_attn_f
        joined = joined[:, :columns].reshape(-1)
        cuts = (width, 2 * width, 2 * width + QUERY_HEADS)
        sums = [joined[at - value.shape[0] : at] for at, value in zip(cuts, sums)]
    else:
        grad_normed_part = product(grad_lin, head_weights, "grad_normed", width)
        grad_normed_attn = scatter_plane(grad_normed_part, 8)
        unused, norm_back = jax.vjp(norm_scale, residual, gain_attn_f)
        grad_residual_part, own_gain = norm_back(grad_normed_attn)
        input_grad = (grad_middle + grad_residual_part).reshape(layer_input.shape)
        *sums, grad_gain_attn = lax.psum((*sums, own_gain), ("ctx", "fsdp"))
    grad_b_out, grad_gain_ffn, grad_sink_logits = sums
    return (
        final_out,
        input_grad,
        grad_w_query,
        grad_w_key,
        grad_w_value,
        grad_w_out,
        own_bias_grads[:q_cols],
        own_bias_grads[q_cols : q_cols + k_cols],
        own_bias_grads[q_cols + k_cols :],
        grad_b_out,
        grad_sink_logits,
        grad_gain_attn,
        grad_gain_ffn,
        grad_w_gate[:, :width].astype(f32).T[None],
        grad_w_up[:, :width].astype(f32).T[None],
        grad_w_down[:, :width].astype(f32)[None],
        grad_b_gate[None],
        grad_b_up[None],
        grad_b_down[None],
    )


def solution(mesh):
    return jax.shard_map(
        shards,
        mesh=mesh,
        in_specs=(
            P("fsdp", "ctx", None),
            P("fsdp", "ctx", None),
            P("fsdp", "ctx", None),
            P("fsdp", "ctx", None),
            P(None, ("ctx", "fsdp")),
            P(None, ("ctx", "fsdp")),
            P(None, ("ctx", "fsdp")),
            P(("ctx", "fsdp"), None),
            P(("ctx", "fsdp")),
            P(("ctx", "fsdp")),
            P(("ctx", "fsdp")),
            P(),
            P(),
            P(),
            P(),
            P("ctx", None, "fsdp"),
            P("ctx", None, "fsdp"),
            P("ctx", "fsdp", None),
            P("ctx", "fsdp"),
            P("ctx", "fsdp"),
            P("ctx", "fsdp"),
        ),
        out_specs=(
            P("fsdp", "ctx", None),
            P("fsdp", "ctx", None),
            P(None, ("ctx", "fsdp")),
            P(None, ("ctx", "fsdp")),
            P(None, ("ctx", "fsdp")),
            P(("ctx", "fsdp"), None),
            P(("ctx", "fsdp")),
            P(("ctx", "fsdp")),
            P(("ctx", "fsdp")),
            P(),
            P(),
            P(),
            P(),
            P("ctx", None, "fsdp"),
            P("ctx", None, "fsdp"),
            P("ctx", "fsdp", None),
            P("ctx", "fsdp"),
            P("ctx", "fsdp"),
            P("ctx", "fsdp"),
        ),
        check_vma=False,
    )
```

```python
import jax
import jax.numpy as jnp
import numpy as np
from jax import lax
from jax.experimental import pallas as pl
from jax.experimental.pallas import tpu as pltpu
from jax.sharding import PartitionSpec as P

MESH = pl.DeviceIdType.MESH
MIB = 1 << 20


def remote(src, dst, send_sem, recv_sem, device):
    return pltpu.make_async_remote_copy(
        src_ref=src,
        dst_ref=dst,
        send_sem=send_sem,
        recv_sem=recv_sem,
        device_id=device,
        device_id_type=MESH,
    )


def neighbours():
    me = lax.axis_index("ctx")
    core = lax.rem(me, 2)
    x_at = lax.rem(me // 2, 2)
    y_at = me // 4
    return me, me + 1 - 2 * core, me + 2 - 4 * x_at, me + 4 - 8 * y_at, 2 - 4 * x_at


def greet(others, line, z_at):
    barrier = pltpu.get_barrier_semaphore()
    for other in others:
        pl.semaphore_signal(barrier, 1, device_id=(other, z_at), device_id_type=MESH)
    if line == 1:
        pl.semaphore_wait(barrier, len(others))
        return
    me = lax.axis_index("ctx")

    @pl.when(z_at > 0)
    def _():
        pl.semaphore_signal(barrier, 1, device_id=(me, z_at - 1), device_id_type=MESH)

    @pl.when(z_at < line - 1)
    def _():
        pl.semaphore_signal(barrier, 1, device_id=(me, z_at + 1), device_id_type=MESH)

    inner = (lax.rem(z_at, 3) + 1) // 2
    pl.semaphore_wait(barrier, len(others) + 1 + inner)


def gather_sems(line, tail=0):
    sems = [
        pltpu.SemaphoreType.DMA,
        pltpu.SemaphoreType.DMA((line, 2)),
        pltpu.SemaphoreType.DMA((line,)),
        pltpu.SemaphoreType.DMA((line, 9)),
        pltpu.SemaphoreType.DMA((line, 9)),
    ]
    if tail:
        sems += [
            pltpu.SemaphoreType.DMA((line, 2, 4)),
            pltpu.SemaphoreType.DMA((line, 4)),
            pltpu.SemaphoreType.DMA((line, 4)),
            pltpu.SemaphoreType.DMA((line, 4)),
        ]
    return sems


class Gather:
    def __init__(self, line, x_ref, o_ref, sems, tail=0, own_blocks=None):
        self.line, self.x_ref, self.o_ref, self.tail = line, x_ref, o_ref, tail
        self.own_sem, self.z_send, self.z_recv, self.p_send, self.p_recv = sems[:5]
        if tail:
            self.t_send, self.t_recv, self.q_send, self.q_recv = sems[5:]
        self.own_blocks = own_blocks
        self.z_at = lax.axis_index("fsdp")
        self.me, self.mate, self.near_x, self.near_y, step_x = neighbours()
        self.across = self.near_y + step_x
        self.places = (self.me, self.near_x, self.near_y, self.across)
        self.rows = x_ref.shape[0]
        self.half = self.rows // 2
        self.middle = (self.z_at == 1) | (self.z_at == 2)
        self.first_slot = self.z_at if line > 1 else 0

    def slot(self, order):
        z_at = self.z_at
        if self.line == 1:
            return 0
        second = z_at + 1 - 2 * lax.rem(z_at, 2)
        third = 2 - z_at // 2
        fourth = 3 - 3 * (z_at // 2)
        return jnp.where(
            order == 0, z_at, jnp.where(order == 1, second, jnp.where(order == 2, third, fourth))
        )

    def each(self, order, act):
        if not self.tail:
            act(True)
        elif isinstance(order, int):
            act(order == 0)
        else:
            pl.when(order == 0)(lambda: act(True))
            pl.when(order > 0)(lambda: act(False))

    def span(self, part, whole):
        count = self.rows if whole else self.rows - self.tail
        return ((0, count), (0, self.half), (self.half, count - self.half))[part]

    def there(self, slot, place, start, count):
        at = (slot * 8 + place) * self.rows + start
        return self.o_ref.at[pl.ds(pl.multiple_of(at, 8), count)]

    def z_copy(self, src_ref, slot, way, target):
        return remote(
            src_ref,
            self.there(slot, self.me, *self.span(0, False)),
            self.z_send.at[slot, way],
            self.z_recv.at[slot],
            (self.me, target),
        )

    def own_main(self):
        start, count = self.span(0, False)
        return self.x_ref.at[pl.ds(start, count)]

    def up(self):
        return self.z_copy(self.own_main(), self.z_at, 0, self.z_at + 1)

    def down(self):
        return self.z_copy(self.own_main(), self.z_at, 1, self.z_at - 1)

    def beyond(self, order):
        return jnp.where(order == 1, 3 - self.z_at, 3 * self.z_at - 3)

    def onward(self, order):
        slot = self.slot(order)
        main = self.there(slot, self.me, *self.span(0, False))
        return self.z_copy(main, slot, 0, self.beyond(order))

    def copy(self, order, place, kind, device, part, whole, src_ref=None):
        dst_ref = self.there(self.slot(order), place, *self.span(part, whole))
        return remote(
            dst_ref if src_ref is None else src_ref,
            dst_ref,
            self.p_send.at[order, kind],
            self.p_recv.at[order, kind],
            (device, self.z_at),
        )

    def out(self, order, whole, src_ref=None):
        return [
            self.copy(order, self.me, 0, self.near_x, 0, whole, src_ref),
            self.copy(order, self.me, 1, self.near_y, 0, whole, src_ref),
            self.copy(order, self.me, 2, self.mate, 0, whole, src_ref),
        ]

    def passed(self, order, whole, *which):
        places = (
            (self.near_x, 3, self.near_y, 1),
            (self.near_x, 5, self.mate, 0),
            (self.near_y, 4, self.near_x, 2),
            (self.near_y, 6, self.mate, 0),
            (self.across, 7, self.mate, 1),
            (self.across, 8, self.mate, 2),
        )
        return [self.copy(order, *places[k], whole) for k in which]

    def begin(self, met=False):
        line, z_at = self.line, self.z_at
        if not met:
            greet((self.mate, self.near_x, self.near_y), line, z_at)
        self.own_copy().start()
        if line > 1:
            self.begin_line()
        for copy in self.out(0, True, self.x_ref):
            copy.start()

    def begin_line(self):
        pl.when(self.z_at < self.line - 1)(lambda: self.up().start())
        pl.when(self.z_at > 0)(lambda: self.down().start())

    def own_copy(self):
        return pltpu.make_async_copy(
            self.x_ref, self.there(self.first_slot, self.me, 0, self.rows), self.own_sem
        )

    def own_block(self):
        self.own_copy().wait()

    def from_line(self, order):
        slot = self.slot(order)
        main = self.there(slot, self.me, *self.span(0, False))
        self.z_copy(main, slot, 0, self.z_at).wait_recv()

    def first(self, order):
        at_end = jnp.logical_not(self.middle)
        pl.when(at_end | (order == 1))(lambda: self.from_line(order))

        @pl.when(self.middle & (order == 1))
        def _():
            self.onward(1).start()
            self.from_line(2)
            self.onward(2).start()

        @pl.when(self.middle & (order == 2))
        def _():
            self.from_line(3)
            self.onward(3).start()

        for copy in self.out(order, False):
            copy.start()

    def second(self, order):
        def act(whole):
            to_y, mate_x, to_x, mate_y = self.passed(order, whole, 0, 1, 2, 3)
            self.copy(order, self.near_x, 0, self.near_x, 0, whole).wait_recv()
            to_y.start()
            mate_x.start()
            self.copy(order, self.near_y, 1, self.near_y, 0, whole).wait_recv()
            to_x.start()
            mate_y.start()

        self.each(order, act)

    def tail_copy(self, slot, k, way, target, own=False):
        start = self.rows - self.tail
        dst_ref = self.there(slot, self.places[k], start, self.tail)
        src_ref = dst_ref
        if own and self.own_blocks is not None:
            at = pl.multiple_of(self.places[k] * self.rows + start, 8)
            src_ref = self.own_blocks.at[pl.ds(at, self.tail)]
        return remote(
            src_ref,
            dst_ref,
            self.t_send.at[slot, way, k],
            self.t_recv.at[slot, k],
            (self.me, target),
        )

    def own_tails(self, act):
        z_at = self.z_at
        for k in range(4):
            pl.when(z_at < self.line - 1)(lambda: act(self.tail_copy(z_at, k, 0, z_at + 1, True)))
            pl.when(z_at > 0)(lambda: act(self.tail_copy(z_at, k, 1, z_at - 1, True)))

    def send_tails(self):
        self.own_tails(lambda copy: copy.start())

    def tails_on(self, order):
        return [self.tail_copy(self.slot(order), k, 0, self.beyond(order)) for k in range(4)]

    def tail_to_mate(self, order, k, place):
        ref = self.there(self.slot(order), place, self.rows - self.tail, self.tail)
        return remote(
            ref, ref, self.q_send.at[order, k], self.q_recv.at[order, k], (self.mate, self.z_at)
        )

    def tails(self, order):
        def arrive(one):
            for k in range(4):
                self.tail_copy(self.slot(one), k, 0, self.z_at).wait_recv()

        def on(one):
            for copy in self.tails_on(one):
                copy.start()

        pl.when(jnp.logical_not(self.middle) | (order == 1))(lambda: arrive(order))

        @pl.when(self.middle & (order == 1))
        def _():
            on(1)
            arrive(2)
            on(2)

        @pl.when(self.middle & (order == 2))
        def _():
            arrive(3)
            on(3)

        for k in range(4):
            self.tail_to_mate(order, k, self.places[k]).start()

    def mates_tails(self, order, *which):
        if self.tail:

            @pl.when(order > 0)
            def _():
                for k in which:
                    place = self.places[k] + self.mate - self.me
                    self.tail_to_mate(order, k, place).wait_recv()

    def near(self, order):
        step = self.mate - self.me

        def act(whole):
            self.copy(order, self.mate, 2, self.mate, 0, whole).wait_recv()
            self.copy(order, self.near_x + step, 5, self.mate, 0, whole).wait_recv()

        self.each(order, act)
        self.mates_tails(order, 0, 1)

    def third(self, order):
        step = self.mate - self.me

        def act(whole):
            top, low = self.passed(order, whole, 4, 5)
            self.copy(order, self.across, 3, self.near_y, 1, whole).wait_recv()
            top.start()
            self.copy(order, self.across, 4, self.near_x, 2, whole).wait_recv()
            low.start()
            self.copy(order, self.near_y + step, 6, self.mate, 0, whole).wait_recv()
            self.copy(order, self.across + step, 7, self.mate, 1, whole).wait_recv()
            self.copy(order, self.across + step, 8, self.mate, 2, whole).wait_recv()

        self.each(order, act)
        self.mates_tails(order, 2, 3)

    def end(self, from_order=0):
        line, z_at = self.line, self.z_at

        def sent(order, carry):
            def act(whole):
                for copy in self.out(order, whole) + self.passed(order, whole, 0, 1, 2, 3, 4, 5):
                    copy.wait_send()

            self.each(order, act)
            return carry

        lax.fori_loop(from_order, line, sent, 0)
        if line > 1:
            pl.when(z_at < line - 1)(lambda: self.up().wait_send())
            pl.when(z_at > 0)(lambda: self.down().wait_send())

            @pl.when(self.middle)
            def _():
                for order in range(1, line):
                    self.onward(order).wait_send()

        if self.tail:
            self.own_tails(lambda copy: copy.wait_send())
            for order in range(1, line):
                for k in range(4):
                    self.tail_to_mate(order, k, self.places[k]).wait_send()

            @pl.when(self.middle)
            def _():
                for order in range(1, line):
                    for copy in self.tails_on(order):
                        copy.wait_send()


def line_sems(line):
    return [
        pltpu.SemaphoreType.DMA,
        pltpu.SemaphoreType.DMA((line, 2)),
        pltpu.SemaphoreType.DMA((line,)),
    ]


class Line:
    def __init__(self, x_ref, o_ref, sems):
        self.x_ref, self.o_ref = x_ref, o_ref
        self.own_sem, self.sends, self.receives = sems
        self.me, self.z_at = lax.axis_index("ctx"), lax.axis_index("fsdp")
        self.middle = (self.z_at == 1) | (self.z_at == 2)
        self.slots = (
            self.z_at,
            self.z_at + 1 - 2 * lax.rem(self.z_at, 2),
            2 - self.z_at // 2,
            3 - 3 * (self.z_at // 2),
        )

    def there(self, slot):
        rows = self.x_ref.shape[0]
        return self.o_ref.at[pl.ds(pl.multiple_of(slot * rows, 16), rows)]

    def copy(self, src_ref, slot, way, target):
        return remote(
            src_ref,
            self.there(slot),
            self.sends.at[slot, way],
            self.receives.at[slot],
            (self.me, target),
        )

    def own(self):
        return pltpu.make_async_copy(self.x_ref, self.there(self.z_at), self.own_sem)

    def up(self):
        return self.copy(self.x_ref, self.z_at, 0, self.z_at + 1)

    def down(self):
        return self.copy(self.x_ref, self.z_at, 1, self.z_at - 1)

    def onward(self, order):
        slot = self.slots[order]
        target = 3 - self.z_at if order == 1 else 3 * self.z_at - 3
        return self.copy(self.there(slot), slot, 0, target)

    def begin(self):
        pl.when(self.z_at < 3)(lambda: self.up().start())
        pl.when(self.z_at > 0)(lambda: self.down().start())
        self.own().start()

    def arrive(self, order):
        slot = self.slots[order]
        self.copy(self.there(slot), slot, 0, self.z_at).wait_recv()

    def pass_on(self, *orders):
        @pl.when(self.middle)
        def _():
            for order in orders:
                self.arrive(order)
                self.onward(order).start()

    def rest(self):
        @pl.when(jnp.logical_not(self.middle))
        def _():
            for order in (1, 2, 3):
                self.arrive(order)

    def end(self):
        self.own().wait()
        pl.when(self.z_at < 3)(lambda: self.up().wait_send())
        pl.when(self.z_at > 0)(lambda: self.down().wait_send())

        @pl.when(self.middle)
        def _():
            for order in (1, 2, 3):
                self.onward(order).wait_send()


def gather_blocks(x, line, collective, name):
    rows, width = x.shape

    def kernel(x_ref, o_ref, *sems):
        gather = Gather(line, x_ref, o_ref, sems)
        gather.begin()

        def body(order, carry):
            gather.second(order)
            if line > 1:
                pl.when(order + 1 < line)(lambda: gather.first(order + 1))
            gather.near(order)
            gather.third(order)
            return carry

        lax.fori_loop(0, line, body, 0)
        gather.own_block()
        gather.end()

    return pl.pallas_call(
        kernel,
        out_shape=jax.ShapeDtypeStruct((line * 8 * rows, width), x.dtype),
        in_specs=[pl.BlockSpec(memory_space=pl.ANY)],
        out_specs=pl.BlockSpec(memory_space=pl.ANY),
        scratch_shapes=gather_sems(line),
        compiler_params=pltpu.CompilerParams(collective_id=collective, has_side_effects=True),
        name=name,
    )(x)


CHUNK = 16


def add_rows(dst_ref, src_refs, start, count, out_ref=None):
    def body(i, carry):
        at = pl.ds(pl.multiple_of(start + i * CHUNK, CHUNK), CHUNK)
        value = dst_ref[at, :].astype(jnp.float32)
        for src_ref in src_refs:
            value = value + src_ref[at, :].astype(jnp.float32)
        to_ref = dst_ref if out_ref is None else out_ref
        to_ref[at, :] = value.astype(to_ref.dtype)
        return carry

    lax.fori_loop(0, count // CHUNK, body, 0)


class Scatter:
    def __init__(self, line, x_ref, o_ref, scratch, columns=None):
        self.columns = columns
        (
            self.mine, self.theirs, self.halves, self.from_x, self.from_y, self.from_z, self.total,
            self.load_sem, self.m_send, self.m_recv, self.p_send, self.p_recv, self.z_send,
            self.z_recv, self.out_sem, *rest,
        ) = scratch
        self.tail = 0
        if rest:
            self.from_t, self.t_send, self.t_recv = rest
            self.tail = self.from_t.shape[2]
        self.line, self.x_ref, self.o_ref = line, x_ref, o_ref
        self.z_at = lax.axis_index("fsdp")
        self.me, self.mate, self.near_x, self.near_y, step_x = neighbours()
        self.places = (self.near_y + step_x, self.near_x, self.near_y, self.me)
        self.rows = self.total.shape[0]
        self.half = self.rows // 2
        self.main = self.rows - self.tail
        self.middle = (self.z_at == 1) | (self.z_at == 2)

    def slot(self, order):
        z_at = self.z_at
        if self.line == 1:
            return 0
        far, next_far, near = 3 - 3 * (z_at // 2), 2 - z_at // 2, z_at + 1 - 2 * lax.rem(z_at, 2)
        return jnp.where(
            order == 0, far, jnp.where(order == 1, next_far, jnp.where(order == 2, near, z_at))
        )

    def each(self, order, act):
        if not self.tail:
            act(self.rows)
        elif isinstance(order, int):
            act(self.rows if order == self.line - 1 else self.main)
        else:
            pl.when(order == self.line - 1)(lambda: act(self.rows))
            pl.when(order < self.line - 1)(lambda: act(self.main))

    def there(self, slot, place):
        at = pl.ds(pl.multiple_of((slot * 8 + place) * self.rows, 16), self.rows)
        return self.x_ref.at[at] if self.columns is None else self.x_ref.at[at, self.columns]

    def give(self, order, k):
        return remote(
            self.there(self.slot(order), self.places[k] + self.mate - self.me),
            self.theirs.at[order, k],
            self.m_send.at[order, k],
            self.m_recv.at[order, k],
            (self.mate, self.z_at),
        )

    def load(self, order, k):
        return pltpu.make_async_copy(
            self.there(self.slot(order), self.places[k]),
            self.mine.at[order, k],
            self.load_sem.at[order, k],
        )

    def send(self, order, kind, count):
        top, low = pl.ds(0, self.half), pl.ds(self.half, count - self.half)
        k, part, to, device = (
            (0, top, self.halves, self.near_x),
            (0, low, self.halves, self.near_y),
            (1, top, self.from_x, self.near_x),
            (1, low, self.from_x, self.near_x),
            (2, low, self.from_y, self.near_y),
            (2, top, self.from_y, self.near_y),
        )[kind]
        return remote(
            self.mine.at[order, k, part],
            to.at[order, part],
            self.p_send.at[order, kind],
            self.p_recv.at[order, kind],
            (device, self.z_at),
        )

    def begin(self, met=False):
        if not met:
            greet((self.mate, self.near_x, self.near_y), self.line, self.z_at)

        def body(order, carry):
            for k in range(4):
                self.start_part(order, k)
            return carry

        lax.fori_loop(0, self.line, body, 0)

    def start_part(self, order, k):
        self.give(order, k).start()
        self.load(order, k).start()

    def produce(self, make):
        for k in range(4):
            make(self.places[k] // 2)
            self.start_part(0, k)
            if k > 0:
                self.part(0, k - 1)
        self.part(0, 3)

    def tail_copy(self, order, k, index, target):
        return remote(
            self.mine.at[order, k, pl.ds(self.main, self.tail)],
            self.from_t.at[index, k],
            self.t_send.at[order, k],
            self.t_recv.at[index, k],
            (self.me, target),
        )

    def toward(self, order):
        return jnp.where(order == 2, self.slot(order), self.z_at + 1 - 2 * (self.z_at // 2))

    def tails_out(self, order):
        slot, target = self.slot(order), self.toward(order)
        above = jnp.where((target == slot) & (self.z_at > target), 1, 0)
        index = above * 4 + (1 - above) * slot
        return [self.tail_copy(order, k, index, target) for k in range(4)]

    def tails_on(self, order):
        slot = self.slot(order)
        copies = self.tails_out(order)
        for k in range(4):
            self.tail_copy(order, k, slot, self.z_at).wait_recv()
            add_rows(self.mine.at[order, k, pl.ds(self.main, self.tail)], [self.from_t.at[slot, k]], 0, self.tail)
            copies[k].start()

    def tails_in(self, order, k):
        z_at = self.z_at
        mine = self.mine.at[order, k, pl.ds(self.main, self.tail)]

        @pl.when(z_at > 0)
        def _():
            self.tail_copy(order, k, z_at, z_at).wait_recv()
            add_rows(mine, [self.from_t.at[z_at, k]], 0, self.tail)

        @pl.when(z_at < self.line - 1)
        def _():
            self.tail_copy(order, k, 4, z_at).wait_recv()
            add_rows(mine, [self.from_t.at[4, k]], 0, self.tail)

    def part(self, order, k):
        self.give(order, k).wait_recv()
        self.load(order, k).wait()
        add_rows(self.mine.at[order, k], [self.theirs.at[order, k]], 0, self.rows)
        if self.tail:
            pl.when(order == self.line - 1)(lambda: self.tails_in(order, k))

        def act(count):
            for kind in ((0, 1), (2,), (4,), ())[k]:
                self.send(order, kind, count).start()

        self.each(order, act)

    def first(self, order):
        for k in range(4):
            self.part(order, k)
        if self.tail:

            @pl.when((order < self.line - 1) & jnp.logical_not(self.middle))
            def _():
                for copy in self.tails_out(order):
                    copy.start()

    def second(self, order):
        def act(count):
            self.send(order, 1, count).wait_recv()
            low = count - self.half
            add_rows(self.mine.at[order, 1], [self.halves.at[order]], self.half, low)
            self.send(order, 3, count).start()
            self.send(order, 0, count).wait_recv()
            add_rows(self.mine.at[order, 2], [self.halves.at[order]], 0, self.half)
            self.send(order, 5, count).start()

        self.each(order, act)

    def third(self, order, out_ref=None):
        sources = [self.from_x.at[order], self.from_y.at[order]]

        def act(count):
            for kind in (2, 3, 4, 5):
                self.send(order, kind, count).wait_recv()
            add_rows(self.mine.at[order, 3], sources, 0, count, out_ref)

        self.each(order, act)

    def z_copy(self, order, slot_at, target):
        at = pl.ds(0, self.main)
        return remote(
            self.mine.at[order, 3, at],
            self.from_z.at[slot_at, at],
            self.z_send.at[order],
            self.z_recv.at[slot_at],
            (self.me, target),
        )

    def z_out(self, order):
        z_at, slot, target = self.z_at, self.slot(order), self.toward(order)
        ends = jnp.where(target == slot, 1, 0)
        return self.z_copy(order, ends * (4 + (z_at - target + 1) // 2) + (1 - ends) * slot, target)

    def pass_on(self, order):
        slot = self.slot(order)
        self.z_copy(order, slot, self.z_at).wait_recv()
        add_rows(self.mine.at[order, 3], [self.from_z.at[slot]], 0, self.main)
        self.z_out(order).start()

    def along(self, order):
        @pl.when((order < self.line - 1) & jnp.logical_not(self.middle))
        def _():
            self.z_out(order).start()

        if self.tail:
            pl.when((order == 0) & self.middle)(lambda: self.tails_on(0))

            @pl.when((order == 1) & self.middle)
            def _():
                self.tails_on(1)
                self.tails_on(2)

        pl.when((order == 1) & self.middle)(lambda: self.pass_on(0))

        @pl.when((order == 2) & self.middle)
        def _():
            self.pass_on(1)
            self.pass_on(2)

    def last(self):
        z_at, line = self.z_at, self.line
        pl.when(z_at > 0)(lambda: self.z_copy(line - 1, 4, z_at).wait_recv())
        pl.when(z_at < line - 1)(lambda: self.z_copy(line - 1, 5, z_at).wait_recv())
        mine = self.mine.at[line - 1, 3]
        below, above = self.from_z.at[4], self.from_z.at[5]
        pl.when(z_at == 0)(lambda: add_rows(mine, [above], 0, self.main, self.total))
        pl.when(z_at == line - 1)(lambda: add_rows(mine, [below], 0, self.main, self.total))
        pl.when(self.middle)(lambda: add_rows(mine, [below, above], 0, self.main, self.total))
        if self.tail:
            add_rows(mine, [], self.main, self.tail, self.total)

    def end(self):
        out = pltpu.make_async_copy(self.total, self.o_ref, self.out_sem)
        out.start()

        def sent(order, carry):
            def act(count):
                for kind in range(6):
                    self.send(order, kind, count).wait_send()

            for k in range(4):
                self.give(order, k).wait_send()
            self.each(order, act)
            if self.line > 1:

                @pl.when(order < self.line - 1)
                def _():
                    self.z_out(order).wait_send()
                    if self.tail:
                        for copy in self.tails_out(order):
                            copy.wait_send()

            return carry

        lax.fori_loop(0, self.line, sent, 0)
        out.wait()

    def plane_sum(self, make=None):
        if make is None:
            self.first(0)
        else:
            self.produce(make)
        self.second(0)
        self.third(0, self.total)
        self.end()

    def run(self, work=None, extra=0, met=False, begun=False):
        if not begun:
            self.begin(met)
        if self.line == 1:
            self.plane_sum()
            return
        if not begun:
            self.first(0)

        def body(step, carry):
            order, phase = step // 3, lax.rem(step, 3)

            @pl.when((phase == 0) & (order < self.line))
            def _():
                self.second(order)
                pl.when(order + 1 < self.line)(lambda: self.first(order + 1))

            pl.when((phase == 1) & (order < self.line))(lambda: self.third(order))
            pl.when((phase == 2) & (order < self.line))(lambda: self.along(order))
            if work is not None:
                work(step)
            return carry

        lax.fori_loop(0, 3 * self.line + extra, body, 0)
        self.last()
        self.end()


TAIL = 16


def scatter_scratch(line, rows, width, dtype, tail=TAIL):
    shard = (rows, width)
    made = [
        pltpu.VMEM((line, 4) + shard, dtype),
        pltpu.VMEM((line, 4) + shard, dtype),
        pltpu.VMEM((line,) + shard, dtype),
        pltpu.VMEM((line,) + shard, dtype),
        pltpu.VMEM((line,) + shard, dtype),
        pltpu.VMEM((6 if line > 1 else 1,) + shard, dtype),
        pltpu.VMEM(shard, jnp.float32),
        pltpu.SemaphoreType.DMA((line, 4)),
        pltpu.SemaphoreType.DMA((line, 4)),
        pltpu.SemaphoreType.DMA((line, 4)),
        pltpu.SemaphoreType.DMA((line, 6)),
        pltpu.SemaphoreType.DMA((line, 6)),
        pltpu.SemaphoreType.DMA((line,)),
        pltpu.SemaphoreType.DMA((6,)),
        pltpu.SemaphoreType.DMA,
    ]
    if line > 1 and tail:
        made += [
            pltpu.VMEM((5, 4, tail, width), dtype),
            pltpu.SemaphoreType.DMA((line, 4)),
            pltpu.SemaphoreType.DMA((5, 4)),
        ]
    return made


def scatter_blocks(x, line, collective, name):
    rows, width = x.shape[0] // (line * 8), x.shape[1]

    def kernel(x_ref, o_ref, *scratch):
        Scatter(line, x_ref, o_ref, scratch).run()

    return pl.pallas_call(
        kernel,
        out_shape=jax.ShapeDtypeStruct((rows, width), jnp.float32),
        in_specs=[pl.BlockSpec(memory_space=pl.ANY)],
        out_specs=pl.BlockSpec(memory_space=pl.ANY),
        scratch_shapes=scatter_scratch(line, rows, width, x.dtype),
        compiler_params=pltpu.CompilerParams(
            collective_id=collective, has_side_effects=True, vmem_limit_bytes=52 * MIB
        ),
        name=name,
    )(x)


QUERY_HEADS = 64
KEY_VALUE_HEADS = 8
HEAD_SIZE = 64
TOP = 4
EPSILON = 1e-05
THETA_BASE = 150000.0
CLAMP_LIMIT = 7.0
GLU_ALPHA = 1.702
MASK_FILL = -1e30
SPAN = 256
SCALE = HEAD_SIZE**-0.5


def contract(left, right, left_axis, right_axis):
    return lax.dot_general(
        left, right, (((left_axis,), (right_axis,)), ((), ())), preferred_element_type=jnp.float32
    )


def norm_scale(value_rows, gain_vec):
    return (
        value_rows
        * lax.rsqrt(jnp.mean(value_rows * value_rows, axis=-1, keepdims=True) + EPSILON)
        * gain_vec
    )


def soft_clamp(value_rows):
    return CLAMP_LIMIT * jnp.tanh(value_rows / CLAMP_LIMIT)


def glu_units(gate_lin, up_lin):
    gated = soft_clamp(gate_lin)
    return (soft_clamp(up_lin) + 1.0) * gated * jax.nn.sigmoid(GLU_ALPHA * gated)


def rotary_tables(length):
    half = HEAD_SIZE // 2
    inverse = np.float32(THETA_BASE) ** (-np.arange(half, dtype=np.float32) / np.float32(half))
    angles = inverse[:, None] * np.arange(length, dtype=np.float32)[None, :]
    return jnp.asarray(np.cos(angles)), jnp.asarray(np.sin(angles))


def turned(value, cosine, sine):
    half = HEAD_SIZE // 2
    first, second = value[:, :half], value[:, half:]
    return jnp.concatenate(
        [first * cosine - second * sine, second * cosine + first * sine], axis=1
    )


def diagonal(length):
    return lax.broadcasted_iota(jnp.int32, (length, length), 0) <= lax.broadcasted_iota(
        jnp.int32, (length, length), 1
    )


def masked_scores(key_rows, query_cols, count):
    scores = contract(key_rows, query_cols, 1, 0)
    edge = jnp.where(diagonal(SPAN), scores[count - SPAN :], MASK_FILL)
    if count == SPAN:
        return edge
    return jnp.concatenate([scores[: count - SPAN], edge], axis=0)


def attend_kernel(sink_ref, q_ref, k_ref, v_ref, out_ref, log_ref):
    sink = sink_ref[pl.program_id(0)]
    length = q_ref.shape[1]
    for start in range(0, length, SPAN):
        count = start + SPAN
        at = pl.ds(start, SPAN)
        query = q_ref[:, at] * jnp.bfloat16(SCALE)
        scores = masked_scores(k_ref[:count, :], query, count)
        row_top = jnp.maximum(jnp.max(scores, axis=0, keepdims=True), sink)
        weights = jnp.exp(scores - row_top)
        denominator = jnp.sum(weights, axis=0, keepdims=True) + jnp.exp(sink - row_top)
        probabilities = (weights / denominator).astype(jnp.bfloat16)
        out_ref[:, at] = contract(v_ref[:, :count], probabilities, 1, 0).astype(jnp.bfloat16)
        log_ref[0, :, at] = row_top + jnp.log(denominator)


def attend(sinks, queries, keys, values):
    heads, length = queries.shape[0] // HEAD_SIZE, queries.shape[1]
    per_head = pl.BlockSpec((HEAD_SIZE, length), lambda h: (h, 0))
    return pl.pallas_call(
        attend_kernel,
        grid=(heads,),
        out_shape=(
            jax.ShapeDtypeStruct(queries.shape, jnp.bfloat16),
            jax.ShapeDtypeStruct((heads, 1, length), jnp.float32),
        ),
        in_specs=[
            pl.BlockSpec(memory_space=pltpu.SMEM),
            per_head,
            pl.BlockSpec((length, HEAD_SIZE), lambda h: (0, 0)),
            pl.BlockSpec((HEAD_SIZE, length), lambda h: (0, 0)),
        ],
        out_specs=(per_head, pl.BlockSpec((1, 1, length), lambda h: (h, 0, 0))),
        compiler_params=pltpu.CompilerParams(vmem_limit_bytes=40 * MIB),
        cost_estimate=pl.CostEstimate(
            flops=heads * length * length * HEAD_SIZE * 4,
            bytes_accessed=heads * length * HEAD_SIZE * 4,
            transcendentals=heads * length * length,
        ),
        name="attend",
    )(sinks, queries, keys, values)


def attention(rows_own, grads_own, weights_own, out_own, sinks, cosine, sine, collective):
    low, f32 = jnp.bfloat16, jnp.float32
    block_rows, wide = rows_own.shape
    length = 8 * block_rows
    own_rows = weights_own.shape[0]
    q_rows, width = out_own.shape
    kv_rows = (own_rows - q_rows) // 2
    heads = 4 * q_rows // HEAD_SIZE
    half = HEAD_SIZE // 2
    per_shard = q_rows // HEAD_SIZE

    def kernel(
        sink_ref, rows_ref, grads_ref, weights_ref, out_ref, cos_ref, sin_ref,
        o_ref, all_rows, all_grads, all_weights, all_out, q_ref, k_ref, kt_ref, v_ref, att_ref, log_ref,
        normed_v, weights_v, lin, vt_v, out_v, branch, held_sems, *scratch,
    ):
        plane = Gather(1, rows_ref, all_rows, scratch[:5])
        later = Gather(1, grads_ref, all_grads, scratch[5:10])
        heads_line = Line(weights_ref, all_weights, scratch[10:13])
        line = Line(out_ref, all_out, scratch[13:16])
        scatter = Scatter(1, branch, o_ref, scratch[16:])
        load_rows = pltpu.make_async_copy(all_rows, normed_v, held_sems.at[0])
        load_weights = pltpu.make_async_copy(all_weights, weights_v, held_sems.at[1])
        greet((plane.mate, plane.near_x, plane.near_y), 4, line.z_at)
        heads_line.begin()
        plane.begin(True)
        heads_line.pass_on(1, 2)
        plane.second(0)
        later.begin(True)
        line.begin()
        plane.near(0)
        plane.third(0)
        plane.own_block()
        load_rows.start()
        heads_line.pass_on(3)
        later.second(0)
        later.near(0)
        later.third(0)
        later.own_block()
        heads_line.rest()
        heads_line.end()
        load_weights.start()
        load_rows.wait()
        load_weights.wait()

        def project(i, carry):
            at = pl.ds(pl.multiple_of(i * SPAN, SPAN), SPAN)
            lin[:, at] = contract(weights_v[...], normed_v[at, :], 1, 1)
            return carry

        lax.fori_loop(0, length // SPAN, project, 0)
        line.pass_on(1, 2)

        def turn(value):
            first, second = value[:half], value[half:]
            cosine, sine = cos_ref[...], sin_ref[...]
            return jnp.concatenate(
                [first * cosine - second * sine, second * cosine + first * sine], axis=0
            ).astype(low)

        def shards_of(offset):
            return jnp.concatenate(
                [
                    lin[z * own_rows + offset : z * own_rows + offset + kv_rows, :]
                    for z in range(4)
                ],
                axis=0,
            )

        keys_t = turn(shards_of(q_rows))
        values_t = shards_of(q_rows + kv_rows).astype(low)
        kt_ref[...] = keys_t
        vt_v[...] = values_t
        k_ref[...] = keys_t.T
        v_ref[...] = values_t.T

        def head(h, carry):
            pl.when(h == heads // 2)(lambda: line.pass_on(3))
            start = (h // per_shard) * own_rows + lax.rem(h, per_shard) * HEAD_SIZE
            queries = turn(lin[pl.ds(pl.multiple_of(start, 16), HEAD_SIZE), :])
            rows = pl.ds(pl.multiple_of(h * HEAD_SIZE, HEAD_SIZE), HEAD_SIZE)
            q_ref[rows, :] = queries
            sink = sink_ref[h]
            for begin in range(0, length, SPAN):
                count = begin + SPAN
                query = queries[:, begin:count] * jnp.bfloat16(SCALE)
                scores = masked_scores(k_ref[:count, :], query, count)
                row_top = jnp.maximum(jnp.max(scores, axis=0, keepdims=True), sink)
                chances = jnp.exp(scores - row_top)
                denominator = jnp.sum(chances, axis=0, keepdims=True) + jnp.exp(sink - row_top)
                chances = (chances / denominator).astype(low)
                att_ref[rows, begin:count] = contract(vt_v[:, :count], chances, 1, 0).astype(low)
                log_ref[h, :, begin:count] = row_top + jnp.log(denominator)
            return carry

        lax.fori_loop(0, heads, head, 0)
        line.rest()
        line.end()
        load = pltpu.make_async_copy(all_out, out_v, held_sems.at[0])
        load.start()
        load.wait()

        def give_back(chip):
            at = pl.ds(pl.multiple_of(chip * SPAN, SPAN), SPAN)
            branch[at, :] = contract(att_ref[:, at], out_v[...], 0, 0).astype(low)

        scatter.plane_sum(give_back)
        plane.end()
        later.end()

    hbm = pl.BlockSpec(memory_space=pl.ANY)
    vmem = pl.BlockSpec(memory_space=pltpu.VMEM)
    return pl.pallas_call(
        kernel,
        out_shape=(
            jax.ShapeDtypeStruct((block_rows, width), f32),
            jax.ShapeDtypeStruct((length, wide), low),
            jax.ShapeDtypeStruct((length, wide), low),
            jax.ShapeDtypeStruct((4 * own_rows, wide), low),
            jax.ShapeDtypeStruct((4 * q_rows, width), low),
            jax.ShapeDtypeStruct((4 * q_rows, length), low),
            jax.ShapeDtypeStruct((length, HEAD_SIZE), low),
            jax.ShapeDtypeStruct((HEAD_SIZE, length), low),
            jax.ShapeDtypeStruct((length, HEAD_SIZE), low),
            jax.ShapeDtypeStruct((4 * q_rows, length), low),
            jax.ShapeDtypeStruct((heads, 1, length), f32),
        ),
        in_specs=[pl.BlockSpec(memory_space=pltpu.SMEM), hbm, hbm, hbm, hbm, vmem, vmem],
        out_specs=(hbm,) * 5 + (vmem,) * 6,
        scratch_shapes=[
            pltpu.VMEM((length, wide), low),
            pltpu.VMEM((4 * own_rows, wide), low),
            pltpu.VMEM((4 * own_rows, length), f32),
            pltpu.VMEM((HEAD_SIZE, length), low),
            pltpu.VMEM((4 * q_rows, width), low),
            pltpu.VMEM((length, width), low),
            pltpu.SemaphoreType.DMA((2,)),
            *gather_sems(1),
            *gather_sems(1),
            *line_sems(4),
            *line_sems(4),
            *scatter_scratch(1, block_rows, width, low),
        ],
        compiler_params=pltpu.CompilerParams(
            collective_id=collective, has_side_effects=True, vmem_limit_bytes=58 * MIB
        ),
        name="attention",
    )(sinks, rows_own, grads_own, weights_own, out_own, cosine, sine)


def attend_back_kernel(
    sink_ref, q_ref, k_ref, kt_ref, v_ref, grad_ref, log_ref, cos_ref, sin_ref,
    dq_ref, dk_ref, dv_ref, dsink_ref,
):
    head = pl.program_id(0)
    sink = sink_ref[head]
    length = q_ref.shape[1]
    half = HEAD_SIZE // 2

    @pl.when(head == 0)
    def _():
        dk_ref[...] = jnp.zeros_like(dk_ref)
        dv_ref[...] = jnp.zeros_like(dv_ref)

    grad_sink = jnp.zeros((1, SPAN), jnp.float32)
    for start in range(0, length, SPAN):
        count = start + SPAN
        at = pl.ds(start, SPAN)
        query = q_ref[:, at] * jnp.bfloat16(SCALE)
        grad = grad_ref[:, at]
        log_sum = log_ref[0, :, at]
        probabilities = jnp.exp(masked_scores(k_ref[:count, :], query, count) - log_sum)
        grad_probs = contract(v_ref[:count, :], grad, 1, 0)
        inner_sum = jnp.sum(probabilities * grad_probs, axis=0, keepdims=True)
        grad_scores = (probabilities * (grad_probs - inner_sum)).astype(jnp.bfloat16)
        grad_query = contract(kt_ref[:, :count], grad_scores, 1, 0) * SCALE
        first, second = grad_query[:half], grad_query[half:]
        cosine, sine = cos_ref[:, at], sin_ref[:, at]
        dq_ref[:half, at] = (first * cosine + second * sine).astype(jnp.bfloat16)
        dq_ref[half:, at] = (second * cosine - first * sine).astype(jnp.bfloat16)
        dk_ref[:count, :] += contract(grad_scores, query, 1, 1)
        dv_ref[:count, :] += contract(probabilities.astype(jnp.bfloat16), grad, 1, 1)
        grad_sink = grad_sink - jnp.exp(sink - log_sum) * inner_sum
    dsink_ref[0] = grad_sink


def attend_back(sinks, queries, keys, keys_t, values, grads, log_sums, cosine, sine):
    heads, length = queries.shape[0] // HEAD_SIZE, queries.shape[1]
    per_head = pl.BlockSpec((HEAD_SIZE, length), lambda h: (h, 0))

    def whole(*shape):
        return pl.BlockSpec(shape, lambda h: (0,) * len(shape))

    return pl.pallas_call(
        attend_back_kernel,
        grid=(heads,),
        out_shape=(
            jax.ShapeDtypeStruct(queries.shape, jnp.bfloat16),
            jax.ShapeDtypeStruct((length, HEAD_SIZE), jnp.float32),
            jax.ShapeDtypeStruct((length, HEAD_SIZE), jnp.float32),
            jax.ShapeDtypeStruct((heads, 1, SPAN), jnp.float32),
        ),
        in_specs=[
            pl.BlockSpec(memory_space=pltpu.SMEM),
            per_head,
            whole(length, HEAD_SIZE),
            whole(HEAD_SIZE, length),
            whole(length, HEAD_SIZE),
            per_head,
            pl.BlockSpec((1, 1, length), lambda h: (h, 0, 0)),
            whole(HEAD_SIZE // 2, length),
            whole(HEAD_SIZE // 2, length),
        ],
        out_specs=(
            per_head,
            whole(length, HEAD_SIZE),
            whole(length, HEAD_SIZE),
            pl.BlockSpec((1, 1, SPAN), lambda h: (h, 0, 0)),
        ),
        compiler_params=pltpu.CompilerParams(vmem_limit_bytes=48 * MIB),
        cost_estimate=pl.CostEstimate(
            flops=heads * length * length * HEAD_SIZE * 10,
            bytes_accessed=heads * length * HEAD_SIZE * 8,
            transcendentals=heads * length * length,
        ),
        name="attend_back",
    )(sinks, queries, keys, keys_t, values, grads, log_sums, cosine, sine)


class Moved:
    def __init__(self, pairs, sems):
        self.copies = [
            pltpu.make_async_copy(source, target, sems.at[k]) for k, (source, target) in enumerate(pairs)
        ]

    def start(self):
        for copy in self.copies:
            copy.start()

    def wait(self):
        for copy in self.copies:
            copy.wait()


def branch_back(parts, columns, grad_own, out_weights, attended, collective):
    low, f32 = jnp.bfloat16, jnp.float32
    block_rows, width = grad_own.shape
    depth, length = attended.shape
    cut = 512

    def kernel(
        parts_ref, grad_ref, out_hbm, att_hbm, o_ref, grad_att_hbm, grad_out_hbm,
        all_grads, out_ref, att_ref, grad_att, grad_out, in_sems, out_sems, *scratch,
    ):
        loads = Moved(((out_hbm, out_ref), (att_hbm, att_ref)), in_sems)
        stores = Moved(((grad_att, grad_att_hbm), (grad_out, grad_out_hbm)), out_sems)
        loads.start()
        gather = Gather(1, grad_ref, all_grads, scratch[:5])
        scatter = Scatter(4, parts_ref, o_ref, scratch[5:], pl.ds(0, columns))
        greet((gather.mate, gather.near_x, gather.near_y), 4, gather.z_at)
        gather.begin(True)
        scatter.begin(True)
        gather.second(0)
        scatter.first(0)
        gather.near(0)
        gather.third(0)
        gather.own_block()

        def work(step):
            pl.when(step == 0)(loads.wait)
            for i in range(length // SPAN):

                @pl.when(step == i)
                def _():
                    at = slice(i * SPAN, (i + 1) * SPAN)
                    grad_att[:, at] = contract(out_ref[...], all_grads[at, :], 1, 1).astype(low)

            for i in range(-(-width // cut)):

                @pl.when(step == i + length // SPAN)
                def _():
                    at = slice(i * cut, min(width, (i + 1) * cut))
                    grad_out[:, at] = contract(att_ref[...], all_grads[:, at], 1, 0).astype(low)

            pl.when(step == length // SPAN)(stores.copies[0].start)
            pl.when(step == steps - 1)(stores.copies[1].start)

        steps = length // SPAN + -(-width // cut) + 1
        scatter.run(work, max(0, steps - 12), begun=True)
        gather.end()
        stores.wait()

    hbm = pl.BlockSpec(memory_space=pl.ANY)
    return pl.pallas_call(
        kernel,
        out_shape=(
            jax.ShapeDtypeStruct((block_rows, columns), f32),
            jax.ShapeDtypeStruct((depth, length), low),
            jax.ShapeDtypeStruct((depth, width), low),
        ),
        in_specs=[hbm] * 4,
        out_specs=(hbm,) * 3,
        scratch_shapes=[
            pltpu.VMEM((length, width), low),
            pltpu.VMEM(out_weights.shape, low),
            pltpu.VMEM(attended.shape, low),
            pltpu.VMEM((depth, length), low),
            pltpu.VMEM((depth, width), low),
            pltpu.SemaphoreType.DMA((2,)),
            pltpu.SemaphoreType.DMA((2,)),
            *gather_sems(1),
            *scatter_scratch(4, block_rows, columns, low),
        ],
        compiler_params=pltpu.CompilerParams(
            collective_id=collective, has_side_effects=True, vmem_limit_bytes=56 * MIB
        ),
        name="branch_back",
    )(parts, grad_own, out_weights, attended)


def attention_back(
    parts, first_column, sinks, queries, keys, keys_t, values, grads, log_sums, cosine, sine, normed,
    own_rows, collective,
):
    low, f32 = jnp.bfloat16, jnp.float32
    length = queries.shape[1]
    heads = queries.shape[0] // HEAD_SIZE
    half = HEAD_SIZE // 2
    block_rows, columns = parts.shape[0] // 32, parts.shape[1] - first_column
    q_rows = queries.shape[0] // 4
    kv_rows = (own_rows - q_rows) // 2
    per_shard = q_rows // HEAD_SIZE
    spans = length // SPAN
    wide = normed.shape[1]

    def kernel(
        sink_ref, parts_ref, *refs
    ):
        sources, refs = refs[:9], refs[9:]
        o_ref, lin_hbm, weights_hbm, dsink_ref, dk_s, dv_s, lin_ref, weights_ref, *refs = refs
        held, (in_sems, out_sems, *scratch) = refs[:9], refs[9:]
        q_ref, k_ref, kt_ref, v_ref, grad_ref, log_ref, cos_ref, sin_ref, normed_v = held
        loads = Moved(tuple(zip(sources, held)), in_sems)
        stores = Moved(((lin_ref, lin_hbm), (weights_ref, weights_hbm)), out_sems)
        loads.start()
        dk_s[...] = jnp.zeros_like(dk_s)
        dv_s[...] = jnp.zeros_like(dv_s)
        dsink_ref[...] = jnp.zeros_like(dsink_ref)

        def one(head, span):
            start, count = span * SPAN, span * SPAN + SPAN
            at = slice(start, count)
            rows = pl.ds(pl.multiple_of(head * HEAD_SIZE, HEAD_SIZE), HEAD_SIZE)
            query = q_ref[rows, at] * jnp.bfloat16(SCALE)
            grad = grad_ref[rows, at]
            log_sum = log_ref[head, :, at]
            chances = jnp.exp(masked_scores(k_ref[:count, :], query, count) - log_sum)
            grad_probs = contract(v_ref[:count, :], grad, 1, 0)
            inner_sum = jnp.sum(chances * grad_probs, axis=0, keepdims=True)
            grad_scores = (chances * (grad_probs - inner_sum)).astype(low)
            grad_query = contract(kt_ref[:, :count], grad_scores, 1, 0) * SCALE
            first, second = grad_query[:half], grad_query[half:]
            cosine, sine = cos_ref[:, at], sin_ref[:, at]
            place = (head // per_shard) * own_rows + lax.rem(head, per_shard) * HEAD_SIZE
            lin_ref[pl.ds(pl.multiple_of(place, 16), HEAD_SIZE), at] = jnp.concatenate(
                [first * cosine + second * sine, second * cosine - first * sine], axis=0
            ).astype(low)
            dk_s[:count, :] += contract(grad_scores, query, 1, 1)
            dv_s[:count, :] += contract(chances.astype(low), grad, 1, 1)
            dsink_ref[head] -= jnp.exp(sink_ref[head] - log_sum) * inner_sum

        def finish():
            grad_keys, grad_values = dk_s[...].T, dv_s[...].T
            first, second = grad_keys[:half], grad_keys[half:]
            cosine, sine = cos_ref[...], sin_ref[...]
            grad_keys = jnp.concatenate(
                [first * cosine + second * sine, second * cosine - first * sine], axis=0
            )
            for z in range(4):
                here = slice(z * kv_rows, (z + 1) * kv_rows)
                start = z * own_rows + q_rows
                lin_ref[start : start + kv_rows, :] = grad_keys[here].astype(low)
                lin_ref[start + kv_rows : start + 2 * kv_rows, :] = grad_values[here].astype(low)
            stores.copies[0].start()

        cut = 512

        def work(step):
            pl.when(step == 0)(loads.wait)
            first_step = 0
            for span in reversed(range(spans)):
                at_once = max(1, 16 // (span + 1))
                count = -(-heads // at_once)
                here = (step >= first_step) & (step < first_step + count)

                @pl.when(here)
                def _():
                    begin = (step - first_step) * at_once

                    def body(head, carry):
                        pl.when(head < heads)(lambda: one(head, span))
                        return carry

                    lax.fori_loop(begin, begin + at_once, body, 0)

                first_step += count
            pl.when(step == first_step)(finish)
            for i in range(-(-wide // cut)):

                @pl.when(step == first_step + i)
                def _():
                    at = slice(i * cut, min(wide, (i + 1) * cut))
                    weights_ref[:, at] = contract(lin_ref[...], normed_v[:, at], 1, 0).astype(low)

            pl.when(step == needed)(stores.copies[1].start)

        needed = sum(-(-heads // max(1, 16 // (span + 1))) for span in range(spans))
        needed += -(-wide // cut)
        late = pl.ds(first_column, columns)
        Scatter(4, parts_ref, o_ref, scratch, late).run(work, max(0, needed + 1 - 12))
        stores.wait()

    taken = (queries, keys, keys_t, values, grads, log_sums, cosine, sine, normed)
    hbm = pl.BlockSpec(memory_space=pl.ANY)
    vmem = pl.BlockSpec(memory_space=pltpu.VMEM)
    return pl.pallas_call(
        kernel,
        out_shape=(
            jax.ShapeDtypeStruct((block_rows, columns), f32),
            jax.ShapeDtypeStruct((4 * own_rows, length), low),
            jax.ShapeDtypeStruct((4 * own_rows, normed.shape[1]), low),
            jax.ShapeDtypeStruct((heads, 1, SPAN), f32),
        ),
        in_specs=[pl.BlockSpec(memory_space=pltpu.SMEM)] + [hbm] * 10,
        out_specs=(hbm, hbm, hbm, vmem),
        scratch_shapes=[
            pltpu.VMEM((length, HEAD_SIZE), f32),
            pltpu.VMEM((length, HEAD_SIZE), f32),
            pltpu.VMEM((4 * own_rows, length), low),
            pltpu.VMEM((4 * own_rows, wide), low),
            *(pltpu.VMEM(array.shape, array.dtype) for array in taken),
            pltpu.SemaphoreType.DMA((len(taken),)),
            pltpu.SemaphoreType.DMA((2,)),
            *scatter_scratch(4, block_rows, columns, low, 0),
        ],
        compiler_params=pltpu.CompilerParams(
            collective_id=collective, has_side_effects=True, vmem_limit_bytes=60 * MIB
        ),
        name="attention_back",
    )(sinks, parts, *taken)


PAIR = 2
STEP = 4


def routed(cols, capacity):
    expert = lax.axis_index("ctx")
    cols = cols.astype(jnp.float32)
    lane = lax.broadcasted_iota(jnp.int32, cols.shape, 1)
    place = jnp.sum(jnp.where(lane == 64 + expert, cols, 0.0), axis=1, keepdims=True)
    gate = jnp.sum(jnp.where(lane == 72 + expert, cols, 0.0), axis=1, keepdims=True)
    slot = lax.broadcasted_iota(jnp.int32, (cols.shape[0], PAIR * capacity), 1)
    picked = place.astype(jnp.int32) == slot
    return (
        jnp.where(picked, 1.0, 0.0).astype(jnp.bfloat16),
        jnp.where(picked, gate, 0.0).astype(jnp.bfloat16),
    )


class Stream:
    def __init__(self, arrays, sems, inward, first_sem=0):
        self.arrays, self.sems, self.inward, self.first_sem = arrays, sems, inward, first_sem

    def copies(self, slot, block):
        made = []
        for k, (array, slots, count, column) in enumerate(self.arrays):
            at = pl.ds(pl.multiple_of(block * count, 16), count)
            far = array.at[at] if column is None else array.at[at, column]
            pair = (far, slots.at[slot]) if self.inward else (slots.at[slot], far)
            made.append(pltpu.make_async_copy(*pair, self.sems.at[slot, self.first_sem + k]))
        return made

    def start(self, slot, block):
        for copy in self.copies(slot, block):
            copy.start()

    def wait(self, slot, block):
        for copy in self.copies(slot, block):
            copy.wait()


def two_of(shape, dtype):
    return pltpu.VMEM((2,) + shape, dtype)


def experts(sent, sent_grads, own_grads, gate_w, up_w, down_w, gate_b, up_b, down_b, capacity, collective):
    low, f32 = jnp.bfloat16, jnp.float32
    block_rows, wide = sent.shape
    share, width = gate_w.shape
    pad_share = -(-share // 128) * 128
    span = PAIR * block_rows
    pairs = STEP // PAIR
    count = PAIR * capacity
    tokens = 32 * block_rows
    slot_rows = 32 * capacity
    line = 4

    def kernel(
        sent_ref, sent_grads_ref, own_grads_ref, gate_hbm, up_hbm, down_hbm, gate_b_ref, up_b_ref, down_b_ref,
        all_ref, all_grads_ref, rows_out, gate_out, up_out, hidden_out, mix_out,
        grad_rows_out, gate_grad_out, up_grad_out, tokens_out, down_sum, gate_sum, up_sum,
        pair_v, down_v, x_s, rows_s, gate_s, up_s, hidden_s, mix_s, cols_s, gate_gs, up_gs,
        held_sems, in_sems, out_sems, *sems,
    ):
        held = [
            pltpu.make_async_copy(source, target, held_sems.at[k])
            for k, (source, target) in enumerate(
                (
                    (gate_hbm, pair_v.at[pl.ds(0, share)]),
                    (up_hbm, pair_v.at[pl.ds(pad_share, share)]),
                    (down_hbm, down_v),
                )
            )
        ]
        for copy in held:
            copy.start()
        pad = jnp.zeros((pairs * count, pad_share - share), low)
        for k in range(2):
            pair_v[k * pad_share + share : (k + 1) * pad_share, :] = jnp.zeros(
                (pad_share - share, width), low
            )
        forward_in = Stream([(all_ref, x_s, pairs * span, None)], in_sems, True)
        forward_out = Stream(
            [
                (rows_out, rows_s, pairs * count, None),
                (gate_out, gate_s, pairs * count, None),
                (up_out, up_s, pairs * count, None),
                (hidden_out, hidden_s, pairs * count, None),
                (mix_out, mix_s, pairs * span, None),
            ],
            out_sems,
            False,
        )
        kept = [
            (all_ref, cols_s, pairs * span, pl.ds(wide - 128, 128)),
            (gate_out, gate_s, pairs * count, None),
            (up_out, up_s, pairs * count, None),
        ]
        back_kept = Stream(kept, in_sems, True)
        back_own = Stream([(own_grads_ref, x_s, pairs * span, None)], in_sems, True, 3)
        back_far = Stream([(all_grads_ref, x_s, pairs * span, None)], in_sems, True, 3)
        back_out = Stream(
            [
                (grad_rows_out, rows_s, pairs * count, None),
                (gate_grad_out, gate_gs, pairs * count, None),
                (up_grad_out, up_gs, pairs * count, None),
                (tokens_out, mix_s, pairs * span, None),
            ],
            out_sems,
            False,
        )
        down_sum[...] = jnp.zeros_like(down_sum)
        gate_sum[...] = jnp.zeros_like(gate_sum)
        up_sum[...] = jnp.zeros_like(up_sum)
        for slot in range(2):
            mix_s[slot, :, width:] = jnp.zeros((pairs * span, wide - width), low)
        spans = [pl.ds(pair * span, span) for pair in range(pairs)]

        def forward(slot):
            picks = [routed(x_s[slot, at, wide - 128 :], capacity) for at in spans]
            rows = jnp.concatenate(
                [contract(picks[k][0], x_s[slot, spans[k], :], 0, 0) for k in range(pairs)],
                axis=0,
            ).astype(low)
            rows_s[slot] = rows
            rows = rows[:, :width]
            gate_lin = contract(rows, pair_v[:share, :], 1, 1) + gate_b_ref[...].astype(f32)
            up_lin = contract(rows, pair_v[pad_share : pad_share + share, :], 1, 1) + up_b_ref[...].astype(f32)
            gate_s[slot] = gate_lin
            up_s[slot] = up_lin
            hidden = glu_units(gate_lin, up_lin).astype(low)
            hidden_s[slot] = hidden
            out = contract(hidden, down_v[...], 1, 0) + down_b_ref[...]
            for k in range(pairs):
                part = out[k * count : (k + 1) * count].astype(low)
                mix_s[slot, spans[k], :width] = contract(picks[k][1], part, 1, 0).astype(low)

        def backward(slot):
            picks = [routed(cols_s[slot, at, :], capacity) for at in spans]
            rows = jnp.concatenate(
                [contract(picks[k][1], x_s[slot, spans[k], :], 0, 0) for k in range(pairs)],
                axis=0,
            ).astype(low)
            rows_s[slot] = rows
            rows = rows[:, :width]
            down_sum[...] += jnp.sum(rows.astype(f32), axis=0, keepdims=True)
            grad_units = contract(rows, down_v[...], 1, 1)
            gate_tanh = jnp.tanh(gate_s[slot] / CLAMP_LIMIT)
            up_tanh = jnp.tanh(up_s[slot] / CLAMP_LIMIT)
            gated = CLAMP_LIMIT * gate_tanh
            lifted = CLAMP_LIMIT * up_tanh + 1.0
            part = jax.nn.sigmoid(GLU_ALPHA * gated)
            grad_up = (grad_units * gated * part * (1.0 - up_tanh * up_tanh)).astype(low)
            slope = part * (1.0 + GLU_ALPHA * gated * (1.0 - part))
            grad_gate = (grad_units * lifted * slope * (1.0 - gate_tanh * gate_tanh)).astype(low)
            gate_gs[slot] = grad_gate
            up_gs[slot] = grad_up
            gate_sum[...] += jnp.sum(grad_gate.astype(f32), axis=0, keepdims=True)
            up_sum[...] += jnp.sum(grad_up.astype(f32), axis=0, keepdims=True)
            both = jnp.concatenate([grad_gate, pad, grad_up, pad], axis=1)
            copies = contract(both, pair_v[...], 1, 0)
            for k in range(pairs):
                part = copies[k * count : (k + 1) * count].astype(low)
                mix_s[slot, spans[k], :width] = contract(picks[k][0], part, 1, 0).astype(low)

        ahead = Gather(line, sent_ref, all_ref, sems[:9], TAIL)
        back = Gather(line, sent_grads_ref, all_grads_ref, sems[9:], TAIL, own_grads_ref)
        y_at = ahead.me // 4

        def block(step):
            half = lax.rem(step, 2)
            return ahead.slot(step // 2) * 2 + (1 - half) * y_at + half * (1 - y_at)

        ahead.begin()

        steps = 2 * line

        def forward_order(order, carry):
            @pl.when(order < line)
            def _():
                ahead.second(order)
                pl.when(order + 1 < line)(lambda: ahead.first(order + 1))
                pl.when(order > 0)(lambda: ahead.tails(order))
                pl.when(order == 1)(back.begin_line)
                pl.when(order == 2)(back.send_tails)
                pl.when(order == line - 1)(lambda: back.first(1))
                ahead.near(order)

                @pl.when(order == 0)
                def _():
                    ahead.own_block()
                    for copy in held:
                        copy.wait()

                forward_in.start(0, block(2 * order))

            def half_plane(step, carry):
                slot = lax.rem(step, 2)
                forward_in.wait(slot, block(step))
                pl.when(step >= 2)(lambda: forward_out.wait(slot, block(step - 2)))
                forward(slot)
                forward_out.start(slot, block(step))
                return carry

            lax.fori_loop(
                jnp.maximum(2 * order - 1, 0), jnp.minimum(2 * order + 1, steps), half_plane, 0
            )

            @pl.when(order < line)
            def _():
                ahead.third(order)
                pl.when(order == 0)(ahead.send_tails)
                forward_in.start(1, block(2 * order + 1))

            return carry

        lax.fori_loop(0, line + 1, forward_order, 0)
        back.second(1)
        back.first(2)
        forward_out.wait(0, block(steps - 2))
        forward_out.wait(1, block(steps - 1))

        def grads_in(step, act):
            order, half = step // 2, lax.rem(step, 2)
            act(back_kept, half, block(step))
            pl.when(order == 0)(
                lambda: act(back_own, half, (1 - half) * y_at + half * (1 - y_at))
            )
            pl.when(order > 0)(lambda: act(back_far, half, block(step)))

        def backward_step(step, carry):
            order, half = step // 2, lax.rem(step, 2)
            pl.when(half == 1)(lambda: grads_in(step, Stream.start))

            @pl.when(step > 0)
            def _():
                slot = 1 - half
                pl.when(step >= 3)(lambda: back_out.wait(slot, block(step - 3)))
                grads_in(step - 1, Stream.wait)
                backward(slot)
                back_out.start(slot, block(step - 1))

            @pl.when((half == 0) & (order < line))
            def _():
                @pl.when(order > 0)
                def _():
                    back.tails(order)
                    back.near(order)
                    back.third(order)

                grads_in(step, Stream.start)

            @pl.when((half == 1) & (order > 0))
            def _():
                pl.when(order + 1 < line)(lambda: back.second(order + 1))
                pl.when(order + 2 < line)(lambda: back.first(order + 2))

            return carry

        lax.fori_loop(0, steps + 1, backward_step, 0)
        back_out.wait(0, block(steps - 2))
        back_out.wait(1, block(steps - 1))
        ahead.end()
        back.end(1)

    hbm = pl.BlockSpec(memory_space=pl.ANY)
    vmem = pl.BlockSpec(memory_space=pltpu.VMEM)

    def made(rows, columns, dtype=low):
        return jax.ShapeDtypeStruct((rows, columns), dtype)

    return pl.pallas_call(
        kernel,
        out_shape=(
            made(tokens, wide),
            made(tokens, wide),
            made(slot_rows, wide),
            made(slot_rows, share, f32),
            made(slot_rows, share, f32),
            made(slot_rows, share),
            made(tokens, wide),
            made(slot_rows, wide),
            made(slot_rows, share),
            made(slot_rows, share),
            made(tokens, wide),
            made(1, width, f32),
            made(1, share, f32),
            made(1, share, f32),
        ),
        in_specs=[hbm] * 6 + [vmem] * 3,
        out_specs=(hbm,) * 11 + (vmem,) * 3,
        scratch_shapes=[
            pltpu.VMEM((2 * pad_share, width), low),
            pltpu.VMEM(down_w.shape, low),
            two_of((pairs * span, wide), low),
            two_of((pairs * count, wide), low),
            two_of((pairs * count, share), f32),
            two_of((pairs * count, share), f32),
            two_of((pairs * count, share), low),
            two_of((pairs * span, wide), low),
            two_of((pairs * span, 128), low),
            two_of((pairs * count, share), low),
            two_of((pairs * count, share), low),
            pltpu.SemaphoreType.DMA((3,)),
            pltpu.SemaphoreType.DMA((2, 4)),
            pltpu.SemaphoreType.DMA((2, 5)),
            *gather_sems(line, TAIL),
            *gather_sems(line, TAIL),
        ],
        compiler_params=pltpu.CompilerParams(
            collective_id=collective, has_side_effects=True, vmem_limit_bytes=60 * MIB
        ),
        name="experts",
    )(sent, sent_grads, own_grads, gate_w, up_w, down_w, gate_b, up_b, down_b)


def expert_weights(parts, rows_in, gate_grad, up_grad, rows_grad, hidden, collective):
    low, f32 = jnp.bfloat16, jnp.float32
    slot_rows, wide = rows_in.shape
    share = gate_grad.shape[1]
    block_rows, width = parts.shape[0] // 32, parts.shape[1]
    cut = 256
    whole, rest = wide // cut, wide % cut
    count = whole + 1

    def kernel(
        parts_ref, rows_hbm, gate_hbm, up_hbm, grad_hbm, hidden_hbm, o_ref, gate_out, up_out, down_out,
        stage, first_t, second_t, in_s, first_s, second_s, held_sem, in_sems, out_sems, *scratch,
    ):
        def held(source):
            return pltpu.make_async_copy(source, stage, held_sem)

        held(gate_hbm).start()

        def begin(copy):
            copy.start()

        def await_it(copy):
            copy.wait()

        def by_width(index, act):
            pl.when((index >= 0) & (index < whole))(lambda: act(cut))
            pl.when(index == whole)(lambda: act(rest))

        def loads(chunk, act):
            slot = lax.rem(chunk, 2)
            for source, index in ((rows_hbm, chunk), (grad_hbm, chunk - count)):

                def one(columns):
                    at = pl.ds(pl.multiple_of(index * cut, cut), columns)
                    here = in_s.at[slot, :, pl.ds(0, columns)]
                    act(pltpu.make_async_copy(source.at[:, at], here, in_sems.at[slot]))

                by_width(index, one)

        def stores(chunk, act):
            slot = lax.rem(chunk, 2)
            for targets, index in (
                (((first_s, gate_out), (second_s, up_out)), chunk),
                (((first_s, down_out),), chunk - count),
            ):

                def one(columns):
                    at = pl.ds(pl.multiple_of(index * cut, cut), columns)
                    for k, (source, target) in enumerate(targets):
                        here = source.at[slot, :, pl.ds(0, columns)]
                        act(pltpu.make_async_copy(here, target.at[:, at], out_sems.at[slot, k]))

                by_width(index, one)

        def work(chunk):
            slot = lax.rem(chunk, 2)

            @pl.when(chunk == 0)
            def _():
                loads(0, begin)
                held(gate_hbm).wait()
                first_t[...] = stage[...].T
                held(up_hbm).start()
                held(up_hbm).wait()
                second_t[...] = stage[...].T
                held(hidden_hbm).start()

            @pl.when(chunk == count)
            def _():
                held(hidden_hbm).wait()
                first_t[...] = stage[...].T

            pl.when(chunk + 1 < 2 * count)(lambda: loads(chunk + 1, begin))
            pl.when(chunk >= 2)(lambda: stores(chunk - 2, await_it))
            loads(chunk, await_it)
            first_s[slot] = contract(first_t[...], in_s[slot], 1, 0).astype(low)

            @pl.when(chunk < count)
            def _():
                second_s[slot] = contract(second_t[...], in_s[slot], 1, 0).astype(low)

            stores(chunk, begin)

        def works(step):
            def body(chunk, carry):
                work(chunk)
                return carry

            lax.fori_loop(2 * step, 2 * step + 2, body, 0)

        Scatter(4, parts_ref, o_ref, scratch).run(works, count - 12)
        stores(2 * count - 2, await_it)
        stores(2 * count - 1, await_it)

    hbm = pl.BlockSpec(memory_space=pl.ANY)
    return pl.pallas_call(
        kernel,
        out_shape=(
            jax.ShapeDtypeStruct((block_rows, width), f32),
            jax.ShapeDtypeStruct((share, wide), low),
            jax.ShapeDtypeStruct((share, wide), low),
            jax.ShapeDtypeStruct((share, wide), low),
        ),
        in_specs=[hbm] * 6,
        out_specs=(hbm,) * 4,
        scratch_shapes=[
            pltpu.VMEM(gate_grad.shape, low),
            pltpu.VMEM(gate_grad.shape[::-1], low),
            pltpu.VMEM(gate_grad.shape[::-1], low),
            two_of((slot_rows, cut), low),
            two_of((share, cut), low),
            two_of((share, cut), low),
            pltpu.SemaphoreType.DMA,
            pltpu.SemaphoreType.DMA((2,)),
            pltpu.SemaphoreType.DMA((2, 2)),
            *scatter_scratch(4, block_rows, width, low),
        ],
        compiler_params=pltpu.CompilerParams(
            collective_id=collective, has_side_effects=True, vmem_limit_bytes=60 * MIB
        ),
        name="expert_weights",
    )(parts, rows_in, gate_grad, up_grad, rows_grad, hidden)


def product_kernel(left_ref, right_ref, out_ref):
    right = right_ref[:, : out_ref.shape[1]]
    out_ref[...] = contract(left_ref[...], right, 0, 0).astype(out_ref.dtype)


def product(left_t, right, name, columns=None):
    depth, rows = left_t.shape
    columns = columns or right.shape[1]
    return pl.pallas_call(
        product_kernel,
        grid=(rows // SPAN,),
        out_shape=jax.ShapeDtypeStruct((rows, columns), jnp.bfloat16),
        in_specs=[
            pl.BlockSpec((depth, SPAN), lambda i: (0, i)),
            pl.BlockSpec(right.shape, lambda i: (0, 0), pipeline_mode=pl.Buffered(1)),
        ],
        out_specs=pl.BlockSpec((SPAN, columns), lambda i: (i, 0)),
        compiler_params=pltpu.CompilerParams(vmem_limit_bytes=40 * MIB),
        cost_estimate=pl.CostEstimate(
            flops=2 * depth * rows * columns, bytes_accessed=4 * rows * columns, transcendentals=0
        ),
        name=name,
    )(left_t, right)


def finish_kernel(
    width, grads_ref, out_grads_ref, query_ref, key_ref, value_ref, query_b, key_b, value_b, out_ref
):
    grads = grads_ref[...].astype(jnp.float32)
    q_rows = query_ref.shape[1]
    kv_rows = key_ref.shape[0]
    query_ref[...] = grads[:q_rows, :width].T
    key_ref[...] = grads[q_rows : q_rows + kv_rows, :width]
    value_ref[...] = grads[q_rows + kv_rows :, :width]
    lane = width // 128 * 128
    bias = grads[:, lane : lane + 128].T[width - lane : width - lane + 1, :]
    query_b[...] = bias[:, :q_rows]
    key_b[...] = bias[:, q_rows : q_rows + kv_rows]
    value_b[...] = bias[:, q_rows + kv_rows :]
    out_ref[...] = out_grads_ref[...].astype(jnp.float32).T


def finished(grads, out_grads, q_rows):
    rows = grads.shape[0]
    width = out_grads.shape[1]
    kv_rows = (rows - q_rows) // 2
    vmem = pl.BlockSpec(memory_space=pltpu.VMEM)
    return pl.pallas_call(
        lambda *refs: finish_kernel(width, *refs),
        out_shape=tuple(
            jax.ShapeDtypeStruct(shape, jnp.float32)
            for shape in (
                (width, q_rows), (kv_rows, width), (kv_rows, width), (1, q_rows), (1, kv_rows),
                (1, kv_rows), (width, out_grads.shape[0]),
            )
        ),
        in_specs=[vmem] * 2,
        out_specs=(vmem,) * 7,
        compiler_params=pltpu.CompilerParams(vmem_limit_bytes=60 * MIB),
        name="finished",
    )(grads, out_grads)


def input_back(grad_lin, weights, normed, rows_in, gain, grad_rows, collective, small):
    low, f32 = jnp.bfloat16, jnp.float32
    depth, length = grad_lin.shape
    block_rows, width = rows_in.shape
    wide = normed.shape[1]
    columns = small.shape[1]
    gain_columns = -(-wide // (16 * 128)) * 128

    def kernel(
        lin_ref, weights_ref, normed_hbm, small_ref, rows_ref, gain_ref, grad_ref, o_ref, all_sums,
        result_ref,
        normed_v, part, found_v, sums_v, grad_v, sem, *scratch,
    ):
        gather = Gather(4, sums_v, all_sums, scratch[:5])
        scatter = Scatter(1, part, o_ref, scratch[5:])
        loads = []
        for k in range(4):
            at = pl.ds(pl.multiple_of(scatter.places[k] // 2 * SPAN, SPAN), SPAN)
            loads.append(pltpu.make_async_copy(normed_hbm.at[at], normed_v.at[at], sem.at[k]))
            loads[k].start()
        greet((gather.mate, gather.near_x, gather.near_y), 4, gather.z_at)
        found_v[...] = jnp.zeros_like(found_v)

        def make(chip):
            at = pl.ds(pl.multiple_of(chip * SPAN, SPAN), SPAN)
            value = contract(lin_ref[:, at], weights_ref[...], 0, 0)
            part[at, :] = value[:, :width].astype(low)
            loads.pop(0).wait()
            found = value * normed_v[at, :].astype(f32)
            found_v[...] += jnp.sum(found, axis=0, keepdims=True)

        scatter.produce(make)
        sums_v[:, :columns] = small_ref[...]
        sums_v[:, columns:] = jnp.zeros((16, gain_columns), f32)
        for k in range(wide // 128):
            row, lane = k // (gain_columns // 128), k % (gain_columns // 128) * 128
            sums_v[row : row + 1, columns + lane : columns + lane + 128] = found_v[
                :, k * 128 : (k + 1) * 128
            ]
        gather.begin(True)
        for order in (1, 2, 3):
            gather.first(order)
        for order in range(4):
            gather.second(order)
        scatter.second(0)
        for order in range(4):
            gather.near(order)
            gather.third(order)
        scatter.third(0, scatter.total)

        def through_norm(i, carry):
            at = pl.ds(pl.multiple_of(i * CHUNK, CHUNK), CHUNK)
            value = rows_ref[at, :].astype(f32)
            scale = lax.rsqrt(jnp.mean(value * value, axis=-1, keepdims=True) + EPSILON)
            grad = scatter.total[at, :] * gain_ref[...]
            inner = jnp.mean(grad * value, axis=-1, keepdims=True)
            grad_v[at, :] = (
                grad_ref[at, :] + grad * scale - value * (scale * scale * scale * inner)
            )
            return carry

        lax.fori_loop(0, block_rows // CHUNK, through_norm, 0)
        result_ref[...] = grad_v[...].T
        scatter.end()
        gather.own_block()
        gather.end()

    hbm = pl.BlockSpec(memory_space=pl.ANY)
    vmem = pl.BlockSpec(memory_space=pltpu.VMEM)
    return pl.pallas_call(
        kernel,
        out_shape=(
            jax.ShapeDtypeStruct((block_rows, width), f32),
            jax.ShapeDtypeStruct((32 * 16, columns + gain_columns), f32),
            jax.ShapeDtypeStruct((width, block_rows), f32),
        ),
        in_specs=[vmem, vmem, hbm] + [vmem] * 4,
        out_specs=(hbm, hbm, vmem),
        scratch_shapes=[
            pltpu.VMEM((length, wide), low),
            pltpu.VMEM((length, width), low),
            pltpu.VMEM((1, wide), f32),
            pltpu.VMEM((16, columns + gain_columns), f32),
            pltpu.VMEM((block_rows, width), f32),
            pltpu.SemaphoreType.DMA((4,)),
            *gather_sems(4),
            *scatter_scratch(1, block_rows, width, low),
        ],
        compiler_params=pltpu.CompilerParams(
            collective_id=collective, has_side_effects=True, vmem_limit_bytes=58 * MIB
        ),
        name="input_back",
    )(grad_lin, weights, normed, small, rows_in, gain, grad_rows)


def shards(
    layer_input, cotangent, gate_weights, routes, w_query, key_projection, value_projection, w_out,
    b_query, key_bias_vector, value_bias_vector, b_out, learned_sink_logits, gain_attn, gain_ffn,
    w_gate, w_up, w_down, b_gate, b_up, b_down,
):
    low = jnp.bfloat16
    ctx_n, z_n = lax.axis_size("ctx"), lax.axis_size("fsdp")
    ctx_at, z_at = lax.axis_index("ctx"), lax.axis_index("fsdp")
    tuned = ctx_n == 8 and z_n == 4
    width = layer_input.shape[-1]
    rows = layer_input.shape[0] * layer_input.shape[1]
    length = rows * ctx_n
    blocks = ctx_n * z_n
    capacity = max(2, rows * TOP * 17 // (16 * ctx_n))
    heads = QUERY_HEADS // ctx_n
    spread = ctx_n // KEY_VALUE_HEADS
    f32 = jnp.float32

    def gather_plane(value, call):
        if tuned:
            return gather_blocks(value, 1, call, f"gather_plane_{call}")
        return lax.all_gather(value, "ctx", axis=0, tiled=True)

    def scatter_plane(value, call):
        if tuned:
            return scatter_blocks(value, 1, call, f"scatter_plane_{call}")
        return lax.psum_scatter(value, "ctx", scatter_dimension=0, tiled=True).astype(f32)

    residual = layer_input.reshape(rows, width).astype(f32)
    grad_final = cotangent.reshape(rows, width)
    gain_attn_f, gain_ffn_f = gain_attn.astype(f32), gain_ffn.astype(f32)
    cosine, sine = rotary_tables(length)

    q_cols, k_cols = w_query.shape[1], key_projection.shape[1]
    own_rows = q_cols + 2 * k_cols
    wide = -(-(width + 2 * ctx_n) // 128) * 128
    biases = jnp.concatenate([b_query, key_bias_vector, value_bias_vector])
    own_weights = jnp.concatenate([w_query, key_projection, value_projection], axis=1).T
    own_weights = jnp.concatenate(
        [own_weights, biases[:, None], jnp.zeros((own_rows, wide - width - 1), low)], axis=1
    )
    ones = jnp.concatenate(
        [jnp.ones((rows, 1), low), jnp.zeros((rows, wide - width - 1), low)], axis=1
    )

    token_routes = routes.reshape(rows, TOP)
    names = jnp.arange(ctx_n, dtype=jnp.int32)
    named = token_routes[:, :, None] == names[None, None, :]
    hits = jnp.sum(named.astype(f32), axis=1)
    gates = jnp.sum(
        jnp.where(named, gate_weights.reshape(rows, TOP)[:, :, None].astype(f32), 0.0), axis=1
    )
    earlier = (
        lax.broadcasted_iota(jnp.int32, (rows, rows), 0)
        > lax.broadcasted_iota(jnp.int32, (rows, rows), 1)
    ).astype(low)
    places = jnp.dot(earlier, hits.astype(low), preferred_element_type=f32)
    first_slot = (lax.rem(ctx_at, PAIR) * capacity).astype(f32) if tuned else 0.0
    places = jnp.where(hits > 0, places + first_slot, -1.0)
    slot_rows = blocks * capacity
    if not tuned:
        slots = jnp.arange(capacity, dtype=f32)[None, :, None]
        picked = places.T[:, None, :] == slots
        select = picked.astype(low)
        mixing = jnp.where(picked, gates.T[:, None, :], 0.0).astype(low)

    def exchanged(slot_values):
        moved = slot_values.reshape(ctx_n, capacity, width)
        return lax.all_to_all(moved, "ctx", split_axis=0, concat_axis=0, tiled=True)

    def to_slots(picks, token_rows):
        dims = (((2,), (0,)), ((), ()))
        moved = lax.dot_general(picks, token_rows, dims, preferred_element_type=f32).astype(low)
        moved = lax.all_gather(exchanged(moved), "fsdp", axis=0, tiled=True)
        return moved.reshape(slot_rows, width)

    def to_tokens(picks, slot_values):
        slot_values = exchanged(
            lax.psum_scatter(slot_values, "fsdp", scatter_dimension=0, tiled=True)
        )
        dims = (((1,), (1,)), ((0,), (0,)))
        moved = lax.dot_general(picks, slot_values, dims, preferred_element_type=f32)
        return jnp.sum(moved, axis=0)

    normed_own = jnp.concatenate([norm_scale(residual, gain_attn_f).astype(low), ones], axis=1)
    sinks = lax.dynamic_slice(learned_sink_logits.astype(f32), (ctx_at * heads,), (heads,))
    swap = [(i, i ^ 1) for i in range(ctx_n)]
    odd = lax.rem(ctx_at, 2) == 1
    if tuned:
        sent_grads = jnp.pad(grad_final, ((0, 0), (0, wide - width)))
        branch, normed_attn, own_grads, head_weights, out_weights, *kept = attention(
            normed_own, sent_grads, own_weights, w_out, sinks, cosine, sine, 1
        )
        queries, keys, keys_t, values, attended, log_sums = kept
    else:
        normed_attn = lax.all_gather(normed_own, "ctx", axis=0, tiled=True)
        head_weights = lax.all_gather(own_weights, "fsdp", axis=0, tiled=True)
        out_weights = lax.all_gather(w_out, "fsdp", axis=0, tiled=True)
        lin = contract(head_weights, normed_attn, 1, 1).reshape(z_n, own_rows, length)
        query_lin = lin[:, :q_cols].reshape(heads, HEAD_SIZE, length)
        kv_lin = jnp.stack([lin[:, q_cols : q_cols + k_cols], lin[:, q_cols + k_cols :]])
        kv_lin = kv_lin.reshape(2, z_n * k_cols, length)
        if spread == 2:
            other = lax.ppermute(kv_lin, "ctx", swap)
            kv_lin = jnp.where(
                odd,
                jnp.concatenate([other, kv_lin], axis=1),
                jnp.concatenate([kv_lin, other], axis=1),
            )
        queries = turned(query_lin, cosine, sine).astype(low).reshape(heads * HEAD_SIZE, length)
        keys_t = turned(kv_lin[:1], cosine, sine)[0].astype(low)
        values_t = kv_lin[1].astype(low)
        keys, values = keys_t.T, values_t.T
        attended, log_sums = attend(sinks, queries, keys, values_t)
        branch = scatter_plane(product(attended, out_weights, "branch"), 2)
    middle = residual + branch + b_out.astype(f32)
    normed_ffn = norm_scale(middle, gain_ffn_f).astype(low)

    gate_w, up_w, down_w = w_gate[0].T, w_up[0].T, w_down[0]
    share = b_down.shape[1]
    down_bias = lax.dynamic_update_slice(
        jnp.zeros((1, width), f32), b_down.astype(f32), (0, z_at * share)
    )
    if tuned:
        sent = jnp.concatenate(
            [
                normed_ffn,
                places.astype(low),
                gates.astype(low),
                jnp.zeros((rows, wide - width - 2 * ctx_n), low),
            ],
            axis=1,
        )
        made = experts(
            sent, sent_grads, own_grads, gate_w, up_w, down_w, b_gate, b_up, down_bias, capacity, 3
        )
        expert_in, hidden_units, mix_part = made[2], made[5], made[6]
        grad_expert_out, grad_gate_lin, grad_up_lin, grad_normed_part = made[7:11]
        grad_biases = made[11:]
        grad_b_down, grad_b_gate, grad_b_up = [value[0] for value in grad_biases]
        grad_normed_ffn, grad_w_gate, grad_w_up, grad_w_down = expert_weights(
            grad_normed_part, expert_in, grad_gate_lin, grad_up_lin, grad_expert_out, hidden_units, 6
        )
        grad_normed_ffn = grad_normed_ffn[:, :width]
    else:
        expert_in = to_slots(select, normed_ffn)
        gate_lin = contract(expert_in, gate_w, 1, 1) + b_gate.astype(f32)
        up_lin = contract(expert_in, up_w, 1, 1) + b_up.astype(f32)
        hidden_f, unit_back = jax.vjp(glu_units, gate_lin, up_lin)
        hidden_units = hidden_f.astype(low)
        expert_out = (contract(hidden_units, down_w, 1, 0) + down_bias).astype(low)
        expert_mix = to_tokens(mixing, expert_out)
        grad_expert_out = to_slots(mixing, grad_final)
        grad_units = contract(grad_expert_out, down_w, 1, 1)
        grad_gate_f, grad_up_f = unit_back(grad_units)
        grad_gate_lin, grad_up_lin = grad_gate_f.astype(low), grad_up_f.astype(low)
        grad_copy = contract(grad_gate_lin, gate_w, 1, 0) + contract(grad_up_lin, up_w, 1, 0)
        grad_normed_ffn = to_tokens(select, grad_copy.astype(low))
        grad_b_down = jnp.sum(grad_expert_out.astype(f32), axis=0)
        grad_b_gate = jnp.sum(grad_gate_lin.astype(f32), axis=0)
        grad_b_up = jnp.sum(grad_up_lin.astype(f32), axis=0)
        grad_w_gate = contract(grad_gate_lin, expert_in, 0, 0)
        grad_w_up = contract(grad_up_lin, expert_in, 0, 0)
        grad_w_down = contract(hidden_units, grad_expert_out, 0, 0)
    grad_b_down = lax.dynamic_slice(grad_b_down, (z_at * share,), (share,))

    unused, norm_back = jax.vjp(norm_scale, middle, gain_ffn_f)
    grad_middle_part, grad_gain_ffn = norm_back(grad_normed_ffn)
    grad_middle = grad_final.astype(f32) + grad_middle_part
    grad_branch_own = grad_middle.astype(low)
    grad_b_out = jnp.sum(grad_branch_own.astype(f32), axis=0)
    if tuned:
        early = 1024
        first_mix, grad_attended, grad_out_part = branch_back(
            mix_part, early, grad_branch_own, out_weights, attended, 7
        )
        late_mix, grad_lin, grad_weights, grad_sink_parts = attention_back(
            mix_part, early, sinks, queries, keys, keys_t, values, grad_attended, log_sums, cosine,
            sine, normed_attn, own_rows, 5,
        )
        expert_mix = jnp.concatenate([first_mix, late_mix[:, : width - early]], axis=1)
    else:
        grad_branch = lax.all_gather(grad_branch_own, "ctx", axis=0, tiled=True)
        grad_attended = contract(out_weights, grad_branch, 1, 1).astype(low)
        grad_out_part = contract(attended, grad_branch, 1, 0).astype(low)
        grad_query, grad_keys, grad_values, grad_sink_parts = attend_back(
            sinks, queries, keys, keys_t, values, grad_attended, log_sums, cosine, sine
        )
        grad_kv = jnp.stack([turned(grad_keys.T[None], cosine, -sine)[0], grad_values.T])
        if spread == 2:
            grad_kv = grad_kv + lax.ppermute(grad_kv, "ctx", swap)
            halves = grad_kv.reshape(2, 2, HEAD_SIZE // 2, length)
            grad_kv = jnp.where(odd, halves[:, 1], halves[:, 0])
        grad_kv = grad_kv.astype(low).reshape(2, z_n, k_cols, length)
        grad_lin = jnp.concatenate(
            [grad_query.reshape(z_n, q_cols, length), grad_kv[0], grad_kv[1]], axis=1
        ).reshape(z_n * own_rows, length)
        grad_weights = contract(grad_lin, normed_attn, 1, 0).astype(low)
    final_out = (middle + expert_mix).astype(low).reshape(layer_input.shape)
    own_out_grads = lax.psum_scatter(grad_out_part, "fsdp", scatter_dimension=0, tiled=True)
    own_grads = lax.psum_scatter(grad_weights, "fsdp", scatter_dimension=0, tiled=True)
    if tuned:
        grad_w_query, grad_w_key, grad_w_value, *own_bias_grads, grad_w_out = finished(
            own_grads, own_out_grads, q_cols
        )
        own_bias_grads, grad_w_out = [value[0] for value in own_bias_grads], grad_w_out.T
    else:
        own_grads = own_grads.astype(f32)
        grad_w_out = own_out_grads.astype(f32)
        grad_w_query = own_grads[:q_cols, :width].T
        grad_w_key = own_grads[q_cols : q_cols + k_cols, :width]
        grad_w_value = own_grads[q_cols + k_cols :, :width]
        own_bias_grads = jnp.split(own_grads[:, width], (q_cols, q_cols + k_cols))
    grad_w_key, grad_w_value = grad_w_key.T, grad_w_value.T
    grad_sinks = lax.dynamic_update_slice(
        jnp.zeros((QUERY_HEADS,), f32), jnp.sum(grad_sink_parts, axis=(1, 2)), (ctx_at * heads,)
    )
    sums = (grad_b_out, grad_gain_ffn, grad_sinks)
    if tuned:
        joined = jnp.concatenate(sums)
        columns = -(-joined.shape[0] // (16 * 128)) * 128
        joined = jnp.pad(joined, (0, 16 * columns - joined.shape[0])).reshape(16, columns)
        unused, joined, input_grad = input_back(
            grad_lin, head_weights, normed_attn, layer_input.reshape(rows, width),
            gain_attn_f.reshape(1, width), grad_middle, 8, joined,
        )
        input_grad = input_grad.T.reshape(layer_input.shape)
        joined = jnp.sum(joined.reshape(blocks, 16, -1), axis=0)
        grad_gain_attn = joined[:, columns:].reshape(-1)[:width] / gain_attn_f
        joined = joined[:, :columns].reshape(-1)
        cuts = (width, 2 * width, 2 * width + QUERY_HEADS)
        sums = [joined[at - value.shape[0] : at] for at, value in zip(cuts, sums)]
    else:
        grad_normed_part = product(grad_lin, head_weights, "grad_normed", width)
        grad_normed_attn = scatter_plane(grad_normed_part, 8)
        unused, norm_back = jax.vjp(norm_scale, residual, gain_attn_f)
        grad_residual_part, own_gain = norm_back(grad_normed_attn)
        input_grad = (grad_middle + grad_residual_part).reshape(layer_input.shape)
        *sums, grad_gain_attn = lax.psum((*sums, own_gain), ("ctx", "fsdp"))
    grad_b_out, grad_gain_ffn, grad_sink_logits = sums
    return (
        final_out,
        input_grad,
        grad_w_query,
        grad_w_key,
        grad_w_value,
        grad_w_out,
        *own_bias_grads,
        grad_b_out,
        grad_sink_logits,
        grad_gain_attn,
        grad_gain_ffn,
        grad_w_gate[:, :width].astype(f32).T[None],
        grad_w_up[:, :width].astype(f32).T[None],
        grad_w_down[:, :width].astype(f32)[None],
        grad_b_gate[None],
        grad_b_up[None],
        grad_b_down[None],
    )


def solution(mesh):
    return jax.shard_map(
        shards,
        mesh=mesh,
        in_specs=(
            P("fsdp", "ctx", None),
            P("fsdp", "ctx", None),
            P("fsdp", "ctx", None),
            P("fsdp", "ctx", None),
            P(None, ("ctx", "fsdp")),
            P(None, ("ctx", "fsdp")),
            P(None, ("ctx", "fsdp")),
            P(("ctx", "fsdp"), None),
            P(("ctx", "fsdp")),
            P(("ctx", "fsdp")),
            P(("ctx", "fsdp")),
            P(),
            P(),
            P(),
            P(),
            P("ctx", None, "fsdp"),
            P("ctx", None, "fsdp"),
            P("ctx", "fsdp", None),
            P("ctx", "fsdp"),
            P("ctx", "fsdp"),
            P("ctx", "fsdp"),
        ),
        out_specs=(
            P("fsdp", "ctx", None),
            P("fsdp", "ctx", None),
            P(None, ("ctx", "fsdp")),
            P(None, ("ctx", "fsdp")),
            P(None, ("ctx", "fsdp")),
            P(("ctx", "fsdp"), None),
            P(("ctx", "fsdp")),
            P(("ctx", "fsdp")),
            P(("ctx", "fsdp")),
            P(),
            P(),
            P(),
            P(),
            P("ctx", None, "fsdp"),
            P("ctx", None, "fsdp"),
            P("ctx", "fsdp", None),
            P("ctx", "fsdp"),
            P("ctx", "fsdp"),
            P("ctx", "fsdp"),
        ),
        check_vma=False,
    )
```

```python
import jax
import jax.numpy as jnp
import numpy as np
from jax import lax
from jax.experimental import pallas as pl
from jax.experimental.pallas import tpu as pltpu
from jax.sharding import PartitionSpec as P

MESH = pl.DeviceIdType.MESH
MIB = 1 << 20


def remote(src, dst, send_sem, recv_sem, device):
    return pltpu.make_async_remote_copy(
        src_ref=src,
        dst_ref=dst,
        send_sem=send_sem,
        recv_sem=recv_sem,
        device_id=device,
        device_id_type=MESH,
    )


def neighbours():
    me = lax.axis_index("ctx")
    core = lax.rem(me, 2)
    x_at = lax.rem(me // 2, 2)
    y_at = me // 4
    return me, me + 1 - 2 * core, me + 2 - 4 * x_at, me + 4 - 8 * y_at, 2 - 4 * x_at


def greet(others, line, z_at):
    barrier = pltpu.get_barrier_semaphore()
    for other in others:
        pl.semaphore_signal(barrier, 1, device_id=(other, z_at), device_id_type=MESH)
    if line == 1:
        pl.semaphore_wait(barrier, len(others))
        return
    me = lax.axis_index("ctx")

    @pl.when(z_at > 0)
    def _():
        pl.semaphore_signal(barrier, 1, device_id=(me, z_at - 1), device_id_type=MESH)

    @pl.when(z_at < line - 1)
    def _():
        pl.semaphore_signal(barrier, 1, device_id=(me, z_at + 1), device_id_type=MESH)

    inner = (lax.rem(z_at, 3) + 1) // 2
    pl.semaphore_wait(barrier, len(others) + 1 + inner)


def gather_sems(line, tail=0):
    sems = [
        pltpu.SemaphoreType.DMA,
        pltpu.SemaphoreType.DMA((line, 2)),
        pltpu.SemaphoreType.DMA((line,)),
        pltpu.SemaphoreType.DMA((line, 9)),
        pltpu.SemaphoreType.DMA((line, 9)),
    ]
    if tail:
        sems += [
            pltpu.SemaphoreType.DMA((line, 2, 4)),
            pltpu.SemaphoreType.DMA((line, 4)),
            pltpu.SemaphoreType.DMA((line, 4)),
            pltpu.SemaphoreType.DMA((line, 4)),
        ]
    return sems


class Gather:
    def __init__(self, line, x_ref, o_ref, sems, tail=0, own_blocks=None):
        self.line, self.x_ref, self.o_ref, self.tail = line, x_ref, o_ref, tail
        self.own_sem, self.z_send, self.z_recv, self.p_send, self.p_recv = sems[:5]
        if tail:
            self.t_send, self.t_recv, self.q_send, self.q_recv = sems[5:]
        self.own_blocks = own_blocks
        self.z_at = lax.axis_index("fsdp")
        self.me, self.mate, self.near_x, self.near_y, step_x = neighbours()
        self.across = self.near_y + step_x
        self.places = (self.me, self.near_x, self.near_y, self.across)
        self.rows = x_ref.shape[0]
        self.half = self.rows // 2
        self.middle = (self.z_at == 1) | (self.z_at == 2)
        self.first_slot = self.z_at if line > 1 else 0

    def slot(self, order):
        z_at = self.z_at
        if self.line == 1:
            return 0
        second = z_at + 1 - 2 * lax.rem(z_at, 2)
        third = 2 - z_at // 2
        fourth = 3 - 3 * (z_at // 2)
        return jnp.where(
            order == 0, z_at, jnp.where(order == 1, second, jnp.where(order == 2, third, fourth))
        )

    def each(self, order, act):
        if not self.tail:
            act(True)
        elif isinstance(order, int):
            act(order == 0)
        else:
            pl.when(order == 0)(lambda: act(True))
            pl.when(order > 0)(lambda: act(False))

    def span(self, part, whole):
        count = self.rows if whole else self.rows - self.tail
        return ((0, count), (0, self.half), (self.half, count - self.half))[part]

    def there(self, slot, place, start, count):
        at = (slot * 8 + place) * self.rows + start
        return self.o_ref.at[pl.ds(pl.multiple_of(at, 8), count)]

    def z_copy(self, src_ref, slot, way, target):
        return remote(
            src_ref,
            self.there(slot, self.me, *self.span(0, False)),
            self.z_send.at[slot, way],
            self.z_recv.at[slot],
            (self.me, target),
        )

    def own_main(self):
        start, count = self.span(0, False)
        return self.x_ref.at[pl.ds(start, count)]

    def up(self):
        return self.z_copy(self.own_main(), self.z_at, 0, self.z_at + 1)

    def down(self):
        return self.z_copy(self.own_main(), self.z_at, 1, self.z_at - 1)

    def beyond(self, order):
        return jnp.where(order == 1, 3 - self.z_at, 3 * self.z_at - 3)

    def onward(self, order):
        slot = self.slot(order)
        main = self.there(slot, self.me, *self.span(0, False))
        return self.z_copy(main, slot, 0, self.beyond(order))

    def copy(self, order, place, kind, device, part, whole, src_ref=None):
        dst_ref = self.there(self.slot(order), place, *self.span(part, whole))
        return remote(
            dst_ref if src_ref is None else src_ref,
            dst_ref,
            self.p_send.at[order, kind],
            self.p_recv.at[order, kind],
            (device, self.z_at),
        )

    def out(self, order, whole, src_ref=None):
        return [
            self.copy(order, self.me, 0, self.near_x, 0, whole, src_ref),
            self.copy(order, self.me, 1, self.near_y, 0, whole, src_ref),
            self.copy(order, self.me, 2, self.mate, 0, whole, src_ref),
        ]

    def passed(self, order, whole, *which):
        places = (
            (self.near_x, 3, self.near_y, 1),
            (self.near_x, 5, self.mate, 0),
            (self.near_y, 4, self.near_x, 2),
            (self.near_y, 6, self.mate, 0),
            (self.across, 7, self.mate, 1),
            (self.across, 8, self.mate, 2),
        )
        return [self.copy(order, *places[k], whole) for k in which]

    def begin(self, met=False):
        line, z_at = self.line, self.z_at
        if not met:
            greet((self.mate, self.near_x, self.near_y), line, z_at)
        self.own_copy().start()
        if line > 1:
            self.begin_line()
        for copy in self.out(0, True, self.x_ref):
            copy.start()

    def begin_line(self):
        pl.when(self.z_at < self.line - 1)(lambda: self.up().start())
        pl.when(self.z_at > 0)(lambda: self.down().start())

    def own_copy(self):
        return pltpu.make_async_copy(
            self.x_ref, self.there(self.first_slot, self.me, 0, self.rows), self.own_sem
        )

    def own_block(self):
        self.own_copy().wait()

    def from_line(self, order):
        slot = self.slot(order)
        main = self.there(slot, self.me, *self.span(0, False))
        self.z_copy(main, slot, 0, self.z_at).wait_recv()

    def first(self, order):
        at_end = jnp.logical_not(self.middle)
        pl.when(at_end | (order == 1))(lambda: self.from_line(order))

        @pl.when(self.middle & (order == 1))
        def _():
            self.onward(1).start()
            self.from_line(2)
            self.onward(2).start()

        @pl.when(self.middle & (order == 2))
        def _():
            self.from_line(3)
            self.onward(3).start()

        for copy in self.out(order, False):
            copy.start()

    def second(self, order):
        def act(whole):
            to_y, mate_x, to_x, mate_y = self.passed(order, whole, 0, 1, 2, 3)
            self.copy(order, self.near_x, 0, self.near_x, 0, whole).wait_recv()
            to_y.start()
            mate_x.start()
            self.copy(order, self.near_y, 1, self.near_y, 0, whole).wait_recv()
            to_x.start()
            mate_y.start()

        self.each(order, act)

    def tail_copy(self, slot, k, way, target, own=False):
        start = self.rows - self.tail
        dst_ref = self.there(slot, self.places[k], start, self.tail)
        src_ref = dst_ref
        if own and self.own_blocks is not None:
            at = pl.multiple_of(self.places[k] * self.rows + start, 8)
            src_ref = self.own_blocks.at[pl.ds(at, self.tail)]
        return remote(
            src_ref,
            dst_ref,
            self.t_send.at[slot, way, k],
            self.t_recv.at[slot, k],
            (self.me, target),
        )

    def own_tails(self, act):
        z_at = self.z_at
        for k in range(4):
            pl.when(z_at < self.line - 1)(lambda: act(self.tail_copy(z_at, k, 0, z_at + 1, True)))
            pl.when(z_at > 0)(lambda: act(self.tail_copy(z_at, k, 1, z_at - 1, True)))

    def send_tails(self):
        self.own_tails(lambda copy: copy.start())

    def tails_on(self, order):
        return [self.tail_copy(self.slot(order), k, 0, self.beyond(order)) for k in range(4)]

    def tail_to_mate(self, order, k, place):
        ref = self.there(self.slot(order), place, self.rows - self.tail, self.tail)
        return remote(
            ref, ref, self.q_send.at[order, k], self.q_recv.at[order, k], (self.mate, self.z_at)
        )

    def tails(self, order):
        def arrive(one):
            for k in range(4):
                self.tail_copy(self.slot(one), k, 0, self.z_at).wait_recv()

        def on(one):
            for copy in self.tails_on(one):
                copy.start()

        pl.when(jnp.logical_not(self.middle) | (order == 1))(lambda: arrive(order))

        @pl.when(self.middle & (order == 1))
        def _():
            on(1)
            arrive(2)
            on(2)

        @pl.when(self.middle & (order == 2))
        def _():
            arrive(3)
            on(3)

        for k in range(4):
            self.tail_to_mate(order, k, self.places[k]).start()

    def mates_tails(self, order, *which):
        if self.tail:

            @pl.when(order > 0)
            def _():
                for k in which:
                    place = self.places[k] + self.mate - self.me
                    self.tail_to_mate(order, k, place).wait_recv()

    def near(self, order):
        step = self.mate - self.me

        def act(whole):
            self.copy(order, self.mate, 2, self.mate, 0, whole).wait_recv()
            self.copy(order, self.near_x + step, 5, self.mate, 0, whole).wait_recv()

        self.each(order, act)
        self.mates_tails(order, 0, 1)

    def third(self, order):
        step = self.mate - self.me

        def act(whole):
            top, low = self.passed(order, whole, 4, 5)
            self.copy(order, self.across, 3, self.near_y, 1, whole).wait_recv()
            top.start()
            self.copy(order, self.across, 4, self.near_x, 2, whole).wait_recv()
            low.start()
            self.copy(order, self.near_y + step, 6, self.mate, 0, whole).wait_recv()
            self.copy(order, self.across + step, 7, self.mate, 1, whole).wait_recv()
            self.copy(order, self.across + step, 8, self.mate, 2, whole).wait_recv()

        self.each(order, act)
        self.mates_tails(order, 2, 3)

    def end(self, from_order=0):
        line, z_at = self.line, self.z_at

        def sent(order, carry):
            def act(whole):
                for copy in self.out(order, whole) + self.passed(order, whole, 0, 1, 2, 3, 4, 5):
                    copy.wait_send()

            self.each(order, act)
            return carry

        lax.fori_loop(from_order, line, sent, 0)
        if line > 1:
            pl.when(z_at < line - 1)(lambda: self.up().wait_send())
            pl.when(z_at > 0)(lambda: self.down().wait_send())

            @pl.when(self.middle)
            def _():
                for order in range(1, line):
                    self.onward(order).wait_send()

        if self.tail:
            self.own_tails(lambda copy: copy.wait_send())
            for order in range(1, line):
                for k in range(4):
                    self.tail_to_mate(order, k, self.places[k]).wait_send()

            @pl.when(self.middle)
            def _():
                for order in range(1, line):
                    for copy in self.tails_on(order):
                        copy.wait_send()


def line_sems(line):
    return [
        pltpu.SemaphoreType.DMA,
        pltpu.SemaphoreType.DMA((line, 2)),
        pltpu.SemaphoreType.DMA((line,)),
    ]


class Line:
    def __init__(self, x_ref, o_ref, sems):
        self.x_ref, self.o_ref = x_ref, o_ref
        self.own_sem, self.sends, self.receives = sems
        self.me, self.z_at = lax.axis_index("ctx"), lax.axis_index("fsdp")
        self.middle = (self.z_at == 1) | (self.z_at == 2)
        self.slots = (
            self.z_at,
            self.z_at + 1 - 2 * lax.rem(self.z_at, 2),
            2 - self.z_at // 2,
            3 - 3 * (self.z_at // 2),
        )

    def there(self, slot):
        rows = self.x_ref.shape[0]
        return self.o_ref.at[pl.ds(pl.multiple_of(slot * rows, 16), rows)]

    def copy(self, src_ref, slot, way, target):
        return remote(
            src_ref,
            self.there(slot),
            self.sends.at[slot, way],
            self.receives.at[slot],
            (self.me, target),
        )

    def own(self):
        return pltpu.make_async_copy(self.x_ref, self.there(self.z_at), self.own_sem)

    def up(self):
        return self.copy(self.x_ref, self.z_at, 0, self.z_at + 1)

    def down(self):
        return self.copy(self.x_ref, self.z_at, 1, self.z_at - 1)

    def onward(self, order):
        slot = self.slots[order]
        target = 3 - self.z_at if order == 1 else 3 * self.z_at - 3
        return self.copy(self.there(slot), slot, 0, target)

    def begin(self):
        pl.when(self.z_at < 3)(lambda: self.up().start())
        pl.when(self.z_at > 0)(lambda: self.down().start())
        self.own().start()

    def arrive(self, order):
        slot = self.slots[order]
        self.copy(self.there(slot), slot, 0, self.z_at).wait_recv()

    def pass_on(self, *orders):
        @pl.when(self.middle)
        def _():
            for order in orders:
                self.arrive(order)
                self.onward(order).start()

    def rest(self):
        @pl.when(jnp.logical_not(self.middle))
        def _():
            for order in (1, 2, 3):
                self.arrive(order)

    def end(self):
        self.own().wait()
        pl.when(self.z_at < 3)(lambda: self.up().wait_send())
        pl.when(self.z_at > 0)(lambda: self.down().wait_send())

        @pl.when(self.middle)
        def _():
            for order in (1, 2, 3):
                self.onward(order).wait_send()


def gather_blocks(x, line, collective, name):
    rows, width = x.shape

    def kernel(x_ref, o_ref, *sems):
        gather = Gather(line, x_ref, o_ref, sems)
        gather.begin()

        def body(order, carry):
            gather.second(order)
            if line > 1:
                pl.when(order + 1 < line)(lambda: gather.first(order + 1))
            gather.near(order)
            gather.third(order)
            return carry

        lax.fori_loop(0, line, body, 0)
        gather.own_block()
        gather.end()

    return pl.pallas_call(
        kernel,
        out_shape=jax.ShapeDtypeStruct((line * 8 * rows, width), x.dtype),
        in_specs=[pl.BlockSpec(memory_space=pl.ANY)],
        out_specs=pl.BlockSpec(memory_space=pl.ANY),
        scratch_shapes=gather_sems(line),
        compiler_params=pltpu.CompilerParams(collective_id=collective, has_side_effects=True),
        name=name,
    )(x)


CHUNK = 16


def add_rows(dst_ref, src_refs, start, count, out_ref=None):
    def body(i, carry):
        at = pl.ds(pl.multiple_of(start + i * CHUNK, CHUNK), CHUNK)
        value = dst_ref[at, :].astype(jnp.float32)
        for src_ref in src_refs:
            value = value + src_ref[at, :].astype(jnp.float32)
        to_ref = dst_ref if out_ref is None else out_ref
        to_ref[at, :] = value.astype(to_ref.dtype)
        return carry

    lax.fori_loop(0, count // CHUNK, body, 0)


class Scatter:
    def __init__(self, line, x_ref, o_ref, scratch, columns=None):
        self.columns = columns
        (
            self.mine, self.theirs, self.halves, self.from_x, self.from_y, self.from_z, self.total,
            self.load_sem, self.m_send, self.m_recv, self.p_send, self.p_recv, self.z_send,
            self.z_recv, self.out_sem, *rest,
        ) = scratch
        self.tail = 0
        if rest:
            self.from_t, self.t_send, self.t_recv = rest
            self.tail = self.from_t.shape[2]
        self.line, self.x_ref, self.o_ref = line, x_ref, o_ref
        self.z_at = lax.axis_index("fsdp")
        self.me, self.mate, self.near_x, self.near_y, step_x = neighbours()
        self.places = (self.near_y + step_x, self.near_x, self.near_y, self.me)
        self.rows = self.total.shape[0]
        self.half = self.rows // 2
        self.main = self.rows - self.tail
        self.middle = (self.z_at == 1) | (self.z_at == 2)

    def slot(self, order):
        z_at = self.z_at
        if self.line == 1:
            return 0
        far, next_far, near = 3 - 3 * (z_at // 2), 2 - z_at // 2, z_at + 1 - 2 * lax.rem(z_at, 2)
        return jnp.where(
            order == 0, far, jnp.where(order == 1, next_far, jnp.where(order == 2, near, z_at))
        )

    def each(self, order, act):
        if not self.tail:
            act(self.rows)
        elif isinstance(order, int):
            act(self.rows if order == self.line - 1 else self.main)
        else:
            pl.when(order == self.line - 1)(lambda: act(self.rows))
            pl.when(order < self.line - 1)(lambda: act(self.main))

    def there(self, slot, place):
        at = pl.ds(pl.multiple_of((slot * 8 + place) * self.rows, 16), self.rows)
        return self.x_ref.at[at] if self.columns is None else self.x_ref.at[at, self.columns]

    def give(self, order, k):
        return remote(
            self.there(self.slot(order), self.places[k] + self.mate - self.me),
            self.theirs.at[order, k],
            self.m_send.at[order, k],
            self.m_recv.at[order, k],
            (self.mate, self.z_at),
        )

    def load(self, order, k):
        return pltpu.make_async_copy(
            self.there(self.slot(order), self.places[k]),
            self.mine.at[order, k],
            self.load_sem.at[order, k],
        )

    def send(self, order, kind, count):
        top, low = pl.ds(0, self.half), pl.ds(self.half, count - self.half)
        k, part, to, device = (
            (0, top, self.halves, self.near_x),
            (0, low, self.halves, self.near_y),
            (1, top, self.from_x, self.near_x),
            (1, low, self.from_x, self.near_x),
            (2, low, self.from_y, self.near_y),
            (2, top, self.from_y, self.near_y),
        )[kind]
        return remote(
            self.mine.at[order, k, part],
            to.at[order, part],
            self.p_send.at[order, kind],
            self.p_recv.at[order, kind],
            (device, self.z_at),
        )

    def begin(self, met=False):
        if not met:
            greet((self.mate, self.near_x, self.near_y), self.line, self.z_at)

        def body(order, carry):
            for k in range(4):
                self.start_part(order, k)
            return carry

        lax.fori_loop(0, self.line, body, 0)

    def start_part(self, order, k):
        self.give(order, k).start()
        self.load(order, k).start()

    def produce(self, make):
        for k in range(4):
            make(self.places[k] // 2)
            self.start_part(0, k)
            if k > 0:
                self.part(0, k - 1)
        self.part(0, 3)

    def tail_copy(self, order, k, index, target):
        return remote(
            self.mine.at[order, k, pl.ds(self.main, self.tail)],
            self.from_t.at[index, k],
            self.t_send.at[order, k],
            self.t_recv.at[index, k],
            (self.me, target),
        )

    def toward(self, order):
        return jnp.where(order == 2, self.slot(order), self.z_at + 1 - 2 * (self.z_at // 2))

    def tails_out(self, order):
        slot, target = self.slot(order), self.toward(order)
        above = jnp.where((target == slot) & (self.z_at > target), 1, 0)
        index = above * 4 + (1 - above) * slot
        return [self.tail_copy(order, k, index, target) for k in range(4)]

    def tails_on(self, order):
        slot = self.slot(order)
        copies = self.tails_out(order)
        for k in range(4):
            self.tail_copy(order, k, slot, self.z_at).wait_recv()
            add_rows(self.mine.at[order, k, pl.ds(self.main, self.tail)], [self.from_t.at[slot, k]], 0, self.tail)
            copies[k].start()

    def tails_in(self, order, k):
        z_at = self.z_at
        mine = self.mine.at[order, k, pl.ds(self.main, self.tail)]

        @pl.when(z_at > 0)
        def _():
            self.tail_copy(order, k, z_at, z_at).wait_recv()
            add_rows(mine, [self.from_t.at[z_at, k]], 0, self.tail)

        @pl.when(z_at < self.line - 1)
        def _():
            self.tail_copy(order, k, 4, z_at).wait_recv()
            add_rows(mine, [self.from_t.at[4, k]], 0, self.tail)

    def part(self, order, k):
        self.give(order, k).wait_recv()
        self.load(order, k).wait()
        add_rows(self.mine.at[order, k], [self.theirs.at[order, k]], 0, self.rows)
        if self.tail:
            pl.when(order == self.line - 1)(lambda: self.tails_in(order, k))

        def act(count):
            for kind in ((0, 1), (2,), (4,), ())[k]:
                self.send(order, kind, count).start()

        self.each(order, act)

    def first(self, order):
        for k in range(4):
            self.part(order, k)
        if self.tail:

            @pl.when((order < self.line - 1) & jnp.logical_not(self.middle))
            def _():
                for copy in self.tails_out(order):
                    copy.start()

    def second(self, order):
        def act(count):
            self.send(order, 1, count).wait_recv()
            low = count - self.half
            add_rows(self.mine.at[order, 1], [self.halves.at[order]], self.half, low)
            self.send(order, 3, count).start()
            self.send(order, 0, count).wait_recv()
            add_rows(self.mine.at[order, 2], [self.halves.at[order]], 0, self.half)
            self.send(order, 5, count).start()

        self.each(order, act)

    def third(self, order, out_ref=None):
        sources = [self.from_x.at[order], self.from_y.at[order]]

        def act(count):
            for kind in (2, 3, 4, 5):
                self.send(order, kind, count).wait_recv()
            add_rows(self.mine.at[order, 3], sources, 0, count, out_ref)

        self.each(order, act)

    def z_copy(self, order, slot_at, target):
        at = pl.ds(0, self.main)
        return remote(
            self.mine.at[order, 3, at],
            self.from_z.at[slot_at, at],
            self.z_send.at[order],
            self.z_recv.at[slot_at],
            (self.me, target),
        )

    def z_out(self, order):
        z_at, slot, target = self.z_at, self.slot(order), self.toward(order)
        ends = jnp.where(target == slot, 1, 0)
        return self.z_copy(order, ends * (4 + (z_at - target + 1) // 2) + (1 - ends) * slot, target)

    def pass_on(self, order):
        slot = self.slot(order)
        self.z_copy(order, slot, self.z_at).wait_recv()
        add_rows(self.mine.at[order, 3], [self.from_z.at[slot]], 0, self.main)
        self.z_out(order).start()

    def along(self, order):
        @pl.when((order < self.line - 1) & jnp.logical_not(self.middle))
        def _():
            self.z_out(order).start()

        if self.tail:
            pl.when((order == 0) & self.middle)(lambda: self.tails_on(0))

            @pl.when((order == 1) & self.middle)
            def _():
                self.tails_on(1)
                self.tails_on(2)

        pl.when((order == 1) & self.middle)(lambda: self.pass_on(0))

        @pl.when((order == 2) & self.middle)
        def _():
            self.pass_on(1)
            self.pass_on(2)

    def last(self):
        z_at, line = self.z_at, self.line
        pl.when(z_at > 0)(lambda: self.z_copy(line - 1, 4, z_at).wait_recv())
        pl.when(z_at < line - 1)(lambda: self.z_copy(line - 1, 5, z_at).wait_recv())
        mine = self.mine.at[line - 1, 3]
        below, above = self.from_z.at[4], self.from_z.at[5]
        pl.when(z_at == 0)(lambda: add_rows(mine, [above], 0, self.main, self.total))
        pl.when(z_at == line - 1)(lambda: add_rows(mine, [below], 0, self.main, self.total))
        pl.when(self.middle)(lambda: add_rows(mine, [below, above], 0, self.main, self.total))
        if self.tail:
            add_rows(mine, [], self.main, self.tail, self.total)

    def end(self):
        out = pltpu.make_async_copy(self.total, self.o_ref, self.out_sem)
        out.start()

        def sent(order, carry):
            def act(count):
                for kind in range(6):
                    self.send(order, kind, count).wait_send()

            for k in range(4):
                self.give(order, k).wait_send()
            self.each(order, act)
            if self.line > 1:

                @pl.when(order < self.line - 1)
                def _():
                    self.z_out(order).wait_send()
                    if self.tail:
                        for copy in self.tails_out(order):
                            copy.wait_send()

            return carry

        lax.fori_loop(0, self.line, sent, 0)
        out.wait()

    def plane_sum(self, make=None):
        if make is None:
            self.first(0)
        else:
            self.produce(make)
        self.second(0)
        self.third(0, self.total)
        self.end()

    def run(self, work=None, extra=0, met=False, begun=False):
        if not begun:
            self.begin(met)
        if self.line == 1:
            self.plane_sum()
            return
        if not begun:
            self.first(0)

        def body(step, carry):
            order, phase = step // 3, lax.rem(step, 3)

            @pl.when((phase == 0) & (order < self.line))
            def _():
                self.second(order)
                pl.when(order + 1 < self.line)(lambda: self.first(order + 1))

            pl.when((phase == 1) & (order < self.line))(lambda: self.third(order))
            pl.when((phase == 2) & (order < self.line))(lambda: self.along(order))
            if work is not None:
                work(step)
            return carry

        lax.fori_loop(0, 3 * self.line + extra, body, 0)
        self.last()
        self.end()


TAIL = 16


def scatter_scratch(line, rows, width, dtype, tail=TAIL):
    shard = (rows, width)
    made = [
        pltpu.VMEM((line, 4) + shard, dtype),
        pltpu.VMEM((line, 4) + shard, dtype),
        pltpu.VMEM((line,) + shard, dtype),
        pltpu.VMEM((line,) + shard, dtype),
        pltpu.VMEM((line,) + shard, dtype),
        pltpu.VMEM((6 if line > 1 else 1,) + shard, dtype),
        pltpu.VMEM(shard, jnp.float32),
        pltpu.SemaphoreType.DMA((line, 4)),
        pltpu.SemaphoreType.DMA((line, 4)),
        pltpu.SemaphoreType.DMA((line, 4)),
        pltpu.SemaphoreType.DMA((line, 6)),
        pltpu.SemaphoreType.DMA((line, 6)),
        pltpu.SemaphoreType.DMA((line,)),
        pltpu.SemaphoreType.DMA((6,)),
        pltpu.SemaphoreType.DMA,
    ]
    if line > 1 and tail:
        made += [
            pltpu.VMEM((5, 4, tail, width), dtype),
            pltpu.SemaphoreType.DMA((line, 4)),
            pltpu.SemaphoreType.DMA((5, 4)),
        ]
    return made


def scatter_blocks(x, line, collective, name):
    rows, width = x.shape[0] // (line * 8), x.shape[1]

    def kernel(x_ref, o_ref, *scratch):
        Scatter(line, x_ref, o_ref, scratch).run()

    return pl.pallas_call(
        kernel,
        out_shape=jax.ShapeDtypeStruct((rows, width), jnp.float32),
        in_specs=[pl.BlockSpec(memory_space=pl.ANY)],
        out_specs=pl.BlockSpec(memory_space=pl.ANY),
        scratch_shapes=scatter_scratch(line, rows, width, x.dtype),
        compiler_params=pltpu.CompilerParams(
            collective_id=collective, has_side_effects=True, vmem_limit_bytes=52 * MIB
        ),
        name=name,
    )(x)


QUERY_HEADS = 64
KEY_VALUE_HEADS = 8
HEAD_SIZE = 64
TOP = 4
EPSILON = 1e-05
THETA_BASE = 150000.0
CLAMP_LIMIT = 7.0
GLU_ALPHA = 1.702
MASK_FILL = -1e30
SPAN = 256
SCALE = HEAD_SIZE**-0.5


def contract(left, right, left_axis, right_axis):
    return lax.dot_general(
        left, right, (((left_axis,), (right_axis,)), ((), ())), preferred_element_type=jnp.float32
    )


def norm_scale(value_rows, gain_vec):
    return (
        value_rows
        * lax.rsqrt(jnp.mean(value_rows * value_rows, axis=-1, keepdims=True) + EPSILON)
        * gain_vec
    )


def soft_clamp(value_rows):
    return CLAMP_LIMIT * jnp.tanh(value_rows / CLAMP_LIMIT)


def glu_units(gate_lin, up_lin):
    gated = soft_clamp(gate_lin)
    return (soft_clamp(up_lin) + 1.0) * gated * jax.nn.sigmoid(GLU_ALPHA * gated)


def rotary_tables(length):
    half = HEAD_SIZE // 2
    inverse = np.float32(THETA_BASE) ** (-np.arange(half, dtype=np.float32) / np.float32(half))
    angles = inverse[:, None] * np.arange(length, dtype=np.float32)[None, :]
    return jnp.asarray(np.cos(angles)), jnp.asarray(np.sin(angles))


def turned(value, cosine, sine):
    half = HEAD_SIZE // 2
    first, second = value[:, :half], value[:, half:]
    return jnp.concatenate(
        [first * cosine - second * sine, second * cosine + first * sine], axis=1
    )


def diagonal(length):
    return lax.broadcasted_iota(jnp.int32, (length, length), 0) <= lax.broadcasted_iota(
        jnp.int32, (length, length), 1
    )


def masked_scores(key_rows, query_cols, count):
    scores = contract(key_rows, query_cols, 1, 0)
    edge = jnp.where(diagonal(SPAN), scores[count - SPAN :], MASK_FILL)
    if count == SPAN:
        return edge
    return jnp.concatenate([scores[: count - SPAN], edge], axis=0)


def attend_kernel(sink_ref, q_ref, k_ref, v_ref, out_ref, log_ref):
    sink = sink_ref[pl.program_id(0)]
    length = q_ref.shape[1]
    for start in range(0, length, SPAN):
        count = start + SPAN
        at = pl.ds(start, SPAN)
        query = q_ref[:, at] * jnp.bfloat16(SCALE)
        scores = masked_scores(k_ref[:count, :], query, count)
        row_top = jnp.maximum(jnp.max(scores, axis=0, keepdims=True), sink)
        weights = jnp.exp(scores - row_top)
        denominator = jnp.sum(weights, axis=0, keepdims=True) + jnp.exp(sink - row_top)
        probabilities = (weights / denominator).astype(jnp.bfloat16)
        out_ref[:, at] = contract(v_ref[:, :count], probabilities, 1, 0).astype(jnp.bfloat16)
        log_ref[0, :, at] = row_top + jnp.log(denominator)


def attend(sinks, queries, keys, values):
    heads, length = queries.shape[0] // HEAD_SIZE, queries.shape[1]
    per_head = pl.BlockSpec((HEAD_SIZE, length), lambda h: (h, 0))
    return pl.pallas_call(
        attend_kernel,
        grid=(heads,),
        out_shape=(
            jax.ShapeDtypeStruct(queries.shape, jnp.bfloat16),
            jax.ShapeDtypeStruct((heads, 1, length), jnp.float32),
        ),
        in_specs=[
            pl.BlockSpec(memory_space=pltpu.SMEM),
            per_head,
            pl.BlockSpec((length, HEAD_SIZE), lambda h: (0, 0)),
            pl.BlockSpec((HEAD_SIZE, length), lambda h: (0, 0)),
        ],
        out_specs=(per_head, pl.BlockSpec((1, 1, length), lambda h: (h, 0, 0))),
        compiler_params=pltpu.CompilerParams(vmem_limit_bytes=40 * MIB),
        cost_estimate=pl.CostEstimate(
            flops=heads * length * length * HEAD_SIZE * 4,
            bytes_accessed=heads * length * HEAD_SIZE * 4,
            transcendentals=heads * length * length,
        ),
        name="attend",
    )(sinks, queries, keys, values)


class Moved:
    def __init__(self, pairs, sems):
        self.copies = [
            pltpu.make_async_copy(source, target, sems.at[k]) for k, (source, target) in enumerate(pairs)
        ]

    def start(self):
        for copy in self.copies:
            copy.start()

    def wait(self):
        for copy in self.copies:
            copy.wait()


def attention(rows_own, grads_own, weights_own, out_own, sinks, cosine, sine, collective):
    low, f32 = jnp.bfloat16, jnp.float32
    block_rows, wide = rows_own.shape
    length = 8 * block_rows
    own_rows = weights_own.shape[0]
    q_rows, width = out_own.shape
    kv_rows = (own_rows - q_rows) // 2
    heads = 4 * q_rows // HEAD_SIZE
    half = HEAD_SIZE // 2
    per_shard = q_rows // HEAD_SIZE

    def kernel(
        sink_ref, rows_ref, grads_ref, weights_ref, out_ref, cos_ref, sin_ref,
        o_ref, all_rows, all_grads, all_weights, all_out, q_hbm, k_ref, kt_ref, v_ref, att_hbm, log_ref,
        q_ref, att_ref, store_sems, normed_v, weights_v, lin, vt_v, out_v, branch, held_sems, *scratch,
    ):
        plane = Gather(1, rows_ref, all_rows, scratch[:5])
        later = Gather(1, grads_ref, all_grads, scratch[5:10])
        heads_line = Line(weights_ref, all_weights, scratch[10:13])
        line = Line(out_ref, all_out, scratch[13:16])
        scatter = Scatter(1, branch, o_ref, scratch[16:])
        load_rows = pltpu.make_async_copy(all_rows, normed_v, held_sems.at[0])
        load_weights = pltpu.make_async_copy(all_weights, weights_v, held_sems.at[1])
        greet((plane.mate, plane.near_x, plane.near_y), 4, line.z_at)
        heads_line.begin()
        plane.begin(True)
        heads_line.pass_on(1, 2)
        plane.second(0)
        later.begin(True)
        line.begin()
        plane.near(0)
        plane.third(0)
        plane.own_block()
        load_rows.start()
        heads_line.pass_on(3)
        later.second(0)
        later.near(0)
        later.third(0)
        later.own_block()
        heads_line.rest()
        heads_line.end()
        load_weights.start()
        load_rows.wait()
        load_weights.wait()

        def project(i, carry):
            at = pl.ds(pl.multiple_of(i * SPAN, SPAN), SPAN)
            lin[:, at] = contract(weights_v[...], normed_v[at, :], 1, 1)
            return carry

        lax.fori_loop(0, length // SPAN, project, 0)
        line.pass_on(1, 2)

        def turn(value):
            first, second = value[:half], value[half:]
            cosine, sine = cos_ref[...], sin_ref[...]
            return jnp.concatenate(
                [first * cosine - second * sine, second * cosine + first * sine], axis=0
            ).astype(low)

        def shards_of(offset):
            return jnp.concatenate(
                [
                    lin[z * own_rows + offset : z * own_rows + offset + kv_rows, :]
                    for z in range(4)
                ],
                axis=0,
            )

        keys_t = turn(shards_of(q_rows))
        values_t = shards_of(q_rows + kv_rows).astype(low)
        kt_ref[...] = keys_t
        vt_v[...] = values_t
        k_ref[...] = keys_t.T
        v_ref[...] = values_t.T

        def head(h, carry):
            pl.when(h == heads // 2)(lambda: line.pass_on(3))
            start = (h // per_shard) * own_rows + lax.rem(h, per_shard) * HEAD_SIZE
            queries = turn(lin[pl.ds(pl.multiple_of(start, 16), HEAD_SIZE), :])
            rows = pl.ds(pl.multiple_of(h * HEAD_SIZE, HEAD_SIZE), HEAD_SIZE)
            q_ref[rows, :] = queries
            sink = sink_ref[h]
            for begin in range(0, length, SPAN):
                count = begin + SPAN
                query = queries[:, begin:count] * jnp.bfloat16(SCALE)
                scores = masked_scores(k_ref[:count, :], query, count)
                row_top = jnp.maximum(jnp.max(scores, axis=0, keepdims=True), sink)
                chances = jnp.exp(scores - row_top)
                denominator = jnp.sum(chances, axis=0, keepdims=True) + jnp.exp(sink - row_top)
                chances = (chances / denominator).astype(low)
                att_ref[rows, begin:count] = contract(vt_v[:, :count], chances, 1, 0).astype(low)
                log_ref[h, :, begin:count] = row_top + jnp.log(denominator)
            return carry

        lax.fori_loop(0, heads, head, 0)
        stores = Moved(((q_ref, q_hbm), (att_ref, att_hbm)), store_sems)
        stores.start()
        line.rest()
        line.end()
        load = pltpu.make_async_copy(all_out, out_v, held_sems.at[0])
        load.start()
        load.wait()

        def give_back(chip):
            at = pl.ds(pl.multiple_of(chip * SPAN, SPAN), SPAN)
            branch[at, :] = contract(att_ref[:, at], out_v[...], 0, 0).astype(low)

        scatter.plane_sum(give_back)
        plane.end()
        later.end()
        stores.wait()

    hbm = pl.BlockSpec(memory_space=pl.ANY)
    vmem = pl.BlockSpec(memory_space=pltpu.VMEM)
    return pl.pallas_call(
        kernel,
        out_shape=(
            jax.ShapeDtypeStruct((block_rows, width), f32),
            jax.ShapeDtypeStruct((length, wide), low),
            jax.ShapeDtypeStruct((length, wide), low),
            jax.ShapeDtypeStruct((4 * own_rows, wide), low),
            jax.ShapeDtypeStruct((4 * q_rows, width), low),
            jax.ShapeDtypeStruct((4 * q_rows, length), low),
            jax.ShapeDtypeStruct((length, HEAD_SIZE), low),
            jax.ShapeDtypeStruct((HEAD_SIZE, length), low),
            jax.ShapeDtypeStruct((length, HEAD_SIZE), low),
            jax.ShapeDtypeStruct((4 * q_rows, length), low),
            jax.ShapeDtypeStruct((heads, 1, length), f32),
        ),
        in_specs=[pl.BlockSpec(memory_space=pltpu.SMEM), hbm, hbm, hbm, hbm, vmem, vmem],
        out_specs=(hbm,) * 6 + (vmem,) * 3 + (hbm, vmem),
        scratch_shapes=[
            pltpu.VMEM((4 * q_rows, length), low),
            pltpu.VMEM((4 * q_rows, length), low),
            pltpu.SemaphoreType.DMA((2,)),
            pltpu.VMEM((length, wide), low),
            pltpu.VMEM((4 * own_rows, wide), low),
            pltpu.VMEM((4 * own_rows, length), f32),
            pltpu.VMEM((HEAD_SIZE, length), low),
            pltpu.VMEM((4 * q_rows, width), low),
            pltpu.VMEM((length, width), low),
            pltpu.SemaphoreType.DMA((2,)),
            *gather_sems(1),
            *gather_sems(1),
            *line_sems(4),
            *line_sems(4),
            *scatter_scratch(1, block_rows, width, low),
        ],
        compiler_params=pltpu.CompilerParams(
            collective_id=collective, has_side_effects=True, vmem_limit_bytes=58 * MIB
        ),
        name="attention",
    )(sinks, rows_own, grads_own, weights_own, out_own, cosine, sine)


def attend_back_kernel(
    sink_ref, q_ref, k_ref, kt_ref, v_ref, grad_ref, log_ref, cos_ref, sin_ref,
    dq_ref, dk_ref, dv_ref, dsink_ref,
):
    head = pl.program_id(0)
    sink = sink_ref[head]
    length = q_ref.shape[1]
    half = HEAD_SIZE // 2

    @pl.when(head == 0)
    def _():
        dk_ref[...] = jnp.zeros_like(dk_ref)
        dv_ref[...] = jnp.zeros_like(dv_ref)

    grad_sink = jnp.zeros((1, SPAN), jnp.float32)
    for start in range(0, length, SPAN):
        count = start + SPAN
        at = pl.ds(start, SPAN)
        query = q_ref[:, at] * jnp.bfloat16(SCALE)
        grad = grad_ref[:, at]
        log_sum = log_ref[0, :, at]
        probabilities = jnp.exp(masked_scores(k_ref[:count, :], query, count) - log_sum)
        grad_probs = contract(v_ref[:count, :], grad, 1, 0)
        inner_sum = jnp.sum(probabilities * grad_probs, axis=0, keepdims=True)
        grad_scores = (probabilities * (grad_probs - inner_sum)).astype(jnp.bfloat16)
        grad_query = contract(kt_ref[:, :count], grad_scores, 1, 0) * SCALE
        first, second = grad_query[:half], grad_query[half:]
        cosine, sine = cos_ref[:, at], sin_ref[:, at]
        dq_ref[:half, at] = (first * cosine + second * sine).astype(jnp.bfloat16)
        dq_ref[half:, at] = (second * cosine - first * sine).astype(jnp.bfloat16)
        dk_ref[:count, :] += contract(grad_scores, query, 1, 1)
        dv_ref[:count, :] += contract(probabilities.astype(jnp.bfloat16), grad, 1, 1)
        grad_sink = grad_sink - jnp.exp(sink - log_sum) * inner_sum
    dsink_ref[0] = grad_sink


def attend_back(sinks, queries, keys, keys_t, values, grads, log_sums, cosine, sine):
    heads, length = queries.shape[0] // HEAD_SIZE, queries.shape[1]
    per_head = pl.BlockSpec((HEAD_SIZE, length), lambda h: (h, 0))

    def whole(*shape):
        return pl.BlockSpec(shape, lambda h: (0,) * len(shape))

    return pl.pallas_call(
        attend_back_kernel,
        grid=(heads,),
        out_shape=(
            jax.ShapeDtypeStruct(queries.shape, jnp.bfloat16),
            jax.ShapeDtypeStruct((length, HEAD_SIZE), jnp.float32),
            jax.ShapeDtypeStruct((length, HEAD_SIZE), jnp.float32),
            jax.ShapeDtypeStruct((heads, 1, SPAN), jnp.float32),
        ),
        in_specs=[
            pl.BlockSpec(memory_space=pltpu.SMEM),
            per_head,
            whole(length, HEAD_SIZE),
            whole(HEAD_SIZE, length),
            whole(length, HEAD_SIZE),
            per_head,
            pl.BlockSpec((1, 1, length), lambda h: (h, 0, 0)),
            whole(HEAD_SIZE // 2, length),
            whole(HEAD_SIZE // 2, length),
        ],
        out_specs=(
            per_head,
            whole(length, HEAD_SIZE),
            whole(length, HEAD_SIZE),
            pl.BlockSpec((1, 1, SPAN), lambda h: (h, 0, 0)),
        ),
        compiler_params=pltpu.CompilerParams(vmem_limit_bytes=48 * MIB),
        cost_estimate=pl.CostEstimate(
            flops=heads * length * length * HEAD_SIZE * 10,
            bytes_accessed=heads * length * HEAD_SIZE * 8,
            transcendentals=heads * length * length,
        ),
        name="attend_back",
    )(sinks, queries, keys, keys_t, values, grads, log_sums, cosine, sine)


def branch_back(parts, columns, grad_own, out_weights, attended, collective):
    low, f32 = jnp.bfloat16, jnp.float32
    block_rows, width = grad_own.shape
    depth, length = attended.shape
    cut = 512

    def kernel(
        parts_ref, grad_ref, out_hbm, att_hbm, o_ref, grad_att_hbm, grad_out_hbm,
        all_grads, out_ref, att_ref, grad_att, grad_out, in_sems, out_sems, *scratch,
    ):
        loads = Moved(((out_hbm, out_ref), (att_hbm, att_ref)), in_sems)
        stores = Moved(((grad_att, grad_att_hbm), (grad_out, grad_out_hbm)), out_sems)
        loads.start()
        gather = Gather(1, grad_ref, all_grads, scratch[:5])
        scatter = Scatter(4, parts_ref, o_ref, scratch[5:], pl.ds(0, columns))
        greet((gather.mate, gather.near_x, gather.near_y), 4, gather.z_at)
        gather.begin(True)
        scatter.begin(True)
        gather.second(0)
        scatter.first(0)
        gather.near(0)
        gather.third(0)
        gather.own_block()

        def work(step):
            pl.when(step == 0)(loads.wait)
            for i in range(length // SPAN):

                @pl.when(step == i)
                def _():
                    at = slice(i * SPAN, (i + 1) * SPAN)
                    grad_att[:, at] = contract(out_ref[...], all_grads[at, :], 1, 1).astype(low)

            for i in range(-(-width // cut)):

                @pl.when(step == i + length // SPAN)
                def _():
                    at = slice(i * cut, min(width, (i + 1) * cut))
                    grad_out[:, at] = contract(att_ref[...], all_grads[:, at], 1, 0).astype(low)

            pl.when(step == length // SPAN)(stores.copies[0].start)
            pl.when(step == steps - 1)(stores.copies[1].start)

        steps = length // SPAN + -(-width // cut) + 1
        scatter.run(work, max(0, steps - 12), begun=True)
        gather.end()
        stores.wait()

    hbm = pl.BlockSpec(memory_space=pl.ANY)
    return pl.pallas_call(
        kernel,
        out_shape=(
            jax.ShapeDtypeStruct((block_rows, columns), f32),
            jax.ShapeDtypeStruct((depth, length), low),
            jax.ShapeDtypeStruct((depth, width), low),
        ),
        in_specs=[hbm] * 4,
        out_specs=(hbm,) * 3,
        scratch_shapes=[
            pltpu.VMEM((length, width), low),
            pltpu.VMEM(out_weights.shape, low),
            pltpu.VMEM(attended.shape, low),
            pltpu.VMEM((depth, length), low),
            pltpu.VMEM((depth, width), low),
            pltpu.SemaphoreType.DMA((2,)),
            pltpu.SemaphoreType.DMA((2,)),
            *gather_sems(1),
            *scatter_scratch(4, block_rows, columns, low),
        ],
        compiler_params=pltpu.CompilerParams(
            collective_id=collective, has_side_effects=True, vmem_limit_bytes=56 * MIB
        ),
        name="branch_back",
    )(parts, grad_own, out_weights, attended)


def attention_back(
    parts, first_column, sinks, queries, keys, keys_t, values, grads, log_sums, cosine, sine, normed,
    own_rows, collective,
):
    low, f32 = jnp.bfloat16, jnp.float32
    length = queries.shape[1]
    heads = queries.shape[0] // HEAD_SIZE
    half = HEAD_SIZE // 2
    block_rows, columns = parts.shape[0] // 32, parts.shape[1] - first_column
    q_rows = queries.shape[0] // 4
    kv_rows = (own_rows - q_rows) // 2
    per_shard = q_rows // HEAD_SIZE
    spans = length // SPAN
    wide = normed.shape[1]

    def kernel(
        sink_ref, parts_ref, *refs
    ):
        sources, refs = refs[:9], refs[9:]
        o_ref, lin_hbm, weights_hbm, dsink_ref, dk_s, dv_s, lin_ref, weights_ref, *refs = refs
        held, (in_sems, out_sems, *scratch) = refs[:9], refs[9:]
        q_ref, k_ref, kt_ref, v_ref, grad_ref, log_ref, cos_ref, sin_ref, normed_v = held
        loads = Moved(tuple(zip(sources, held)), in_sems)
        stores = Moved(((lin_ref, lin_hbm), (weights_ref, weights_hbm)), out_sems)
        loads.start()
        dk_s[...] = jnp.zeros_like(dk_s)
        dv_s[...] = jnp.zeros_like(dv_s)
        dsink_ref[...] = jnp.zeros_like(dsink_ref)

        def one(head, span):
            start, count = span * SPAN, span * SPAN + SPAN
            at = slice(start, count)
            rows = pl.ds(pl.multiple_of(head * HEAD_SIZE, HEAD_SIZE), HEAD_SIZE)
            query = q_ref[rows, at] * jnp.bfloat16(SCALE)
            grad = grad_ref[rows, at]
            log_sum = log_ref[head, :, at]
            chances = jnp.exp(masked_scores(k_ref[:count, :], query, count) - log_sum)
            grad_probs = contract(v_ref[:count, :], grad, 1, 0)
            inner_sum = jnp.sum(chances * grad_probs, axis=0, keepdims=True)
            grad_scores = (chances * (grad_probs - inner_sum)).astype(low)
            grad_query = contract(kt_ref[:, :count], grad_scores, 1, 0) * SCALE
            first, second = grad_query[:half], grad_query[half:]
            cosine, sine = cos_ref[:, at], sin_ref[:, at]
            place = (head // per_shard) * own_rows + lax.rem(head, per_shard) * HEAD_SIZE
            lin_ref[pl.ds(pl.multiple_of(place, 16), HEAD_SIZE), at] = jnp.concatenate(
                [first * cosine + second * sine, second * cosine - first * sine], axis=0
            ).astype(low)
            dk_s[:count, :] += contract(grad_scores, query, 1, 1)
            dv_s[:count, :] += contract(chances.astype(low), grad, 1, 1)
            dsink_ref[head] -= jnp.exp(sink_ref[head] - log_sum) * inner_sum

        def finish():
            grad_keys, grad_values = dk_s[...].T, dv_s[...].T
            first, second = grad_keys[:half], grad_keys[half:]
            cosine, sine = cos_ref[...], sin_ref[...]
            grad_keys = jnp.concatenate(
                [first * cosine + second * sine, second * cosine - first * sine], axis=0
            )
            for z in range(4):
                here = slice(z * kv_rows, (z + 1) * kv_rows)
                start = z * own_rows + q_rows
                lin_ref[start : start + kv_rows, :] = grad_keys[here].astype(low)
                lin_ref[start + kv_rows : start + 2 * kv_rows, :] = grad_values[here].astype(low)
            stores.copies[0].start()

        cut = 512

        def work(step):
            pl.when(step == 0)(loads.wait)
            first_step = 0
            for span in reversed(range(spans)):
                at_once = max(1, 16 // (span + 1))
                count = -(-heads // at_once)
                here = (step >= first_step) & (step < first_step + count)

                @pl.when(here)
                def _():
                    begin = (step - first_step) * at_once

                    def body(head, carry):
                        pl.when(head < heads)(lambda: one(head, span))
                        return carry

                    lax.fori_loop(begin, begin + at_once, body, 0)

                first_step += count
            pl.when(step == first_step)(finish)
            for i in range(-(-wide // cut)):

                @pl.when(step == first_step + i)
                def _():
                    at = slice(i * cut, min(wide, (i + 1) * cut))
                    weights_ref[:, at] = contract(lin_ref[...], normed_v[:, at], 1, 0).astype(low)

            pl.when(step == needed)(stores.copies[1].start)

        needed = sum(-(-heads // max(1, 16 // (span + 1))) for span in range(spans))
        needed += -(-wide // cut)
        late = pl.ds(first_column, columns)
        Scatter(4, parts_ref, o_ref, scratch, late).run(work, max(0, needed + 1 - 12))
        stores.wait()

    taken = (queries, keys, keys_t, values, grads, log_sums, cosine, sine, normed)
    hbm = pl.BlockSpec(memory_space=pl.ANY)
    vmem = pl.BlockSpec(memory_space=pltpu.VMEM)
    return pl.pallas_call(
        kernel,
        out_shape=(
            jax.ShapeDtypeStruct((block_rows, columns), f32),
            jax.ShapeDtypeStruct((4 * own_rows, length), low),
            jax.ShapeDtypeStruct((4 * own_rows, normed.shape[1]), low),
            jax.ShapeDtypeStruct((heads, 1, SPAN), f32),
        ),
        in_specs=[pl.BlockSpec(memory_space=pltpu.SMEM)] + [hbm] * 10,
        out_specs=(hbm, hbm, hbm, vmem),
        scratch_shapes=[
            pltpu.VMEM((length, HEAD_SIZE), f32),
            pltpu.VMEM((length, HEAD_SIZE), f32),
            pltpu.VMEM((4 * own_rows, length), low),
            pltpu.VMEM((4 * own_rows, wide), low),
            *(pltpu.VMEM(array.shape, array.dtype) for array in taken),
            pltpu.SemaphoreType.DMA((len(taken),)),
            pltpu.SemaphoreType.DMA((2,)),
            *scatter_scratch(4, block_rows, columns, low, 0),
        ],
        compiler_params=pltpu.CompilerParams(
            collective_id=collective, has_side_effects=True, vmem_limit_bytes=60 * MIB
        ),
        name="attention_back",
    )(sinks, parts, *taken)


PAIR = 2
STEP = 4


def routed(cols, capacity):
    expert = lax.axis_index("ctx")
    cols = cols.astype(jnp.float32)
    lane = lax.broadcasted_iota(jnp.int32, cols.shape, 1)
    place = jnp.sum(jnp.where(lane == 64 + expert, cols, 0.0), axis=1, keepdims=True)
    gate = jnp.sum(jnp.where(lane == 72 + expert, cols, 0.0), axis=1, keepdims=True)
    slot = lax.broadcasted_iota(jnp.int32, (cols.shape[0], PAIR * capacity), 1)
    picked = place.astype(jnp.int32) == slot
    return (
        jnp.where(picked, 1.0, 0.0).astype(jnp.bfloat16),
        jnp.where(picked, gate, 0.0).astype(jnp.bfloat16),
    )


class Stream:
    def __init__(self, arrays, sems, inward, first_sem=0):
        self.arrays, self.sems, self.inward, self.first_sem = arrays, sems, inward, first_sem

    def copies(self, slot, block):
        made = []
        for k, (array, slots, count, column) in enumerate(self.arrays):
            at = pl.ds(pl.multiple_of(block * count, 16), count)
            far = array.at[at] if column is None else array.at[at, column]
            pair = (far, slots.at[slot]) if self.inward else (slots.at[slot], far)
            made.append(pltpu.make_async_copy(*pair, self.sems.at[slot, self.first_sem + k]))
        return made

    def start(self, slot, block):
        for copy in self.copies(slot, block):
            copy.start()

    def wait(self, slot, block):
        for copy in self.copies(slot, block):
            copy.wait()


def two_of(shape, dtype):
    return pltpu.VMEM((2,) + shape, dtype)


def experts(sent, sent_grads, own_grads, gate_w, up_w, down_w, gate_b, up_b, down_b, capacity, collective):
    low, f32 = jnp.bfloat16, jnp.float32
    block_rows, wide = sent.shape
    share, width = gate_w.shape
    pad_share = -(-share // 128) * 128
    span = PAIR * block_rows
    pairs = STEP // PAIR
    count = PAIR * capacity
    tokens = 32 * block_rows
    slot_rows = 32 * capacity
    line = 4

    def kernel(
        sent_ref, sent_grads_ref, own_grads_ref, gate_hbm, up_hbm, down_hbm, gate_b_ref, up_b_ref, down_b_ref,
        all_ref, all_grads_ref, rows_out, gate_out, up_out, hidden_out, mix_out,
        grad_rows_out, gate_grad_out, up_grad_out, tokens_out, down_sum, gate_sum, up_sum,
        pair_v, down_v, x_s, rows_s, gate_s, up_s, hidden_s, mix_s, cols_s, gate_gs, up_gs,
        held_sems, in_sems, out_sems, *sems,
    ):
        held = [
            pltpu.make_async_copy(source, target, held_sems.at[k])
            for k, (source, target) in enumerate(
                (
                    (gate_hbm, pair_v.at[pl.ds(0, share)]),
                    (up_hbm, pair_v.at[pl.ds(pad_share, share)]),
                    (down_hbm, down_v),
                )
            )
        ]
        for copy in held:
            copy.start()
        pad = jnp.zeros((pairs * count, pad_share - share), low)
        for k in range(2):
            pair_v[k * pad_share + share : (k + 1) * pad_share, :] = jnp.zeros(
                (pad_share - share, width), low
            )
        forward_in = Stream([(all_ref, x_s, pairs * span, None)], in_sems, True)
        forward_out = Stream(
            [
                (rows_out, rows_s, pairs * count, None),
                (gate_out, gate_s, pairs * count, None),
                (up_out, up_s, pairs * count, None),
                (hidden_out, hidden_s, pairs * count, None),
                (mix_out, mix_s, pairs * span, None),
            ],
            out_sems,
            False,
        )
        kept = [
            (all_ref, cols_s, pairs * span, pl.ds(wide - 128, 128)),
            (gate_out, gate_s, pairs * count, None),
            (up_out, up_s, pairs * count, None),
        ]
        back_kept = Stream(kept, in_sems, True)
        back_own = Stream([(own_grads_ref, x_s, pairs * span, None)], in_sems, True, 3)
        back_far = Stream([(all_grads_ref, x_s, pairs * span, None)], in_sems, True, 3)
        back_out = Stream(
            [
                (grad_rows_out, rows_s, pairs * count, None),
                (gate_grad_out, gate_gs, pairs * count, None),
                (up_grad_out, up_gs, pairs * count, None),
                (tokens_out, mix_s, pairs * span, None),
            ],
            out_sems,
            False,
        )
        down_sum[...] = jnp.zeros_like(down_sum)
        gate_sum[...] = jnp.zeros_like(gate_sum)
        up_sum[...] = jnp.zeros_like(up_sum)
        for slot in range(2):
            mix_s[slot, :, width:] = jnp.zeros((pairs * span, wide - width), low)
        spans = [pl.ds(pair * span, span) for pair in range(pairs)]

        def forward(slot):
            picks = [routed(x_s[slot, at, wide - 128 :], capacity) for at in spans]
            rows = jnp.concatenate(
                [contract(picks[k][0], x_s[slot, spans[k], :], 0, 0) for k in range(pairs)],
                axis=0,
            ).astype(low)
            rows_s[slot] = rows
            rows = rows[:, :width]
            gate_lin = contract(rows, pair_v[:share, :], 1, 1) + gate_b_ref[...].astype(f32)
            up_lin = contract(rows, pair_v[pad_share : pad_share + share, :], 1, 1) + up_b_ref[...].astype(f32)
            gate_s[slot] = gate_lin
            up_s[slot] = up_lin
            hidden = glu_units(gate_lin, up_lin).astype(low)
            hidden_s[slot] = hidden
            out = contract(hidden, down_v[...], 1, 0) + down_b_ref[...]
            for k in range(pairs):
                part = out[k * count : (k + 1) * count].astype(low)
                mix_s[slot, spans[k], :width] = contract(picks[k][1], part, 1, 0).astype(low)

        def backward(slot):
            picks = [routed(cols_s[slot, at, :], capacity) for at in spans]
            rows = jnp.concatenate(
                [contract(picks[k][1], x_s[slot, spans[k], :], 0, 0) for k in range(pairs)],
                axis=0,
            ).astype(low)
            rows_s[slot] = rows
            rows = rows[:, :width]
            down_sum[...] += jnp.sum(rows.astype(f32), axis=0, keepdims=True)
            grad_units = contract(rows, down_v[...], 1, 1)
            gate_tanh = jnp.tanh(gate_s[slot] / CLAMP_LIMIT)
            up_tanh = jnp.tanh(up_s[slot] / CLAMP_LIMIT)
            gated = CLAMP_LIMIT * gate_tanh
            lifted = CLAMP_LIMIT * up_tanh + 1.0
            part = jax.nn.sigmoid(GLU_ALPHA * gated)
            grad_up = (grad_units * gated * part * (1.0 - up_tanh * up_tanh)).astype(low)
            slope = part * (1.0 + GLU_ALPHA * gated * (1.0 - part))
            grad_gate = (grad_units * lifted * slope * (1.0 - gate_tanh * gate_tanh)).astype(low)
            gate_gs[slot] = grad_gate
            up_gs[slot] = grad_up
            gate_sum[...] += jnp.sum(grad_gate.astype(f32), axis=0, keepdims=True)
            up_sum[...] += jnp.sum(grad_up.astype(f32), axis=0, keepdims=True)
            both = jnp.concatenate([grad_gate, pad, grad_up, pad], axis=1)
            copies = contract(both, pair_v[...], 1, 0)
            for k in range(pairs):
                part = copies[k * count : (k + 1) * count].astype(low)
                mix_s[slot, spans[k], :width] = contract(picks[k][0], part, 1, 0).astype(low)

        ahead = Gather(line, sent_ref, all_ref, sems[:9], TAIL)
        back = Gather(line, sent_grads_ref, all_grads_ref, sems[9:], TAIL, own_grads_ref)
        y_at = ahead.me // 4

        def block(step):
            half = lax.rem(step, 2)
            return ahead.slot(step // 2) * 2 + (1 - half) * y_at + half * (1 - y_at)

        ahead.begin()

        steps = 2 * line

        def forward_order(order, carry):
            @pl.when(order < line)
            def _():
                ahead.second(order)
                pl.when(order + 1 < line)(lambda: ahead.first(order + 1))
                pl.when(order > 0)(lambda: ahead.tails(order))
                pl.when(order == 1)(back.begin_line)
                pl.when(order == 2)(back.send_tails)
                pl.when(order == line - 1)(lambda: back.first(1))
                ahead.near(order)

                @pl.when(order == 0)
                def _():
                    ahead.own_block()
                    for copy in held:
                        copy.wait()

                forward_in.start(0, block(2 * order))

            def half_plane(step, carry):
                slot = lax.rem(step, 2)
                forward_in.wait(slot, block(step))
                pl.when(step >= 2)(lambda: forward_out.wait(slot, block(step - 2)))
                forward(slot)
                forward_out.start(slot, block(step))
                return carry

            lax.fori_loop(
                jnp.maximum(2 * order - 1, 0), jnp.minimum(2 * order + 1, steps), half_plane, 0
            )

            @pl.when(order < line)
            def _():
                ahead.third(order)
                pl.when(order == 0)(ahead.send_tails)
                forward_in.start(1, block(2 * order + 1))

            return carry

        lax.fori_loop(0, line + 1, forward_order, 0)
        back.second(1)
        back.first(2)
        forward_out.wait(0, block(steps - 2))
        forward_out.wait(1, block(steps - 1))

        def grads_in(step, act):
            order, half = step // 2, lax.rem(step, 2)
            act(back_kept, half, block(step))
            pl.when(order == 0)(
                lambda: act(back_own, half, (1 - half) * y_at + half * (1 - y_at))
            )
            pl.when(order > 0)(lambda: act(back_far, half, block(step)))

        def backward_step(step, carry):
            order, half = step // 2, lax.rem(step, 2)
            pl.when(half == 1)(lambda: grads_in(step, Stream.start))

            @pl.when(step > 0)
            def _():
                slot = 1 - half
                pl.when(step >= 3)(lambda: back_out.wait(slot, block(step - 3)))
                grads_in(step - 1, Stream.wait)
                backward(slot)
                back_out.start(slot, block(step - 1))

            @pl.when((half == 0) & (order < line))
            def _():
                @pl.when(order > 0)
                def _():
                    back.tails(order)
                    back.near(order)
                    back.third(order)

                grads_in(step, Stream.start)

            @pl.when((half == 1) & (order > 0))
            def _():
                pl.when(order + 1 < line)(lambda: back.second(order + 1))
                pl.when(order + 2 < line)(lambda: back.first(order + 2))

            return carry

        lax.fori_loop(0, steps + 1, backward_step, 0)
        back_out.wait(0, block(steps - 2))
        back_out.wait(1, block(steps - 1))
        ahead.end()
        back.end(1)

    hbm = pl.BlockSpec(memory_space=pl.ANY)
    vmem = pl.BlockSpec(memory_space=pltpu.VMEM)

    def made(rows, columns, dtype=low):
        return jax.ShapeDtypeStruct((rows, columns), dtype)

    return pl.pallas_call(
        kernel,
        out_shape=(
            made(tokens, wide),
            made(tokens, wide),
            made(slot_rows, wide),
            made(slot_rows, share, f32),
            made(slot_rows, share, f32),
            made(slot_rows, share),
            made(tokens, wide),
            made(slot_rows, wide),
            made(slot_rows, share),
            made(slot_rows, share),
            made(tokens, wide),
            made(1, width, f32),
            made(1, share, f32),
            made(1, share, f32),
        ),
        in_specs=[hbm] * 6 + [vmem] * 3,
        out_specs=(hbm,) * 11 + (vmem,) * 3,
        scratch_shapes=[
            pltpu.VMEM((2 * pad_share, width), low),
            pltpu.VMEM(down_w.shape, low),
            two_of((pairs * span, wide), low),
            two_of((pairs * count, wide), low),
            two_of((pairs * count, share), f32),
            two_of((pairs * count, share), f32),
            two_of((pairs * count, share), low),
            two_of((pairs * span, wide), low),
            two_of((pairs * span, 128), low),
            two_of((pairs * count, share), low),
            two_of((pairs * count, share), low),
            pltpu.SemaphoreType.DMA((3,)),
            pltpu.SemaphoreType.DMA((2, 4)),
            pltpu.SemaphoreType.DMA((2, 5)),
            *gather_sems(line, TAIL),
            *gather_sems(line, TAIL),
        ],
        compiler_params=pltpu.CompilerParams(
            collective_id=collective, has_side_effects=True, vmem_limit_bytes=60 * MIB
        ),
        name="experts",
    )(sent, sent_grads, own_grads, gate_w, up_w, down_w, gate_b, up_b, down_b)


def expert_weights(parts, rows_in, gate_grad, up_grad, rows_grad, hidden, collective):
    low, f32 = jnp.bfloat16, jnp.float32
    slot_rows, wide = rows_in.shape
    share = gate_grad.shape[1]
    block_rows, width = parts.shape[0] // 32, parts.shape[1]
    cut = 256
    whole, rest = wide // cut, wide % cut
    count = whole + 1

    def kernel(
        parts_ref, rows_hbm, gate_hbm, up_hbm, grad_hbm, hidden_hbm, o_ref, gate_out, up_out, down_out,
        stage, first_t, second_t, in_s, first_s, second_s, held_sem, in_sems, out_sems, *scratch,
    ):
        def held(source):
            return pltpu.make_async_copy(source, stage, held_sem)

        held(gate_hbm).start()

        def begin(copy):
            copy.start()

        def await_it(copy):
            copy.wait()

        def by_width(index, act):
            pl.when((index >= 0) & (index < whole))(lambda: act(cut))
            pl.when(index == whole)(lambda: act(rest))

        def loads(chunk, act):
            slot = lax.rem(chunk, 2)
            for source, index in ((rows_hbm, chunk), (grad_hbm, chunk - count)):

                def one(columns):
                    at = pl.ds(pl.multiple_of(index * cut, cut), columns)
                    here = in_s.at[slot, :, pl.ds(0, columns)]
                    act(pltpu.make_async_copy(source.at[:, at], here, in_sems.at[slot]))

                by_width(index, one)

        def stores(chunk, act):
            slot = lax.rem(chunk, 2)
            for targets, index in (
                (((first_s, gate_out), (second_s, up_out)), chunk),
                (((first_s, down_out),), chunk - count),
            ):

                def one(columns):
                    at = pl.ds(pl.multiple_of(index * cut, cut), columns)
                    for k, (source, target) in enumerate(targets):
                        here = source.at[slot, :, pl.ds(0, columns)]
                        act(pltpu.make_async_copy(here, target.at[:, at], out_sems.at[slot, k]))

                by_width(index, one)

        def work(chunk):
            slot = lax.rem(chunk, 2)

            @pl.when(chunk == 0)
            def _():
                loads(0, begin)
                held(gate_hbm).wait()
                first_t[...] = stage[...].T
                held(up_hbm).start()
                held(up_hbm).wait()
                second_t[...] = stage[...].T
                held(hidden_hbm).start()

            @pl.when(chunk == count)
            def _():
                held(hidden_hbm).wait()
                first_t[...] = stage[...].T

            pl.when(chunk + 1 < 2 * count)(lambda: loads(chunk + 1, begin))
            pl.when(chunk >= 2)(lambda: stores(chunk - 2, await_it))
            loads(chunk, await_it)
            first_s[slot] = contract(first_t[...], in_s[slot], 1, 0).astype(low)

            @pl.when(chunk < count)
            def _():
                second_s[slot] = contract(second_t[...], in_s[slot], 1, 0).astype(low)

            stores(chunk, begin)

        def works(step):
            def body(chunk, carry):
                work(chunk)
                return carry

            lax.fori_loop(2 * step, 2 * step + 2, body, 0)

        Scatter(4, parts_ref, o_ref, scratch).run(works, count - 12)
        stores(2 * count - 2, await_it)
        stores(2 * count - 1, await_it)

    hbm = pl.BlockSpec(memory_space=pl.ANY)
    return pl.pallas_call(
        kernel,
        out_shape=(
            jax.ShapeDtypeStruct((block_rows, width), f32),
            jax.ShapeDtypeStruct((share, wide), low),
            jax.ShapeDtypeStruct((share, wide), low),
            jax.ShapeDtypeStruct((share, wide), low),
        ),
        in_specs=[hbm] * 6,
        out_specs=(hbm,) * 4,
        scratch_shapes=[
            pltpu.VMEM(gate_grad.shape, low),
            pltpu.VMEM(gate_grad.shape[::-1], low),
            pltpu.VMEM(gate_grad.shape[::-1], low),
            two_of((slot_rows, cut), low),
            two_of((share, cut), low),
            two_of((share, cut), low),
            pltpu.SemaphoreType.DMA,
            pltpu.SemaphoreType.DMA((2,)),
            pltpu.SemaphoreType.DMA((2, 2)),
            *scatter_scratch(4, block_rows, width, low),
        ],
        compiler_params=pltpu.CompilerParams(
            collective_id=collective, has_side_effects=True, vmem_limit_bytes=60 * MIB
        ),
        name="expert_weights",
    )(parts, rows_in, gate_grad, up_grad, rows_grad, hidden)


def product_kernel(left_ref, right_ref, out_ref):
    right = right_ref[:, : out_ref.shape[1]]
    out_ref[...] = contract(left_ref[...], right, 0, 0).astype(out_ref.dtype)


def product(left_t, right, name, columns=None):
    depth, rows = left_t.shape
    columns = columns or right.shape[1]
    return pl.pallas_call(
        product_kernel,
        grid=(rows // SPAN,),
        out_shape=jax.ShapeDtypeStruct((rows, columns), jnp.bfloat16),
        in_specs=[
            pl.BlockSpec((depth, SPAN), lambda i: (0, i)),
            pl.BlockSpec(right.shape, lambda i: (0, 0), pipeline_mode=pl.Buffered(1)),
        ],
        out_specs=pl.BlockSpec((SPAN, columns), lambda i: (i, 0)),
        compiler_params=pltpu.CompilerParams(vmem_limit_bytes=40 * MIB),
        cost_estimate=pl.CostEstimate(
            flops=2 * depth * rows * columns, bytes_accessed=4 * rows * columns, transcendentals=0
        ),
        name=name,
    )(left_t, right)


def finish_kernel(
    width, grads_ref, out_grads_ref, query_ref, key_ref, value_ref, query_b, key_b, value_b, out_ref
):
    grads = grads_ref[...].astype(jnp.float32)
    q_rows = query_ref.shape[1]
    kv_rows = key_ref.shape[0]
    query_ref[...] = grads[:q_rows, :width].T
    key_ref[...] = grads[q_rows : q_rows + kv_rows, :width]
    value_ref[...] = grads[q_rows + kv_rows :, :width]
    lane = width // 128 * 128
    bias = grads[:, lane : lane + 128].T[width - lane : width - lane + 1, :]
    query_b[...] = bias[:, :q_rows]
    key_b[...] = bias[:, q_rows : q_rows + kv_rows]
    value_b[...] = bias[:, q_rows + kv_rows :]
    out_ref[...] = out_grads_ref[...].astype(jnp.float32).T


def finished(grads, out_grads, q_rows):
    rows = grads.shape[0]
    width = out_grads.shape[1]
    kv_rows = (rows - q_rows) // 2
    vmem = pl.BlockSpec(memory_space=pltpu.VMEM)
    return pl.pallas_call(
        lambda *refs: finish_kernel(width, *refs),
        out_shape=tuple(
            jax.ShapeDtypeStruct(shape, jnp.float32)
            for shape in (
                (width, q_rows), (kv_rows, width), (kv_rows, width), (1, q_rows), (1, kv_rows),
                (1, kv_rows), (width, out_grads.shape[0]),
            )
        ),
        in_specs=[vmem] * 2,
        out_specs=(vmem,) * 7,
        compiler_params=pltpu.CompilerParams(vmem_limit_bytes=60 * MIB),
        name="finished",
    )(grads, out_grads)


def input_back(grad_lin, weights, normed, rows_in, gain, grad_rows, collective, small):
    low, f32 = jnp.bfloat16, jnp.float32
    depth, length = grad_lin.shape
    block_rows, width = rows_in.shape
    wide = normed.shape[1]
    columns = small.shape[1]
    gain_columns = -(-wide // (16 * 128)) * 128

    def kernel(
        lin_ref, weights_ref, normed_hbm, small_ref, rows_hbm, gain_ref, grad_hbm, o_ref, all_sums,
        result_ref,
        normed_v, part, found_v, sums_v, grad_v, rows_ref, grad_ref, late_sems, sem, *scratch,
    ):
        late = Moved(((rows_hbm, rows_ref), (grad_hbm, grad_ref)), late_sems)
        gather = Gather(4, sums_v, all_sums, scratch[:5])
        scatter = Scatter(1, part, o_ref, scratch[5:])
        loads = []
        for k in range(4):
            at = pl.ds(pl.multiple_of(scatter.places[k] // 2 * SPAN, SPAN), SPAN)
            loads.append(pltpu.make_async_copy(normed_hbm.at[at], normed_v.at[at], sem.at[k]))
            loads[k].start()
        greet((gather.mate, gather.near_x, gather.near_y), 4, gather.z_at)
        found_v[...] = jnp.zeros_like(found_v)
        late.start()

        def make(chip):
            at = pl.ds(pl.multiple_of(chip * SPAN, SPAN), SPAN)
            value = contract(lin_ref[:, at], weights_ref[...], 0, 0)
            part[at, :] = value[:, :width].astype(low)
            loads.pop(0).wait()
            found = value * normed_v[at, :].astype(f32)
            found_v[...] += jnp.sum(found, axis=0, keepdims=True)

        scatter.produce(make)
        sums_v[:, :columns] = small_ref[...]
        sums_v[:, columns:] = jnp.zeros((16, gain_columns), f32)
        for k in range(wide // 128):
            row, lane = k // (gain_columns // 128), k % (gain_columns // 128) * 128
            sums_v[row : row + 1, columns + lane : columns + lane + 128] = found_v[
                :, k * 128 : (k + 1) * 128
            ]
        gather.begin(True)
        for order in (1, 2, 3):
            gather.first(order)
        for order in range(4):
            gather.second(order)
        scatter.second(0)
        for order in range(4):
            gather.near(order)
            gather.third(order)
        scatter.third(0, scatter.total)

        late.wait()

        def through_norm(i, carry):
            at = pl.ds(pl.multiple_of(i * CHUNK, CHUNK), CHUNK)
            value = rows_ref[at, :].astype(f32)
            scale = lax.rsqrt(jnp.mean(value * value, axis=-1, keepdims=True) + EPSILON)
            grad = scatter.total[at, :] * gain_ref[...]
            inner = jnp.mean(grad * value, axis=-1, keepdims=True)
            grad_v[at, :] = (
                grad_ref[at, :] + grad * scale - value * (scale * scale * scale * inner)
            )
            return carry

        lax.fori_loop(0, block_rows // CHUNK, through_norm, 0)
        result_ref[...] = grad_v[...].T
        scatter.end()
        gather.own_block()
        gather.end()

    hbm = pl.BlockSpec(memory_space=pl.ANY)
    vmem = pl.BlockSpec(memory_space=pltpu.VMEM)
    return pl.pallas_call(
        kernel,
        out_shape=(
            jax.ShapeDtypeStruct((block_rows, width), f32),
            jax.ShapeDtypeStruct((32 * 16, columns + gain_columns), f32),
            jax.ShapeDtypeStruct((width, block_rows), f32),
        ),
        in_specs=[vmem, vmem, hbm, vmem, hbm, vmem, hbm],
        out_specs=(hbm, hbm, vmem),
        scratch_shapes=[
            pltpu.VMEM((length, wide), low),
            pltpu.VMEM((length, width), low),
            pltpu.VMEM((1, wide), f32),
            pltpu.VMEM((16, columns + gain_columns), f32),
            pltpu.VMEM((block_rows, width), f32),
            pltpu.VMEM((block_rows, width), low),
            pltpu.VMEM((block_rows, width), f32),
            pltpu.SemaphoreType.DMA((2,)),
            pltpu.SemaphoreType.DMA((4,)),
            *gather_sems(4),
            *scatter_scratch(1, block_rows, width, low),
        ],
        compiler_params=pltpu.CompilerParams(
            collective_id=collective, has_side_effects=True, vmem_limit_bytes=58 * MIB
        ),
        name="input_back",
    )(grad_lin, weights, normed, small, rows_in, gain, grad_rows)


def shards(
    layer_input, cotangent, gate_weights, routes, w_query, key_projection, value_projection, w_out,
    b_query, key_bias_vector, value_bias_vector, b_out, learned_sink_logits, gain_attn, gain_ffn,
    w_gate, w_up, w_down, b_gate, b_up, b_down,
):
    low = jnp.bfloat16
    ctx_n, z_n = lax.axis_size("ctx"), lax.axis_size("fsdp")
    ctx_at, z_at = lax.axis_index("ctx"), lax.axis_index("fsdp")
    tuned = ctx_n == 8 and z_n == 4
    width = layer_input.shape[-1]
    rows = layer_input.shape[0] * layer_input.shape[1]
    length = rows * ctx_n
    blocks = ctx_n * z_n
    capacity = max(2, rows * TOP * 17 // (16 * ctx_n))
    heads = QUERY_HEADS // ctx_n
    spread = ctx_n // KEY_VALUE_HEADS
    f32 = jnp.float32

    def gather_plane(value, call):
        if tuned:
            return gather_blocks(value, 1, call, f"gather_plane_{call}")
        return lax.all_gather(value, "ctx", axis=0, tiled=True)

    def scatter_plane(value, call):
        if tuned:
            return scatter_blocks(value, 1, call, f"scatter_plane_{call}")
        return lax.psum_scatter(value, "ctx", scatter_dimension=0, tiled=True).astype(f32)

    residual = layer_input.reshape(rows, width).astype(f32)
    grad_final = cotangent.reshape(rows, width)
    gain_attn_f, gain_ffn_f = gain_attn.astype(f32), gain_ffn.astype(f32)
    cosine, sine = rotary_tables(length)

    q_cols, k_cols = w_query.shape[1], key_projection.shape[1]
    own_rows = q_cols + 2 * k_cols
    wide = -(-(width + 2 * ctx_n) // 128) * 128
    biases = jnp.concatenate([b_query, key_bias_vector, value_bias_vector])
    own_weights = jnp.concatenate([w_query, key_projection, value_projection], axis=1).T
    own_weights = jnp.concatenate(
        [own_weights, biases[:, None], jnp.zeros((own_rows, wide - width - 1), low)], axis=1
    )
    ones = jnp.concatenate(
        [jnp.ones((rows, 1), low), jnp.zeros((rows, wide - width - 1), low)], axis=1
    )

    token_routes = routes.reshape(rows, TOP)
    names = jnp.arange(ctx_n, dtype=jnp.int32)
    named = token_routes[:, :, None] == names[None, None, :]
    hits = jnp.sum(named.astype(f32), axis=1)
    gates = jnp.sum(
        jnp.where(named, gate_weights.reshape(rows, TOP)[:, :, None].astype(f32), 0.0), axis=1
    )
    earlier = (
        lax.broadcasted_iota(jnp.int32, (rows, rows), 0)
        > lax.broadcasted_iota(jnp.int32, (rows, rows), 1)
    ).astype(low)
    places = jnp.dot(earlier, hits.astype(low), preferred_element_type=f32)
    first_slot = (lax.rem(ctx_at, PAIR) * capacity).astype(f32) if tuned else 0.0
    places = jnp.where(hits > 0, places + first_slot, -1.0)
    slot_rows = blocks * capacity
    if not tuned:
        slots = jnp.arange(capacity, dtype=f32)[None, :, None]
        picked = places.T[:, None, :] == slots
        select = picked.astype(low)
        mixing = jnp.where(picked, gates.T[:, None, :], 0.0).astype(low)

    def exchanged(slot_values):
        moved = slot_values.reshape(ctx_n, capacity, width)
        return lax.all_to_all(moved, "ctx", split_axis=0, concat_axis=0, tiled=True)

    def to_slots(picks, token_rows):
        dims = (((2,), (0,)), ((), ()))
        moved = lax.dot_general(picks, token_rows, dims, preferred_element_type=f32).astype(low)
        moved = lax.all_gather(exchanged(moved), "fsdp", axis=0, tiled=True)
        return moved.reshape(slot_rows, width)

    def to_tokens(picks, slot_values):
        slot_values = exchanged(
            lax.psum_scatter(slot_values, "fsdp", scatter_dimension=0, tiled=True)
        )
        dims = (((1,), (1,)), ((0,), (0,)))
        moved = lax.dot_general(picks, slot_values, dims, preferred_element_type=f32)
        return jnp.sum(moved, axis=0)

    normed_own = jnp.concatenate([norm_scale(residual, gain_attn_f).astype(low), ones], axis=1)
    sinks = lax.dynamic_slice(learned_sink_logits.astype(f32), (ctx_at * heads,), (heads,))
    swap = [(i, i ^ 1) for i in range(ctx_n)]
    odd = lax.rem(ctx_at, 2) == 1
    if tuned:
        sent_grads = jnp.pad(grad_final, ((0, 0), (0, wide - width)))
        branch, normed_attn, own_grads, head_weights, out_weights, *kept = attention(
            normed_own, sent_grads, own_weights, w_out, sinks, cosine, sine, 1
        )
        queries, keys, keys_t, values, attended, log_sums = kept
    else:
        normed_attn = lax.all_gather(normed_own, "ctx", axis=0, tiled=True)
        head_weights = lax.all_gather(own_weights, "fsdp", axis=0, tiled=True)
        out_weights = lax.all_gather(w_out, "fsdp", axis=0, tiled=True)
        lin = contract(head_weights, normed_attn, 1, 1).reshape(z_n, own_rows, length)
        query_lin = lin[:, :q_cols].reshape(heads, HEAD_SIZE, length)
        kv_lin = jnp.stack([lin[:, q_cols : q_cols + k_cols], lin[:, q_cols + k_cols :]])
        kv_lin = kv_lin.reshape(2, z_n * k_cols, length)
        if spread == 2:
            other = lax.ppermute(kv_lin, "ctx", swap)
            kv_lin = jnp.where(
                odd,
                jnp.concatenate([other, kv_lin], axis=1),
                jnp.concatenate([kv_lin, other], axis=1),
            )
        queries = turned(query_lin, cosine, sine).astype(low).reshape(heads * HEAD_SIZE, length)
        keys_t = turned(kv_lin[:1], cosine, sine)[0].astype(low)
        values_t = kv_lin[1].astype(low)
        keys, values = keys_t.T, values_t.T
        attended, log_sums = attend(sinks, queries, keys, values_t)
        branch = scatter_plane(product(attended, out_weights, "branch"), 2)
    middle = residual + branch + b_out.astype(f32)
    normed_ffn = norm_scale(middle, gain_ffn_f).astype(low)

    gate_w, up_w, down_w = w_gate[0].T, w_up[0].T, w_down[0]
    share = b_down.shape[1]
    down_bias = lax.dynamic_update_slice(
        jnp.zeros((1, width), f32), b_down.astype(f32), (0, z_at * share)
    )
    if tuned:
        sent = jnp.concatenate(
            [
                normed_ffn,
                places.astype(low),
                gates.astype(low),
                jnp.zeros((rows, wide - width - 2 * ctx_n), low),
            ],
            axis=1,
        )
        made = experts(
            sent, sent_grads, own_grads, gate_w, up_w, down_w, b_gate, b_up, down_bias, capacity, 3
        )
        expert_in, hidden_units, mix_part = made[2], made[5], made[6]
        grad_expert_out, grad_gate_lin, grad_up_lin, grad_normed_part = made[7:11]
        grad_biases = made[11:]
        grad_b_down, grad_b_gate, grad_b_up = [value[0] for value in grad_biases]
        grad_normed_ffn, grad_w_gate, grad_w_up, grad_w_down = expert_weights(
            grad_normed_part, expert_in, grad_gate_lin, grad_up_lin, grad_expert_out, hidden_units, 6
        )
        grad_normed_ffn = grad_normed_ffn[:, :width]
    else:
        expert_in = to_slots(select, normed_ffn)
        gate_lin = contract(expert_in, gate_w, 1, 1) + b_gate.astype(f32)
        up_lin = contract(expert_in, up_w, 1, 1) + b_up.astype(f32)
        hidden_f, unit_back = jax.vjp(glu_units, gate_lin, up_lin)
        hidden_units = hidden_f.astype(low)
        expert_out = (contract(hidden_units, down_w, 1, 0) + down_bias).astype(low)
        expert_mix = to_tokens(mixing, expert_out)
        grad_expert_out = to_slots(mixing, grad_final)
        grad_units = contract(grad_expert_out, down_w, 1, 1)
        grad_gate_f, grad_up_f = unit_back(grad_units)
        grad_gate_lin, grad_up_lin = grad_gate_f.astype(low), grad_up_f.astype(low)
        grad_copy = contract(grad_gate_lin, gate_w, 1, 0) + contract(grad_up_lin, up_w, 1, 0)
        grad_normed_ffn = to_tokens(select, grad_copy.astype(low))
        grad_b_down = jnp.sum(grad_expert_out.astype(f32), axis=0)
        grad_b_gate = jnp.sum(grad_gate_lin.astype(f32), axis=0)
        grad_b_up = jnp.sum(grad_up_lin.astype(f32), axis=0)
        grad_w_gate = contract(grad_gate_lin, expert_in, 0, 0)
        grad_w_up = contract(grad_up_lin, expert_in, 0, 0)
        grad_w_down = contract(hidden_units, grad_expert_out, 0, 0)
    grad_b_down = lax.dynamic_slice(grad_b_down, (z_at * share,), (share,))

    unused, norm_back = jax.vjp(norm_scale, middle, gain_ffn_f)
    grad_middle_part, grad_gain_ffn = norm_back(grad_normed_ffn)
    grad_middle = grad_final.astype(f32) + grad_middle_part
    grad_branch_own = grad_middle.astype(low)
    grad_b_out = jnp.sum(grad_branch_own.astype(f32), axis=0)
    if tuned:
        early = 1024
        first_mix, grad_attended, grad_out_part = branch_back(
            mix_part, early, grad_branch_own, out_weights, attended, 7
        )
        late_mix, grad_lin, grad_weights, grad_sink_parts = attention_back(
            mix_part, early, sinks, queries, keys, keys_t, values, grad_attended, log_sums, cosine,
            sine, normed_attn, own_rows, 5,
        )
        expert_mix = jnp.concatenate([first_mix, late_mix[:, : width - early]], axis=1)
    else:
        grad_branch = lax.all_gather(grad_branch_own, "ctx", axis=0, tiled=True)
        grad_attended = contract(out_weights, grad_branch, 1, 1).astype(low)
        grad_out_part = contract(attended, grad_branch, 1, 0).astype(low)
        grad_query, grad_keys, grad_values, grad_sink_parts = attend_back(
            sinks, queries, keys, keys_t, values, grad_attended, log_sums, cosine, sine
        )
        grad_kv = jnp.stack([turned(grad_keys.T[None], cosine, -sine)[0], grad_values.T])
        if spread == 2:
            grad_kv = grad_kv + lax.ppermute(grad_kv, "ctx", swap)
            halves = grad_kv.reshape(2, 2, HEAD_SIZE // 2, length)
            grad_kv = jnp.where(odd, halves[:, 1], halves[:, 0])
        grad_kv = grad_kv.astype(low).reshape(2, z_n, k_cols, length)
        grad_lin = jnp.concatenate(
            [grad_query.reshape(z_n, q_cols, length), grad_kv[0], grad_kv[1]], axis=1
        ).reshape(z_n * own_rows, length)
        grad_weights = contract(grad_lin, normed_attn, 1, 0).astype(low)
    final_out = (middle + expert_mix).astype(low).reshape(layer_input.shape)
    own_out_grads = lax.psum_scatter(grad_out_part, "fsdp", scatter_dimension=0, tiled=True)
    own_grads = lax.psum_scatter(grad_weights, "fsdp", scatter_dimension=0, tiled=True)
    if tuned:
        grad_w_query, grad_w_key, grad_w_value, *own_bias_grads, grad_w_out = finished(
            own_grads, own_out_grads, q_cols
        )
        own_bias_grads, grad_w_out = [value[0] for value in own_bias_grads], grad_w_out.T
    else:
        own_grads = own_grads.astype(f32)
        grad_w_out = own_out_grads.astype(f32)
        grad_w_query = own_grads[:q_cols, :width].T
        grad_w_key = own_grads[q_cols : q_cols + k_cols, :width]
        grad_w_value = own_grads[q_cols + k_cols :, :width]
        own_bias_grads = jnp.split(own_grads[:, width], (q_cols, q_cols + k_cols))
    grad_w_key, grad_w_value = grad_w_key.T, grad_w_value.T
    grad_sinks = lax.dynamic_update_slice(
        jnp.zeros((QUERY_HEADS,), f32), jnp.sum(grad_sink_parts, axis=(1, 2)), (ctx_at * heads,)
    )
    sums = (grad_b_out, grad_gain_ffn, grad_sinks)
    if tuned:
        joined = jnp.concatenate(sums)
        columns = -(-joined.shape[0] // (16 * 128)) * 128
        joined = jnp.pad(joined, (0, 16 * columns - joined.shape[0])).reshape(16, columns)
        unused, joined, input_grad = input_back(
            grad_lin, head_weights, normed_attn, layer_input.reshape(rows, width),
            gain_attn_f.reshape(1, width), grad_middle, 8, joined,
        )
        input_grad = input_grad.T.reshape(layer_input.shape)
        joined = jnp.sum(joined.reshape(blocks, 16, -1), axis=0)
        grad_gain_attn = joined[:, columns:].reshape(-1)[:width] / gain_attn_f
        joined = joined[:, :columns].reshape(-1)
        cuts = (width, 2 * width, 2 * width + QUERY_HEADS)
        sums = [joined[at - value.shape[0] : at] for at, value in zip(cuts, sums)]
    else:
        grad_normed_part = product(grad_lin, head_weights, "grad_normed", width)
        grad_normed_attn = scatter_plane(grad_normed_part, 8)
        unused, norm_back = jax.vjp(norm_scale, residual, gain_attn_f)
        grad_residual_part, own_gain = norm_back(grad_normed_attn)
        input_grad = (grad_middle + grad_residual_part).reshape(layer_input.shape)
        *sums, grad_gain_attn = lax.psum((*sums, own_gain), ("ctx", "fsdp"))
    grad_b_out, grad_gain_ffn, grad_sink_logits = sums
    return (
        final_out,
        input_grad,
        grad_w_query,
        grad_w_key,
        grad_w_value,
        grad_w_out,
        *own_bias_grads,
        grad_b_out,
        grad_sink_logits,
        grad_gain_attn,
        grad_gain_ffn,
        grad_w_gate[:, :width].astype(f32).T[None],
        grad_w_up[:, :width].astype(f32).T[None],
        grad_w_down[:, :width].astype(f32)[None],
        grad_b_gate[None],
        grad_b_up[None],
        grad_b_down[None],
    )


def solution(mesh):
    return jax.shard_map(
        shards,
        mesh=mesh,
        in_specs=(
            P("fsdp", "ctx", None),
            P("fsdp", "ctx", None),
            P("fsdp", "ctx", None),
            P("fsdp", "ctx", None),
            P(None, ("ctx", "fsdp")),
            P(None, ("ctx", "fsdp")),
            P(None, ("ctx", "fsdp")),
            P(("ctx", "fsdp"), None),
            P(("ctx", "fsdp")),
            P(("ctx", "fsdp")),
            P(("ctx", "fsdp")),
            P(),
            P(),
            P(),
            P(),
            P("ctx", None, "fsdp"),
            P("ctx", None, "fsdp"),
            P("ctx", "fsdp", None),
            P("ctx", "fsdp"),
            P("ctx", "fsdp"),
            P("ctx", "fsdp"),
        ),
        out_specs=(
            P("fsdp", "ctx", None),
            P("fsdp", "ctx", None),
            P(None, ("ctx", "fsdp")),
            P(None, ("ctx", "fsdp")),
            P(None, ("ctx", "fsdp")),
            P(("ctx", "fsdp"), None),
            P(("ctx", "fsdp")),
            P(("ctx", "fsdp")),
            P(("ctx", "fsdp")),
            P(),
            P(),
            P(),
            P(),
            P("ctx", None, "fsdp"),
            P("ctx", None, "fsdp"),
            P("ctx", "fsdp", None),
            P("ctx", "fsdp"),
            P("ctx", "fsdp"),
            P("ctx", "fsdp"),
        ),
        check_vma=False,
    )
```
